32 devices in a mesh: req: 8 (over z, y), tp: 4 (over x, core).
Axes of the slice: x: 2, y: 2, z: 4, core: 2. Of those that a mesh axis runs over, the one named last changes fastest.
Arguments:
- states: bfloat16 [16, 512, 1024], P('req', 'tp'), may hold values from -45 to 45
- lengths: int32 [16], P('req'), may hold values from 3 to 512, as said below
- w_qkv: bfloat16 [1024, 3, 1024], P(None, None, 'tp'), may hold values from -0.1875 to 0.1875
- b_qkv: float32 [3, 1024], P(None, 'tp'), may hold values from -3 to 3
- w_out: bfloat16 [1024, 1024], P('tp'), may hold values from -0.1875 to 0.1875
- b_out: float32 [1024], replicated, may hold values from -3 to 3
- ln1_gain: float32 [1024], replicated, may hold values from 0.1 to 1.9
- ln1_shift: float32 [1024], replicated, may hold values from -3 to 3
- w_up: bfloat16 [1024, 4096], P(None, 'tp'), may hold values from -0.1875 to 0.1875
- b_up: float32 [4096], P('tp'), may hold values from -3 to 3
- w_down: bfloat16 [4096, 1024], P('tp'), may hold values from -0.09375 to 0.09375
- b_down: float32 [1024], replicated, may hold values from -3 to 3
- ln2_gain: float32 [1024], replicated, may hold values from 0.1 to 1.9
- ln2_shift: float32 [1024], replicated, may hold values from -3 to 3
- index_rows: bfloat16 [131072, 1024], P(('req', 'tp')), may hold values from -0.1875 to 0.1875
- cand_ids: int32 [16, 64], P('req', 'tp'), may hold values from 0 to 131071
Outputs:
- hidden_out: bfloat16 [16, 512, 1024], P('req', 'tp')
- scores: float32 [16, 64], P('req', 'tp')
The draws below stay inside these ranges and needn't reach their ends.
Inputs may be any that keep to these rules, and one draw needn't show every extreme that they name: Valid positions are the first lengths ones of a text; in every draw some text has 512.
All inputs are finite; a program needn't handle non-finite values.
Results may differ from the reference program's by a relative error of at most 0.015.
Values may be sent and summed in bfloat16 or wider, within the bound.
No kernel may reach another device: no remote copies, remote signals or barrier semaphores. Data moves between devices by JAX's collectives and lax.ppermute only.
A program may use at most 128 MiB of HBM per device.

```python
import jax
import jax.numpy as jnp
from jax import lax

D = 1024
HEADS = 16
HEAD_DIM = 64
FF = 4096
WINDOW = 512
SEQ = 512
CANDS = 64
TEXTS_ALL = 16
INDEX = 131072
N_TP = 4


def draw_states(key, part):
    key_base = jax.random.fold_in(key, 0)
    return jnp.clip(jax.random.normal(key_base, (TEXTS_ALL, SEQ, D), jnp.float32), -6.0, 6.0).astype(jnp.bfloat16)


def draw_lengths(key, part):
    key_len, key_pick = jax.random.split(key, 2)
    drawn = jax.random.randint(key_len, (TEXTS_ALL,), 3, SEQ + 1, dtype=jnp.int32)
    chosen = jax.random.randint(key_pick, (), 0, TEXTS_ALL, dtype=jnp.int32)
    return jnp.where(jnp.arange(TEXTS_ALL, dtype=jnp.int32) == chosen, jnp.int32(SEQ), drawn).astype(jnp.int32)


def plant(values, stream_key, low, largest):
    extent = values.shape
    index_at = [jax.random.randint(jax.random.fold_in(stream_key, axis), (), 0, extent[axis]) for axis in range(len(extent))]
    values = values.at[tuple(index_at)].set(low)
    longest = extent.index(max(extent))
    index_at[longest] = (index_at[longest] + 1) % extent[longest]
    return values.at[tuple(index_at)].set(largest)


def shard_levels(key, shape, shards, low, largest):
    def one(position, blocks):
        draws = jax.random.uniform(jax.random.fold_in(jax.random.fold_in(key, 6), position), (blocks,), jnp.float32, low / len(shards), largest / len(shards))
        return jnp.repeat(jnp.exp(draws), shape[position] // blocks).reshape((-1,) + (1,) * (len(shape) - position - 1))

    level = one(*shards[0])
    for cut in shards[1:]:
        level = level * one(*cut)
    return level


def noise(rng, extent, scale, reach, cuts=(), kind=jnp.bfloat16):
    result = scale * jax.random.normal(rng, extent, jnp.float32)
    if cuts:
        result = result * shard_levels(rng, extent, cuts, -0.22, 0.18)
    return jnp.clip(result, -reach, reach).astype(kind)


def setup_inputs(seed: int = 0) -> dict:
    keys = jax.random.split(jax.random.key(seed), 17)
    states = draw_states(jax.random.fold_in(keys[16], 71), 0)
    lengths = draw_lengths(jax.random.fold_in(keys[16], 71), 0)
    w_qkv = noise(keys[2], (D, 3, D), D ** -0.5, 0.1875, ((2, 4),))
    b_qkv = noise(keys[3], (3, D), 0.5, 3.0, ((1, 4),), jnp.float32)
    w_out = noise(keys[4], (D, D), D ** -0.5, 0.1875, ((0, 4),))
    b_out = noise(keys[5], (D,), 0.5, 3.0, (), jnp.float32)
    ln1_gain = jnp.clip(1.0 + 0.18 * jax.random.normal(keys[6], (D,), jnp.float32), 0.1, 1.9)
    ln1_shift = noise(keys[7], (D,), 0.5, 3.0, (), jnp.float32)
    w_up = noise(keys[8], (D, FF), D ** -0.5, 0.1875, ((1, 4),))
    b_up = noise(keys[9], (FF,), 0.5, 3.0, ((0, 4),), jnp.float32)
    w_down = noise(keys[10], (FF, D), FF ** -0.5, 0.09375, ((0, 4),))
    b_down = noise(keys[11], (D,), 0.5, 3.0, (), jnp.float32)
    ln2_gain = jnp.clip(1.0 + 0.18 * jax.random.normal(keys[12], (D,), jnp.float32), 0.1, 1.9)
    ln2_shift = noise(keys[13], (D,), 0.5, 3.0, (), jnp.float32)
    index_rows = noise(keys[14], (INDEX, D), D ** -0.5, 0.1875, ((0, 32),))
    cand_ids = plant(jax.random.randint(keys[15], (TEXTS_ALL, CANDS), 0, INDEX), jax.random.fold_in(keys[15], 1), 0, INDEX - 1).astype(jnp.int32)
    return {"states": states, "lengths": lengths, "w_qkv": w_qkv, "b_qkv": b_qkv, "w_out": w_out, "b_out": b_out, "ln1_gain": ln1_gain, "ln1_shift": ln1_shift, "w_up": w_up, "b_up": b_up, "w_down": w_down, "b_down": b_down, "ln2_gain": ln2_gain, "ln2_shift": ln2_shift, "index_rows": index_rows, "cand_ids": cand_ids}


layer_eps = 1e-05
norm_eps = 1e-06

def layer_norm(values, gain, shift):
    centre = values - lax.optimization_barrier(jnp.mean(values, axis=-1, keepdims=True))
    spread = lax.optimization_barrier(jnp.mean(centre * centre, axis=-1, keepdims=True))
    return centre * lax.rsqrt(spread + layer_eps) * gain + shift

def window_attention(queries_h, keys_h, values_h, length):
    seq_len = queries_h.shape[0]
    half_window = WINDOW // 2
    padding = ((half_window, half_window), (0, 0), (0, 0))
    keys_padded = jnp.pad(keys_h, padding)
    values_padded = jnp.pad(values_h, padding)
    scale_factor = HEAD_DIM ** (-0.5)

    def one_block(block_idx):
        blk_start = block_idx * WINDOW
        query_blk = lax.dynamic_slice_in_dim(queries_h, blk_start, WINDOW, 0)
        key_blk = lax.dynamic_slice_in_dim(keys_padded, blk_start, 2 * WINDOW, 0)
        value_blk = lax.dynamic_slice_in_dim(values_padded, blk_start, 2 * WINDOW, 0)
        query_pos = blk_start + jnp.arange(WINDOW, dtype=jnp.int32)
        key_pos = blk_start - half_window + jnp.arange(2 * WINDOW, dtype=jnp.int32)
        keep_mask = (jnp.abs(query_pos[:, None] - key_pos[None, :]) <= half_window) & (key_pos[None, :] >= 0) & (key_pos[None, :] < length)
        logits = jnp.einsum('qhe,khe->hqk', query_blk.astype(jnp.float32), key_blk.astype(jnp.float32)) * scale_factor
        logits = jnp.where(keep_mask[None], logits, jnp.float32(-1e+30))
        top_val = lax.optimization_barrier(jnp.max(logits, axis=-1, keepdims=True))
        expo = jnp.exp(logits - top_val)
        attn_weights = (expo / lax.optimization_barrier(jnp.sum(expo, axis=-1, keepdims=True))).astype(jnp.bfloat16)
        context = jnp.einsum('hqk,khe->qhe', attn_weights.astype(jnp.float32), value_blk.astype(jnp.float32))
        context = jnp.where((query_pos < length)[:, None, None], context, jnp.float32(0.0))
        return context.astype(jnp.bfloat16)
    blocks = lax.map(one_block, jnp.arange(seq_len // WINDOW, dtype=jnp.int32))
    return blocks.reshape(seq_len, HEADS * HEAD_DIM)

def group_sum(left, right, groups):
    seq_len = left.shape[0]
    inner = left.shape[1] // groups
    partial_value = jnp.einsum('sgk,gkd->gsd', left.reshape(seq_len, groups, inner).astype(jnp.float32), right.reshape(groups, inner, right.shape[1]).astype(jnp.float32))
    rounded = lax.optimization_barrier(partial_value.astype(jnp.bfloat16))
    return lax.optimization_barrier(jnp.sum(rounded.astype(jnp.float32), axis=0))

def reference(states, lengths, w_qkv, b_qkv, w_out, b_out, ln1_gain, ln1_shift, w_up, b_up, w_down, b_down, ln2_gain, ln2_shift, index_rows, cand_ids):

    def text_layer(pair):
        text_states, length = pair
        projected = jnp.einsum('sd,dce->sce', text_states.astype(jnp.float32), w_qkv.astype(jnp.float32)) + b_qkv
        projected = projected.astype(jnp.bfloat16)
        seq_len = text_states.shape[0]
        queries_h = projected[:, 0].reshape(seq_len, HEADS, HEAD_DIM)
        keys_h = projected[:, 1].reshape(seq_len, HEADS, HEAD_DIM)
        values_h = projected[:, 2].reshape(seq_len, HEADS, HEAD_DIM)
        context = window_attention(queries_h, keys_h, values_h, length)
        attn_sum = group_sum(context, w_out, N_TP)
        normed = layer_norm(text_states.astype(jnp.float32) + attn_sum + b_out, ln1_gain, ln1_shift).astype(jnp.bfloat16)
        up_act = jax.nn.gelu(jnp.dot(normed, w_up, preferred_element_type=jnp.float32) + b_up, approximate=False).astype(jnp.bfloat16)
        down_sum = group_sum(up_act, w_down, N_TP)
        return layer_norm(normed.astype(jnp.float32) + down_sum + b_down, ln2_gain, ln2_shift).astype(jnp.bfloat16)
    hidden_out = lax.map(text_layer, (states, lengths))
    is_valid = jnp.arange(SEQ, dtype=jnp.int32)[None, :] < lengths[:, None]
    pooled = lax.optimization_barrier(jnp.sum(jnp.where(is_valid[:, :, None], hidden_out.astype(jnp.float32), jnp.float32(0.0)), axis=1)) / lengths.astype(jnp.float32)[:, None]
    query_vec = (pooled * lax.rsqrt(lax.optimization_barrier(jnp.mean(pooled * pooled, axis=-1, keepdims=True)) + norm_eps)).astype(jnp.bfloat16)
    cand_rows = jnp.take(index_rows, cand_ids, axis=0)
    scores = jnp.einsum('td,tcd->tc', query_vec.astype(jnp.float32), cand_rows.astype(jnp.float32))
    return (hidden_out, scores)
```

```python
import jax
import jax.numpy as jnp
from jax import lax
from jax.sharding import PartitionSpec as P

HEAD_DIM = 64
WINDOW = 512
BF16 = jnp.bfloat16
F32 = jnp.float32

layer_eps = 1e-05
norm_eps = 1e-06


def layer_norm(values, gain, shift):
    centre = values - jnp.mean(values, axis=-1, keepdims=True)
    spread = jnp.mean(centre * centre, axis=-1, keepdims=True)
    return centre * lax.rsqrt(spread + layer_eps) * gain + shift


def swap(value, axis, bit):
    count = lax.axis_size(axis)
    return lax.ppermute(value, axis, [(i, i ^ bit) for i in range(count)])


def gather_ids(cand_ids):
    held = cand_ids[None]
    for axis in ("tp", "req"):
        bit = 1
        while bit < lax.axis_size(axis):
            other = swap(held, axis, bit)
            upper = (lax.axis_index(axis) & bit) != 0
            held = jnp.where(
                upper, jnp.concatenate([other, held]), jnp.concatenate([held, other])
            )
            bit *= 2
    return held


def per_device(
    states,
    lengths,
    w_qkv,
    b_qkv,
    w_out,
    b_out,
    ln1_gain,
    ln1_shift,
    w_up,
    b_up,
    w_down,
    b_down,
    ln2_gain,
    ln2_shift,
    index_rows,
    cand_ids,
):
    rank = lax.axis_index("tp")
    core = rank & 1
    text_count, row_share, width = states.shape
    local_width = w_qkv.shape[2]
    heads_here = local_width // HEAD_DIM
    half = 2 * row_share
    seq_len = 4 * row_share

    mine = lax.dynamic_index_in_dim(states, core, 0, keepdims=False)
    theirs = lax.dynamic_index_in_dim(states, 1 - core, 0, keepdims=False)
    length = lax.dynamic_index_in_dim(lengths, core, 0, keepdims=False)
    from_core = swap(theirs, "tp", 1)
    from_chip = swap(mine, "tp", 2)
    from_diag = swap(theirs, "tp", 3)
    w_qkv_t = w_qkv.transpose(1, 0, 2)
    w_qkv_p = swap(w_qkv_t, "tp", 1)
    small = jnp.concatenate([b_qkv.reshape(-1), b_up])
    small_p = swap(small, "tp", 1)
    ids = gather_ids(cand_ids)
    w_up_p = swap(w_up, "tp", 1)
    w_down_p = swap(w_down, "tp", 1)

    text = jnp.concatenate([mine, from_core, from_chip, from_diag])
    w_out_p = swap(w_out, "tp", 1)
    w_out_late, _ = lax.optimization_barrier((w_out, text))
    w_out_x = swap(w_out_late, "tp", 2)
    w_out_d = swap(w_out_x, "tp", 1)

    rows_here = index_rows.shape[0]
    first_row = (lax.axis_index("req") * 4 + rank) * rows_here
    local_ids = ids.reshape(-1) - first_row
    is_owned = (local_ids >= 0) & (local_ids < rows_here)
    fetched = jnp.take(index_rows, jnp.clip(local_ids, 0, rows_here - 1), axis=0)
    fetched = jnp.where(is_owned[:, None], fetched, jnp.zeros((), BF16))
    rows = lax.psum_scatter(fetched, ("req", "tp"), scatter_dimension=0, tiled=True)

    w_all = jnp.concatenate([w_qkv_t, w_qkv_p], axis=2)
    b_all = jnp.concatenate(
        [b_qkv, small_p[: 3 * local_width].reshape(3, local_width)], axis=1
    )
    projected = (
        jnp.einsum("sd,cde->cse", text, w_all, preferred_element_type=F32) + b_all[:, None]
    ).astype(BF16)
    parts = projected.reshape(3, seq_len, 2 * heads_here, HEAD_DIM)
    block = jnp.arange(4, dtype=jnp.int32) ^ rank
    pos = (block[:, None] * row_share + jnp.arange(row_share, dtype=jnp.int32)).reshape(-1)
    keep = (jnp.abs(pos[:, None] - pos[None, :]) <= WINDOW // 2) & (pos[None, :] < length)
    logits = jnp.einsum("qhe,khe->hqk", parts[0], parts[1], preferred_element_type=F32)
    logits = jnp.where(keep[None], logits * HEAD_DIM**-0.5, F32(-1e30))
    expo = jnp.exp(logits - jnp.max(logits, axis=-1, keepdims=True))
    weights = (expo / jnp.sum(expo, axis=-1, keepdims=True)).astype(BF16)
    context = jnp.einsum("hqk,khe->qhe", weights, parts[2], preferred_element_type=F32)
    context = jnp.where((pos < length)[:, None, None], context, F32(0.0)).astype(BF16)
    context = context.reshape(seq_len, 2 * local_width)
    context_x = swap(context, "tp", 2)
    context_x = jnp.concatenate([context_x[half:], context_x[:half]])

    w_out_here = jnp.concatenate([w_out, w_out_p])
    w_out_there = jnp.concatenate([w_out_x, w_out_d])
    attn_sum = jnp.dot(context, w_out_here, preferred_element_type=F32)
    attn_sum = attn_sum + jnp.dot(context_x, w_out_there, preferred_element_type=F32)
    normed = layer_norm(text.astype(F32) + attn_sum + b_out, ln1_gain, ln1_shift).astype(BF16)

    w_up_all = jnp.concatenate([w_up, w_up_p], axis=1)
    b_up_all = jnp.concatenate([b_up, small_p[3 * local_width :]])
    w_down_all = jnp.concatenate([w_down, w_down_p])

    def feed_forward(rows_in):
        up = jnp.dot(rows_in, w_up_all, preferred_element_type=F32) + b_up_all
        act = jax.nn.gelu(up, approximate=False).astype(BF16)
        return jnp.dot(act, w_down_all, preferred_element_type=F32)

    down_there = feed_forward(normed[half:]).astype(BF16)
    down_x = swap(down_there, "tp", 2)
    down_here = feed_forward(normed[:half])
    down_sum = down_here + down_x.astype(F32)
    hidden = layer_norm(
        normed[:half].astype(F32) + down_sum + b_down, ln2_gain, ln2_shift
    ).astype(BF16)

    valid = (pos[:half] < length)[:, None]
    pool = jnp.sum(jnp.where(valid, hidden.astype(F32), F32(0.0)), axis=0)
    hidden_p = swap(hidden[row_share:], "tp", 1)
    hidden_out = jnp.where(
        core == 0,
        jnp.stack([hidden[:row_share], hidden_p]),
        jnp.stack([hidden_p, hidden[:row_share]]),
    )
    pool_core = swap(pool, "tp", 1)
    pool_chip = swap(pool, "tp", 2)
    pool_diag = swap(pool, "tp", 3)
    pool_mine = pool + pool_chip
    pool_theirs = pool_core + pool_diag
    pools = jnp.where(
        core == 0, jnp.stack([pool_mine, pool_theirs]), jnp.stack([pool_theirs, pool_mine])
    )
    pooled = pools / lengths.astype(F32)[:, None]
    query_vec = (
        pooled * lax.rsqrt(jnp.mean(pooled * pooled, axis=-1, keepdims=True) + norm_eps)
    ).astype(BF16)
    rows = rows.reshape(text_count, -1, width)
    scores = jnp.einsum("td,tcd->tc", query_vec, rows, preferred_element_type=F32)
    return (hidden_out, scores)


def solution(mesh):
    placed = (
        P("req", "tp", None),
        P("req"),
        P(None, None, "tp"),
        P(None, "tp"),
        P("tp", None),
        P(),
        P(),
        P(),
        P(None, "tp"),
        P("tp"),
        P("tp", None),
        P(),
        P(),
        P(),
        P(("req", "tp"), None),
        P("req", "tp"),
    )
    return jax.shard_map(
        per_device,
        mesh=mesh,
        in_specs=placed,
        out_specs=(P("req", "tp", None), P("req", "tp")),
        check_vma=False,
    )
```

```python
import jax
import jax.numpy as jnp
from jax import lax
from jax.experimental import pallas as pl
from jax.experimental.pallas import tpu as pltpu
from jax.sharding import PartitionSpec as P

HEAD_DIM = 64
WINDOW = 512
SLOTS = 16
BF16 = jnp.bfloat16
F32 = jnp.float32
I32 = jnp.int32
VMEM_LIMIT = 56 * 1024 * 1024

layer_eps = 1e-05
norm_eps = 1e-06

VMEM = pl.BlockSpec(memory_space=pltpu.VMEM)
SMEM = pl.BlockSpec(memory_space=pltpu.SMEM)
HBM = pl.BlockSpec(memory_space=pl.ANY)


def layer_norm(values, gain, shift):
    centre = values - jnp.mean(values, axis=-1, keepdims=True)
    spread = jnp.mean(centre * centre, axis=-1, keepdims=True)
    return centre * lax.rsqrt(spread + layer_eps) * gain + shift


def swap(value, axis, mask):
    count = lax.axis_size(axis)
    return lax.ppermute(value, axis, [(i, i ^ mask) for i in range(count)])


def matmul(left, right):
    return jnp.dot(left, right, preferred_element_type=F32)


def params(**kwargs):
    return pltpu.CompilerParams(vmem_limit_bytes=VMEM_LIMIT, **kwargs)


def split_kernel(meta, states, mine, theirs, sems):
    core = meta[1]
    first = pltpu.make_async_copy(states.at[core], mine, sems.at[0])
    second = pltpu.make_async_copy(states.at[1 - core], theirs, sems.at[1])
    first.start()
    second.start()
    first.wait()
    second.wait()


def split_texts(meta, states):
    block = jax.ShapeDtypeStruct(states.shape[1:], states.dtype)
    return pl.pallas_call(
        split_kernel,
        out_shape=(block, block),
        in_specs=[SMEM, HBM],
        out_specs=(HBM, HBM),
        scratch_shapes=[pltpu.SemaphoreType.DMA((2,))],
        compiler_params=params(),
        name="split_texts",
    )(meta, states)


def attention_kernel(meta, s0, s1, s2, s3, w, b, out, bias):
    rank = meta[0]
    length = meta[2]
    share = s0.shape[0]
    seq_len = 4 * share
    wide = w.shape[2]
    text = jnp.concatenate([s0[...], s1[...], s2[...], s3[...]])

    def project(which):
        return (matmul(text, w[which]) + b[which : which + 1, :]).astype(BF16)

    queries = project(0) * jnp.asarray(HEAD_DIM**-0.5, BF16)
    keys = project(1)
    values = project(2)

    def position(index):
        return ((index // share) ^ rank) * share + index % share

    row_pos = position(lax.broadcasted_iota(I32, (seq_len, 1), 0))
    col_pos = position(lax.broadcasted_iota(I32, (1, seq_len), 1))
    keep = (jnp.abs(row_pos - col_pos) <= WINDOW // 2) & (col_pos < length)
    bias[...] = jnp.where(keep, F32(0.0), F32(-1e30))
    ones = jnp.ones((seq_len, 128), BF16)
    low = lax.broadcasted_iota(I32, (1, 128), 1) < HEAD_DIM
    for pair in range(wide // 128):
        lanes = slice(pair * 128, (pair + 1) * 128)
        q_pair = queries[:, lanes]
        k_pair = keys[:, lanes]
        v_ones = jnp.concatenate([values[:, lanes], ones], axis=1)
        for block in range(4):
            rows = slice(block * share, (block + 1) * share)
            found = []
            for head in range(2):
                chosen = low if head == 0 else jnp.logical_not(low)
                q_head = jnp.where(chosen, q_pair[rows], jnp.zeros((), BF16))
                logits = lax.dot_general(
                    q_head, k_pair, (((1,), (1,)), ((), ())), preferred_element_type=F32
                )
                logits = logits + bias[rows, :]
                top = jnp.max(logits, axis=-1, keepdims=True)
                expo = jnp.exp(logits - top).astype(BF16)
                summed = matmul(expo, v_ones)
                found.append(summed[:, :128] / summed[:, 128:])
            context = jnp.where(low, found[0], found[1])
            context = jnp.where(row_pos[rows] < length, context, F32(0.0))
            out[rows, lanes] = context.astype(BF16)


def attention(meta, blocks, w, b, name):
    share = blocks[0].shape[0]
    return pl.pallas_call(
        attention_kernel,
        out_shape=jax.ShapeDtypeStruct((4 * share, w.shape[2]), BF16),
        in_specs=[SMEM] + [VMEM] * 6,
        out_specs=VMEM,
        scratch_shapes=[pltpu.VMEM((4 * share, 4 * share), F32)],
        compiler_params=params(),
        cost_estimate=pl.CostEstimate(
            flops=2 * 10**9, bytes_accessed=3 * 2**20, transcendentals=2**20
        ),
        name=name,
    )(meta, *blocks, w, b)


def project_kernel(s0, s1, s2, s3, c0, c1, w0, w1, b, out):
    share = s0.shape[0]
    for index, block in enumerate((s0, s1, s2, s3)):
        rows = slice(index * share, (index + 1) * share)
        total = matmul(c0[rows, :], w0[...]) + matmul(c1[rows, :], w1[...])
        out[rows, :] = total + (block[...].astype(F32) + b[...])


def project_here(blocks, c0, c1, w0, w1, b_out):
    share, width = blocks[0].shape
    return pl.pallas_call(
        project_kernel,
        out_shape=jax.ShapeDtypeStruct((4 * share, width), F32),
        in_specs=[VMEM] * 9,
        out_specs=VMEM,
        compiler_params=params(),
        cost_estimate=pl.CostEstimate(flops=10**9, bytes_accessed=5 * 2**20, transcendentals=0),
        name="project_here",
    )(*blocks, c0, c1, w0, w1, b_out)


def feed_kernel(
    keep_rest, base, c0, c1, w0, w1, gain, shift, b0, b1, b_down,
    up0, up1, down0, down1, out, up_buf, down_buf, act, sems,
):
    hidden = up0.shape[1]
    copies = [
        pltpu.make_async_copy(source, target, sems.at[index])
        for index, (source, target) in enumerate(
            (
                (up0, up_buf.at[0]),
                (up1, up_buf.at[1]),
                (down0, down_buf.at[0]),
                (down1, down_buf.at[1]),
            )
        )
    ]
    for copy in copies:
        copy.start()
    total = base[...] + matmul(c0[...], w0[...]) + matmul(c1[...], w1[...])
    normed = layer_norm(total, gain[...], shift[...]).astype(BF16)
    step = 512
    for part in range(2):
        copies[part].wait()
        biases = (b0, b1)[part]
        for first in range(0, hidden, step):
            up = matmul(normed, up_buf[part, :, first : first + step])
            up = up + biases[:, first : first + step]
            activated = 0.5 * up * (1.0 + lax.erf(up * F32(0.5**0.5)))
            act[:, part * hidden + first : part * hidden + first + step] = activated.astype(BF16)
    copies[2].wait()
    down = matmul(act[:, :hidden], down_buf[0])
    copies[3].wait()
    down = down + matmul(act[:, hidden:], down_buf[1])
    if keep_rest:
        down = down + (normed.astype(F32) + b_down[...])
    out[...] = down.astype(out.dtype)


def feed_forward(keep_rest, base, context_x, w_x, w_d, gain, shift, biases, b_down, ups, downs):
    seq_len, width = base.shape
    half = seq_len // 2
    here = 0 if keep_rest else 1
    hidden = ups[0].shape[1]
    heads_wide = context_x[0].shape[1]
    base_spec = pl.BlockSpec((half, width), lambda i: (here, 0))
    context_spec = pl.BlockSpec((half, heads_wide), lambda i: (1 - here, 0))
    return pl.pallas_call(
        lambda *refs: feed_kernel(keep_rest, *refs),
        out_shape=jax.ShapeDtypeStruct((half, width), F32 if keep_rest else BF16),
        grid=(1,),
        in_specs=[base_spec, context_spec, context_spec] + [VMEM] * 7 + [HBM] * 4,
        out_specs=VMEM,
        scratch_shapes=[
            pltpu.VMEM((2, width, hidden), BF16),
            pltpu.VMEM((2, hidden, width), BF16),
            pltpu.VMEM((half, 2 * hidden), BF16),
            pltpu.SemaphoreType.DMA((4,)),
        ],
        compiler_params=params(),
        cost_estimate=pl.CostEstimate(
            flops=3 * 10**9, bytes_accessed=10 * 2**20, transcendentals=2**19
        ),
        name="feed_here" if keep_rest else "feed_there",
    )(base, *context_x, w_x, w_d, gain, shift, *biases, b_down, *ups, *downs)


def finish_kernel(meta, here, there, gain, shift, own, other, pool):
    rank = meta[0]
    length = meta[2]
    share = own.shape[0]
    total = here[...] + there[...].astype(F32)
    hidden = layer_norm(total, gain[...], shift[...]).astype(BF16)
    own[...] = hidden[:share]
    other[...] = hidden[share:]
    index = lax.broadcasted_iota(I32, (2 * share, 1), 0)
    pos = ((index // share) ^ rank) * share + index % share
    valid = jnp.where(pos < length, hidden.astype(F32), F32(0.0))
    pool[...] = jnp.sum(valid, axis=0, keepdims=True)


def finish(meta, here, there, gain, shift):
    half, width = here.shape
    block = jax.ShapeDtypeStruct((half // 2, width), BF16)
    return pl.pallas_call(
        finish_kernel,
        out_shape=(block, block, jax.ShapeDtypeStruct((1, width), F32)),
        in_specs=[SMEM] + [VMEM] * 4,
        out_specs=(VMEM, VMEM, VMEM),
        compiler_params=params(),
        cost_estimate=pl.CostEstimate(flops=10**7, bytes_accessed=2**21, transcendentals=0),
        name="finish",
    )(meta, here, there, gain, shift)


def score_kernel(meta, pool, pool_core, pool_chip, pool_diag, rows, out):
    core = meta[1]
    width = pool.shape[1]
    mine = pool[...] + pool_chip[...]
    theirs = pool_core[...] + pool_diag[...]
    first = jnp.where(core == 0, mine, theirs) / meta[3].astype(F32)
    second = jnp.where(core == 0, theirs, mine) / meta[4].astype(F32)
    row = lax.broadcasted_iota(I32, (8, width), 0)
    pooled = jnp.where(row == 0, first, jnp.where(row == 1, second, F32(0.0)))
    scale = lax.rsqrt(jnp.mean(pooled * pooled, axis=-1, keepdims=True) + norm_eps)
    queries = (pooled * scale).astype(BF16)
    found = lax.dot_general(
        queries, rows[...], (((1,), (1,)), ((), ())), preferred_element_type=F32
    )
    each = rows.shape[0] // 2
    out[0:1, :] = found[0:1, :each]
    out[1:2, :] = found[1:2, each:]


def score(meta, pools, rows):
    return pl.pallas_call(
        score_kernel,
        out_shape=jax.ShapeDtypeStruct((2, rows.shape[0] // 2), F32),
        in_specs=[SMEM] + [VMEM] * 5,
        out_specs=VMEM,
        compiler_params=params(),
        cost_estimate=pl.CostEstimate(flops=10**6, bytes_accessed=2**17, transcendentals=0),
        name="score",
    )(meta, *pools, rows)


def ranked(mask):
    count = mask.shape[-1]
    before = jnp.arange(count)[:, None] < jnp.arange(count)[None, :]
    return matmul(mask.astype(BF16), before.astype(BF16)).astype(I32)


def candidate_rows(cand_ids, index_rows):
    rank = lax.axis_index("tp")
    group = lax.axis_index("req")
    groups = lax.axis_size("req")
    rows_here, width = index_rows.shape
    own = cand_ids.reshape(1, -1)
    asked = jnp.concatenate([own] + [swap(own, "tp", mask) for mask in (1, 2, 3)])
    wanted = asked.shape[1]
    asked = asked.reshape(1, -1)
    everyone = jnp.concatenate([asked] + [swap(asked, "req", mask) for mask in range(1, groups)])

    owner = lax.div(everyone, I32(rows_here))
    shards = jnp.arange(4 * groups, dtype=I32)
    load = jnp.sum((owner[:, :, None] == shards).astype(I32), axis=1)
    rounds = lax.div(jnp.max(load) + SLOTS - 1, I32(SLOTS))

    send_mask = owner == group * 4 + rank
    send_rank = jnp.where(send_mask, ranked(send_mask), -1)
    local = everyone - (group * 4 + rank) * rows_here
    sources = (jnp.arange(groups, dtype=I32) ^ group) * 4 + rank
    take_mask = owner[:1] == sources[:, None]
    take_rank = jnp.where(take_mask, ranked(take_mask), -1)
    slots = jnp.arange(SLOTS, dtype=I32)

    def one_round(number):
        places = slots + number * SLOTS
        chosen = send_rank[:, None, :] == places[:, None]
        rows = jnp.sum(jnp.where(chosen, local[:, None, :], 0), axis=-1)
        sent = jnp.take(index_rows, rows.reshape(-1), axis=0, mode="clip")
        sent = sent.reshape(groups, SLOTS, width)
        here = [sent[0]] + [swap(sent[mask], "req", mask) for mask in range(1, groups)]
        here = jnp.concatenate(here)
        place = (take_rank[:, None, :] == places[:, None]).reshape(groups * SLOTS, -1)
        return lax.dot_general(
            place.astype(BF16), here, (((0,), (0,)), ((), ())), preferred_element_type=F32
        ).astype(BF16)

    found = one_round(0)
    found = lax.fori_loop(1, rounds, lambda n, total: total + one_round(n), found)
    found = found.reshape(4, wanted, width)
    parts = [swap(found[mask], "tp", mask) for mask in (1, 2, 3)]
    return found[0] + parts[0] + parts[1] + parts[2]


def per_device(
    states,
    lengths,
    w_qkv,
    b_qkv,
    w_out,
    b_out,
    ln1_gain,
    ln1_shift,
    w_up,
    b_up,
    w_down,
    b_down,
    ln2_gain,
    ln2_shift,
    index_rows,
    cand_ids,
):
    rank = lax.axis_index("tp")
    core = rank & 1
    share = states.shape[1]
    local_width = w_qkv.shape[2]

    length = jnp.where(core == 0, lengths[0], lengths[1])
    meta = jnp.stack([rank, core, length, lengths[0], lengths[1]]).astype(I32)
    mine, theirs = split_texts(meta, states)
    from_chip = swap(mine, "tp", 2)
    from_diag = swap(theirs, "tp", 3)
    from_core = swap(theirs, "tp", 1)
    blocks = (mine, from_core, from_chip, from_diag)
    w_qkv_t = w_qkv.transpose(1, 0, 2)
    w_qkv_p = swap(w_qkv_t, "tp", 1)
    small = jnp.concatenate([b_qkv.reshape(-1), b_up])
    small_p = swap(small, "tp", 1)
    b_qkv_p = small_p[: 3 * local_width].reshape(3, local_width)
    b_up_p = small_p[3 * local_width :]
    w_out_p = swap(w_out, "tp", 1)
    w_up_p = swap(w_up, "tp", 1)
    w_down_p = swap(w_down, "tp", 1)
    rows = candidate_rows(cand_ids, index_rows)
    w_out_late, _, _ = lax.optimization_barrier((w_out, from_chip, from_diag))
    w_out_x = swap(w_out_late, "tp", 2)
    w_out_d = swap(w_out_x, "tp", 1)

    context_0 = attention(meta, blocks, w_qkv_t, b_qkv, "attention_own")
    context_0x = swap(context_0, "tp", 2)
    context_1 = attention(meta, blocks, w_qkv_p, b_qkv_p, "attention_partner")
    context_1x = swap(context_1, "tp", 2)

    base = project_here(blocks, context_0, context_1, w_out, w_out_p, b_out[None])
    common = (
        (context_0x, context_1x), w_out_x, w_out_d, ln1_gain[None], ln1_shift[None],
        (b_up[None], b_up_p[None]), b_down[None], (w_up, w_up_p), (w_down, w_down_p),
    )
    down_there = feed_forward(False, base, *common)
    down_x = swap(down_there, "tp", 2)
    down_here = feed_forward(True, base, *common)
    hidden, hidden_other, pool = finish(meta, down_here, down_x, ln2_gain[None], ln2_shift[None])

    pools = (pool,) + tuple(swap(pool, "tp", mask) for mask in (1, 2, 3))
    hidden_p = swap(hidden_other, "tp", 1)
    scores = score(meta, pools, rows)
    hidden_out = jnp.where(
        core == 0, jnp.stack([hidden, hidden_p]), jnp.stack([hidden_p, hidden])
    )
    return (hidden_out, scores)


def solution(mesh):
    placed = (
        P("req", "tp", None),
        P("req"),
        P(None, None, "tp"),
        P(None, "tp"),
        P("tp", None),
        P(),
        P(),
        P(),
        P(None, "tp"),
        P("tp"),
        P("tp", None),
        P(),
        P(),
        P(),
        P(("req", "tp"), None),
        P("req", "tp"),
    )
    return jax.shard_map(
        per_device,
        mesh=mesh,
        in_specs=placed,
        out_specs=(P("req", "tp", None), P("req", "tp")),
        check_vma=False,
    )
```

```python
import jax
import jax.numpy as jnp
from jax import lax
from jax.experimental import pallas as pl
from jax.experimental.pallas import tpu as pltpu
from jax.sharding import PartitionSpec as P

HEAD_DIM = 64
WINDOW = 512
SLOTS = 16
BF16 = jnp.bfloat16
F32 = jnp.float32
I32 = jnp.int32
MIB = 1024 * 1024
NO_COST = pl.CostEstimate(flops=1, bytes_accessed=1, transcendentals=0)


def cost(gflop):
    return pl.CostEstimate(flops=int(gflop * 10**9), bytes_accessed=MIB, transcendentals=0)


layer_eps = 1e-05
norm_eps = 1e-06

VMEM = pl.BlockSpec(memory_space=pltpu.VMEM)
SMEM = pl.BlockSpec(memory_space=pltpu.SMEM)
HBM = pl.BlockSpec(memory_space=pl.ANY)


def layer_norm(values, gain, shift):
    centre = values - jnp.mean(values, axis=-1, keepdims=True)
    spread = jnp.mean(centre * centre, axis=-1, keepdims=True)
    return centre * lax.rsqrt(spread + layer_eps) * gain + shift


def swap(value, axis, mask):
    count = lax.axis_size(axis)
    return lax.ppermute(value, axis, [(i, i ^ mask) for i in range(count)])


def matmul(left, right):
    return jnp.dot(left, right, preferred_element_type=F32)


def params(mib):
    return pltpu.CompilerParams(vmem_limit_bytes=mib * MIB)


def after(value, *others):
    return lax.optimization_barrier((value,) + others)[0]


def split_kernel(meta, states, mine, theirs):
    mine[...] = states[meta[1]]
    theirs[...] = states[1 - meta[1]]


def split_texts(meta, states):
    block = jax.ShapeDtypeStruct(states.shape[1:], states.dtype)
    return pl.pallas_call(
        split_kernel,
        out_shape=(block, block),
        in_specs=[SMEM, VMEM],
        out_specs=(VMEM, VMEM),
        compiler_params=params(8),
        cost_estimate=NO_COST,
        name="split_texts",
    )(meta, states)


def project_three(text, w, b, out):
    for which in range(3):
        out[which] = (matmul(text, w[which]) + b[which : which + 1, :]).astype(BF16)


def early_kernel(s0, s1, w, b, out):
    project_three(jnp.concatenate([s0[...], s1[...]]), w, b, out)


def early_projections(s0, s1, w, b, name):
    return pl.pallas_call(
        early_kernel,
        out_shape=jax.ShapeDtypeStruct((3, 2 * s0.shape[0], w.shape[2]), BF16),
        in_specs=[VMEM] * 4,
        out_specs=VMEM,
        compiler_params=params(12),
        cost_estimate=NO_COST,
        name=name,
    )(s0, s1, w, b)


def attention_kernel(meta, lengths, early, s2, s3, w, b, out, late, bias):
    rank = meta[0]
    length = lengths[meta[1]]
    share = s2.shape[0]
    half = 2 * share
    seq_len = 4 * share
    wide = w.shape[2]
    project_three(jnp.concatenate([s2[...], s3[...]]), w, b, late)

    def position(index):
        return ((index // share) ^ rank) * share + index % share

    row_pos = position(lax.broadcasted_iota(I32, (seq_len, 1), 0))
    col_pos = position(lax.broadcasted_iota(I32, (1, seq_len), 1))
    keep = (jnp.abs(row_pos - col_pos) <= WINDOW // 2) & (col_pos < length)
    bias[...] = jnp.where(keep, F32(0.0), F32(-1e30))
    ones = jnp.ones((seq_len, 128), BF16)
    low = lax.broadcasted_iota(I32, (1, 128), 1) < HEAD_DIM
    scale = jnp.asarray(HEAD_DIM**-0.5, BF16)
    for pair in range(wide // 128):
        lanes = slice(pair * 128, (pair + 1) * 128)
        k_pair = jnp.concatenate([early[1, :, lanes], late[1, :, lanes]])
        v_pair = jnp.concatenate([early[2, :, lanes], late[2, :, lanes]])
        v_ones = jnp.concatenate([v_pair, ones], axis=1)
        for block in range(4):
            rows = slice(block * share, (block + 1) * share)
            first = (block % 2) * share
            q_pair = (early, late)[block // 2][0, first : first + share, lanes] * scale
            found = []
            for head in range(2):
                chosen = low if head == 0 else jnp.logical_not(low)
                q_head = jnp.where(chosen, q_pair, jnp.zeros((), BF16))
                logits = lax.dot_general(
                    q_head, k_pair, (((1,), (1,)), ((), ())), preferred_element_type=F32
                )
                logits = logits + bias[rows, :]
                top = jnp.max(logits, axis=-1, keepdims=True)
                expo = jnp.exp(logits - top).astype(BF16)
                summed = matmul(expo, v_ones)
                found.append(summed[:, :128] / summed[:, 128:])
            context = jnp.where(low, found[0], found[1])
            context = jnp.where(row_pos[rows] < length, context, F32(0.0))
            out[rows, lanes] = context.astype(BF16)


def attention(meta, lengths, early, s2, s3, w, b, name):
    seq_len = 4 * s2.shape[0]
    wide = w.shape[2]
    return pl.pallas_call(
        attention_kernel,
        out_shape=jax.ShapeDtypeStruct((seq_len, wide), BF16),
        in_specs=[SMEM] * 2 + [VMEM] * 5,
        out_specs=VMEM,
        scratch_shapes=[
            pltpu.VMEM((3, seq_len // 2, wide), BF16),
            pltpu.VMEM((seq_len, seq_len), F32),
        ],
        compiler_params=params(20),
        cost_estimate=cost(6),
        name=name,
    )(meta, lengths, early, s2, s3, w, b)


def project_kernel(s0, s1, s2, s3, c0, c1, c2, w0, w1, w2, b, out):
    share = s0.shape[0]
    for index, block in enumerate((s0, s1, s2, s3)):
        rows = slice(index * share, (index + 1) * share)
        there = (index ^ 2) * share
        total = matmul(c0[rows, :], w0[...]) + matmul(c1[rows, :], w1[...])
        total = total + matmul(c2[there : there + share, :], w2[...])
        out[rows, :] = total + (block[...].astype(F32) + b[...])


def project_here(blocks, contexts, weights, b_out):
    share, width = blocks[0].shape
    return pl.pallas_call(
        project_kernel,
        out_shape=jax.ShapeDtypeStruct((4 * share, width), F32),
        in_specs=[VMEM] * 11,
        out_specs=VMEM,
        compiler_params=params(16),
        cost_estimate=cost(4),
        name="project_here",
    )(*blocks, *contexts, *weights, b_out)


def feed_kernel(
    keep_rest, base, c3, w3, gain, shift, b0, b1, b_down,
    up0, up1, down0, down1, out, up_buf, down_buf, act, sems,
):
    hidden = up0.shape[1]
    copies = [
        pltpu.make_async_copy(source, target, sems.at[index])
        for index, (source, target) in enumerate(
            (
                (up0, up_buf.at[0]),
                (up1, up_buf.at[1]),
                (down0, down_buf.at[0]),
                (down1, down_buf.at[1]),
            )
        )
    ]
    for copy in copies:
        copy.start()
    total = base[...] + matmul(c3[...], w3[...])
    normed = layer_norm(total, gain[...], shift[...]).astype(BF16)
    step = 512
    for part in range(2):
        copies[part].wait()
        biases = (b0, b1)[part]
        for first in range(0, hidden, step):
            up = matmul(normed, up_buf[part, :, first : first + step])
            up = up + biases[:, first : first + step]
            activated = 0.5 * up * (1.0 + lax.erf(up * F32(0.5**0.5)))
            act[:, part * hidden + first : part * hidden + first + step] = activated.astype(BF16)
    copies[2].wait()
    down = matmul(act[:, :hidden], down_buf[0])
    copies[3].wait()
    down = down + matmul(act[:, hidden:], down_buf[1])
    if keep_rest:
        down = down + (normed.astype(F32) + b_down[...])
    out[...] = down.astype(out.dtype)


def feed_forward(keep_rest, base, context, w, gain, shift, biases, b_down, ups, downs):
    seq_len, width = base.shape
    half = seq_len // 2
    here = 0 if keep_rest else 1
    hidden = ups[0].shape[1]
    heads_wide = context.shape[1]
    base_spec = pl.BlockSpec((half, width), lambda i: (here, 0))
    context_spec = pl.BlockSpec((half, heads_wide), lambda i: (1 - here, 0))
    return pl.pallas_call(
        lambda *refs: feed_kernel(keep_rest, *refs),
        out_shape=jax.ShapeDtypeStruct((half, width), F32 if keep_rest else BF16),
        grid=(1,),
        in_specs=[base_spec, context_spec] + [VMEM] * 6 + [HBM] * 4,
        out_specs=VMEM,
        scratch_shapes=[
            pltpu.VMEM((2, width, hidden), BF16),
            pltpu.VMEM((2, hidden, width), BF16),
            pltpu.VMEM((half, 2 * hidden), BF16),
            pltpu.SemaphoreType.DMA((4,)),
        ],
        compiler_params=params(32),
        cost_estimate=cost(8),
        name="feed_here" if keep_rest else "feed_there",
    )(base, context, w, gain, shift, *biases, b_down, *ups, *downs)


def finish_kernel(meta, lengths, here, there, gain, shift, own, other, pool):
    rank = meta[0]
    length = lengths[meta[1]]
    share = own.shape[0]
    total = here[...] + there[...].astype(F32)
    hidden = layer_norm(total, gain[...], shift[...]).astype(BF16)
    own[...] = hidden[:share]
    other[...] = hidden[share:]
    index = lax.broadcasted_iota(I32, (2 * share, 1), 0)
    pos = ((index // share) ^ rank) * share + index % share
    valid = jnp.where(pos < length, hidden.astype(F32), F32(0.0))
    pool[...] = jnp.sum(valid, axis=0, keepdims=True)


def finish(meta, lengths, here, there, gain, shift):
    half, width = here.shape
    block = jax.ShapeDtypeStruct((half // 2, width), BF16)
    return pl.pallas_call(
        finish_kernel,
        out_shape=(block, block, jax.ShapeDtypeStruct((1, width), F32)),
        in_specs=[SMEM] * 2 + [VMEM] * 4,
        out_specs=(VMEM, VMEM, VMEM),
        compiler_params=params(8),
        cost_estimate=cost(2),
        name="finish",
    )(meta, lengths, here, there, gain, shift)


def score_kernel(meta, lengths, pool, pool_core, pool_chip, pool_diag, rows, out):
    core = meta[1]
    width = pool.shape[1]
    mine = pool[...] + pool_chip[...]
    theirs = pool_core[...] + pool_diag[...]
    first = jnp.where(core == 0, mine, theirs) / lengths[0].astype(F32)
    second = jnp.where(core == 0, theirs, mine) / lengths[1].astype(F32)
    row = lax.broadcasted_iota(I32, (8, width), 0)
    pooled = jnp.where(row == 0, first, jnp.where(row == 1, second, F32(0.0)))
    scale = lax.rsqrt(jnp.mean(pooled * pooled, axis=-1, keepdims=True) + norm_eps)
    queries = (pooled * scale).astype(BF16)
    found = lax.dot_general(
        queries, rows[...], (((1,), (1,)), ((), ())), preferred_element_type=F32
    )
    each = rows.shape[0] // 2
    out[0:1, :] = found[0:1, :each]
    out[1:2, :] = found[1:2, each:]


def score(meta, lengths, pools, rows):
    return pl.pallas_call(
        score_kernel,
        out_shape=jax.ShapeDtypeStruct((2, rows.shape[0] // 2), F32),
        in_specs=[SMEM] * 2 + [VMEM] * 5,
        out_specs=VMEM,
        compiler_params=params(8),
        cost_estimate=cost(1),
        name="score",
    )(meta, lengths, *pools, rows)


def take_kernel(wanted, index, out, tiles, rows, sems):
    count = tiles.shape[0]
    deep = tiles.shape[1]
    rows[...] = jnp.zeros_like(rows)

    def tile_copy(slot):
        first = pl.multiple_of((wanted[slot] // deep) * deep, deep)
        return pltpu.make_async_copy(index.at[pl.ds(first, deep)], tiles.at[slot], sems.at[slot])

    def start(slot, carry):
        @pl.when(wanted[slot] >= 0)
        def _():
            tile_copy(slot).start()

        return carry

    def select(slot, carry):
        @pl.when(wanted[slot] >= 0)
        def _():
            tile_copy(slot).wait()
            line = lax.broadcasted_iota(I32, (deep, 1), 0) == wanted[slot] % deep
            chosen = jnp.where(line, tiles[slot].astype(F32), F32(0.0))
            rows[pl.ds(slot, 1), :] = jnp.sum(chosen, axis=0, keepdims=True)

        return carry

    lax.fori_loop(0, count, start, 0)
    lax.fori_loop(0, count, select, 0)
    out[...] = rows[...].astype(BF16)


def take_rows(wanted, index_rows):
    count = wanted.shape[0]
    width = index_rows.shape[1]
    return pl.pallas_call(
        take_kernel,
        out_shape=jax.ShapeDtypeStruct((count, width), BF16),
        in_specs=[SMEM, HBM],
        out_specs=VMEM,
        scratch_shapes=[
            pltpu.VMEM((count, 16, width), BF16),
            pltpu.VMEM((count, width), F32),
            pltpu.SemaphoreType.DMA((count,)),
        ],
        compiler_params=params(8 + count // 16),
        cost_estimate=NO_COST,
        name="take_rows",
    )(wanted, index_rows)


def place_kernel(place, *refs):
    out = refs[-1]
    received = jnp.concatenate([each[...] for each in refs[:-1]])
    chosen = lax.dot_general(
        place[...], received, (((0,), (0,)), ((), ())), preferred_element_type=F32
    )
    out[...] = chosen.astype(BF16)


def place_rows(place, received):
    width = received[0].shape[1]
    return pl.pallas_call(
        place_kernel,
        out_shape=jax.ShapeDtypeStruct((place.shape[1], width), BF16),
        in_specs=[VMEM] * (1 + len(received)),
        out_specs=VMEM,
        compiler_params=params(8),
        cost_estimate=NO_COST,
        name="place_rows",
    )(place, *received)


def ranked(mask):
    count = mask.shape[-1]
    before = jnp.arange(count)[:, None] < jnp.arange(count)[None, :]
    return matmul(mask.astype(BF16), before.astype(BF16)).astype(I32)


def all_ids(cand_ids):
    asked = jnp.stack([cand_ids] + [swap(cand_ids, "tp", mask) for mask in (1, 2, 3)])
    asked = asked.reshape(1, -1)
    groups = lax.axis_size("req")
    return jnp.concatenate([asked] + [swap(asked, "req", mask) for mask in range(1, groups)])


def candidate_rows(everyone, index_rows):
    rank = lax.axis_index("tp")
    group = lax.axis_index("req")
    groups = lax.axis_size("req")
    rows_here, width = index_rows.shape

    owner = lax.div(everyone, I32(rows_here))
    shards = jnp.arange(4 * groups, dtype=I32)
    load = jnp.sum((owner[:, :, None] == shards).astype(I32), axis=1)
    rounds = lax.div(jnp.max(load) + SLOTS - 1, I32(SLOTS))

    send_mask = owner == group * 4 + rank
    send_rank = jnp.where(send_mask, ranked(send_mask), -1)
    local = everyone - (group * 4 + rank) * rows_here
    sources = (jnp.arange(groups, dtype=I32) ^ group) * 4 + rank
    take_mask = owner[:1] == sources[:, None]
    take_rank = jnp.where(take_mask, ranked(take_mask), -1)
    slots = jnp.arange(SLOTS, dtype=I32)

    def take(number):
        places = slots + number * SLOTS
        chosen = send_rank[:, None, :] == places[:, None]
        wanted = jnp.sum(jnp.where(chosen, local[:, None, :] + 1, 0), axis=-1) - 1
        return take_rows(wanted.reshape(-1), index_rows)

    def gathered(number, sent, gate):
        sent = sent.reshape(groups, SLOTS, width)
        here = [sent[0]] + [swap(sent[mask], "req", mask) for mask in range(1, groups)]
        places = slots + number * SLOTS
        place = (take_rank[:, None, :] == places[:, None]).reshape(groups * SLOTS, -1)
        found = place_rows(after(place.astype(BF16), *gate), here).reshape(4, -1, width)
        parts = [swap(found[mask], "tp", mask) for mask in (1, 2, 3)]
        return found[0] + parts[0] + parts[1] + parts[2]

    def further(rows):
        return lax.fori_loop(
            1, rounds, lambda n, total: total + gathered(n, take(n), ()), rows
        )

    return take(0), lambda sent, gate: gathered(0, sent, (gate,)), further


def per_device(
    states,
    lengths,
    w_qkv,
    b_qkv,
    w_out,
    b_out,
    ln1_gain,
    ln1_shift,
    w_up,
    b_up,
    w_down,
    b_down,
    ln2_gain,
    ln2_shift,
    index_rows,
    cand_ids,
):
    rank = lax.axis_index("tp")
    core = rank & 1
    meta = jnp.stack([rank, core]).astype(I32)

    mine, theirs = split_texts(meta, states)
    from_chip = swap(mine, "tp", 2)
    from_diag = swap(theirs, "tp", 3)
    from_core = swap(theirs, "tp", 1)
    w_qkv_t = w_qkv.transpose(1, 0, 2)
    w_qkv_p = swap(after(w_qkv_t, mine), "tp", 1)
    b_qkv_p = swap(after(b_qkv, mine), "tp", 1)
    early_0 = early_projections(mine, from_core, w_qkv_t, b_qkv, "early_own")
    everyone = all_ids(after(cand_ids, early_0))
    sent, gathered, further = candidate_rows(everyone, index_rows)
    early_1 = early_projections(
        mine, after(from_core, sent), w_qkv_p, b_qkv_p, "early_partner"
    )
    early_0 = after(early_0, early_1)
    blocks = (mine, from_core, from_chip, from_diag)

    w_out_x = swap(after(w_out, from_chip, from_diag, early_1), "tp", 2)
    w_out_p = swap(after(w_out, mine), "tp", 1)
    w_up_p = swap(after(w_up, mine), "tp", 1)
    w_down_p = swap(after(w_down, mine), "tp", 1)
    b_up_p = swap(after(b_up, mine), "tp", 1)

    context_0 = attention(
        meta, lengths, early_0, from_chip, from_diag, w_qkv_t, b_qkv, "attention_own"
    )
    context_0x = swap(context_0, "tp", 2)
    context_1 = attention(
        meta, lengths, after(early_1, context_0), from_chip, from_diag, w_qkv_p, b_qkv_p,
        "attention_partner",
    )
    context_1x = swap(context_1, "tp", 2)
    w_out_d = swap(after(w_out_x, context_1), "tp", 1)

    base = project_here(
        blocks, (context_0, context_1, context_0x), (w_out, w_out_p, w_out_x), b_out[None]
    )
    common = (
        context_1x, w_out_d, ln1_gain[None], ln1_shift[None],
        (b_up[None], b_up_p[None]), b_down[None], (w_up, w_up_p), (w_down, w_down_p),
    )
    down_there = feed_forward(False, base, *common)
    down_x = swap(down_there, "tp", 2)
    base = after(base, down_there)
    down_here = feed_forward(True, base, *common)
    hidden, hidden_other, pool = finish(
        meta, lengths, down_here, down_x, ln2_gain[None], ln2_shift[None]
    )

    rows = gathered(sent, base)
    pools = (pool,) + tuple(swap(pool, "tp", mask) for mask in (1, 2, 3))
    hidden_p = swap(hidden_other, "tp", 1)
    scores = score(meta, lengths, pools, further(after(rows, *pools)))
    hidden_out = jnp.where(
        core == 0, jnp.stack([hidden, hidden_p]), jnp.stack([hidden_p, hidden])
    )
    return (hidden_out, scores)


def solution(mesh):
    placed = (
        P("req", "tp", None),
        P("req"),
        P(None, None, "tp"),
        P(None, "tp"),
        P("tp", None),
        P(),
        P(),
        P(),
        P(None, "tp"),
        P("tp"),
        P("tp", None),
        P(),
        P(),
        P(),
        P(("req", "tp"), None),
        P("req", "tp"),
    )
    return jax.shard_map(
        per_device,
        mesh=mesh,
        in_specs=placed,
        out_specs=(P("req", "tp", None), P("req", "tp")),
        check_vma=False,
    )
```

```python
import jax
import jax.numpy as jnp
from jax import lax
from jax.experimental import pallas as pl
from jax.experimental.pallas import tpu as pltpu
from jax.sharding import PartitionSpec as P

HEAD_DIM = 64
WINDOW = 512
SLOTS = 16
BF16 = jnp.bfloat16
F32 = jnp.float32
I32 = jnp.int32
MIB = 1024 * 1024
NO_COST = pl.CostEstimate(flops=1, bytes_accessed=1, transcendentals=0)


def cost(gflop):
    return pl.CostEstimate(flops=int(gflop * 10**9), bytes_accessed=MIB, transcendentals=0)


layer_eps = 1e-05
norm_eps = 1e-06

VMEM = pl.BlockSpec(memory_space=pltpu.VMEM)
SMEM = pl.BlockSpec(memory_space=pltpu.SMEM)
HBM = pl.BlockSpec(memory_space=pl.ANY)


def layer_norm(values, gain, shift):
    centre = values - jnp.mean(values, axis=-1, keepdims=True)
    spread = jnp.mean(centre * centre, axis=-1, keepdims=True)
    return centre * lax.rsqrt(spread + layer_eps) * gain + shift


def swap(value, axis, mask):
    count = lax.axis_size(axis)
    return lax.ppermute(value, axis, [(i, i ^ mask) for i in range(count)])


def matmul(left, right):
    return jnp.dot(left, right, preferred_element_type=F32)


def params(mib):
    return pltpu.CompilerParams(vmem_limit_bytes=mib * MIB)


def after(value, *others):
    return lax.optimization_barrier((value,) + others)[0]


def project_three(text, w, b, out):
    for which in range(3):
        out[which] = (matmul(text, w[which]) + b[which : which + 1, :]).astype(BF16)


def early_kernel(meta, s0, s1, w, b, out):
    core = meta[1]
    project_three(jnp.concatenate([s0[core], s1[core]]), w, b, out)


def early_projections(meta, s0, s1, w, b, name):
    return pl.pallas_call(
        early_kernel,
        out_shape=jax.ShapeDtypeStruct((3, 2 * s0.shape[1], w.shape[2]), BF16),
        in_specs=[SMEM] + [VMEM] * 4,
        out_specs=VMEM,
        compiler_params=params(12),
        cost_estimate=NO_COST,
        name=name,
    )(meta, s0, s1, w, b)


def attention_kernel(meta, lengths, early, s2, s3, w, b, out, late, bias):
    rank = meta[0]
    core = meta[1]
    length = lengths[core]
    share = s2.shape[1]
    half = 2 * share
    seq_len = 4 * share
    wide = w.shape[2]
    project_three(jnp.concatenate([s2[core], s3[core]]), w, b, late)

    def position(index):
        return ((index // share) ^ rank) * share + index % share

    row_pos = position(lax.broadcasted_iota(I32, (seq_len, 1), 0))
    col_pos = position(lax.broadcasted_iota(I32, (1, seq_len), 1))
    keep = (jnp.abs(row_pos - col_pos) <= WINDOW // 2) & (col_pos < length)
    bias[...] = jnp.where(keep, F32(0.0), F32(-1e30))
    ones = jnp.ones((seq_len, 128), BF16)
    low = lax.broadcasted_iota(I32, (1, 128), 1) < HEAD_DIM
    scale = jnp.asarray(HEAD_DIM**-0.5, BF16)
    for pair in range(wide // 128):
        lanes = slice(pair * 128, (pair + 1) * 128)
        k_pair = jnp.concatenate([early[1, :, lanes], late[1, :, lanes]])
        v_pair = jnp.concatenate([early[2, :, lanes], late[2, :, lanes]])
        v_ones = jnp.concatenate([v_pair, ones], axis=1)
        for block in range(4):
            rows = slice(block * share, (block + 1) * share)
            first = (block % 2) * share
            q_pair = (early, late)[block // 2][0, first : first + share, lanes] * scale
            found = []
            for head in range(2):
                chosen = low if head == 0 else jnp.logical_not(low)
                q_head = jnp.where(chosen, q_pair, jnp.zeros((), BF16))
                logits = lax.dot_general(
                    q_head, k_pair, (((1,), (1,)), ((), ())), preferred_element_type=F32
                )
                logits = logits + bias[rows, :]
                top = jnp.max(logits, axis=-1, keepdims=True)
                expo = jnp.exp(logits - top).astype(BF16)
                summed = matmul(expo, v_ones)
                found.append(summed[:, :128] / summed[:, 128:])
            context = jnp.where(low, found[0], found[1])
            context = jnp.where(row_pos[rows] < length, context, F32(0.0))
            out[rows, lanes] = context.astype(BF16)


def attention(meta, lengths, early, s2, s3, w, b, gflop, name):
    seq_len = 4 * s2.shape[1]
    wide = w.shape[2]
    return pl.pallas_call(
        attention_kernel,
        out_shape=jax.ShapeDtypeStruct((seq_len, wide), BF16),
        in_specs=[SMEM] * 2 + [VMEM] * 5,
        out_specs=VMEM,
        scratch_shapes=[
            pltpu.VMEM((3, seq_len // 2, wide), BF16),
            pltpu.VMEM((seq_len, seq_len), F32),
        ],
        compiler_params=params(20),
        cost_estimate=cost(gflop),
        name=name,
    )(meta, lengths, early, s2, s3, w, b)


def project_kernel(meta, s0, s1, s2, s3, c0, c1, w0, w1, b, out):
    share = s0.shape[1]
    for index, block in enumerate((s0, s1, s2, s3)):
        rows = slice(index * share, (index + 1) * share)
        total = matmul(c0[rows, :], w0[...]) + matmul(c1[rows, :], w1[...])
        out[rows, :] = total + (block[meta[1]].astype(F32) + b[...])


def project_here(meta, blocks, contexts, weights, b_out):
    _, share, width = blocks[0].shape
    return pl.pallas_call(
        project_kernel,
        out_shape=jax.ShapeDtypeStruct((4 * share, width), F32),
        in_specs=[SMEM] + [VMEM] * 9,
        out_specs=VMEM,
        compiler_params=params(16),
        cost_estimate=cost(2),
        name="project_here",
    )(meta, *blocks, *contexts, *weights, b_out)


def joined(meta, first, second):
    swapped = (meta[2] & 1) != 0
    low = jnp.where(swapped, second[...], first[...])
    high = jnp.where(swapped, first[...], second[...])
    return jnp.concatenate([low, high])


def project_there_kernel(meta, base, context, first, second, out):
    half = base.shape[0] // 2
    weight = joined(meta, first, second)
    out[:half, :] = base[:half, :] + matmul(context[half:, :], weight)
    out[half:, :] = base[half:, :] + matmul(context[:half, :], weight)


def project_there(meta, base, context, pieces):
    return pl.pallas_call(
        project_there_kernel,
        out_shape=jax.ShapeDtypeStruct(base.shape, F32),
        in_specs=[SMEM] + [VMEM] * 4,
        out_specs=VMEM,
        input_output_aliases={1: 0},
        compiler_params=params(12),
        cost_estimate=NO_COST,
        name="project_there",
    )(meta, base, context, *pieces)


def feed_kernel(
    keep_rest, meta, base, c3, first, second, gain, shift, b0, b1, b_down,
    up0, up1, down0, down1, out, up_buf, down_buf, act, sems,
):
    hidden = up0.shape[1]
    copies = [
        pltpu.make_async_copy(source, target, sems.at[index])
        for index, (source, target) in enumerate(
            (
                (up0, up_buf.at[0]),
                (up1, up_buf.at[1]),
                (down0, down_buf.at[0]),
                (down1, down_buf.at[1]),
            )
        )
    ]
    for copy in copies:
        copy.start()
    total = base[...] + matmul(c3[...], joined(meta, first, second))
    normed = layer_norm(total, gain[...], shift[...]).astype(BF16)
    step = 512
    for part in range(2):
        copies[part].wait()
        biases = (b0, b1)[part]
        for low in range(0, hidden, step):
            up = matmul(normed, up_buf[part, :, low : low + step]) + biases[:, low : low + step]
            activated = 0.5 * up * (1.0 + lax.erf(up * F32(0.5**0.5)))
            act[:, part * hidden + low : part * hidden + low + step] = activated.astype(BF16)
    copies[2].wait()
    down = matmul(act[:, :hidden], down_buf[0])
    copies[3].wait()
    down = down + matmul(act[:, hidden:], down_buf[1])
    if keep_rest:
        down = down + (normed.astype(F32) + b_down[...])
    out[...] = down.astype(out.dtype)


def feed_forward(keep_rest, meta, base, context, pieces, gain, shift, biases, b_down, ups, downs):
    seq_len, width = base.shape
    half = seq_len // 2
    here = 0 if keep_rest else 1
    hidden = ups[0].shape[1]
    heads_wide = context.shape[1]
    base_spec = pl.BlockSpec((half, width), lambda i: (here, 0))
    context_spec = pl.BlockSpec((half, heads_wide), lambda i: (1 - here, 0))
    return pl.pallas_call(
        lambda *refs: feed_kernel(keep_rest, *refs),
        out_shape=jax.ShapeDtypeStruct((half, width), F32 if keep_rest else BF16),
        grid=(1,),
        in_specs=[SMEM, base_spec, context_spec] + [VMEM] * 7 + [HBM] * 4,
        out_specs=VMEM,
        scratch_shapes=[
            pltpu.VMEM((2, width, hidden), BF16),
            pltpu.VMEM((2, hidden, width), BF16),
            pltpu.VMEM((half, 2 * hidden), BF16),
            pltpu.SemaphoreType.DMA((4,)),
        ],
        compiler_params=params(32),
        cost_estimate=cost(8),
        name="feed_here" if keep_rest else "feed_there",
    )(meta, base, context, *pieces, gain, shift, *biases, b_down, *ups, *downs)


def finish_kernel(meta, lengths, here, there, gain, shift, own, other, pool):
    rank = meta[0]
    length = lengths[meta[1]]
    share = own.shape[0]
    total = here[...] + there[...].astype(F32)
    hidden = layer_norm(total, gain[...], shift[...]).astype(BF16)
    own[...] = hidden[:share]
    other[...] = hidden[share:]
    index = lax.broadcasted_iota(I32, (2 * share, 1), 0)
    pos = ((index // share) ^ rank) * share + index % share
    valid = jnp.where(pos < length, hidden.astype(F32), F32(0.0))
    pool[...] = jnp.sum(valid, axis=0, keepdims=True)


def finish(meta, lengths, here, there, gain, shift):
    half, width = here.shape
    block = jax.ShapeDtypeStruct((half // 2, width), BF16)
    return pl.pallas_call(
        finish_kernel,
        out_shape=(block, block, jax.ShapeDtypeStruct((1, width), F32)),
        in_specs=[SMEM] * 2 + [VMEM] * 4,
        out_specs=(VMEM, VMEM, VMEM),
        compiler_params=params(8),
        cost_estimate=cost(2),
        name="finish",
    )(meta, lengths, here, there, gain, shift)


def score_kernel(
    meta, lengths, pool, pool_core, pool_chip, pool_diag, rows, own, other, out, hidden_out
):
    core = meta[1]
    width = pool.shape[1]
    mine = pool[...] + pool_chip[...]
    theirs = pool_core[...] + pool_diag[...]
    first = jnp.where(core == 0, mine, theirs) / lengths[0].astype(F32)
    second = jnp.where(core == 0, theirs, mine) / lengths[1].astype(F32)
    row = lax.broadcasted_iota(I32, (8, width), 0)
    pooled = jnp.where(row == 0, first, jnp.where(row == 1, second, F32(0.0)))
    scale = lax.rsqrt(jnp.mean(pooled * pooled, axis=-1, keepdims=True) + norm_eps)
    queries = (pooled * scale).astype(BF16)
    found = lax.dot_general(
        queries, rows[...], (((1,), (1,)), ((), ())), preferred_element_type=F32
    )
    each = rows.shape[0] // 2
    out[0:1, :] = found[0:1, :each]
    out[1:2, :] = found[1:2, each:]
    hidden_out[core] = own[...]
    hidden_out[1 - core] = other[...]


def score(meta, lengths, pools, rows, own, other):
    return pl.pallas_call(
        score_kernel,
        out_shape=(
            jax.ShapeDtypeStruct((2, rows.shape[0] // 2), F32),
            jax.ShapeDtypeStruct((2,) + own.shape, BF16),
        ),
        in_specs=[SMEM] * 2 + [VMEM] * 7,
        out_specs=(VMEM, VMEM),
        compiler_params=params(8),
        cost_estimate=cost(1),
        name="score",
    )(meta, lengths, *pools, rows, own, other)


def take_kernel(wanted, counts, index, out, tiles, rows, sems):
    deep = tiles.shape[1]
    rows[...] = jnp.zeros_like(rows)

    def tile_copy(slot):
        first = pl.multiple_of((wanted[slot] // deep) * deep, deep)
        return pltpu.make_async_copy(index.at[pl.ds(first, deep)], tiles.at[slot], sems.at[slot])

    def start(slot, carry):
        tile_copy(slot).start()
        return carry

    def select(slot, carry):
        tile_copy(slot).wait()
        line = lax.broadcasted_iota(I32, (deep, 1), 0) == wanted[slot] % deep
        chosen = jnp.where(line, tiles[slot].astype(F32), F32(0.0))
        rows[pl.ds(slot, 1), :] = jnp.sum(chosen, axis=0, keepdims=True)
        return carry

    def each_group(action):
        def group(number, carry):
            first = number * SLOTS
            return lax.fori_loop(first, first + counts[number], action, carry)

        lax.fori_loop(0, counts.shape[0], group, 0)

    each_group(start)
    each_group(select)
    out[...] = rows[...].astype(BF16)


def take_rows(wanted, counts, index_rows):
    slots = wanted.shape[0]
    width = index_rows.shape[1]
    return pl.pallas_call(
        take_kernel,
        out_shape=jax.ShapeDtypeStruct((slots, width), BF16),
        in_specs=[SMEM, SMEM, HBM],
        out_specs=VMEM,
        scratch_shapes=[
            pltpu.VMEM((slots, 16, width), BF16),
            pltpu.VMEM((slots, width), F32),
            pltpu.SemaphoreType.DMA((slots,)),
        ],
        compiler_params=params(8 + slots // 16),
        cost_estimate=NO_COST,
        name="take_rows",
    )(wanted, counts, index_rows)


def place_kernel(place, received, out):
    chosen = lax.dot_general(
        place[...], received[...], (((0,), (0,)), ((), ())), preferred_element_type=F32
    )
    out[...] = chosen.astype(BF16)


def place_rows(place, received):
    return pl.pallas_call(
        place_kernel,
        out_shape=jax.ShapeDtypeStruct((place.shape[1], received.shape[1]), BF16),
        in_specs=[VMEM] * 2,
        out_specs=VMEM,
        compiler_params=params(8),
        cost_estimate=NO_COST,
        name="place_rows",
    )(place, received)


def ranked(mask):
    count = mask.shape[-1]
    before = jnp.arange(count)[:, None] < jnp.arange(count)[None, :]
    return matmul(mask.astype(BF16), before.astype(BF16)).astype(I32)


def masks(axis):
    mask = 1
    while mask < lax.axis_size(axis):
        yield mask
        mask *= 2


def all_ids(cand_ids, gates):
    held = jnp.stack([cand_ids] + [swap(cand_ids, "tp", mask) for mask in (1, 2, 3)])
    held = held.reshape(1, -1)
    steps = list(masks("req"))
    for mask in steps:
        if mask in steps[-len(gates) :]:
            held = after(held, gates[steps.index(mask) - len(steps)])
        held = jnp.concatenate([held, swap(held, "req", mask)])
    return held


def candidate_rows(everyone, index_rows):
    rank = lax.axis_index("tp")
    group = lax.axis_index("req")
    groups = lax.axis_size("req")
    rows_here, width = index_rows.shape

    owner = lax.div(everyone, I32(rows_here))
    shards = jnp.arange(4 * groups, dtype=I32)
    load = jnp.sum((owner[:, :, None] == shards).astype(I32), axis=1)
    rounds = lax.div(jnp.max(load) + SLOTS - 1, I32(SLOTS))

    send_mask = owner == group * 4 + rank
    send_rank = jnp.where(send_mask, ranked(send_mask), -1)
    send_count = jnp.sum(send_mask.astype(I32), axis=1)
    local = everyone - (group * 4 + rank) * rows_here
    order = [0]
    for mask in reversed(list(masks("req"))):
        order = order + [entry + mask for entry in order]
    sources = (jnp.array(order, I32) ^ group) * 4 + rank
    take_mask = owner[:1] == sources[:, None]
    take_rank = jnp.where(take_mask, ranked(take_mask), -1)
    slots = jnp.arange(SLOTS, dtype=I32)

    def take(number, gate):
        places = slots + number * SLOTS
        chosen = send_rank[:, None, :] == places[:, None]
        wanted = jnp.sum(jnp.where(chosen, local[:, None, :], 0), axis=-1).reshape(-1)
        counts = jnp.clip(send_count - number * SLOTS, 0, SLOTS)
        return take_rows(after(wanted, *gate), counts, index_rows)

    def gathered(number, sent, gates=()):
        held = sent.reshape(1, groups, SLOTS * width)
        for step, mask in enumerate(reversed(list(masks("req")))):
            if step < len(gates) and gates[step] is not None:
                held = after(held, gates[step])
            other = swap(held[:, mask:], "req", mask)
            held = jnp.concatenate([held[:, :mask], other])
        places = slots + number * SLOTS
        place = (take_rank[:, None, :] == places[:, None]).reshape(groups * SLOTS, -1)
        found = place_rows(place.astype(BF16), held.reshape(groups * SLOTS, width))
        found = found.reshape(4, -1, width)
        parts = [swap(found[mask], "tp", mask) for mask in (1, 2, 3)]
        return found[0] + parts[0] + parts[1] + parts[2]

    def further(rows):
        return lax.fori_loop(
            1, rounds, lambda n, total: total + gathered(n, take(n, ())), rows
        )

    return lambda *gate: take(0, gate), lambda sent, *gates: gathered(0, sent, gates), further


def per_device(
    states,
    lengths,
    w_qkv,
    b_qkv,
    w_out,
    b_out,
    ln1_gain,
    ln1_shift,
    w_up,
    b_up,
    w_down,
    b_down,
    ln2_gain,
    ln2_shift,
    index_rows,
    cand_ids,
):
    rank = lax.axis_index("tp")
    group = lax.axis_index("req")
    meta = jnp.stack([rank, rank & 1, group]).astype(I32)

    from_chip = swap(states, "tp", 2)
    from_core = swap(states, "tp", 1)
    from_diag = swap(from_chip, "tp", 1)
    blocks = (states, from_core, from_chip, from_diag)
    w_qkv_t = w_qkv.transpose(1, 0, 2)
    w_qkv_p = swap(after(w_qkv_t, from_core), "tp", 1)
    biases = jnp.concatenate([b_qkv, b_up.reshape(-1, b_qkv.shape[1])])
    biases_p = swap(after(biases, from_core), "tp", 1)
    early_0 = early_projections(meta, states, from_core, w_qkv_t, b_qkv, "early_own")
    everyone = all_ids(after(cand_ids, from_core), (early_0, from_chip))
    take, gathered, further = candidate_rows(everyone, index_rows)
    early_1 = early_projections(
        meta, states, after(from_core, everyone), w_qkv_p, biases_p, "early_partner"
    )
    early_0 = after(early_0, early_1)
    w_out_p = swap(after(w_out, from_core), "tp", 1)
    w_up_p = swap(after(w_up, from_core), "tp", 1)
    w_down_p = swap(after(w_down, from_core), "tp", 1)

    part = w_out.shape[0] // 2
    w_half = lax.dynamic_slice_in_dim(w_out, (group & 1) * part, part)
    w_x0 = swap(after(w_half, from_chip), "tp", 2)

    context_0 = attention(
        meta, lengths, early_0, from_chip, from_diag, w_qkv_t, b_qkv, 1, "attention_own"
    )
    context_0x = swap(context_0, "tp", 2)
    w_x1 = swap(after(w_x0, context_0), "req", 1)
    context_1 = attention(
        meta, lengths, after(early_1, context_0), from_chip, from_diag, w_qkv_p, biases_p,
        6, "attention_partner",
    )
    context_1x = swap(context_1, "tp", 2)
    w_d0 = swap(after(w_x0, context_0), "tp", 1)
    w_d1 = swap(after(w_x1, context_1), "tp", 1)
    base = project_here(
        meta, blocks, (after(context_0, w_up_p, w_down_p), context_1), (w_out, w_out_p), b_out[None]
    )
    base = project_there(meta, base, context_0x, (w_x0, w_x1))
    sent = take(base)
    common = (
        context_1x, (w_d0, w_d1), ln1_gain[None], ln1_shift[None],
        (b_up[None], biases_p[3:].reshape(1, -1)), b_down[None], (w_up, w_up_p),
        (w_down, w_down_p),
    )
    down_there = feed_forward(False, meta, base, *common)
    down_x = swap(down_there, "tp", 2)
    down_here = feed_forward(True, meta, after(base, down_there), *common)
    rows = gathered(sent, context_1x, down_there, down_x)
    hidden, hidden_other, pool = finish(
        meta, lengths, down_here, down_x, ln2_gain[None], ln2_shift[None]
    )

    pools = (pool,) + tuple(swap(pool, "tp", mask) for mask in (1, 2, 3))
    hidden_p = swap(hidden_other, "tp", 1)
    rows = further(after(rows, *pools))
    scores, hidden_out = score(meta, lengths, pools, rows, hidden, hidden_p)
    return (hidden_out, scores)


def solution(mesh):
    placed = (
        P("req", "tp", None),
        P("req"),
        P(None, None, "tp"),
        P(None, "tp"),
        P("tp", None),
        P(),
        P(),
        P(),
        P(None, "tp"),
        P("tp"),
        P("tp", None),
        P(),
        P(),
        P(),
        P(("req", "tp"), None),
        P("req", "tp"),
    )
    return jax.shard_map(
        per_device,
        mesh=mesh,
        in_specs=placed,
        out_specs=(P("req", "tp", None), P("req", "tp")),
        check_vma=False,
    )
```

```python
import jax
import jax.numpy as jnp
from jax import lax
from jax.experimental import pallas as pl
from jax.experimental.pallas import tpu as pltpu
from jax.sharding import PartitionSpec as P

HEAD_DIM = 64
WINDOW = 512
SLOTS = 16
BF16 = jnp.bfloat16
F32 = jnp.float32
I32 = jnp.int32
MIB = 1024 * 1024
NO_COST = pl.CostEstimate(flops=1, bytes_accessed=1, transcendentals=0)


def cost(gflop):
    return pl.CostEstimate(flops=int(gflop * 10**9), bytes_accessed=MIB, transcendentals=0)


layer_eps = 1e-05
norm_eps = 1e-06

VMEM = pl.BlockSpec(memory_space=pltpu.VMEM)
SMEM = pl.BlockSpec(memory_space=pltpu.SMEM)
HBM = pl.BlockSpec(memory_space=pltpu.HBM)
ANY = pl.BlockSpec(memory_space=pl.ANY)


def layer_norm(values, gain, shift):
    centre = values - jnp.mean(values, axis=-1, keepdims=True)
    spread = jnp.mean(centre * centre, axis=-1, keepdims=True)
    return centre * lax.rsqrt(spread + layer_eps) * gain + shift


def swap(value, axis, mask):
    count = lax.axis_size(axis)
    return lax.ppermute(value, axis, [(i, i ^ mask) for i in range(count)])


def matmul(left, right):
    return jnp.dot(left, right, preferred_element_type=F32)


def params(mib):
    return pltpu.CompilerParams(vmem_limit_bytes=mib * MIB)


def after(value, *others):
    return lax.optimization_barrier((value,) + others)[0]


def project_three(text, w, b, out):
    for which in range(3):
        out[which] = (matmul(text, w[which]) + b[which : which + 1, :]).astype(BF16)


def early_kernel(meta, s0, s1, w, b, out):
    core = meta[1]
    project_three(jnp.concatenate([s0[core], s1[core]]), w, b, out)


def early_projections(meta, s0, s1, w, b, name):
    return pl.pallas_call(
        early_kernel,
        out_shape=jax.ShapeDtypeStruct((3, 2 * s0.shape[1], w.shape[2]), BF16),
        in_specs=[SMEM] + [VMEM] * 4,
        out_specs=VMEM,
        compiler_params=params(12),
        cost_estimate=NO_COST,
        name=name,
    )(meta, s0, s1, w, b)


def attention_kernel(meta, lengths, early, s2, s3, w, b, out, late, bias):
    rank = meta[0]
    core = meta[1]
    length = lengths[core]
    share = s2.shape[1]
    half = 2 * share
    seq_len = 4 * share
    wide = w.shape[2]
    project_three(jnp.concatenate([s2[core], s3[core]]), w, b, late)

    def position(index):
        return ((index // share) ^ rank) * share + index % share

    row_pos = position(lax.broadcasted_iota(I32, (seq_len, 1), 0))
    col_pos = position(lax.broadcasted_iota(I32, (1, seq_len), 1))
    keep = (jnp.abs(row_pos - col_pos) <= WINDOW // 2) & (col_pos < length)
    bias[...] = jnp.where(keep, F32(0.0), F32(-1e30))
    ones = jnp.ones((seq_len, 128), BF16)
    low = lax.broadcasted_iota(I32, (1, 128), 1) < HEAD_DIM
    scale = jnp.asarray(HEAD_DIM**-0.5, BF16)
    for pair in range(wide // 128):
        lanes = slice(pair * 128, (pair + 1) * 128)
        k_pair = jnp.concatenate([early[1, :, lanes], late[1, :, lanes]])
        v_pair = jnp.concatenate([early[2, :, lanes], late[2, :, lanes]])
        v_ones = jnp.concatenate([v_pair, ones], axis=1)
        for block in range(4):
            rows = slice(block * share, (block + 1) * share)
            first = (block % 2) * share
            q_pair = (early, late)[block // 2][0, first : first + share, lanes] * scale
            found = []
            for head in range(2):
                chosen = low if head == 0 else jnp.logical_not(low)
                q_head = jnp.where(chosen, q_pair, jnp.zeros((), BF16))
                logits = lax.dot_general(
                    q_head, k_pair, (((1,), (1,)), ((), ())), preferred_element_type=F32
                )
                logits = logits + bias[rows, :]
                top = jnp.max(logits, axis=-1, keepdims=True)
                expo = jnp.exp(logits - top).astype(BF16)
                summed = matmul(expo, v_ones)
                found.append(summed[:, :128] / summed[:, 128:])
            context = jnp.where(low, found[0], found[1])
            context = jnp.where(row_pos[rows] < length, context, F32(0.0))
            out[rows, lanes] = context.astype(BF16)


def attention(meta, lengths, early, s2, s3, w, b, gflop, name):
    seq_len = 4 * s2.shape[1]
    wide = w.shape[2]
    return pl.pallas_call(
        attention_kernel,
        out_shape=jax.ShapeDtypeStruct((seq_len, wide), BF16),
        in_specs=[SMEM] * 2 + [VMEM] * 5,
        out_specs=VMEM,
        scratch_shapes=[
            pltpu.VMEM((3, seq_len // 2, wide), BF16),
            pltpu.VMEM((seq_len, seq_len), F32),
        ],
        compiler_params=params(20),
        cost_estimate=cost(gflop),
        name=name,
    )(meta, lengths, early, s2, s3, w, b)


def joined(meta, first, second):
    swapped = (meta[2] & 1) != 0
    low = jnp.where(swapped, second[...], first[...])
    high = jnp.where(swapped, first[...], second[...])
    return jnp.concatenate([low, high])


def project_first_kernel(meta, s0, s1, s2, s3, here, there, w, first, second, b, out):
    share = s0.shape[1]
    weight = joined(meta, first, second)
    for index, block in enumerate((s0, s1, s2, s3)):
        rows = slice(index * share, (index + 1) * share)
        other = (index ^ 2) * share
        total = matmul(here[rows, :], w[...]) + matmul(there[other : other + share, :], weight)
        out[rows, :] = total + (block[meta[1]].astype(F32) + b[...])


def project_first(meta, blocks, here, there, w, pieces, b_out):
    _, share, width = blocks[0].shape
    return pl.pallas_call(
        project_first_kernel,
        out_shape=jax.ShapeDtypeStruct((4 * share, width), F32),
        in_specs=[SMEM] + [VMEM] * 10,
        out_specs=VMEM,
        compiler_params=params(16),
        cost_estimate=cost(1),
        name="project_first",
    )(meta, *blocks, here, there, w, *pieces, b_out)


def project_second_kernel(base, context, w, out):
    out[...] = base[...] + matmul(context[...], w[...])


def project_second(base, context, w):
    return pl.pallas_call(
        project_second_kernel,
        out_shape=jax.ShapeDtypeStruct(base.shape, F32),
        in_specs=[VMEM] * 3,
        out_specs=VMEM,
        input_output_aliases={0: 0},
        compiler_params=params(12),
        cost_estimate=cost(1),
        name="project_second",
    )(base, context, w)


def feed_kernel(
    keep_rest, meta, base, c3, first, second, gain, shift, b0, b1, b_down,
    up0, up1, down0, down1, out, up_buf, down_buf, act, sems,
):
    hidden = up0.shape[1]
    copies = [
        pltpu.make_async_copy(source, target, sems.at[index])
        for index, (source, target) in enumerate(
            (
                (up0, up_buf.at[0]),
                (up1, up_buf.at[1]),
                (down0, down_buf.at[0]),
                (down1, down_buf.at[1]),
            )
        )
    ]
    for copy in copies:
        copy.start()
    total = base[...] + matmul(c3[...], joined(meta, first, second))
    normed = layer_norm(total, gain[...], shift[...]).astype(BF16)
    step = 512
    for part in range(2):
        copies[part].wait()
        biases = (b0, b1)[part]
        for low in range(0, hidden, step):
            up = matmul(normed, up_buf[part, :, low : low + step]) + biases[:, low : low + step]
            activated = 0.5 * up * (1.0 + lax.erf(up * F32(0.5**0.5)))
            act[:, part * hidden + low : part * hidden + low + step] = activated.astype(BF16)
    copies[2].wait()
    down = matmul(act[:, :hidden], down_buf[0])
    copies[3].wait()
    down = down + matmul(act[:, hidden:], down_buf[1])
    if keep_rest:
        down = down + (normed.astype(F32) + b_down[...])
    out[...] = down.astype(out.dtype)


def feed_forward(keep_rest, meta, base, context, pieces, gain, shift, biases, b_down, ups, downs):
    seq_len, width = base.shape
    half = seq_len // 2
    here = 0 if keep_rest else 1
    hidden = ups[0].shape[1]
    heads_wide = context.shape[1]
    base_spec = pl.BlockSpec((half, width), lambda i: (here, 0))
    context_spec = pl.BlockSpec((half, heads_wide), lambda i: (1 - here, 0))
    return pl.pallas_call(
        lambda *refs: feed_kernel(keep_rest, *refs),
        out_shape=jax.ShapeDtypeStruct((half, width), F32 if keep_rest else BF16),
        grid=(1,),
        in_specs=[SMEM, base_spec, context_spec] + [VMEM] * 7 + [ANY] * 4,
        out_specs=VMEM,
        scratch_shapes=[
            pltpu.VMEM((2, width, hidden), BF16),
            pltpu.VMEM((2, hidden, width), BF16),
            pltpu.VMEM((half, 2 * hidden), BF16),
            pltpu.SemaphoreType.DMA((4,)),
        ],
        compiler_params=params(32),
        cost_estimate=cost(8),
        name="feed_here" if keep_rest else "feed_there",
    )(meta, base, context, *pieces, gain, shift, *biases, b_down, *ups, *downs)


def finish_kernel(meta, lengths, here, there, gain, shift, own, other, pool):
    rank = meta[0]
    length = lengths[meta[1]]
    share = own.shape[0]
    total = here[...] + there[...].astype(F32)
    hidden = layer_norm(total, gain[...], shift[...]).astype(BF16)
    own[...] = hidden[:share]
    other[...] = hidden[share:]
    index = lax.broadcasted_iota(I32, (2 * share, 1), 0)
    pos = ((index // share) ^ rank) * share + index % share
    valid = jnp.where(pos < length, hidden.astype(F32), F32(0.0))
    pool[...] = jnp.sum(valid, axis=0, keepdims=True)


def finish(meta, lengths, here, there, gain, shift):
    half, width = here.shape
    block = jax.ShapeDtypeStruct((half // 2, width), BF16)
    return pl.pallas_call(
        finish_kernel,
        out_shape=(block, block, jax.ShapeDtypeStruct((1, width), F32)),
        in_specs=[SMEM] * 2 + [VMEM] * 4,
        out_specs=(VMEM, VMEM, VMEM),
        compiler_params=params(8),
        cost_estimate=cost(2),
        name="finish",
    )(meta, lengths, here, there, gain, shift)


def score_kernel(
    meta, lengths, pool, pool_core, pool_chip, pool_diag, rows, own, other, out, hidden_out
):
    core = meta[1]
    width = pool.shape[1]
    mine = pool[...] + pool_chip[...]
    theirs = pool_core[...] + pool_diag[...]
    first = jnp.where(core == 0, mine, theirs) / lengths[0].astype(F32)
    second = jnp.where(core == 0, theirs, mine) / lengths[1].astype(F32)
    row = lax.broadcasted_iota(I32, (8, width), 0)
    pooled = jnp.where(row == 0, first, jnp.where(row == 1, second, F32(0.0)))
    scale = lax.rsqrt(jnp.mean(pooled * pooled, axis=-1, keepdims=True) + norm_eps)
    queries = (pooled * scale).astype(BF16)
    found = lax.dot_general(
        queries, rows[...], (((1,), (1,)), ((), ())), preferred_element_type=F32
    )
    each = rows.shape[0] // 2
    out[0:1, :] = found[0:1, :each]
    out[1:2, :] = found[1:2, each:]
    hidden_out[core] = own[...]
    hidden_out[1 - core] = other[...]


def score(meta, lengths, pools, rows, own, other):
    return pl.pallas_call(
        score_kernel,
        out_shape=(
            jax.ShapeDtypeStruct((2, rows.shape[0] // 2), F32),
            jax.ShapeDtypeStruct((2,) + own.shape, BF16),
        ),
        in_specs=[SMEM] * 2 + [VMEM] * 7,
        out_specs=(VMEM, VMEM),
        compiler_params=params(8),
        cost_estimate=cost(1),
        name="score",
    )(meta, lengths, *pools, rows, own, other)


def take_kernel(wanted, counts, index, out, tiles, rows, sems):
    deep = tiles.shape[1]
    rows[...] = jnp.zeros_like(rows)

    def tile_copy(slot):
        first = pl.multiple_of((wanted[slot] // deep) * deep, deep)
        return pltpu.make_async_copy(index.at[pl.ds(first, deep)], tiles.at[slot], sems.at[slot])

    step = 4

    def start(number, carry):
        for slot in range(step):
            tile_copy(number * step + slot).start()
        return carry

    def select(number, carry):
        for slot in range(step):
            tile_copy(number * step + slot).wait()
        for slot in range(step):
            slot = number * step + slot
            line = lax.broadcasted_iota(I32, (deep, 1), 0) == wanted[slot] % deep
            chosen = jnp.where(line, tiles[slot].astype(F32), F32(0.0))
            rows[pl.ds(slot, 1), :] = jnp.sum(chosen, axis=0, keepdims=True)
        return carry

    def each_group(action):
        def group(number, carry):
            first = number * (SLOTS // step)
            return lax.fori_loop(first, first + (counts[number] + step - 1) // step, action, carry)

        lax.fori_loop(0, counts.shape[0], group, 0)

    each_group(start)
    each_group(select)
    out[...] = rows[...].astype(BF16)


def take_rows(wanted, counts, index_rows):
    slots = wanted.shape[0]
    width = index_rows.shape[1]
    return pl.pallas_call(
        take_kernel,
        out_shape=jax.ShapeDtypeStruct((slots, width), BF16),
        in_specs=[SMEM, SMEM, HBM],
        out_specs=VMEM,
        scratch_shapes=[
            pltpu.VMEM((slots, 16, width), BF16),
            pltpu.VMEM((slots, width), F32),
            pltpu.SemaphoreType.DMA((slots,)),
        ],
        compiler_params=params(8 + slots // 16),
        cost_estimate=NO_COST,
        name="take_rows",
    )(wanted, counts, index_rows)


def place_kernel(place, received, out):
    chosen = lax.dot_general(
        place[...], received[...], (((0,), (0,)), ((), ())), preferred_element_type=F32
    )
    out[...] = chosen.astype(BF16)


def place_rows(place, received):
    return pl.pallas_call(
        place_kernel,
        out_shape=jax.ShapeDtypeStruct((place.shape[1], received.shape[1]), BF16),
        in_specs=[VMEM] * 2,
        out_specs=VMEM,
        compiler_params=params(8),
        cost_estimate=NO_COST,
        name="place_rows",
    )(place, received)


def ranked(mask):
    count = mask.shape[-1]
    before = jnp.arange(count)[:, None] < jnp.arange(count)[None, :]
    return matmul(mask.astype(BF16), before.astype(BF16)).astype(I32)


def masks(axis):
    mask = 1
    while mask < lax.axis_size(axis):
        yield mask
        mask *= 2


def all_ids(cand_ids, early, late):
    held = cand_ids.reshape(1, -1)
    for mask in masks("req"):
        held = jnp.concatenate([held, swap(held, "req", mask)])
        if mask == 1:
            held = after(held, early)
    held = after(held, *late)
    parts = [held] + [swap(held, "tp", mask) for mask in (1, 2, 3)]
    return jnp.concatenate(parts, axis=1)


def candidate_rows(everyone, index_rows):
    rank = lax.axis_index("tp")
    group = lax.axis_index("req")
    groups = lax.axis_size("req")
    rows_here, width = index_rows.shape

    owner = lax.div(everyone, I32(rows_here))
    shards = jnp.arange(4 * groups, dtype=I32)
    load = jnp.sum((owner[:, :, None] == shards).astype(I32), axis=1)
    rounds = lax.div(jnp.max(load) + SLOTS - 1, I32(SLOTS))

    send_mask = owner == group * 4 + rank
    send_rank = jnp.where(send_mask, ranked(send_mask), -1)
    send_count = jnp.sum(send_mask.astype(I32), axis=1)
    local = everyone - (group * 4 + rank) * rows_here
    order = [0]
    for mask in reversed(list(masks("req"))):
        order = order + [entry + mask for entry in order]
    sources = (jnp.array(order, I32) ^ group) * 4 + rank
    take_mask = owner[:1] == sources[:, None]
    take_rank = jnp.where(take_mask, ranked(take_mask), -1)
    slots = jnp.arange(SLOTS, dtype=I32)

    def take(number, gate):
        places = slots + number * SLOTS
        chosen = send_rank[:, None, :] == places[:, None]
        wanted = jnp.sum(jnp.where(chosen, local[:, None, :], 0), axis=-1).reshape(-1)
        counts = jnp.clip(send_count - number * SLOTS, 0, SLOTS)
        return take_rows(after(wanted, *gate), counts, index_rows)

    def gathered(number, sent, gates=()):
        held = sent.reshape(1, groups, SLOTS * width)
        for step, mask in enumerate(reversed(list(masks("req")))):
            if step < len(gates) and gates[step] is not None:
                held = after(held, gates[step])
            other = swap(held[:, mask:], "req", mask)
            held = jnp.concatenate([held[:, :mask], other])
        places = slots + number * SLOTS
        place = (take_rank[:, None, :] == places[:, None]).reshape(groups * SLOTS, -1)
        found = place_rows(place.astype(BF16), held.reshape(groups * SLOTS, width))
        found = found.reshape(4, -1, width)
        parts = [swap(found[mask], "tp", mask) for mask in (1, 2, 3)]
        return found[0] + parts[0] + parts[1] + parts[2]

    def further(rows):
        return lax.fori_loop(
            1, rounds, lambda n, total: total + gathered(n, take(n, ())), rows
        )

    return lambda *gate: take(0, gate), lambda sent, *gates: gathered(0, sent, gates), further


def per_device(
    states,
    lengths,
    w_qkv,
    b_qkv,
    w_out,
    b_out,
    ln1_gain,
    ln1_shift,
    w_up,
    b_up,
    w_down,
    b_down,
    ln2_gain,
    ln2_shift,
    index_rows,
    cand_ids,
):
    rank = lax.axis_index("tp")
    group = lax.axis_index("req")
    meta = jnp.stack([rank, rank & 1, group]).astype(I32)

    from_chip = swap(states, "tp", 2)
    from_core = swap(states, "tp", 1)
    from_diag = swap(from_chip, "tp", 1)
    blocks = (states, from_core, from_chip, from_diag)
    w_qkv_t = w_qkv.transpose(1, 0, 2)
    w_qkv_p = swap(w_qkv_t, "tp", 1)
    biases = jnp.concatenate([b_qkv, b_up.reshape(-1, b_qkv.shape[1])])
    biases_p = swap(after(biases, from_core), "tp", 1)
    early_0 = early_projections(meta, states, from_core, w_qkv_t, b_qkv, "early_own")
    everyone = all_ids(after(cand_ids, from_core), early_0, (from_chip,))
    take, gathered, further = candidate_rows(everyone, index_rows)
    early_1 = early_projections(
        meta, states, after(from_core, everyone), w_qkv_p, biases_p, "early_partner"
    )
    early_0 = after(early_0, early_1)
    w_out_p = swap(after(w_out, from_core), "tp", 1)
    w_up_p = swap(w_up, "tp", 1)
    w_down_p = swap(w_down, "tp", 1)

    part = w_out.shape[0] // 2
    w_half = lax.dynamic_slice_in_dim(w_out, (group & 1) * part, part)
    w_x0 = swap(after(w_half, from_chip), "tp", 2)

    context_0 = attention(
        meta, lengths, after(early_0, w_up_p, w_down_p), from_chip, from_diag, w_qkv_t, b_qkv, 1,
        "attention_own",
    )
    context_0x = swap(context_0, "tp", 2)
    w_x1 = swap(after(w_x0, context_0), "req", 1)
    context_1 = attention(
        meta, lengths, after(early_1, context_0), from_chip, from_diag, w_qkv_p, biases_p,
        6, "attention_partner",
    )
    context_1x = swap(context_1, "tp", 2)
    w_d0 = swap(after(w_x0, context_0), "tp", 1)
    w_d1 = swap(after(w_x1, context_1), "tp", 1)
    base = project_first(
        meta, blocks, context_0, context_0x, w_out, (w_x0, w_x1), b_out[None]
    )
    base = project_second(base, context_1, w_out_p)
    sent = take(base)
    common = (
        context_1x, (w_d0, w_d1), ln1_gain[None], ln1_shift[None],
        (b_up[None], biases_p[3:].reshape(1, -1)), b_down[None], (w_up, w_up_p),
        (w_down, w_down_p),
    )
    down_there = feed_forward(False, meta, base, *common)
    down_x = swap(down_there, "tp", 2)
    down_here = feed_forward(True, meta, after(base, down_there), *common)
    down_x = after(down_x, down_here)
    rows = gathered(sent, context_1x, down_there, down_x)
    hidden, hidden_other, pool = finish(
        meta, lengths, down_here, down_x, ln2_gain[None], ln2_shift[None]
    )

    pools = (pool,) + tuple(swap(pool, "tp", mask) for mask in (1, 2, 3))
    hidden_p = swap(hidden_other, "tp", 1)
    rows = further(after(rows, *pools))
    scores, hidden_out = score(meta, lengths, pools, rows, hidden, hidden_p)
    return (hidden_out, scores)


def solution(mesh):
    placed = (
        P("req", "tp", None),
        P("req"),
        P(None, None, "tp"),
        P(None, "tp"),
        P("tp", None),
        P(),
        P(),
        P(),
        P(None, "tp"),
        P("tp"),
        P("tp", None),
        P(),
        P(),
        P(),
        P(("req", "tp"), None),
        P("req", "tp"),
    )
    return jax.shard_map(
        per_device,
        mesh=mesh,
        in_specs=placed,
        out_specs=(P("req", "tp", None), P("req", "tp")),
        check_vma=False,
    )
```

```python
import jax
import jax.numpy as jnp
from jax import lax
from jax.experimental import pallas as pl
from jax.experimental.pallas import tpu as pltpu
from jax.sharding import PartitionSpec as P

HEAD_DIM = 64
WINDOW = 512
SLOTS = 16
BF16 = jnp.bfloat16
F32 = jnp.float32
I32 = jnp.int32
MIB = 1024 * 1024
NO_COST = pl.CostEstimate(flops=1, bytes_accessed=1, transcendentals=0)


def cost(gflop):
    return pl.CostEstimate(flops=int(gflop * 10**9), bytes_accessed=MIB, transcendentals=0)


layer_eps = 1e-05
norm_eps = 1e-06

VMEM = pl.BlockSpec(memory_space=pltpu.VMEM)
SMEM = pl.BlockSpec(memory_space=pltpu.SMEM)
HBM = pl.BlockSpec(memory_space=pltpu.HBM)
ANY = pl.BlockSpec(memory_space=pl.ANY)


def layer_norm(values, gain, shift):
    centre = values - jnp.mean(values, axis=-1, keepdims=True)
    spread = jnp.mean(centre * centre, axis=-1, keepdims=True)
    return centre * lax.rsqrt(spread + layer_eps) * gain + shift


def swap(value, axis, mask):
    count = lax.axis_size(axis)
    return lax.ppermute(value, axis, [(i, i ^ mask) for i in range(count)])


def matmul(left, right):
    return jnp.dot(left, right, preferred_element_type=F32)


def params(mib):
    return pltpu.CompilerParams(vmem_limit_bytes=mib * MIB)


def after(value, *others):
    return lax.optimization_barrier((value,) + others)[0]


def project_three(text, w, b, out):
    for which in range(3):
        out[which] = (matmul(text, w[which]) + b[which : which + 1, :]).astype(BF16)


def early_kernel(s0, s1, w, b, out):
    core = lax.axis_index("tp") & 1
    project_three(jnp.concatenate([s0[core], s1[core]]), w, b, out)


def early_and_half_kernel(s0, s1, w, b, w_out, out, half):
    early_kernel(s0, s1, w, b, out)
    part = half.shape[0]
    first = pl.multiple_of((lax.axis_index("req") & 1) * part, part)
    half[...] = w_out[pl.ds(first, part), :]


def early_projections(s0, s1, w, b, name, w_out=None):
    result = jax.ShapeDtypeStruct((3, 2 * s0.shape[1], w.shape[2]), BF16)
    operands = (s0, s1, w, b)
    if w_out is not None:
        operands += (w_out,)
        result = (result, jax.ShapeDtypeStruct((w_out.shape[0] // 2, w_out.shape[1]), BF16))
    return pl.pallas_call(
        early_kernel if w_out is None else early_and_half_kernel,
        out_shape=result,
        in_specs=[VMEM] * len(operands),
        out_specs=VMEM if w_out is None else (VMEM, VMEM),
        compiler_params=params(12),
        cost_estimate=NO_COST,
        name=name,
    )(*operands)


def attention_kernel(lengths, early, s2, s3, w, b, out, late, bias):
    rank = lax.axis_index("tp")
    core = rank & 1
    length = lengths[core]
    share = s2.shape[1]
    half = 2 * share
    seq_len = 4 * share
    wide = w.shape[2]
    project_three(jnp.concatenate([s2[core], s3[core]]), w, b, late)

    def position(index):
        return ((index // share) ^ rank) * share + index % share

    row_pos = position(lax.broadcasted_iota(I32, (seq_len, 1), 0))
    col_pos = position(lax.broadcasted_iota(I32, (1, seq_len), 1))
    keep = (jnp.abs(row_pos - col_pos) <= WINDOW // 2) & (col_pos < length)
    bias[...] = jnp.where(keep, F32(0.0), F32(-1e30))
    ones = jnp.ones((seq_len, 128), BF16)
    low = lax.broadcasted_iota(I32, (1, 128), 1) < HEAD_DIM
    scale = jnp.asarray(HEAD_DIM**-0.5, BF16)
    for pair in range(wide // 128):
        lanes = slice(pair * 128, (pair + 1) * 128)
        k_pair = jnp.concatenate([early[1, :, lanes], late[1, :, lanes]])
        v_pair = jnp.concatenate([early[2, :, lanes], late[2, :, lanes]])
        v_ones = jnp.concatenate([v_pair, ones], axis=1)
        for block in range(4):
            rows = slice(block * share, (block + 1) * share)
            first = (block % 2) * share
            q_pair = (early, late)[block // 2][0, first : first + share, lanes] * scale
            found = []
            for head in range(2):
                chosen = low if head == 0 else jnp.logical_not(low)
                q_head = jnp.where(chosen, q_pair, jnp.zeros((), BF16))
                logits = lax.dot_general(
                    q_head, k_pair, (((1,), (1,)), ((), ())), preferred_element_type=F32
                )
                logits = logits + bias[rows, :]
                top = jnp.max(logits, axis=-1, keepdims=True)
                expo = jnp.exp(logits - top).astype(BF16)
                summed = matmul(expo, v_ones)
                found.append(summed[:, :128] / summed[:, 128:])
            context = jnp.where(low, found[0], found[1])
            context = jnp.where(row_pos[rows] < length, context, F32(0.0))
            out[rows, lanes] = context.astype(BF16)


def attention(lengths, early, s2, s3, w, b, gflop, name):
    seq_len = 4 * s2.shape[1]
    wide = w.shape[2]
    return pl.pallas_call(
        attention_kernel,
        out_shape=jax.ShapeDtypeStruct((seq_len, wide), BF16),
        in_specs=[SMEM] + [VMEM] * 5,
        out_specs=VMEM,
        scratch_shapes=[
            pltpu.VMEM((3, seq_len // 2, wide), BF16),
            pltpu.VMEM((seq_len, seq_len), F32),
        ],
        compiler_params=params(20),
        cost_estimate=cost(gflop),
        name=name,
    )(lengths, early, s2, s3, w, b)


def joined(first, second):
    swapped = (lax.axis_index("req") & 1) != 0
    low = jnp.where(swapped, second[...], first[...])
    high = jnp.where(swapped, first[...], second[...])
    return jnp.concatenate([low, high])


def project_first_kernel(s0, s1, s2, s3, here, there, w, first, second, b, out):
    share = s0.shape[1]
    core = lax.axis_index("tp") & 1
    weight = joined(first, second)
    for index, block in enumerate((s0, s1, s2, s3)):
        rows = slice(index * share, (index + 1) * share)
        other = (index ^ 2) * share
        total = matmul(here[rows, :], w[...]) + matmul(there[other : other + share, :], weight)
        out[rows, :] = total + (block[core].astype(F32) + b[...])


def project_first(blocks, here, there, w, pieces, b_out):
    _, share, width = blocks[0].shape
    return pl.pallas_call(
        project_first_kernel,
        out_shape=jax.ShapeDtypeStruct((4 * share, width), F32),
        in_specs=[VMEM] * 10,
        out_specs=VMEM,
        compiler_params=params(16),
        cost_estimate=cost(1),
        name="project_first",
    )(*blocks, here, there, w, *pieces, b_out)


def project_second_kernel(base, context, w, out):
    out[...] = base[...] + matmul(context[...], w[...])


def project_second(base, context, w):
    return pl.pallas_call(
        project_second_kernel,
        out_shape=jax.ShapeDtypeStruct(base.shape, F32),
        in_specs=[VMEM] * 3,
        out_specs=VMEM,
        input_output_aliases={0: 0},
        compiler_params=params(12),
        cost_estimate=cost(1),
        name="project_second",
    )(base, context, w)


def feed_kernel(
    keep_rest, base, c3, first, second, gain, shift, b0, b1, b_down,
    up0, up1, down0, down1, out, up_buf, down_buf, act, sems,
):
    hidden = up0.shape[1]
    copies = [
        pltpu.make_async_copy(source, target, sems.at[index])
        for index, (source, target) in enumerate(
            (
                (up0, up_buf.at[0]),
                (up1, up_buf.at[1]),
                (down0, down_buf.at[0]),
                (down1, down_buf.at[1]),
            )
        )
    ]
    for copy in copies:
        copy.start()
    total = base[...] + matmul(c3[...], joined(first, second))
    normed = layer_norm(total, gain[...], shift[...]).astype(BF16)
    step = 512
    for part in range(2):
        copies[part].wait()
        biases = (b0, b1)[part]
        for low in range(0, hidden, step):
            up = matmul(normed, up_buf[part, :, low : low + step]) + biases[:, low : low + step]
            activated = 0.5 * up * (1.0 + lax.erf(up * F32(0.5**0.5)))
            act[:, part * hidden + low : part * hidden + low + step] = activated.astype(BF16)
    copies[2].wait()
    down = matmul(act[:, :hidden], down_buf[0])
    copies[3].wait()
    down = down + matmul(act[:, hidden:], down_buf[1])
    if keep_rest:
        down = down + (normed.astype(F32) + b_down[...])
    out[...] = down.astype(out.dtype)


def feed_forward(keep_rest, base, context, pieces, gain, shift, biases, b_down, ups, downs):
    seq_len, width = base.shape
    half = seq_len // 2
    here = 0 if keep_rest else 1
    hidden = ups[0].shape[1]
    heads_wide = context.shape[1]
    base_spec = pl.BlockSpec((half, width), lambda i: (here, 0))
    context_spec = pl.BlockSpec((half, heads_wide), lambda i: (1 - here, 0))
    return pl.pallas_call(
        lambda *refs: feed_kernel(keep_rest, *refs),
        out_shape=jax.ShapeDtypeStruct((half, width), F32 if keep_rest else BF16),
        grid=(1,),
        in_specs=[base_spec, context_spec] + [VMEM] * 7 + [ANY] * 4,
        out_specs=VMEM,
        scratch_shapes=[
            pltpu.VMEM((2, width, hidden), BF16),
            pltpu.VMEM((2, hidden, width), BF16),
            pltpu.VMEM((half, 2 * hidden), BF16),
            pltpu.SemaphoreType.DMA((4,)),
        ],
        compiler_params=params(32),
        cost_estimate=cost(8),
        name="feed_here" if keep_rest else "feed_there",
    )(base, context, *pieces, gain, shift, *biases, b_down, *ups, *downs)


def finish_kernel(lengths, here, there, gain, shift, own, other, pool):
    rank = lax.axis_index("tp")
    length = lengths[rank & 1]
    share = own.shape[0]
    total = here[...] + there[...].astype(F32)
    hidden = layer_norm(total, gain[...], shift[...]).astype(BF16)
    own[...] = hidden[:share]
    other[...] = hidden[share:]
    index = lax.broadcasted_iota(I32, (2 * share, 1), 0)
    pos = ((index // share) ^ rank) * share + index % share
    valid = jnp.where(pos < length, hidden.astype(F32), F32(0.0))
    pool[...] = jnp.sum(valid, axis=0, keepdims=True)


def finish(lengths, here, there, gain, shift):
    half, width = here.shape
    block = jax.ShapeDtypeStruct((half // 2, width), BF16)
    return pl.pallas_call(
        finish_kernel,
        out_shape=(block, block, jax.ShapeDtypeStruct((1, width), F32)),
        in_specs=[SMEM] + [VMEM] * 4,
        out_specs=(VMEM, VMEM, VMEM),
        compiler_params=params(8),
        cost_estimate=cost(2),
        name="finish",
    )(lengths, here, there, gain, shift)


def score_kernel(
    lengths, pool, pool_core, pool_chip, pool_diag, rows, own, other, out, hidden_out
):
    core = lax.axis_index("tp") & 1
    width = pool.shape[1]
    mine = pool[...] + pool_chip[...]
    theirs = pool_core[...] + pool_diag[...]
    first = jnp.where(core == 0, mine, theirs) / lengths[0].astype(F32)
    second = jnp.where(core == 0, theirs, mine) / lengths[1].astype(F32)
    row = lax.broadcasted_iota(I32, (8, width), 0)
    pooled = jnp.where(row == 0, first, jnp.where(row == 1, second, F32(0.0)))
    scale = lax.rsqrt(jnp.mean(pooled * pooled, axis=-1, keepdims=True) + norm_eps)
    queries = (pooled * scale).astype(BF16)
    found = lax.dot_general(
        queries, rows[...], (((1,), (1,)), ((), ())), preferred_element_type=F32
    )
    each = rows.shape[0] // 2
    out[0:1, :] = found[0:1, :each]
    out[1:2, :] = found[1:2, each:]
    hidden_out[core] = own[...]
    hidden_out[1 - core] = other[...]


def score(lengths, pools, rows, own, other):
    return pl.pallas_call(
        score_kernel,
        out_shape=(
            jax.ShapeDtypeStruct((2, rows.shape[0] // 2), F32),
            jax.ShapeDtypeStruct((2,) + own.shape, BF16),
        ),
        in_specs=[SMEM] + [VMEM] * 7,
        out_specs=(VMEM, VMEM),
        compiler_params=params(8),
        cost_estimate=cost(1),
        name="score",
    )(lengths, *pools, rows, own, other)


def take_kernel(
    number, i0, i1, i2, i3, index, out, place, rounds, numbers, chosen, tiles, rows, sems, sem
):
    rank = lax.axis_index("tp")
    group = lax.axis_index("req")
    deep = tiles.shape[1]
    groups = i0.shape[0]
    rows_here = index.shape[0]
    first_place = number[0] * SLOTS
    ids = jnp.concatenate([i0[...], i1[...], i2[...], i3[...]], axis=1)
    count = ids.shape[1]
    owner = lax.shift_right_logical(ids, I32(rows_here.bit_length() - 1))
    before = lax.broadcasted_iota(I32, (count, count), 0) < lax.broadcasted_iota(
        I32, (count, count), 1
    )
    before = before.astype(F32).astype(BF16)
    slot = lax.broadcasted_iota(I32, (SLOTS, 1), 0) + first_place

    def ranked(mask):
        ranks = matmul(mask.astype(F32).astype(BF16), before).astype(I32)
        return jnp.where(mask, ranks, -1)

    mine = owner == group * 4 + rank
    send_rank = ranked(mine)
    local = ids - (group * 4 + rank) * rows_here
    for k in range(groups):
        wanted = jnp.where(send_rank[k : k + 1] == slot, local[k : k + 1], 0)
        wanted = jnp.sum(wanted, axis=1, keepdims=True)
        numbers[k * SLOTS : (k + 1) * SLOTS, :] = jnp.broadcast_to(wanted, (SLOTS, 128))
    counts = jnp.sum(mine.astype(I32), axis=1, keepdims=True)
    numbers[groups * SLOTS :, :] = jnp.broadcast_to(counts, (groups, 128))
    copy = pltpu.make_async_copy(numbers, chosen, sem)
    copy.start()

    sources = lax.broadcasted_iota(I32, (groups, 1), 0) * 4 + rank
    take_rank = ranked(owner[:1] == sources)
    for k in range(groups):
        here = (take_rank[k : k + 1] == slot).astype(F32)
        place[k * SLOTS : (k + 1) * SLOTS, :] = here.astype(BF16)
    most = jnp.zeros((groups, 1), I32)
    for shard in range(4 * groups):
        load = jnp.sum((owner == shard).astype(I32), axis=1, keepdims=True)
        most = jnp.maximum(most, load)
    rounds[0] = (jnp.max(most) + SLOTS - 1) // SLOTS
    rows[...] = jnp.zeros_like(rows)
    copy.wait()

    def tile_copy(slot):
        first = pl.multiple_of((chosen[slot, 0] // deep) * deep, deep)
        return pltpu.make_async_copy(index.at[pl.ds(first, deep)], tiles.at[slot], sems.at[slot])

    step = 4

    def start(number, carry):
        for each in range(step):
            tile_copy(number * step + each).start()
        return carry

    def select(number, carry):
        for each in range(step):
            tile_copy(number * step + each).wait()
        for each in range(step):
            source = number * step + each
            line = lax.broadcasted_iota(I32, (deep, 1), 0) == chosen[source, 0] % deep
            row = jnp.where(line, tiles[source].astype(F32), F32(0.0))
            target = ((source // SLOTS) ^ group) * SLOTS + source % SLOTS
            rows[pl.ds(target, 1), :] = jnp.sum(row, axis=0, keepdims=True)
        return carry

    def each_group(action):
        def one(number, carry):
            first = number * (SLOTS // step)
            left = jnp.clip(chosen[groups * SLOTS + number, 0] - first_place, 0, SLOTS)
            return lax.fori_loop(first, first + (left + step - 1) // step, action, carry)

        lax.fori_loop(0, groups, one, 0)

    each_group(start)
    each_group(select)
    out[...] = rows[...].astype(BF16)


def take_rows(number, ids, index_rows):
    groups, each = ids[0].shape
    slots = groups * SLOTS
    width = index_rows.shape[1]
    return pl.pallas_call(
        take_kernel,
        out_shape=(
            jax.ShapeDtypeStruct((slots, width), BF16),
            jax.ShapeDtypeStruct((slots, 4 * each), BF16),
            jax.ShapeDtypeStruct((1,), I32),
        ),
        in_specs=[SMEM] + [VMEM] * 4 + [HBM],
        out_specs=(VMEM, VMEM, SMEM),
        scratch_shapes=[
            pltpu.VMEM((slots + groups, 128), I32),
            pltpu.SMEM((slots + groups, 128), I32),
            pltpu.VMEM((slots, 16, width), BF16),
            pltpu.VMEM((slots, width), F32),
            pltpu.SemaphoreType.DMA((slots,)),
            pltpu.SemaphoreType.DMA,
        ],
        compiler_params=params(8 + slots // 16),
        cost_estimate=NO_COST,
        name="take_rows",
    )(number, *ids, index_rows)


def place_kernel(place, received, out):
    chosen = lax.dot_general(
        place[...], received[...], (((0,), (0,)), ((), ())), preferred_element_type=F32
    )
    out[...] = chosen.astype(BF16)


def place_rows(place, received):
    return pl.pallas_call(
        place_kernel,
        out_shape=jax.ShapeDtypeStruct((place.shape[1], received.shape[1]), BF16),
        in_specs=[VMEM] * 2,
        out_specs=VMEM,
        compiler_params=params(8),
        cost_estimate=NO_COST,
        name="place_rows",
    )(place, received)


def masks(axis):
    mask = 1
    while mask < lax.axis_size(axis):
        yield mask
        mask *= 2


def ids_over_groups(cand_ids, early):
    held = cand_ids.reshape(1, -1)
    for mask in masks("req"):
        held = jnp.concatenate([held, swap(held, "req", mask)])
        if mask == 1:
            held = after(held, early)
    return held


def candidate_rows(ids, index_rows, gate):
    width = index_rows.shape[1]

    def gathered(sent, place):
        sent = lax.all_to_all(sent, "req", 0, 0, tiled=True)
        found = place_rows(place, sent).reshape(4, -1, width)
        parts = [swap(found[mask], "tp", mask) for mask in (1, 2, 3)]
        return found[0] + parts[0] + parts[1] + parts[2]

    first = (after(ids[0], gate),) + ids[1:]
    sent, place, rounds = take_rows(jnp.zeros((1,), I32), first, index_rows)

    def one_more(number, total):
        sent, place, _ = take_rows(number.reshape(1), ids, index_rows)
        return total + gathered(sent, place)

    def further(rows):
        return lax.fori_loop(1, rounds[0], one_more, rows)

    return lambda gate: gathered(after(sent, gate), place), further


def per_device(
    states,
    lengths,
    w_qkv,
    b_qkv,
    w_out,
    b_out,
    ln1_gain,
    ln1_shift,
    w_up,
    b_up,
    w_down,
    b_down,
    ln2_gain,
    ln2_shift,
    index_rows,
    cand_ids,
):
    from_chip = swap(states, "tp", 2)
    from_core = swap(states, "tp", 1)
    w_qkv_t = w_qkv.transpose(1, 0, 2)
    w_qkv_p = swap(w_qkv_t, "tp", 1)
    b_qkv_p = swap(b_qkv, "tp", 1)
    b_up_p = swap(b_up, "tp", 1)
    early_0, w_half = early_projections(states, from_core, w_qkv_t, b_qkv, "early_own", w_out)
    own_ids = ids_over_groups(after(cand_ids, from_core), early_0)
    from_chip, own_ids = lax.optimization_barrier((from_chip, own_ids))
    from_diag = swap(from_chip, "tp", 1)
    blocks = (states, from_core, from_chip, from_diag)
    ids = (own_ids,) + tuple(swap(own_ids, "tp", mask) for mask in (1, 2, 3))
    early_1 = early_projections(
        states, after(from_core, *ids, b_up_p), w_qkv_p, b_qkv_p, "early_partner"
    )
    early_0 = after(early_0, early_1)
    w_out_p = swap(after(w_out, from_core), "tp", 1)
    w_up_p = swap(w_up, "tp", 1)
    w_down_p = swap(w_down, "tp", 1)

    w_x0 = swap(after(w_half, from_chip), "tp", 2)

    context_0 = attention(
        lengths, after(early_0, w_up_p, w_down_p), from_chip, from_diag, w_qkv_t, b_qkv, 1,
        "attention_own",
    )
    context_0x = swap(context_0, "tp", 2)
    w_x1 = swap(after(w_x0, context_0), "req", 1)
    context_1 = attention(
        lengths, after(early_1, context_0), from_chip, from_diag, w_qkv_p, b_qkv_p,
        6, "attention_partner",
    )
    context_1x = swap(context_1, "tp", 2)
    w_d0 = swap(after(w_x0, context_0), "tp", 1)
    w_d1 = swap(after(w_x1, context_1), "tp", 1)
    base = project_first(
        blocks, context_0, context_0x, w_out, (w_x0, w_x1), b_out[None]
    )
    base = project_second(base, context_1, w_out_p)
    gathered, further = candidate_rows(ids, index_rows, base)
    common = (
        context_1x, (w_d0, w_d1), ln1_gain[None], ln1_shift[None],
        (b_up[None], b_up_p[None]), b_down[None], (w_up, w_up_p),
        (w_down, w_down_p),
    )
    down_there = feed_forward(False, base, *common)
    down_x = swap(down_there, "tp", 2)
    down_here = feed_forward(True, after(base, down_there), *common)
    down_x = after(down_x, down_here)
    rows = gathered(down_here)
    hidden, hidden_other, pool = finish(
        lengths, down_here, down_x, ln2_gain[None], ln2_shift[None]
    )

    pools = (pool,) + tuple(swap(pool, "tp", mask) for mask in (1, 2, 3))
    hidden_p = swap(hidden_other, "tp", 1)
    rows = further(after(rows, *pools))
    scores, hidden_out = score(lengths, pools, rows, hidden, hidden_p)
    return (hidden_out, scores)


def solution(mesh):
    placed = (
        P("req", "tp", None),
        P("req"),
        P(None, None, "tp"),
        P(None, "tp"),
        P("tp", None),
        P(),
        P(),
        P(),
        P(None, "tp"),
        P("tp"),
        P("tp", None),
        P(),
        P(),
        P(),
        P(("req", "tp"), None),
        P("req", "tp"),
    )
    return jax.shard_map(
        per_device,
        mesh=mesh,
        in_specs=placed,
        out_specs=(P("req", "tp", None), P("req", "tp")),
        check_vma=False,
    )
```

```python
import jax
import jax.numpy as jnp
from jax import lax
from jax.experimental import pallas as pl
from jax.experimental.pallas import tpu as pltpu
from jax.sharding import PartitionSpec as P

HEAD_DIM = 64
WINDOW = 512
SLOTS = 16
BF16 = jnp.bfloat16
F32 = jnp.float32
I32 = jnp.int32
MIB = 1024 * 1024
NO_COST = pl.CostEstimate(flops=1, bytes_accessed=1, transcendentals=0)


def cost(gflop):
    return pl.CostEstimate(flops=int(gflop * 10**9) + 1, bytes_accessed=MIB, transcendentals=0)


layer_eps = 1e-05
norm_eps = 1e-06

VMEM = pl.BlockSpec(memory_space=pltpu.VMEM)
SMEM = pl.BlockSpec(memory_space=pltpu.SMEM)
HBM = pl.BlockSpec(memory_space=pltpu.HBM)
ANY = pl.BlockSpec(memory_space=pl.ANY)


def layer_norm(values, gain, shift):
    centre = values - jnp.mean(values, axis=-1, keepdims=True)
    spread = jnp.mean(centre * centre, axis=-1, keepdims=True)
    return centre * lax.rsqrt(spread + layer_eps) * gain + shift


def swap(value, axis, mask):
    count = lax.axis_size(axis)
    return lax.ppermute(value, axis, [(i, i ^ mask) for i in range(count)])


def matmul(left, right):
    return jnp.dot(left, right, preferred_element_type=F32)


def params(mib):
    return pltpu.CompilerParams(vmem_limit_bytes=mib * MIB)


def after(value, *others):
    return lax.optimization_barrier((value,) + others)[0]


def project_three(text, w, b, out):
    for which in range(3):
        out[which] = (matmul(text, w[which]) + b[which : which + 1, :]).astype(BF16)


def early_kernel(s0, s1, w, b, out):
    core = lax.axis_index("tp") & 1
    project_three(jnp.concatenate([s0[core], s1[core]]), w, b, out)


def early_own_kernel(s0, s1, w, b, b_up, w_out, out, biases, half):
    early_kernel(s0, s1, w, b, out)
    wide = b.shape[1]
    biases[0:3, :] = b[...]
    for chunk in range(b_up.shape[1] // wide):
        biases[3 + chunk : 4 + chunk, :] = b_up[:, chunk * wide : (chunk + 1) * wide]
    part = half.shape[0]
    first = pl.multiple_of((lax.axis_index("req") & 1) * part, part)
    half[...] = w_out[pl.ds(first, part), :]


def early_own(s0, s1, w, b, b_up, w_out):
    wide = w.shape[2]
    return pl.pallas_call(
        early_own_kernel,
        out_shape=(
            jax.ShapeDtypeStruct((3, 2 * s0.shape[1], wide), BF16),
            jax.ShapeDtypeStruct((3 + b_up.shape[1] // wide, wide), F32),
            jax.ShapeDtypeStruct((w_out.shape[0] // 2, w_out.shape[1]), BF16),
        ),
        in_specs=[VMEM] * 6,
        out_specs=(VMEM, VMEM, VMEM),
        compiler_params=params(12),
        cost_estimate=NO_COST,
        name="early_own",
    )(s0, s1, w, b, b_up, w_out)


def early_partner(s0, s1, w, biases):
    return pl.pallas_call(
        early_kernel,
        out_shape=jax.ShapeDtypeStruct((3, 2 * s0.shape[1], w.shape[2]), BF16),
        in_specs=[VMEM] * 4,
        out_specs=VMEM,
        compiler_params=params(12),
        cost_estimate=NO_COST,
        name="early_partner",
    )(s0, s1, w, biases)


def attention_kernel(lengths, early, s2, s3, w, b, out, late, bias):
    rank = lax.axis_index("tp")
    core = rank & 1
    length = lengths[core]
    share = s2.shape[1]
    half = 2 * share
    seq_len = 4 * share
    wide = w.shape[2]
    project_three(jnp.concatenate([s2[core], s3[core]]), w, b, late)

    def position(index):
        return ((index // share) ^ rank) * share + index % share

    row_pos = position(lax.broadcasted_iota(I32, (seq_len, 1), 0))
    col_pos = position(lax.broadcasted_iota(I32, (1, seq_len), 1))
    keep = (jnp.abs(row_pos - col_pos) <= WINDOW // 2) & (col_pos < length)
    bias[...] = jnp.where(keep, F32(0.0), F32(-1e30))
    ones = jnp.ones((seq_len, 128), BF16)
    low = lax.broadcasted_iota(I32, (1, 128), 1) < HEAD_DIM
    scale = jnp.asarray(HEAD_DIM**-0.5, BF16)
    for pair in range(wide // 128):
        lanes = slice(pair * 128, (pair + 1) * 128)
        k_pair = jnp.concatenate([early[1, :, lanes], late[1, :, lanes]])
        v_pair = jnp.concatenate([early[2, :, lanes], late[2, :, lanes]])
        v_ones = jnp.concatenate([v_pair, ones], axis=1)
        for block in range(4):
            rows = slice(block * share, (block + 1) * share)
            first = (block % 2) * share
            q_pair = (early, late)[block // 2][0, first : first + share, lanes] * scale
            found = []
            for head in range(2):
                chosen = low if head == 0 else jnp.logical_not(low)
                q_head = jnp.where(chosen, q_pair, jnp.zeros((), BF16))
                logits = lax.dot_general(
                    q_head, k_pair, (((1,), (1,)), ((), ())), preferred_element_type=F32
                )
                logits = logits + bias[rows, :]
                top = jnp.max(logits, axis=-1, keepdims=True)
                expo = jnp.exp(logits - top).astype(BF16)
                summed = matmul(expo, v_ones)
                found.append(summed[:, :128] / summed[:, 128:])
            context = jnp.where(low, found[0], found[1])
            context = jnp.where(row_pos[rows] < length, context, F32(0.0))
            out[rows, lanes] = context.astype(BF16)


def attention(lengths, early, s2, s3, w, b, gflop, name):
    seq_len = 4 * s2.shape[1]
    wide = w.shape[2]
    return pl.pallas_call(
        attention_kernel,
        out_shape=jax.ShapeDtypeStruct((seq_len, wide), BF16),
        in_specs=[SMEM] + [VMEM] * 5,
        out_specs=VMEM,
        scratch_shapes=[
            pltpu.VMEM((3, seq_len // 2, wide), BF16),
            pltpu.VMEM((seq_len, seq_len), F32),
        ],
        compiler_params=params(20),
        cost_estimate=cost(gflop),
        name=name,
    )(lengths, early, s2, s3, w, b)


def joined(first, second):
    swapped = (lax.axis_index("req") & 1) != 0
    low = jnp.where(swapped, second[...], first[...])
    high = jnp.where(swapped, first[...], second[...])
    return jnp.concatenate([low, high])


def project_first_kernel(s0, s1, s2, s3, here, there, w, first, second, b, out):
    share = s0.shape[1]
    core = lax.axis_index("tp") & 1
    weight = joined(first, second)
    for index, block in enumerate((s0, s1, s2, s3)):
        rows = slice(index * share, (index + 1) * share)
        other = (index ^ 2) * share
        total = matmul(here[rows, :], w[...]) + matmul(there[other : other + share, :], weight)
        out[rows, :] = total + (block[core].astype(F32) + b[...])


def project_first(blocks, here, there, w, pieces, b_out):
    _, share, width = blocks[0].shape
    return pl.pallas_call(
        project_first_kernel,
        out_shape=jax.ShapeDtypeStruct((4 * share, width), F32),
        in_specs=[VMEM] * 10,
        out_specs=VMEM,
        compiler_params=params(16),
        cost_estimate=cost(1),
        name="project_first",
    )(*blocks, here, there, w, *pieces, b_out)


def project_second_kernel(base, context, w, out):
    out[...] = base[...] + matmul(context[...], w[...])


def project_second(base, context, w):
    return pl.pallas_call(
        project_second_kernel,
        out_shape=jax.ShapeDtypeStruct(base.shape, F32),
        in_specs=[VMEM] * 3,
        out_specs=VMEM,
        input_output_aliases={0: 0},
        compiler_params=params(12),
        cost_estimate=cost(1),
        name="project_second",
    )(base, context, w)


def feed_kernel(
    keep_rest, base, c3, first, second, gain, shift, b0, b1, b_down,
    up0, up1, down0, down1, out, up_buf, down_buf, act, sems,
):
    hidden = up0.shape[1]
    copies = [
        pltpu.make_async_copy(source, target, sems.at[index])
        for index, (source, target) in enumerate(
            (
                (up0, up_buf.at[0]),
                (up1, up_buf.at[1]),
                (down0, down_buf.at[0]),
                (down1, down_buf.at[1]),
            )
        )
    ]
    for copy in copies:
        copy.start()
    total = base[...] + matmul(c3[...], joined(first, second))
    normed = layer_norm(total, gain[...], shift[...]).astype(BF16)
    step = 512
    wide = b1.shape[1]
    for part in range(2):
        copies[part].wait()
        for low in range(0, hidden, step):
            if part == 0:
                bias = b0[:, low : low + step]
            else:
                rows = range(3 + low // wide, 3 + (low + step) // wide)
                bias = jnp.concatenate([b1[row : row + 1, :] for row in rows], axis=1)
            up = matmul(normed, up_buf[part, :, low : low + step]) + bias
            activated = 0.5 * up * (1.0 + lax.erf(up * F32(0.5**0.5)))
            act[:, part * hidden + low : part * hidden + low + step] = activated.astype(BF16)
    copies[2].wait()
    down = matmul(act[:, :hidden], down_buf[0])
    copies[3].wait()
    down = down + matmul(act[:, hidden:], down_buf[1])
    if keep_rest:
        down = down + (normed.astype(F32) + b_down[...])
    out[...] = down.astype(out.dtype)


def feed_forward(keep_rest, base, context, pieces, gain, shift, biases, b_down, ups, downs):
    seq_len, width = base.shape
    half = seq_len // 2
    here = 0 if keep_rest else 1
    hidden = ups[0].shape[1]
    heads_wide = context.shape[1]
    base_spec = pl.BlockSpec((half, width), lambda i: (here, 0))
    context_spec = pl.BlockSpec((half, heads_wide), lambda i: (1 - here, 0))
    return pl.pallas_call(
        lambda *refs: feed_kernel(keep_rest, *refs),
        out_shape=jax.ShapeDtypeStruct((half, width), F32 if keep_rest else BF16),
        grid=(1,),
        in_specs=[base_spec, context_spec] + [VMEM] * 7 + [ANY] * 4,
        out_specs=VMEM,
        scratch_shapes=[
            pltpu.VMEM((2, width, hidden), BF16),
            pltpu.VMEM((2, hidden, width), BF16),
            pltpu.VMEM((half, 2 * hidden), BF16),
            pltpu.SemaphoreType.DMA((4,)),
        ],
        compiler_params=params(32),
        cost_estimate=cost(8),
        name="feed_here" if keep_rest else "feed_there",
    )(base, context, *pieces, gain, shift, *biases, b_down, *ups, *downs)


def finish_kernel(lengths, here, there, gain, shift, own, other, pool):
    rank = lax.axis_index("tp")
    length = lengths[rank & 1]
    share = own.shape[0]
    total = here[...] + there[...].astype(F32)
    hidden = layer_norm(total, gain[...], shift[...]).astype(BF16)
    own[...] = hidden[:share]
    other[...] = hidden[share:]
    index = lax.broadcasted_iota(I32, (2 * share, 1), 0)
    pos = ((index // share) ^ rank) * share + index % share
    valid = jnp.where(pos < length, hidden.astype(F32), F32(0.0))
    pool[...] = jnp.sum(valid, axis=0, keepdims=True)


def finish(lengths, here, there, gain, shift):
    half, width = here.shape
    block = jax.ShapeDtypeStruct((half // 2, width), BF16)
    return pl.pallas_call(
        finish_kernel,
        out_shape=(block, block, jax.ShapeDtypeStruct((1, width), F32)),
        in_specs=[SMEM] + [VMEM] * 4,
        out_specs=(VMEM, VMEM, VMEM),
        compiler_params=params(8),
        cost_estimate=cost(2),
        name="finish",
    )(lengths, here, there, gain, shift)


def score_kernel(
    lengths, pool, pool_core, pool_chip, pool_diag, rows, own, other, out, hidden_out
):
    core = lax.axis_index("tp") & 1
    width = pool.shape[1]
    mine = pool[...] + pool_chip[...]
    theirs = pool_core[...] + pool_diag[...]
    first = jnp.where(core == 0, mine, theirs) / lengths[0].astype(F32)
    second = jnp.where(core == 0, theirs, mine) / lengths[1].astype(F32)
    row = lax.broadcasted_iota(I32, (8, width), 0)
    pooled = jnp.where(row == 0, first, jnp.where(row == 1, second, F32(0.0)))
    scale = lax.rsqrt(jnp.mean(pooled * pooled, axis=-1, keepdims=True) + norm_eps)
    queries = (pooled * scale).astype(BF16)
    found = lax.dot_general(
        queries, rows[...], (((1,), (1,)), ((), ())), preferred_element_type=F32
    )
    each = rows.shape[0] // 2
    out[0:1, :] = found[0:1, :each]
    out[1:2, :] = found[1:2, each:]
    hidden_out[core] = own[...]
    hidden_out[1 - core] = other[...]


def score(lengths, pools, rows, own, other):
    return pl.pallas_call(
        score_kernel,
        out_shape=(
            jax.ShapeDtypeStruct((2, rows.shape[0] // 2), F32),
            jax.ShapeDtypeStruct((2,) + own.shape, BF16),
        ),
        in_specs=[SMEM] + [VMEM] * 7,
        out_specs=(VMEM, VMEM),
        compiler_params=params(8),
        cost_estimate=cost(1),
        name="score",
    )(lengths, *pools, rows, own, other)


def halving_order(groups):
    order = [0]
    mask = groups // 2
    while mask:
        order = order + [entry + mask for entry in order]
        mask //= 2
    return order


def as_ones(mask):
    return mask.astype(F32).astype(BF16)


def take_kernel(
    number, i0, i1, index, keep, send, place, rounds, numbers, chosen, tiles, rows, sems, sem
):
    rank = lax.axis_index("tp")
    group = lax.axis_index("req")
    deep = tiles.shape[1]
    groups = i0.shape[0]
    rows_here = index.shape[0]
    slots = groups * SLOTS
    first_place = number[0] * SLOTS
    ids = jnp.concatenate([i0[...], i1[...]], axis=1)
    count = ids.shape[1]
    owner = lax.shift_right_logical(ids, I32(rows_here.bit_length() - 1))
    before = as_ones(
        lax.broadcasted_iota(I32, (count, count), 0)
        < lax.broadcasted_iota(I32, (count, count), 1)
    )
    ones = jnp.ones((count, 128), BF16)
    slot = lax.broadcasted_iota(I32, (SLOTS, 1), 0) + first_place

    mine = owner == group * 4 + rank
    asked = jnp.concatenate(
        [
            (owner[:1] == (group ^ source) * 4 + rank).astype(F32)
            for source in halving_order(groups)
        ]
    )
    masks_two = jnp.concatenate([mine.astype(F32), asked]).astype(BF16)
    ranks = matmul(masks_two, before).astype(I32)
    send_rank = jnp.where(mine, ranks[:groups], -1)
    take_rank = jnp.where(asked > 0, ranks[groups:], -1)

    local = ids - (group * 4 + rank) * rows_here
    wanted = jnp.concatenate(
        [jnp.where(send_rank[k : k + 1] == slot, local[k : k + 1], 0) for k in range(groups)]
    )
    high = matmul((wanted >> 6).astype(F32).astype(BF16), ones).astype(I32)
    low = matmul((wanted & 63).astype(F32).astype(BF16), ones).astype(I32)
    numbers[:slots, :] = high * 64 + low
    numbers[slots:, :] = matmul(as_ones(mine), ones).astype(I32)
    copy = pltpu.make_async_copy(numbers, chosen, sem)
    copy.start()

    for k in range(groups):
        place[k * SLOTS : (k + 1) * SLOTS, :] = as_ones(take_rank[k : k + 1] == slot)
    shard = lax.broadcasted_iota(I32, (4 * groups, 1), 0)
    load = jnp.concatenate(
        [(owner[k : k + 1] == shard).astype(F32) for k in range(groups)]
    ).astype(BF16)
    most = jnp.max(matmul(load, ones)).astype(I32)
    rounds[0] = (most + SLOTS - 1) // SLOTS
    rows[...] = jnp.zeros_like(rows)
    copy.wait()

    def tile_copy(slot):
        first = pl.multiple_of((chosen[slot, 0] // deep) * deep, deep)
        return pltpu.make_async_copy(index.at[pl.ds(first, deep)], tiles.at[slot], sems.at[slot])

    step = 4

    def start(number, carry):
        for each in range(step):
            tile_copy(number * step + each).start()
        return carry

    def select(number, carry):
        for each in range(step):
            tile_copy(number * step + each).wait()
        for each in range(step):
            source = number * step + each
            line = lax.broadcasted_iota(I32, (deep, 1), 0) == chosen[source, 0] % deep
            row = jnp.where(line, tiles[source].astype(F32), F32(0.0))
            rows[pl.ds(source, 1), :] = jnp.sum(row, axis=0, keepdims=True)
        return carry

    def each_group(action):
        def one(number, carry):
            first = number * (SLOTS // step)
            left = jnp.clip(chosen[slots + number, 0] - first_place, 0, SLOTS)
            return lax.fori_loop(first, first + (left + step - 1) // step, action, carry)

        lax.fori_loop(0, groups, one, 0)

    each_group(start)
    each_group(select)
    keep[...] = rows[: slots // 2, :].astype(BF16)
    send[...] = rows[slots // 2 :, :].astype(BF16)


def take_rows(number, ids, index_rows):
    groups, each = ids[0].shape
    slots = groups * SLOTS
    width = index_rows.shape[1]
    half = jax.ShapeDtypeStruct((slots // 2, width), BF16)
    return pl.pallas_call(
        take_kernel,
        out_shape=(
            half,
            half,
            jax.ShapeDtypeStruct((slots, 2 * each), BF16),
            jax.ShapeDtypeStruct((1,), I32),
        ),
        in_specs=[SMEM] + [VMEM] * 2 + [HBM],
        out_specs=(VMEM, VMEM, VMEM, SMEM),
        scratch_shapes=[
            pltpu.VMEM((slots + groups, 128), I32),
            pltpu.SMEM((slots + groups, 128), I32),
            pltpu.VMEM((slots, 16, width), BF16),
            pltpu.VMEM((slots, width), F32),
            pltpu.SemaphoreType.DMA((slots,)),
            pltpu.SemaphoreType.DMA,
        ],
        compiler_params=params(8 + slots // 16),
        cost_estimate=NO_COST,
        name="take_rows",
    )(number, *ids, index_rows)


def place_kernel(place, received, out):
    chosen = lax.dot_general(
        place[...], received[...], (((0,), (0,)), ((), ())), preferred_element_type=F32
    )
    out[...] = chosen.astype(BF16)


def place_rows(place, received):
    return pl.pallas_call(
        place_kernel,
        out_shape=jax.ShapeDtypeStruct((place.shape[1], received.shape[1]), BF16),
        in_specs=[VMEM] * 2,
        out_specs=VMEM,
        compiler_params=params(8),
        cost_estimate=NO_COST,
        name="place_rows",
    )(place, received)


def masks(axis):
    mask = 1
    while mask < lax.axis_size(axis):
        yield mask
        mask *= 2


def candidate_rows(ids, index_rows, gate):
    width = index_rows.shape[1]

    def gathered(keep, send, place, gates=()):
        steps = list(masks("req"))[::-1]
        gates = list(gates) + [()] * (len(steps) + 1)
        keep = keep.reshape(1, -1, SLOTS, width)
        send = send.reshape(1, -1, SLOTS, width)
        held = None
        for number, mask in enumerate(steps):
            if held is not None:
                keep, send = held[:, :mask], held[:, mask:]
            other = after(swap(send, "req", mask), *gates[number])
            held = jnp.concatenate([keep, other])
        found = place_rows(place, held.reshape(-1, width))
        found = after(found, *gates[len(steps)]).reshape(4, -1, width)
        parts = [swap(found[mask], "tp", mask) for mask in (1, 2, 3)]
        return found[0] + parts[0] + parts[1] + parts[2]

    first = (after(ids[0], gate),) + ids[1:]
    keep, send, place, rounds = take_rows(jnp.zeros((1,), I32), first, index_rows)

    def one_more(number, total):
        keep, send, place, _ = take_rows(number.reshape(1), ids, index_rows)
        return total + gathered(keep, send, place)

    def further(rows):
        return lax.fori_loop(1, rounds[0], one_more, rows)

    return lambda *gates: gathered(keep, send, place, gates), further


def per_device(
    states,
    lengths,
    w_qkv,
    b_qkv,
    w_out,
    b_out,
    ln1_gain,
    ln1_shift,
    w_up,
    b_up,
    w_down,
    b_down,
    ln2_gain,
    ln2_shift,
    index_rows,
    cand_ids,
):
    from_chip = swap(states, "tp", 2)
    from_core = swap(states, "tp", 1)
    w_qkv_t = w_qkv.transpose(1, 0, 2)
    w_qkv_p = swap(after(w_qkv_t, from_core), "tp", 1)
    early_0, biases, w_half = early_own(states, from_core, w_qkv_t, b_qkv, b_up[None], w_out)

    held = jnp.stack([cand_ids, swap(cand_ids, "tp", 1)]).reshape(1, -1)
    for mask in masks("req"):
        if mask * 2 == lax.axis_size("req"):
            held, early_0, from_chip = lax.optimization_barrier((held, early_0, from_chip))
        held = jnp.concatenate([held, swap(held, "req", mask)])
    ids = (held, swap(held, "tp", 2))
    from_diag = swap(from_chip, "tp", 1)
    blocks = (states, from_core, from_chip, from_diag)
    biases_p = swap(biases, "tp", 1)
    early_1 = early_partner(states, after(from_core, held), w_qkv_p, biases_p)
    early_0 = after(early_0, early_1)
    w_out_p = swap(after(w_out, from_core), "tp", 1)
    w_up_p = swap(after(w_up, from_core), "tp", 1)
    w_down_p = swap(after(w_down, from_core), "tp", 1)

    w_x0 = swap(w_half, "tp", 2)

    context_0 = attention(
        lengths, after(early_0, w_up_p, w_down_p), from_chip, from_diag, w_qkv_t, b_qkv, 0,
        "attention_own",
    )
    context_0x = swap(context_0, "tp", 2)
    w_x1 = swap(after(w_x0, context_0), "req", 1)
    context_1 = attention(
        lengths, after(early_1, context_0, ids[1]), from_chip, from_diag, w_qkv_p, biases_p,
        6, "attention_partner",
    )
    context_1x = swap(context_1, "tp", 2)
    w_d0 = swap(after(w_x0, context_0), "tp", 1)
    w_d1 = swap(after(w_x1, context_1), "tp", 1)
    base = project_first(
        blocks, context_0, context_0x, w_out, (w_x0, w_x1), b_out[None]
    )
    base = project_second(base, context_1, w_out_p)
    gathered, further = candidate_rows(ids, index_rows, base)
    common = (
        context_1x, (w_d0, w_d1), ln1_gain[None], ln1_shift[None],
        (b_up[None], biases_p), b_down[None], (w_up, w_up_p),
        (w_down, w_down_p),
    )
    down_there = feed_forward(False, base, *common)
    down_x = swap(down_there, "tp", 2)
    down_here = feed_forward(True, after(base, down_there), *common)
    down_x = after(down_x, down_here)
    hidden, hidden_other, pool = finish(
        lengths, down_here, down_x, ln2_gain[None], ln2_shift[None]
    )

    rows = gathered((down_there,), (down_here,), (), (hidden,))
    pools = (pool,) + tuple(swap(pool, "tp", mask) for mask in (1, 2, 3))
    hidden_p = swap(hidden_other, "tp", 1)
    rows = further(after(rows, *pools))
    scores, hidden_out = score(lengths, pools, rows, hidden, hidden_p)
    return (hidden_out, scores)


def solution(mesh):
    placed = (
        P("req", "tp", None),
        P("req"),
        P(None, None, "tp"),
        P(None, "tp"),
        P("tp", None),
        P(),
        P(),
        P(),
        P(None, "tp"),
        P("tp"),
        P("tp", None),
        P(),
        P(),
        P(),
        P(("req", "tp"), None),
        P("req", "tp"),
    )
    return jax.shard_map(
        per_device,
        mesh=mesh,
        in_specs=placed,
        out_specs=(P("req", "tp", None), P("req", "tp")),
        check_vma=False,
    )
```

```python
import functools

import jax
import jax.numpy as jnp
from jax import lax
from jax.experimental import pallas as pl
from jax.experimental.pallas import tpu as pltpu
from jax.sharding import PartitionSpec as P

HEAD_DIM = 64
WINDOW = 512
SLOTS = 16
BF16 = jnp.bfloat16
F32 = jnp.float32
I32 = jnp.int32
MIB = 1024 * 1024
NO_COST = pl.CostEstimate(flops=1, bytes_accessed=1, transcendentals=0)


def cost(gflop):
    return pl.CostEstimate(flops=int(gflop * 10**9) + 1, bytes_accessed=MIB, transcendentals=0)


layer_eps = 1e-05
norm_eps = 1e-06

VMEM = pl.BlockSpec(memory_space=pltpu.VMEM)
SMEM = pl.BlockSpec(memory_space=pltpu.SMEM)
HBM = pl.BlockSpec(memory_space=pltpu.HBM)
ANY = pl.BlockSpec(memory_space=pl.ANY)


def layer_norm(values, gain, shift):
    centre = values - jnp.mean(values, axis=-1, keepdims=True)
    spread = jnp.mean(centre * centre, axis=-1, keepdims=True)
    return centre * lax.rsqrt(spread + layer_eps) * gain + shift


def swap(value, axis, mask):
    count = lax.axis_size(axis)
    return lax.ppermute(value, axis, [(i, i ^ mask) for i in range(count)])


def matmul(left, right):
    return jnp.dot(left, right, preferred_element_type=F32)


def params(mib):
    return pltpu.CompilerParams(vmem_limit_bytes=mib * MIB)


def after(value, *others):
    return lax.optimization_barrier((value,) + others)[0]


def project_three(text, w, b, out):
    for which in range(3):
        out[which] = (matmul(text, w[which]) + b[which : which + 1, :]).astype(BF16)


def early_kernel(s0, s1, w, b, out):
    core = lax.axis_index("tp") & 1
    project_three(jnp.concatenate([s0[core], s1[core]]), w, b, out)


def early_own_kernel(s0, s1, w, b, b_up, w_out, out, biases, half):
    early_kernel(s0, s1, w, b, out)
    wide = b.shape[1]
    biases[0:3, :] = b[...]
    for chunk in range(b_up.shape[1] // wide):
        biases[3 + chunk : 4 + chunk, :] = b_up[:, chunk * wide : (chunk + 1) * wide]
    part = half.shape[0]
    first = pl.multiple_of((lax.axis_index("req") & 1) * part, part)
    half[...] = w_out[pl.ds(first, part), :]


def early_own(s0, s1, w, b, b_up, w_out):
    wide = w.shape[2]
    return pl.pallas_call(
        early_own_kernel,
        out_shape=(
            jax.ShapeDtypeStruct((3, 2 * s0.shape[1], wide), BF16),
            jax.ShapeDtypeStruct((3 + b_up.shape[1] // wide, wide), F32),
            jax.ShapeDtypeStruct((w_out.shape[0] // 2, w_out.shape[1]), BF16),
        ),
        in_specs=[VMEM] * 6,
        out_specs=(VMEM, VMEM, VMEM),
        compiler_params=params(12),
        cost_estimate=NO_COST,
        name="early_own",
    )(s0, s1, w, b, b_up, w_out)


def early_partner(s0, s1, w, biases):
    return pl.pallas_call(
        early_kernel,
        out_shape=jax.ShapeDtypeStruct((3, 2 * s0.shape[1], w.shape[2]), BF16),
        in_specs=[VMEM] * 4,
        out_specs=VMEM,
        compiler_params=params(12),
        cost_estimate=NO_COST,
        name="early_partner",
    )(s0, s1, w, biases)


def attention_and_plan_kernel(
    rows_here, lengths, early, s2, s3, w, b, i0, i1, i2, i3, out, numbers, place, rounds,
    late, bias,
):
    plan_rows(0, rows_here, (i0, i1, i2, i3), numbers, place, rounds)
    attention_kernel(lengths, early, s2, s3, w, b, out, late, bias)


def attention_kernel(lengths, early, s2, s3, w, b, out, late, bias):
    rank = lax.axis_index("tp")
    core = rank & 1
    length = lengths[core]
    share = s2.shape[1]
    half = 2 * share
    seq_len = 4 * share
    wide = w.shape[2]
    project_three(jnp.concatenate([s2[core], s3[core]]), w, b, late)

    def position(index):
        return ((index // share) ^ rank) * share + index % share

    row_pos = position(lax.broadcasted_iota(I32, (seq_len, 1), 0))
    col_pos = position(lax.broadcasted_iota(I32, (1, seq_len), 1))
    keep = (jnp.abs(row_pos - col_pos) <= WINDOW // 2) & (col_pos < length)
    bias[...] = jnp.where(keep, F32(0.0), F32(-1e30))
    ones = jnp.ones((seq_len, 128), BF16)
    low = lax.broadcasted_iota(I32, (1, 128), 1) < HEAD_DIM
    scale = jnp.asarray(HEAD_DIM**-0.5, BF16)
    for pair in range(wide // 128):
        lanes = slice(pair * 128, (pair + 1) * 128)
        k_pair = jnp.concatenate([early[1, :, lanes], late[1, :, lanes]])
        v_pair = jnp.concatenate([early[2, :, lanes], late[2, :, lanes]])
        v_ones = jnp.concatenate([v_pair, ones], axis=1)
        for block in range(4):
            rows = slice(block * share, (block + 1) * share)
            first = (block % 2) * share
            q_pair = (early, late)[block // 2][0, first : first + share, lanes] * scale
            found = []
            for head in range(2):
                chosen = low if head == 0 else jnp.logical_not(low)
                q_head = jnp.where(chosen, q_pair, jnp.zeros((), BF16))
                logits = lax.dot_general(
                    q_head, k_pair, (((1,), (1,)), ((), ())), preferred_element_type=F32
                )
                logits = logits + bias[rows, :]
                top = jnp.max(logits, axis=-1, keepdims=True)
                expo = jnp.exp(logits - top).astype(BF16)
                summed = matmul(expo, v_ones)
                found.append(summed[:, :128] / summed[:, 128:])
            context = jnp.where(low, found[0], found[1])
            context = jnp.where(row_pos[rows] < length, context, F32(0.0))
            out[rows, lanes] = context.astype(BF16)


def attention(lengths, early, s2, s3, w, b, gflop, name, plan=()):
    seq_len = 4 * s2.shape[1]
    wide = w.shape[2]
    kernel = attention_kernel
    results = (jax.ShapeDtypeStruct((seq_len, wide), BF16),)
    out_specs = (VMEM,)
    ids = ()
    if plan:
        ids, rows_here = plan
        groups, each = ids[0].shape
        kernel = functools.partial(attention_and_plan_kernel, rows_here)
        results += (
            jax.ShapeDtypeStruct((groups * SLOTS + groups, 128), I32),
            jax.ShapeDtypeStruct((groups * SLOTS, 4 * each), BF16),
            jax.ShapeDtypeStruct((1,), I32),
        )
        out_specs += (VMEM, VMEM, SMEM)
    return pl.pallas_call(
        kernel,
        out_shape=results,
        in_specs=[SMEM] + [VMEM] * (5 + len(ids)),
        out_specs=out_specs,
        scratch_shapes=[
            pltpu.VMEM((3, seq_len // 2, wide), BF16),
            pltpu.VMEM((seq_len, seq_len), F32),
        ],
        compiler_params=params(20),
        cost_estimate=cost(gflop),
        name=name,
    )(lengths, early, s2, s3, w, b, *ids)


def joined(first, second):
    swapped = (lax.axis_index("req") & 1) != 0
    low = jnp.where(swapped, second[...], first[...])
    high = jnp.where(swapped, first[...], second[...])
    return jnp.concatenate([low, high])


def project_first_kernel(
    s0, s1, s2, s3, here, there, w, first, second, b, numbers, index, out, keep, send,
    chosen, tiles, rows, sems, sem,
):
    copy = pltpu.make_async_copy(numbers, chosen, sem)
    copy.start()
    share = s0.shape[1]
    core = lax.axis_index("tp") & 1
    weight = joined(first, second)
    copy.wait()
    finish_rows = fetch_rows(chosen, index, tiles, rows, sems)
    for number, block in enumerate((s0, s1, s2, s3)):
        span = slice(number * share, (number + 1) * share)
        other = (number ^ 2) * share
        total = matmul(here[span, :], w[...]) + matmul(there[other : other + share, :], weight)
        out[span, :] = total + (block[core].astype(F32) + b[...])
    finish_rows(keep, send)


def project_first(blocks, here, there, w, pieces, b_out, numbers, index_rows):
    _, share, width = blocks[0].shape
    groups = numbers.shape[0] // (SLOTS + 1)
    slots = groups * SLOTS
    half = jax.ShapeDtypeStruct((slots // 2, width), BF16)
    return pl.pallas_call(
        project_first_kernel,
        out_shape=(jax.ShapeDtypeStruct((4 * share, width), F32), half, half),
        in_specs=[VMEM] * 11 + [HBM],
        out_specs=(VMEM, VMEM, VMEM),
        scratch_shapes=fetch_scratch(slots, width),
        compiler_params=params(18 + slots // 16),
        cost_estimate=cost(1),
        name="project_first",
    )(*blocks, here, there, w, *pieces, b_out, numbers, index_rows)


def project_second_kernel(base, context, w, out):
    out[...] = base[...] + matmul(context[...], w[...])


def project_second(base, context, w):
    return pl.pallas_call(
        project_second_kernel,
        out_shape=jax.ShapeDtypeStruct(base.shape, F32),
        in_specs=[VMEM] * 3,
        out_specs=VMEM,
        input_output_aliases={0: 0},
        compiler_params=params(12),
        cost_estimate=cost(1),
        name="project_second",
    )(base, context, w)


def feed_kernel(
    keep_rest, base, c3, first, second, gain, shift, b0, b1, b_down,
    up0, up1, down0, down1, out, up_buf, down_buf, act, sems,
):
    hidden = up0.shape[1]
    copies = [
        pltpu.make_async_copy(source, target, sems.at[index])
        for index, (source, target) in enumerate(
            (
                (up0, up_buf.at[0]),
                (up1, up_buf.at[1]),
                (down0, down_buf.at[0]),
                (down1, down_buf.at[1]),
            )
        )
    ]
    for copy in copies:
        copy.start()
    total = base[...] + matmul(c3[...], joined(first, second))
    normed = layer_norm(total, gain[...], shift[...]).astype(BF16)
    step = 512
    wide = b1.shape[1]
    for part in range(2):
        copies[part].wait()
        for low in range(0, hidden, step):
            if part == 0:
                bias = b0[:, low : low + step]
            else:
                rows = range(3 + low // wide, 3 + (low + step) // wide)
                bias = jnp.concatenate([b1[row : row + 1, :] for row in rows], axis=1)
            up = matmul(normed, up_buf[part, :, low : low + step]) + bias
            activated = 0.5 * up * (1.0 + lax.erf(up * F32(0.5**0.5)))
            act[:, part * hidden + low : part * hidden + low + step] = activated.astype(BF16)
    copies[2].wait()
    down = matmul(act[:, :hidden], down_buf[0])
    copies[3].wait()
    down = down + matmul(act[:, hidden:], down_buf[1])
    if keep_rest:
        down = down + (normed.astype(F32) + b_down[...])
    out[...] = down.astype(out.dtype)


def feed_forward(keep_rest, base, context, pieces, gain, shift, biases, b_down, ups, downs):
    seq_len, width = base.shape
    half = seq_len // 2
    here = 0 if keep_rest else 1
    hidden = ups[0].shape[1]
    heads_wide = context.shape[1]
    base_spec = pl.BlockSpec((half, width), lambda i: (here, 0))
    context_spec = pl.BlockSpec((half, heads_wide), lambda i: (1 - here, 0))
    return pl.pallas_call(
        lambda *refs: feed_kernel(keep_rest, *refs),
        out_shape=jax.ShapeDtypeStruct((half, width), F32 if keep_rest else BF16),
        grid=(1,),
        in_specs=[base_spec, context_spec] + [VMEM] * 7 + [ANY] * 4,
        out_specs=VMEM,
        scratch_shapes=[
            pltpu.VMEM((2, width, hidden), BF16),
            pltpu.VMEM((2, hidden, width), BF16),
            pltpu.VMEM((half, 2 * hidden), BF16),
            pltpu.SemaphoreType.DMA((4,)),
        ],
        compiler_params=params(32),
        cost_estimate=cost(8),
        name="feed_here" if keep_rest else "feed_there",
    )(base, context, *pieces, gain, shift, *biases, b_down, *ups, *downs)


def finish_kernel(lengths, here, there, gain, shift, own, other, pool):
    rank = lax.axis_index("tp")
    length = lengths[rank & 1]
    share = own.shape[0]
    total = here[...] + there[...].astype(F32)
    hidden = layer_norm(total, gain[...], shift[...]).astype(BF16)
    own[...] = hidden[:share]
    other[...] = hidden[share:]
    index = lax.broadcasted_iota(I32, (2 * share, 1), 0)
    pos = ((index // share) ^ rank) * share + index % share
    valid = jnp.where(pos < length, hidden.astype(F32), F32(0.0))
    pool[...] = jnp.sum(valid, axis=0, keepdims=True)


def finish(lengths, here, there, gain, shift):
    half, width = here.shape
    block = jax.ShapeDtypeStruct((half // 2, width), BF16)
    return pl.pallas_call(
        finish_kernel,
        out_shape=(block, block, jax.ShapeDtypeStruct((1, width), F32)),
        in_specs=[SMEM] + [VMEM] * 4,
        out_specs=(VMEM, VMEM, VMEM),
        compiler_params=params(8),
        cost_estimate=cost(2),
        name="finish",
    )(lengths, here, there, gain, shift)


def score_kernel(
    lengths, pool, pool_core, pool_chip, pool_diag, rows, own, other, out, hidden_out
):
    core = lax.axis_index("tp") & 1
    width = pool.shape[1]
    mine = pool[...] + pool_chip[...]
    theirs = pool_core[...] + pool_diag[...]
    first = jnp.where(core == 0, mine, theirs) / lengths[0].astype(F32)
    second = jnp.where(core == 0, theirs, mine) / lengths[1].astype(F32)
    row = lax.broadcasted_iota(I32, (8, width), 0)
    pooled = jnp.where(row == 0, first, jnp.where(row == 1, second, F32(0.0)))
    scale = lax.rsqrt(jnp.mean(pooled * pooled, axis=-1, keepdims=True) + norm_eps)
    queries = (pooled * scale).astype(BF16)
    found = lax.dot_general(
        queries, rows[...], (((1,), (1,)), ((), ())), preferred_element_type=F32
    )
    each = rows.shape[0] // 2
    out[0:1, :] = found[0:1, :each]
    out[1:2, :] = found[1:2, each:]
    hidden_out[core] = own[...]
    hidden_out[1 - core] = other[...]


def score(lengths, pools, rows, own, other):
    return pl.pallas_call(
        score_kernel,
        out_shape=(
            jax.ShapeDtypeStruct((2, rows.shape[0] // 2), F32),
            jax.ShapeDtypeStruct((2,) + own.shape, BF16),
        ),
        in_specs=[SMEM] + [VMEM] * 7,
        out_specs=(VMEM, VMEM),
        compiler_params=params(8),
        cost_estimate=cost(1),
        name="score",
    )(lengths, *pools, rows, own, other)


def halving_order(groups):
    order = [0]
    mask = groups // 2
    while mask:
        order = order + [entry + mask for entry in order]
        mask //= 2
    return order


def as_ones(mask):
    return mask.astype(F32).astype(BF16)


def plan_rows(first_place, rows_here, parts, numbers, place, rounds):
    rank = lax.axis_index("tp")
    group = lax.axis_index("req")
    groups = parts[0].shape[0]
    slots = groups * SLOTS
    ids = jnp.concatenate([part[...] for part in parts], axis=1)
    count = ids.shape[1]
    owner = lax.shift_right_logical(ids, I32(rows_here.bit_length() - 1))
    before = as_ones(
        lax.broadcasted_iota(I32, (count, count), 0)
        < lax.broadcasted_iota(I32, (count, count), 1)
    )
    ones = jnp.ones((count, 128), BF16)
    slot = lax.broadcasted_iota(I32, (SLOTS, 1), 0) + first_place

    mine = owner == group * 4 + rank
    asked = jnp.concatenate(
        [
            (owner[:1] == (group ^ source) * 4 + rank).astype(F32)
            for source in halving_order(groups)
        ]
    )
    both = jnp.concatenate([mine.astype(F32), asked]).astype(BF16)
    ranks = matmul(both, before).astype(I32)
    send_rank = jnp.where(mine, ranks[:groups], -1)
    take_rank = jnp.where(asked > 0, ranks[groups:], -1)

    local = ids - (group * 4 + rank) * rows_here
    wanted = jnp.concatenate(
        [jnp.where(send_rank[k : k + 1] == slot, local[k : k + 1], 0) for k in range(groups)]
    )
    high = matmul((wanted >> 6).astype(F32).astype(BF16), ones).astype(I32)
    low = matmul((wanted & 63).astype(F32).astype(BF16), ones).astype(I32)
    numbers[:slots, :] = high * 64 + low
    numbers[slots:, :] = matmul(as_ones(mine), ones).astype(I32) - first_place

    for k in range(groups):
        place[k * SLOTS : (k + 1) * SLOTS, :] = as_ones(take_rank[k : k + 1] == slot)
    shard = lax.broadcasted_iota(I32, (4 * groups, 1), 0)
    load = jnp.concatenate(
        [(owner[k : k + 1] == shard).astype(F32) for k in range(groups)]
    ).astype(BF16)
    most = jnp.max(matmul(load, ones)).astype(I32)
    rounds[0] = (most + SLOTS - 1) // SLOTS


def fetch_rows(chosen, index, tiles, rows, sems):
    deep = tiles.shape[1]
    slots = tiles.shape[0]

    def tile_copy(slot):
        first = pl.multiple_of((chosen[slot, 0] // deep) * deep, deep)
        return pltpu.make_async_copy(index.at[pl.ds(first, deep)], tiles.at[slot], sems.at[slot])

    step = 4

    def start(number, carry):
        for each in range(step):
            tile_copy(number * step + each).start()
        return carry

    def select(number, carry):
        for each in range(step):
            tile_copy(number * step + each).wait()
        for each in range(step):
            source = number * step + each
            line = lax.broadcasted_iota(I32, (deep, 1), 0) == chosen[source, 0] % deep
            row = jnp.where(line, tiles[source].astype(F32), F32(0.0))
            rows[pl.ds(source, 1), :] = jnp.sum(row, axis=0, keepdims=True)
        return carry

    def each_group(action):
        def one(number, carry):
            first = number * (SLOTS // step)
            left = jnp.clip(chosen[slots + number, 0], 0, SLOTS)
            return lax.fori_loop(first, first + (left + step - 1) // step, action, carry)

        lax.fori_loop(0, slots // SLOTS, one, 0)

    rows[...] = jnp.zeros_like(rows)
    each_group(start)

    def finish_rows(keep, send):
        each_group(select)
        keep[...] = rows[: slots // 2, :].astype(BF16)
        send[...] = rows[slots // 2 :, :].astype(BF16)

    return finish_rows


def take_kernel(
    number, i0, i1, i2, i3, index, keep, send, place, rounds, numbers, chosen, tiles, rows,
    sems, sem,
):
    plan_rows(number[0] * SLOTS, index.shape[0], (i0, i1, i2, i3), numbers, place, rounds)
    copy = pltpu.make_async_copy(numbers, chosen, sem)
    copy.start()
    copy.wait()
    fetch_rows(chosen, index, tiles, rows, sems)(keep, send)


def fetch_scratch(slots, width):
    groups = slots // SLOTS
    return [
        pltpu.SMEM((slots + groups, 128), I32),
        pltpu.VMEM((slots, 16, width), BF16),
        pltpu.VMEM((slots, width), F32),
        pltpu.SemaphoreType.DMA((slots,)),
        pltpu.SemaphoreType.DMA,
    ]


def take_rows(number, ids, index_rows):
    groups, each = ids[0].shape
    slots = groups * SLOTS
    width = index_rows.shape[1]
    half = jax.ShapeDtypeStruct((slots // 2, width), BF16)
    return pl.pallas_call(
        take_kernel,
        out_shape=(
            half,
            half,
            jax.ShapeDtypeStruct((slots, 4 * each), BF16),
            jax.ShapeDtypeStruct((1,), I32),
        ),
        in_specs=[SMEM] + [VMEM] * 4 + [HBM],
        out_specs=(VMEM, VMEM, VMEM, SMEM),
        scratch_shapes=[pltpu.VMEM((slots + groups, 128), I32)] + fetch_scratch(slots, width),
        compiler_params=params(8 + slots // 16),
        cost_estimate=NO_COST,
        name="take_rows",
    )(number, *ids, index_rows)


def place_kernel(place, received, out):
    chosen = lax.dot_general(
        place[...], received[...], (((0,), (0,)), ((), ())), preferred_element_type=F32
    )
    out[...] = chosen.astype(BF16)


def place_rows(place, received):
    return pl.pallas_call(
        place_kernel,
        out_shape=jax.ShapeDtypeStruct((place.shape[1], received.shape[1]), BF16),
        in_specs=[VMEM] * 2,
        out_specs=VMEM,
        compiler_params=params(8),
        cost_estimate=NO_COST,
        name="place_rows",
    )(place, received)


def masks(axis):
    mask = 1
    while mask < lax.axis_size(axis):
        yield mask
        mask *= 2


def row_exchange(ids, index_rows, place, rounds):
    width = index_rows.shape[1]

    def gathered(keep, send, place, gates=()):
        steps = list(masks("req"))[::-1]
        gates = list(gates) + [()] * (len(steps) + 1)
        keep = keep.reshape(1, -1, SLOTS, width)
        send = send.reshape(1, -1, SLOTS, width)
        held = None
        for number, mask in enumerate(steps):
            if held is not None:
                keep, send = held[:, :mask], held[:, mask:]
            other = after(swap(send, "req", mask), *gates[number])
            held = jnp.concatenate([keep, other])
        found = place_rows(place, held.reshape(-1, width))
        found = after(found, *gates[len(steps)]).reshape(4, -1, width)
        parts = [swap(found[mask], "tp", mask) for mask in (1, 2, 3)]
        return found[0] + parts[0] + parts[1] + parts[2]

    def one_more(number, total):
        keep, send, place, _ = take_rows(number.reshape(1), ids, index_rows)
        return total + gathered(keep, send, place)

    def further(rows):
        return lax.fori_loop(1, rounds[0], one_more, rows)

    return lambda keep, send, *gates: gathered(keep, send, place, gates), further


def per_device(
    states,
    lengths,
    w_qkv,
    b_qkv,
    w_out,
    b_out,
    ln1_gain,
    ln1_shift,
    w_up,
    b_up,
    w_down,
    b_down,
    ln2_gain,
    ln2_shift,
    index_rows,
    cand_ids,
):
    from_chip = swap(states, "tp", 2)
    from_core = swap(states, "tp", 1)
    w_qkv_t = w_qkv.transpose(1, 0, 2)

    w_up_p = swap(w_up, "tp", 1)
    w_down_p = swap(w_down, "tp", 1)
    w_qkv_p = swap(w_qkv_t, "tp", 1)

    held = cand_ids.reshape(1, -1)
    early_0 = None
    for mask in masks("req"):
        last = mask * 2 == lax.axis_size("req")
        if last:
            held, from_chip = lax.optimization_barrier((held, from_chip))
        other = swap(held, "req", mask)
        if last:
            early_0, biases, w_half = early_own(
                states, after(from_core, held), w_qkv_t, b_qkv, b_up[None], w_out
            )
            other, early_0 = lax.optimization_barrier((other, early_0))
        held = jnp.concatenate([held, other])
    ids = (held,) + tuple(swap(held, "tp", mask) for mask in (1, 2, 3))
    from_diag = swap(from_chip, "tp", 1)
    blocks = (states, from_core, from_chip, from_diag)
    biases_p = swap(biases, "tp", 1)
    early_1 = early_partner(states, after(from_core, held), w_qkv_p, biases_p)
    early_0 = after(early_0, early_1)
    w_out_p = swap(after(w_out, from_core), "tp", 1)

    w_x0 = swap(w_half, "tp", 2)

    (context_0,) = attention(
        lengths, after(early_0, w_up_p, w_down_p), from_chip, from_diag, w_qkv_t, b_qkv, 2,
        "attention_own",
    )
    context_0x = swap(context_0, "tp", 2)
    w_x1 = swap(after(w_x0, context_0), "req", 1)
    context_1, numbers, place, rounds = attention(
        lengths, after(early_1, context_0), from_chip, from_diag, w_qkv_p, biases_p, 6,
        "attention_partner", (ids, index_rows.shape[0]),
    )
    context_1x = swap(context_1, "tp", 2)
    w_d0 = swap(after(w_x0, context_0), "tp", 1)
    w_d1 = swap(after(w_x1, context_1), "tp", 1)
    base, keep, send = project_first(
        blocks, context_0, context_0x, w_out, (w_x0, w_x1), b_out[None], numbers, index_rows
    )
    base = project_second(base, context_1, w_out_p)
    gathered, further = row_exchange(ids, index_rows, place, rounds)
    common = (
        context_1x, (w_d0, w_d1), ln1_gain[None], ln1_shift[None],
        (b_up[None], biases_p), b_down[None], (w_up, w_up_p),
        (w_down, w_down_p),
    )
    down_there = feed_forward(False, base, *common)
    down_x = swap(down_there, "tp", 2)
    down_here = feed_forward(True, after(base, down_there), *common)
    down_x = after(down_x, down_here)
    hidden, hidden_other, pool = finish(
        lengths, down_here, down_x, ln2_gain[None], ln2_shift[None]
    )

    rows = gathered(keep, send, (down_there,), (down_here,), (), (hidden,))
    pools = (pool,) + tuple(swap(pool, "tp", mask) for mask in (1, 2, 3))
    hidden_p = swap(hidden_other, "tp", 1)
    rows = further(after(rows, *pools))
    scores, hidden_out = score(lengths, pools, rows, hidden, hidden_p)
    return (hidden_out, scores)


def solution(mesh):
    placed = (
        P("req", "tp", None),
        P("req"),
        P(None, None, "tp"),
        P(None, "tp"),
        P("tp", None),
        P(),
        P(),
        P(),
        P(None, "tp"),
        P("tp"),
        P("tp", None),
        P(),
        P(),
        P(),
        P(("req", "tp"), None),
        P("req", "tp"),
    )
    return jax.shard_map(
        per_device,
        mesh=mesh,
        in_specs=placed,
        out_specs=(P("req", "tp", None), P("req", "tp")),
        check_vma=False,
    )
```

```python
import functools

import jax
import jax.numpy as jnp
from jax import lax
from jax.experimental import pallas as pl
from jax.experimental.pallas import tpu as pltpu
from jax.sharding import PartitionSpec as P

HEAD_DIM = 64
WINDOW = 512
SLOTS = 16
BF16 = jnp.bfloat16
F32 = jnp.float32
I32 = jnp.int32
MIB = 1024 * 1024
NO_COST = pl.CostEstimate(flops=1, bytes_accessed=1, transcendentals=0)


def cost(gflop):
    return pl.CostEstimate(flops=int(gflop * 10**9) + 1, bytes_accessed=MIB, transcendentals=0)


layer_eps = 1e-05
norm_eps = 1e-06

VMEM = pl.BlockSpec(memory_space=pltpu.VMEM)
SMEM = pl.BlockSpec(memory_space=pltpu.SMEM)
HBM = pl.BlockSpec(memory_space=pltpu.HBM)
ANY = pl.BlockSpec(memory_space=pl.ANY)


def layer_norm(values, gain, shift):
    centre = values - jnp.mean(values, axis=-1, keepdims=True)
    spread = jnp.mean(centre * centre, axis=-1, keepdims=True)
    return centre * lax.rsqrt(spread + layer_eps) * gain + shift


def swap(value, axis, mask):
    count = lax.axis_size(axis)
    return lax.ppermute(value, axis, [(i, i ^ mask) for i in range(count)])


def matmul(left, right):
    return jnp.dot(left, right, preferred_element_type=F32)


def params(mib):
    return pltpu.CompilerParams(vmem_limit_bytes=mib * MIB)


def after(value, *others):
    return lax.optimization_barrier((value,) + others)[0]


def project_three(text, w, b, out):
    for which in range(3):
        out[which] = (matmul(text, w[which]) + b[which : which + 1, :]).astype(BF16)


def early_kernel(s0, s1, w, b, out):
    core = lax.axis_index("tp") & 1
    project_three(jnp.concatenate([s0[core], s1[core]]), w, b, out)


def early_own_kernel(s0, s1, w, b, b_up, w_out, out, biases, half):
    early_kernel(s0, s1, w, b, out)
    wide = b.shape[1]
    biases[0:3, :] = b[...]
    for chunk in range(b_up.shape[1] // wide):
        biases[3 + chunk : 4 + chunk, :] = b_up[:, chunk * wide : (chunk + 1) * wide]
    part = half.shape[0]
    first = pl.multiple_of((lax.axis_index("req") & 1) * part, part)
    half[...] = w_out[pl.ds(first, part), :]


def early_own(s0, s1, w, b, b_up, w_out):
    wide = w.shape[2]
    return pl.pallas_call(
        early_own_kernel,
        out_shape=(
            jax.ShapeDtypeStruct((3, 2 * s0.shape[1], wide), BF16),
            jax.ShapeDtypeStruct((3 + b_up.shape[1] // wide, wide), F32),
            jax.ShapeDtypeStruct((w_out.shape[0] // 2, w_out.shape[1]), BF16),
        ),
        in_specs=[VMEM] * 6,
        out_specs=(VMEM, VMEM, VMEM),
        compiler_params=params(12),
        cost_estimate=NO_COST,
        name="early_own",
    )(s0, s1, w, b, b_up, w_out)


def early_partner(s0, s1, w, biases):
    return pl.pallas_call(
        early_kernel,
        out_shape=jax.ShapeDtypeStruct((3, 2 * s0.shape[1], w.shape[2]), BF16),
        in_specs=[VMEM] * 4,
        out_specs=VMEM,
        compiler_params=params(12),
        cost_estimate=NO_COST,
        name="early_partner",
    )(s0, s1, w, biases)


def attention_and_plan_kernel(
    rows_here, lengths, early, s2, s3, w, b, i0, i1, i2, i3, out, numbers, place, rounds,
    late, bias,
):
    plan_rows(0, rows_here, (i0, i1, i2, i3), numbers, place, rounds)
    attention_kernel(lengths, early, s2, s3, w, b, out, late, bias)


def attention_kernel(lengths, early, s2, s3, w, b, out, late, bias):
    rank = lax.axis_index("tp")
    core = rank & 1
    length = lengths[core]
    share = s2.shape[1]
    half = 2 * share
    seq_len = 4 * share
    wide = w.shape[2]
    project_three(jnp.concatenate([s2[core], s3[core]]), w, b, late)

    def position(index):
        return ((index // share) ^ rank) * share + index % share

    row_pos = position(lax.broadcasted_iota(I32, (seq_len, 1), 0))
    col_pos = position(lax.broadcasted_iota(I32, (1, seq_len), 1))
    keep = (jnp.abs(row_pos - col_pos) <= WINDOW // 2) & (col_pos < length)
    bias[...] = jnp.where(keep, F32(0.0), F32(-1e30))
    ones = jnp.ones((seq_len, 128), BF16)
    low = lax.broadcasted_iota(I32, (1, 128), 1) < HEAD_DIM
    scale = jnp.asarray(HEAD_DIM**-0.5, BF16)
    for pair in range(wide // 128):
        lanes = slice(pair * 128, (pair + 1) * 128)
        k_pair = jnp.concatenate([early[1, :, lanes], late[1, :, lanes]])
        v_pair = jnp.concatenate([early[2, :, lanes], late[2, :, lanes]])
        v_ones = jnp.concatenate([v_pair, ones], axis=1)
        for block in range(4):
            rows = slice(block * share, (block + 1) * share)
            first = (block % 2) * share
            q_pair = (early, late)[block // 2][0, first : first + share, lanes] * scale
            found = []
            for head in range(2):
                chosen = low if head == 0 else jnp.logical_not(low)
                q_head = jnp.where(chosen, q_pair, jnp.zeros((), BF16))
                logits = lax.dot_general(
                    q_head, k_pair, (((1,), (1,)), ((), ())), preferred_element_type=F32
                )
                logits = logits + bias[rows, :]
                top = jnp.max(logits, axis=-1, keepdims=True)
                expo = jnp.exp(logits - top).astype(BF16)
                summed = matmul(expo, v_ones)
                found.append(summed[:, :128] / summed[:, 128:])
            context = jnp.where(low, found[0], found[1])
            context = jnp.where(row_pos[rows] < length, context, F32(0.0))
            out[rows, lanes] = context.astype(BF16)


def attention(lengths, early, s2, s3, w, b, gflop, name, plan=()):
    seq_len = 4 * s2.shape[1]
    wide = w.shape[2]
    kernel = attention_kernel
    results = (jax.ShapeDtypeStruct((seq_len, wide), BF16),)
    out_specs = (VMEM,)
    ids = ()
    if plan:
        ids, rows_here = plan
        groups, each = ids[0].shape
        kernel = functools.partial(attention_and_plan_kernel, rows_here)
        results += (
            jax.ShapeDtypeStruct((groups * SLOTS + groups, 128), I32),
            jax.ShapeDtypeStruct((groups * SLOTS, 4 * each), BF16),
            jax.ShapeDtypeStruct((1,), I32),
        )
        out_specs += (VMEM, VMEM, SMEM)
    return pl.pallas_call(
        kernel,
        out_shape=results,
        in_specs=[SMEM] + [VMEM] * (5 + len(ids)),
        out_specs=out_specs,
        scratch_shapes=[
            pltpu.VMEM((3, seq_len // 2, wide), BF16),
            pltpu.VMEM((seq_len, seq_len), F32),
        ],
        compiler_params=params(12),
        cost_estimate=cost(gflop),
        name=name,
    )(lengths, early, s2, s3, w, b, *ids)


def joined(first, second):
    swapped = (lax.axis_index("req") & 1) != 0
    low = jnp.where(swapped, second[...], first[...])
    high = jnp.where(swapped, first[...], second[...])
    return jnp.concatenate([low, high])


def project_first_kernel(
    s0, s1, s2, s3, here, there, w, first, second, b, numbers, index, out, keep, send,
    chosen, tiles, rows, sems, sem,
):
    copy = pltpu.make_async_copy(numbers, chosen, sem)
    copy.start()
    share = s0.shape[1]
    core = lax.axis_index("tp") & 1
    weight = joined(first, second)
    copy.wait()
    finish_rows = fetch_rows(numbers, chosen, index, tiles, rows, sems)
    for number, block in enumerate((s0, s1, s2, s3)):
        span = slice(number * share, (number + 1) * share)
        other = (number ^ 2) * share
        total = matmul(here[span, :], w[...]) + matmul(there[other : other + share, :], weight)
        out[span, :] = total + (block[core].astype(F32) + b[...])
    finish_rows(keep, send)


def project_first(blocks, here, there, w, pieces, b_out, numbers, index_rows):
    _, share, width = blocks[0].shape
    groups = numbers.shape[0] // (SLOTS + 1)
    slots = groups * SLOTS
    half = jax.ShapeDtypeStruct((slots // 2, width), BF16)
    return pl.pallas_call(
        project_first_kernel,
        out_shape=(jax.ShapeDtypeStruct((4 * share, width), F32), half, half),
        in_specs=[VMEM] * 11 + [HBM],
        out_specs=(VMEM, VMEM, VMEM),
        scratch_shapes=fetch_scratch(slots, width),
        compiler_params=params(12 + slots // 16),
        cost_estimate=cost(1),
        name="project_first",
    )(*blocks, here, there, w, *pieces, b_out, numbers, index_rows)


def project_second_kernel(base, context, w, out):
    out[...] = base[...] + matmul(context[...], w[...])


def project_second(base, context, w):
    return pl.pallas_call(
        project_second_kernel,
        out_shape=jax.ShapeDtypeStruct(base.shape, F32),
        in_specs=[VMEM] * 3,
        out_specs=VMEM,
        input_output_aliases={0: 0},
        compiler_params=params(12),
        cost_estimate=cost(1),
        name="project_second",
    )(base, context, w)


def feed_kernel(
    keep_rest, base, c3, first, second, gain, shift, b0, b1, b_down,
    up0, up1, down0, down1, out, up_buf, down_buf, act, sems,
):
    hidden = up0.shape[1]
    copies = [
        pltpu.make_async_copy(source, target, sems.at[index])
        for index, (source, target) in enumerate(
            (
                (up0, up_buf.at[0]),
                (up1, up_buf.at[1]),
                (down0, down_buf.at[0]),
                (down1, down_buf.at[1]),
            )
        )
    ]
    for copy in copies:
        copy.start()
    total = base[...] + matmul(c3[...], joined(first, second))
    normed = layer_norm(total, gain[...], shift[...]).astype(BF16)
    step = 512
    wide = b1.shape[1]
    for part in range(2):
        copies[part].wait()
        for low in range(0, hidden, step):
            if part == 0:
                bias = b0[:, low : low + step]
            else:
                rows = range(3 + low // wide, 3 + (low + step) // wide)
                bias = jnp.concatenate([b1[row : row + 1, :] for row in rows], axis=1)
            up = matmul(normed, up_buf[part, :, low : low + step]) + bias
            activated = 0.5 * up * (1.0 + lax.erf(up * F32(0.5**0.5)))
            act[:, part * hidden + low : part * hidden + low + step] = activated.astype(BF16)
    copies[2].wait()
    down = matmul(act[:, :hidden], down_buf[0])
    copies[3].wait()
    down = down + matmul(act[:, hidden:], down_buf[1])
    if keep_rest:
        down = down + (normed.astype(F32) + b_down[...])
    out[...] = down.astype(out.dtype)


def feed_forward(keep_rest, base, context, pieces, gain, shift, biases, b_down, ups, downs):
    seq_len, width = base.shape
    half = seq_len // 2
    here = 0 if keep_rest else 1
    hidden = ups[0].shape[1]
    heads_wide = context.shape[1]
    base_spec = pl.BlockSpec((half, width), lambda i: (here, 0))
    context_spec = pl.BlockSpec((half, heads_wide), lambda i: (1 - here, 0))
    return pl.pallas_call(
        lambda *refs: feed_kernel(keep_rest, *refs),
        out_shape=jax.ShapeDtypeStruct((half, width), F32 if keep_rest else BF16),
        grid=(1,),
        in_specs=[base_spec, context_spec] + [VMEM] * 7 + [ANY] * 4,
        out_specs=VMEM,
        scratch_shapes=[
            pltpu.VMEM((2, width, hidden), BF16),
            pltpu.VMEM((2, hidden, width), BF16),
            pltpu.VMEM((half, 2 * hidden), BF16),
            pltpu.SemaphoreType.DMA((4,)),
        ],
        compiler_params=params(20),
        cost_estimate=cost(8),
        name="feed_here" if keep_rest else "feed_there",
    )(base, context, *pieces, gain, shift, *biases, b_down, *ups, *downs)


def finish_kernel(lengths, here, there, gain, shift, own, other, pool):
    rank = lax.axis_index("tp")
    length = lengths[rank & 1]
    share = own.shape[0]
    total = here[...] + there[...].astype(F32)
    hidden = layer_norm(total, gain[...], shift[...]).astype(BF16)
    own[...] = hidden[:share]
    other[...] = hidden[share:]
    index = lax.broadcasted_iota(I32, (2 * share, 1), 0)
    pos = ((index // share) ^ rank) * share + index % share
    valid = jnp.where(pos < length, hidden.astype(F32), F32(0.0))
    pool[...] = jnp.sum(valid, axis=0, keepdims=True)


def finish(lengths, here, there, gain, shift):
    half, width = here.shape
    block = jax.ShapeDtypeStruct((half // 2, width), BF16)
    return pl.pallas_call(
        finish_kernel,
        out_shape=(block, block, jax.ShapeDtypeStruct((1, width), F32)),
        in_specs=[SMEM] + [VMEM] * 4,
        out_specs=(VMEM, VMEM, VMEM),
        compiler_params=params(8),
        cost_estimate=cost(2),
        name="finish",
    )(lengths, here, there, gain, shift)


def score_kernel(
    lengths, pool, pool_core, pool_chip, pool_diag, rows, own, other, out, hidden_out
):
    core = lax.axis_index("tp") & 1
    width = pool.shape[1]
    mine = pool[...] + pool_chip[...]
    theirs = pool_core[...] + pool_diag[...]
    first = jnp.where(core == 0, mine, theirs) / lengths[0].astype(F32)
    second = jnp.where(core == 0, theirs, mine) / lengths[1].astype(F32)
    row = lax.broadcasted_iota(I32, (8, width), 0)
    pooled = jnp.where(row == 0, first, jnp.where(row == 1, second, F32(0.0)))
    scale = lax.rsqrt(jnp.mean(pooled * pooled, axis=-1, keepdims=True) + norm_eps)
    queries = (pooled * scale).astype(BF16)
    found = lax.dot_general(
        queries, rows[...], (((1,), (1,)), ((), ())), preferred_element_type=F32
    )
    each = rows.shape[0] // 2
    out[0:1, :] = found[0:1, :each]
    out[1:2, :] = found[1:2, each:]
    hidden_out[core] = own[...]
    hidden_out[1 - core] = other[...]


def score(lengths, pools, rows, own, other):
    return pl.pallas_call(
        score_kernel,
        out_shape=(
            jax.ShapeDtypeStruct((2, rows.shape[0] // 2), F32),
            jax.ShapeDtypeStruct((2,) + own.shape, BF16),
        ),
        in_specs=[SMEM] + [VMEM] * 7,
        out_specs=(VMEM, VMEM),
        compiler_params=params(8),
        cost_estimate=cost(1),
        name="score",
    )(lengths, *pools, rows, own, other)


def source_order(groups):
    order = [0]
    mask = groups // 2
    while mask >= 4:
        order = order + [entry + mask for entry in order]
        mask //= 2
    return [entry + last for last in range(4) for entry in order]


def as_ones(mask):
    return mask.astype(F32).astype(BF16)


def plan_rows(first_place, rows_here, parts, numbers, place, rounds):
    rank = lax.axis_index("tp")
    group = lax.axis_index("req")
    groups = parts[0].shape[0]
    slots = groups * SLOTS
    ids = jnp.concatenate([part[...] for part in parts], axis=1)
    count = ids.shape[1]
    owner = lax.shift_right_logical(ids, I32(rows_here.bit_length() - 1))
    before = as_ones(
        lax.broadcasted_iota(I32, (count, count), 0)
        < lax.broadcasted_iota(I32, (count, count), 1)
    )
    ones = jnp.ones((count, 128), BF16)
    slot = lax.broadcasted_iota(I32, (SLOTS, 1), 0) + first_place

    mine = owner == group * 4 + rank
    asked = jnp.concatenate(
        [
            (owner[:1] == (group ^ source) * 4 + rank).astype(F32)
            for source in source_order(groups)
        ]
    )
    both = jnp.concatenate([mine.astype(F32), asked]).astype(BF16)
    ranks = matmul(both, before).astype(I32)
    send_rank = jnp.where(mine, ranks[:groups], -1)
    take_rank = jnp.where(asked > 0, ranks[groups:], -1)

    local = ids - (group * 4 + rank) * rows_here
    wanted = jnp.concatenate(
        [jnp.where(send_rank[k : k + 1] == slot, local[k : k + 1], 0) for k in range(groups)]
    )
    high = matmul((wanted >> 6).astype(F32).astype(BF16), ones).astype(I32)
    low = matmul((wanted & 63).astype(F32).astype(BF16), ones).astype(I32)
    numbers[:slots, :] = high * 64 + low
    numbers[slots:, :] = matmul(as_ones(mine), ones).astype(I32) - first_place

    for k in range(groups):
        place[k * SLOTS : (k + 1) * SLOTS, :] = as_ones(take_rank[k : k + 1] == slot)
    shard = lax.broadcasted_iota(I32, (4 * groups, 1), 0)
    load = jnp.concatenate(
        [(owner[k : k + 1] == shard).astype(F32) for k in range(groups)]
    ).astype(BF16)
    most = jnp.max(matmul(load, ones)).astype(I32)
    rounds[0] = (most + SLOTS - 1) // SLOTS


def fetch_rows(numbers, chosen, index, tiles, rows, sems):
    deep = tiles.shape[1]
    slots, width = rows.shape
    step = 8

    def tile_copy(slot):
        first = pl.multiple_of((chosen[slot, 0] // deep) * deep, deep)
        return pltpu.make_async_copy(index.at[pl.ds(first, deep)], tiles.at[slot], sems.at[slot])

    def start(number, carry):
        for each in range(step):
            tile_copy(number * step + each).start()
        return carry

    def select(number, carry):
        for each in range(step):
            tile_copy(number * step + each).wait()
        first = pl.multiple_of(number * step, step)
        lanes = step * deep
        line = lax.broadcasted_iota(I32, (step, lanes), 0) * deep + lax.rem(
            numbers[pl.ds(first, step), :], deep
        )
        pick = as_ones(lax.broadcasted_iota(I32, (step, lanes), 1) == line)
        found = tiles[pl.ds(first, step)].reshape(lanes, width)
        rows[pl.ds(first, step), :] = matmul(pick, found)
        return carry

    def each_group(action):
        def one(number, carry):
            first = number * (SLOTS // step)
            left = jnp.clip(chosen[slots + number, 0], 0, SLOTS)
            return lax.fori_loop(first, first + (left + step - 1) // step, action, carry)

        lax.fori_loop(0, slots // SLOTS, one, 0)

    rows[...] = jnp.zeros_like(rows)
    each_group(start)

    def finish_rows(keep, send):
        each_group(select)
        keep[...] = rows[: slots // 2, :].astype(BF16)
        send[...] = rows[slots // 2 :, :].astype(BF16)

    return finish_rows


def take_kernel(
    number, i0, i1, i2, i3, index, keep, send, place, rounds, numbers, chosen, tiles, rows,
    sems, sem,
):
    plan_rows(number[0] * SLOTS, index.shape[0], (i0, i1, i2, i3), numbers, place, rounds)
    copy = pltpu.make_async_copy(numbers, chosen, sem)
    copy.start()
    copy.wait()
    fetch_rows(numbers, chosen, index, tiles, rows, sems)(keep, send)


def fetch_scratch(slots, width):
    groups = slots // SLOTS
    return [
        pltpu.SMEM((slots + groups, 128), I32),
        pltpu.VMEM((slots, 16, width), BF16),
        pltpu.VMEM((slots, width), F32),
        pltpu.SemaphoreType.DMA((slots,)),
        pltpu.SemaphoreType.DMA,
    ]


def take_rows(number, ids, index_rows):
    groups, each = ids[0].shape
    slots = groups * SLOTS
    width = index_rows.shape[1]
    half = jax.ShapeDtypeStruct((slots // 2, width), BF16)
    return pl.pallas_call(
        take_kernel,
        out_shape=(
            half,
            half,
            jax.ShapeDtypeStruct((slots, 4 * each), BF16),
            jax.ShapeDtypeStruct((1,), I32),
        ),
        in_specs=[SMEM] + [VMEM] * 4 + [HBM],
        out_specs=(VMEM, VMEM, VMEM, SMEM),
        scratch_shapes=[pltpu.VMEM((slots + groups, 128), I32)] + fetch_scratch(slots, width),
        compiler_params=params(8 + slots // 16),
        cost_estimate=NO_COST,
        name="take_rows",
    )(number, *ids, index_rows)


def place_kernel(place, h0, h1, h2, h3, out):
    received = jnp.concatenate([h0[...], h1[...], h2[...], h3[...]])
    chosen = lax.dot_general(
        place[...], received, (((0,), (0,)), ((), ())), preferred_element_type=F32
    )
    out[...] = chosen.astype(BF16)


def place_rows(place, received):
    return pl.pallas_call(
        place_kernel,
        out_shape=jax.ShapeDtypeStruct((place.shape[1], received[0].shape[1]), BF16),
        in_specs=[VMEM] * 5,
        out_specs=VMEM,
        compiler_params=params(8),
        cost_estimate=NO_COST,
        name="place_rows",
    )(place, *received)


def masks(axis):
    mask = 1
    while mask < lax.axis_size(axis):
        yield mask
        mask *= 2


def row_exchange(ids, index_rows, place, rounds):
    width = index_rows.shape[1]

    def gathered(keep, send, place, gates=((), (), ())):
        keep = keep.reshape(1, -1, SLOTS, width)
        send = send.reshape(1, -1, SLOTS, width)
        held = None
        for mask in list(masks("req"))[:1:-1]:
            if held is not None:
                keep, send = held[:, :mask], held[:, mask:]
            other = swap(send, "req", mask)
            if mask == 4:
                other = after(other, *gates[0])
            held = jnp.concatenate([keep, other])
        others = [swap(held[:, mask], "req", mask) for mask in (1, 2, 3)]
        others = list(after(tuple(others), *gates[1]))
        held = [part.reshape(-1, width) for part in [held[:, 0]] + others]
        found = place_rows(place, held)
        found = after(found, *gates[2]).reshape(4, -1, width)
        parts = [swap(found[mask], "tp", mask) for mask in (1, 2, 3)]
        return found[0] + parts[0] + parts[1] + parts[2]

    def one_more(number, total):
        keep, send, place, _ = take_rows(number.reshape(1), ids, index_rows)
        return total + gathered(keep, send, place)

    def further(rows):
        return lax.fori_loop(1, rounds[0], one_more, rows)

    return lambda keep, send, *gates: gathered(keep, send, place, gates), further


def per_device(
    states,
    lengths,
    w_qkv,
    b_qkv,
    w_out,
    b_out,
    ln1_gain,
    ln1_shift,
    w_up,
    b_up,
    w_down,
    b_down,
    ln2_gain,
    ln2_shift,
    index_rows,
    cand_ids,
):
    from_chip = swap(states, "tp", 2)
    from_core = swap(states, "tp", 1)
    w_qkv_t = w_qkv.transpose(1, 0, 2)

    w_up_p = swap(w_up, "tp", 1)
    w_qkv_p = swap(w_qkv_t, "tp", 1)

    held = cand_ids.reshape(1, -1)
    for mask in masks("req"):
        other = swap(held, "req", mask)
        if mask * 2 == lax.axis_size("req"):
            early_0, biases, w_half = early_own(
                states, after(from_core, held, w_qkv_p), w_qkv_t, b_qkv, b_up[None], w_out
            )
            other, early_0 = lax.optimization_barrier((other, early_0))
        held = jnp.concatenate([held, other])
    from_chip, early_0, held = lax.optimization_barrier((from_chip, early_0, held))
    ids = (held,) + tuple(swap(held, "tp", mask) for mask in (1, 2, 3))
    from_diag = swap(from_chip, "tp", 1)
    blocks = (states, from_core, from_chip, from_diag)
    w_down_p = swap(after(w_down, from_diag), "tp", 1)
    biases_p = swap(biases, "tp", 1)
    early_1 = early_partner(states, after(from_core, held), w_qkv_p, biases_p)
    early_0 = after(early_0, early_1)
    w_out_p = swap(after(w_out, from_core), "tp", 1)

    w_x0 = swap(w_half, "tp", 2)

    (context_0,) = attention(
        lengths, after(early_0, w_up_p), from_chip, from_diag, w_qkv_t, b_qkv, 2,
        "attention_own",
    )
    context_0x = swap(context_0, "tp", 2)
    w_x1 = swap(after(w_x0, context_0), "req", 1)
    context_1, numbers, place, rounds = attention(
        lengths, after(early_1, context_0), from_chip, from_diag, w_qkv_p, biases_p, 6,
        "attention_partner", (ids, index_rows.shape[0]),
    )
    context_1x = swap(context_1, "tp", 2)
    w_d0 = swap(after(w_x0, context_0), "tp", 1)
    w_d1 = swap(after(w_x1, context_1), "tp", 1)
    base, keep, send = project_first(
        blocks, after(context_0, w_down_p), context_0x, w_out, (w_x0, w_x1), b_out[None], numbers, index_rows
    )
    base = project_second(base, context_1, w_out_p)
    gathered, further = row_exchange(ids, index_rows, place, rounds)
    common = (
        context_1x, (w_d0, w_d1), ln1_gain[None], ln1_shift[None],
        (b_up[None], biases_p), b_down[None], (w_up, w_up_p),
        (w_down, w_down_p),
    )
    down_there = feed_forward(False, base, *common)
    down_x = swap(down_there, "tp", 2)
    down_here = feed_forward(True, after(base, down_there), *common)
    down_x = after(down_x, down_here)
    hidden, hidden_other, pool = finish(
        lengths, down_here, down_x, ln2_gain[None], ln2_shift[None]
    )

    rows = gathered(keep, send, (down_there,), (down_here,), (hidden,))
    pools = (pool,) + tuple(swap(pool, "tp", mask) for mask in (1, 2, 3))
    hidden_p = swap(hidden_other, "tp", 1)
    rows = further(after(rows, *pools))
    scores, hidden_out = score(lengths, pools, rows, hidden, hidden_p)
    return (hidden_out, scores)


def solution(mesh):
    placed = (
        P("req", "tp", None),
        P("req"),
        P(None, None, "tp"),
        P(None, "tp"),
        P("tp", None),
        P(),
        P(),
        P(),
        P(None, "tp"),
        P("tp"),
        P("tp", None),
        P(),
        P(),
        P(),
        P(("req", "tp"), None),
        P("req", "tp"),
    )
    return jax.shard_map(
        per_device,
        mesh=mesh,
        in_specs=placed,
        out_specs=(P("req", "tp", None), P("req", "tp")),
        check_vma=False,
    )
```

```python
import functools

import jax
import jax.numpy as jnp
from jax import lax
from jax.experimental import pallas as pl
from jax.experimental.pallas import tpu as pltpu
from jax.sharding import PartitionSpec as P

HEAD_DIM = 64
WINDOW = 512
SLOTS = 16
BF16 = jnp.bfloat16
F32 = jnp.float32
I32 = jnp.int32
MIB = 1024 * 1024
NO_COST = pl.CostEstimate(flops=1, bytes_accessed=1, transcendentals=0)


def cost(gflop):
    return pl.CostEstimate(flops=int(gflop * 10**9) + 1, bytes_accessed=MIB, transcendentals=0)


layer_eps = 1e-05
norm_eps = 1e-06

VMEM = pl.BlockSpec(memory_space=pltpu.VMEM)
SMEM = pl.BlockSpec(memory_space=pltpu.SMEM)
HBM = pl.BlockSpec(memory_space=pltpu.HBM)
ANY = pl.BlockSpec(memory_space=pl.ANY)


def layer_norm(values, gain, shift):
    centre = values - jnp.mean(values, axis=-1, keepdims=True)
    spread = jnp.mean(centre * centre, axis=-1, keepdims=True)
    return centre * lax.rsqrt(spread + layer_eps) * gain + shift


def swap(value, axis, mask):
    count = lax.axis_size(axis)
    return lax.ppermute(value, axis, [(i, i ^ mask) for i in range(count)])


def matmul(left, right):
    return jnp.dot(left, right, preferred_element_type=F32)


def params(mib):
    return pltpu.CompilerParams(vmem_limit_bytes=mib * MIB)


def after(value, *others):
    return lax.optimization_barrier((value,) + others)[0]


def half_kernel(w_out, half, sem):
    part = half.shape[0]
    first = pl.multiple_of((lax.axis_index("req") & 1) * part, part)
    copy = pltpu.make_async_copy(w_out.at[pl.ds(first, part)], half, sem)
    copy.start()
    copy.wait()


def half_of(w_out):
    return pl.pallas_call(
        half_kernel,
        out_shape=jax.ShapeDtypeStruct((w_out.shape[0] // 2, w_out.shape[1]), BF16),
        in_specs=[ANY],
        out_specs=VMEM,
        scratch_shapes=[pltpu.SemaphoreType.DMA],
        compiler_params=params(4),
        cost_estimate=NO_COST,
        name="half_of",
    )(w_out)


def attention_and_plan_kernel(
    rows_here, lengths, s0, s1, s2, s3, w, b, i0, i1, i2, i3, out, numbers, place, rounds,
    parts, bias,
):
    plan_rows(0, rows_here, (i0, i1, i2, i3), numbers, place, rounds)
    attention_kernel(lengths, s0, s1, s2, s3, w, b, out, parts, bias)


def attention_kernel(lengths, s0, s1, s2, s3, w, b, out, parts, bias):
    rank = lax.axis_index("tp")
    core = rank & 1
    length = lengths[core]
    share = s2.shape[1]
    seq_len = 4 * share
    wide = w.shape[2]
    text = jnp.concatenate([s0[core], s1[core], s2[core], s3[core]])
    for which in range(3):
        parts[which] = (matmul(text, w[which]) + b[which : which + 1, :]).astype(BF16)

    def position(index):
        return ((index // share) ^ rank) * share + index % share

    row_pos = position(lax.broadcasted_iota(I32, (seq_len, 1), 0))
    col_pos = position(lax.broadcasted_iota(I32, (1, seq_len), 1))
    keep = (jnp.abs(row_pos - col_pos) <= WINDOW // 2) & (col_pos < length)
    bias[...] = jnp.where(keep, F32(0.0), F32(-1e30))
    ones = jnp.ones((seq_len, 128), BF16)
    low = lax.broadcasted_iota(I32, (1, 128), 1) < HEAD_DIM
    scale = jnp.asarray(HEAD_DIM**-0.5, BF16)
    for pair in range(wide // 128):
        lanes = slice(pair * 128, (pair + 1) * 128)
        k_pair = parts[1, :, lanes]
        v_ones = jnp.concatenate([parts[2, :, lanes], ones], axis=1)
        for block in range(4):
            rows = slice(block * share, (block + 1) * share)
            q_pair = parts[0, rows, lanes] * scale
            found = []
            for head in range(2):
                chosen = low if head == 0 else jnp.logical_not(low)
                q_head = jnp.where(chosen, q_pair, jnp.zeros((), BF16))
                logits = lax.dot_general(
                    q_head, k_pair, (((1,), (1,)), ((), ())), preferred_element_type=F32
                )
                logits = logits + bias[rows, :]
                top = jnp.max(logits, axis=-1, keepdims=True)
                expo = jnp.exp(logits - top).astype(BF16)
                summed = matmul(expo, v_ones)
                found.append(summed[:, :128] / summed[:, 128:])
            context = jnp.where(low, found[0], found[1])
            context = jnp.where(row_pos[rows] < length, context, F32(0.0))
            out[rows, lanes] = context.astype(BF16)


def attention(lengths, blocks, w, b, gflop, name, plan=()):
    seq_len = 4 * blocks[0].shape[1]
    wide = w.shape[2]
    kernel = attention_kernel
    results = (jax.ShapeDtypeStruct((seq_len, wide), BF16),)
    out_specs = (VMEM,)
    ids = ()
    if plan:
        ids, rows_here = plan
        groups, each = ids[0].shape
        kernel = functools.partial(attention_and_plan_kernel, rows_here)
        results += (
            jax.ShapeDtypeStruct((2, groups * SLOTS), I32),
            jax.ShapeDtypeStruct((groups * SLOTS, 4 * each), BF16),
            jax.ShapeDtypeStruct((1,), I32),
        )
        out_specs += (VMEM, VMEM, SMEM)
    return pl.pallas_call(
        kernel,
        out_shape=results,
        in_specs=[SMEM] + [VMEM] * (6 + len(ids)),
        out_specs=out_specs,
        scratch_shapes=[
            pltpu.VMEM((3, seq_len, wide), BF16),
            pltpu.VMEM((seq_len, seq_len), F32),
        ],
        compiler_params=params(12),
        cost_estimate=cost(gflop),
        name=name,
    )(lengths, *blocks, w, b, *ids)


def joined(first, second):
    swapped = (lax.axis_index("req") & 1) != 0
    low = jnp.where(swapped, second[...], first[...])
    high = jnp.where(swapped, first[...], second[...])
    return jnp.concatenate([low, high])


def project_first_kernel(
    s0, s1, s2, s3, here, there, w, half_0, half_1, b, numbers, index, out, keep, send,
    chosen, tiles, rows, sems, sem,
):
    copy = pltpu.make_async_copy(numbers, chosen, sem)
    copy.start()
    share = s0.shape[1]
    core = lax.axis_index("tp") & 1
    w_there = joined(half_0, half_1)
    copy.wait()
    finish_rows = fetch_rows(chosen, index, tiles, rows, sems)
    for number, block in enumerate((s0, s1, s2, s3)):
        span = slice(number * share, (number + 1) * share)
        other = (number ^ 2) * share
        total = matmul(here[span, :], w[...]) + matmul(there[other : other + share, :], w_there)
        out[span, :] = total + (block[core].astype(F32) + b[...])
    finish_rows(keep, send)


def project_first(blocks, here, there, w, halves, b_out, numbers, index_rows):
    _, share, width = blocks[0].shape
    slots = numbers.shape[1]
    half = jax.ShapeDtypeStruct((slots // 2, width), BF16)
    return pl.pallas_call(
        project_first_kernel,
        out_shape=(jax.ShapeDtypeStruct((4 * share, width), F32), half, half),
        in_specs=[VMEM] * 11 + [HBM],
        out_specs=(VMEM, VMEM, VMEM),
        scratch_shapes=fetch_scratch(slots, width),
        compiler_params=params(12 + slots // 16),
        cost_estimate=cost(1),
        name="project_first",
    )(*blocks, here, there, w, *halves, b_out, numbers, index_rows)


def project_second_kernel(base, context, w, out):
    out[...] = base[...] + matmul(context[...], w[...])


def project_second(base, context, w):
    return pl.pallas_call(
        project_second_kernel,
        out_shape=jax.ShapeDtypeStruct(base.shape, F32),
        in_specs=[VMEM] * 3,
        out_specs=VMEM,
        input_output_aliases={0: 0},
        compiler_params=params(12),
        cost_estimate=cost(1),
        name="project_second",
    )(base, context, w)


def feed_kernel(
    keep_rest, base, c3, half_0, half_1, gain, shift, b0, b1, b_down,
    up0, up1, down0, down1, out, up_buf, down_buf, act, sems,
):
    hidden = up0.shape[1]
    copies = [
        pltpu.make_async_copy(source, target, sems.at[index])
        for index, (source, target) in enumerate(
            (
                (up0, up_buf.at[0]),
                (up1, up_buf.at[1]),
                (down0, down_buf.at[0]),
                (down1, down_buf.at[1]),
            )
        )
    ]
    for copy in copies:
        copy.start()
    total = base[...] + matmul(c3[...], joined(half_0, half_1))
    normed = layer_norm(total, gain[...], shift[...]).astype(BF16)
    step = 512
    for part in range(2):
        copies[part].wait()
        for low in range(0, hidden, step):
            up = matmul(normed, up_buf[part, :, low : low + step])
            up = up + (b0, b1)[part][:, low : low + step]
            activated = 0.5 * up * (1.0 + lax.erf(up * F32(0.5**0.5)))
            act[:, part * hidden + low : part * hidden + low + step] = activated.astype(BF16)
    copies[2].wait()
    down = matmul(act[:, :hidden], down_buf[0])
    copies[3].wait()
    down = down + matmul(act[:, hidden:], down_buf[1])
    if keep_rest:
        down = down + (normed.astype(F32) + b_down[...])
    out[...] = down.astype(out.dtype)


def feed_forward(keep_rest, base, context, halves, gain, shift, biases, b_down, ups, downs):
    seq_len, width = base.shape
    half = seq_len // 2
    here = 0 if keep_rest else 1
    hidden = ups[0].shape[1]
    heads_wide = context.shape[1]
    base_spec = pl.BlockSpec((half, width), lambda i: (here, 0))
    context_spec = pl.BlockSpec((half, heads_wide), lambda i: (1 - here, 0))
    return pl.pallas_call(
        lambda *refs: feed_kernel(keep_rest, *refs),
        out_shape=jax.ShapeDtypeStruct((half, width), F32 if keep_rest else BF16),
        grid=(1,),
        in_specs=[base_spec, context_spec] + [VMEM] * 7 + [ANY] * 4,
        out_specs=VMEM,
        scratch_shapes=[
            pltpu.VMEM((2, width, hidden), BF16),
            pltpu.VMEM((2, hidden, width), BF16),
            pltpu.VMEM((half, 2 * hidden), BF16),
            pltpu.SemaphoreType.DMA((4,)),
        ],
        compiler_params=params(20),
        cost_estimate=cost(8),
        name="feed_here" if keep_rest else "feed_there",
    )(base, context, *halves, gain, shift, *biases, b_down, *ups, *downs)


def finish_kernel(lengths, here, there, gain, shift, own, other, pool):
    rank = lax.axis_index("tp")
    length = lengths[rank & 1]
    share = own.shape[0]
    total = here[...] + there[...].astype(F32)
    hidden = layer_norm(total, gain[...], shift[...]).astype(BF16)
    own[...] = hidden[:share]
    other[...] = hidden[share:]
    index = lax.broadcasted_iota(I32, (2 * share, 1), 0)
    pos = ((index // share) ^ rank) * share + index % share
    valid = jnp.where(pos < length, hidden.astype(F32), F32(0.0))
    pool[...] = jnp.sum(valid, axis=0, keepdims=True)


def finish(lengths, here, there, gain, shift):
    half, width = here.shape
    block = jax.ShapeDtypeStruct((half // 2, width), BF16)
    return pl.pallas_call(
        finish_kernel,
        out_shape=(block, block, jax.ShapeDtypeStruct((1, width), F32)),
        in_specs=[SMEM] + [VMEM] * 4,
        out_specs=(VMEM, VMEM, VMEM),
        compiler_params=params(8),
        cost_estimate=cost(2),
        name="finish",
    )(lengths, here, there, gain, shift)


def score_kernel(
    lengths, pool, pool_core, pool_chip, pool_diag, rows, own, other, out, hidden_out
):
    core = lax.axis_index("tp") & 1
    width = pool.shape[1]
    mine = pool[...] + pool_chip[...]
    theirs = pool_core[...] + pool_diag[...]
    first = jnp.where(core == 0, mine, theirs) / lengths[0].astype(F32)
    second = jnp.where(core == 0, theirs, mine) / lengths[1].astype(F32)
    row = lax.broadcasted_iota(I32, (8, width), 0)
    pooled = jnp.where(row == 0, first, jnp.where(row == 1, second, F32(0.0)))
    scale = lax.rsqrt(jnp.mean(pooled * pooled, axis=-1, keepdims=True) + norm_eps)
    queries = (pooled * scale).astype(BF16)
    found = lax.dot_general(
        queries, rows[...], (((1,), (1,)), ((), ())), preferred_element_type=F32
    )
    each = rows.shape[0] // 2
    out[0:1, :] = found[0:1, :each]
    out[1:2, :] = found[1:2, each:]
    hidden_out[core] = own[...]
    hidden_out[1 - core] = other[...]


def score(lengths, pools, rows, own, other):
    return pl.pallas_call(
        score_kernel,
        out_shape=(
            jax.ShapeDtypeStruct((2, rows.shape[0] // 2), F32),
            jax.ShapeDtypeStruct((2,) + own.shape, BF16),
        ),
        in_specs=[SMEM] + [VMEM] * 7,
        out_specs=(VMEM, VMEM),
        compiler_params=params(8),
        cost_estimate=cost(1),
        name="score",
    )(lengths, *pools, rows, own, other)


def source_order(groups):
    order = [0]
    mask = groups // 2
    while mask >= 4:
        order = order + [entry + mask for entry in order]
        mask //= 2
    return [entry + last for last in range(4) for entry in order]


def as_ones(mask):
    return mask.astype(F32).astype(BF16)


def plan_rows(first_place, rows_here, parts, numbers, place, rounds):
    rank = lax.axis_index("tp")
    group = lax.axis_index("req")
    groups = parts[0].shape[0]
    slots = groups * SLOTS
    ids = jnp.concatenate([part[...] for part in parts], axis=1)
    count = ids.shape[1]
    owner = lax.shift_right_logical(ids, I32(rows_here.bit_length() - 1))
    before = as_ones(
        lax.broadcasted_iota(I32, (count, count), 0)
        < lax.broadcasted_iota(I32, (count, count), 1)
    )
    ones = jnp.ones((count, 128), BF16)
    slot = lax.broadcasted_iota(I32, (SLOTS, 1), 0) + first_place

    mine = owner == group * 4 + rank
    asked = jnp.concatenate(
        [
            (owner[:1] == (group ^ source) * 4 + rank).astype(F32)
            for source in source_order(groups)
        ]
    )
    both = jnp.concatenate([mine.astype(F32), asked]).astype(BF16)
    ranks = matmul(both, before).astype(I32)
    send_rank = jnp.where(mine, ranks[:groups], -1)
    take_rank = jnp.where(asked > 0, ranks[groups:], -1)

    local = jnp.where(mine, ids - (group * 4 + rank) * rows_here, 0)
    high = (local >> 6).astype(F32).astype(BF16)
    low = (local & 63).astype(F32).astype(BF16)
    chosen = jnp.concatenate(
        [(send_rank[k : k + 1] == slot).astype(F32) for k in range(groups)]
    ).astype(BF16)
    spread = (((1,), (1,)), ((), ()))
    wanted = 64.0 * lax.dot_general(high, chosen, spread, preferred_element_type=F32)
    wanted = wanted + lax.dot_general(low, chosen, spread, preferred_element_type=F32)
    counts = matmul(as_ones(mine), jnp.ones((count, slots), BF16))
    own = lax.broadcasted_iota(I32, (groups, slots), 0) == lax.div(
        lax.broadcasted_iota(I32, (groups, slots), 1), I32(SLOTS)
    )
    numbers[0:1, :] = jnp.sum(jnp.where(own, wanted, 0.0), axis=0, keepdims=True).astype(I32)
    counts = jnp.sum(jnp.where(own, counts, 0.0), axis=0, keepdims=True).astype(I32)
    numbers[1:2, :] = counts - first_place

    for k in range(groups):
        place[k * SLOTS : (k + 1) * SLOTS, :] = as_ones(take_rank[k : k + 1] == slot)
    shard = lax.broadcasted_iota(I32, (4 * groups, 1), 0)
    load = jnp.concatenate(
        [(owner[k : k + 1] == shard).astype(F32) for k in range(groups)]
    ).astype(BF16)
    most = jnp.max(matmul(load, ones)).astype(I32)
    rounds[0] = (most + SLOTS - 1) // SLOTS


def fetch_rows(chosen, index, tiles, rows, sems):
    deep = tiles.shape[1]
    slots = tiles.shape[0]
    step = 4

    def tile_copy(slot):
        first = pl.multiple_of((chosen[0, slot] // deep) * deep, deep)
        return pltpu.make_async_copy(index.at[pl.ds(first, deep)], tiles.at[slot], sems.at[slot])

    def start(number, carry):
        for each in range(step):
            tile_copy(number * step + each).start()
        return carry

    def select(number, carry):
        for each in range(step):
            tile_copy(number * step + each).wait()
        for each in range(step):
            source = number * step + each
            line = lax.broadcasted_iota(I32, (deep, 1), 0) == chosen[0, source] % deep
            row = jnp.where(line, tiles[source].astype(F32), F32(0.0))
            rows[pl.ds(source, 1), :] = jnp.sum(row, axis=0, keepdims=True)
        return carry

    def each_group(action):
        def one(number, carry):
            first = number * (SLOTS // step)
            left = jnp.clip(chosen[1, number * SLOTS], 0, SLOTS)
            return lax.fori_loop(first, first + (left + step - 1) // step, action, carry)

        lax.fori_loop(0, slots // SLOTS, one, 0)

    rows[...] = jnp.zeros_like(rows)
    each_group(start)

    def finish_rows(keep, send):
        each_group(select)
        keep[...] = rows[: slots // 2, :].astype(BF16)
        send[...] = rows[slots // 2 :, :].astype(BF16)

    return finish_rows


def take_kernel(
    number, i0, i1, i2, i3, index, keep, send, place, rounds, numbers, chosen, tiles, rows,
    sems, sem,
):
    plan_rows(number[0] * SLOTS, index.shape[0], (i0, i1, i2, i3), numbers, place, rounds)
    copy = pltpu.make_async_copy(numbers, chosen, sem)
    copy.start()
    copy.wait()
    fetch_rows(chosen, index, tiles, rows, sems)(keep, send)


def fetch_scratch(slots, width):
    return [
        pltpu.SMEM((2, slots), I32),
        pltpu.VMEM((slots, 16, width), BF16),
        pltpu.VMEM((slots, width), F32),
        pltpu.SemaphoreType.DMA((slots,)),
        pltpu.SemaphoreType.DMA,
    ]


def take_rows(number, ids, index_rows):
    groups, each = ids[0].shape
    slots = groups * SLOTS
    width = index_rows.shape[1]
    half = jax.ShapeDtypeStruct((slots // 2, width), BF16)
    return pl.pallas_call(
        take_kernel,
        out_shape=(
            half,
            half,
            jax.ShapeDtypeStruct((slots, 4 * each), BF16),
            jax.ShapeDtypeStruct((1,), I32),
        ),
        in_specs=[SMEM] + [VMEM] * 4 + [HBM],
        out_specs=(VMEM, VMEM, VMEM, SMEM),
        scratch_shapes=[pltpu.VMEM((2, slots), I32)] + fetch_scratch(slots, width),
        compiler_params=params(8 + slots // 16),
        cost_estimate=NO_COST,
        name="take_rows",
    )(number, *ids, index_rows)


def place_kernel(place, h0, h1, h2, h3, out):
    received = jnp.concatenate([h0[...], h1[...], h2[...], h3[...]])
    chosen = lax.dot_general(
        place[...], received, (((0,), (0,)), ((), ())), preferred_element_type=F32
    )
    out[...] = chosen.astype(BF16)


def place_rows(place, received):
    return pl.pallas_call(
        place_kernel,
        out_shape=jax.ShapeDtypeStruct((place.shape[1], received[0].shape[1]), BF16),
        in_specs=[VMEM] * 5,
        out_specs=VMEM,
        compiler_params=params(8),
        cost_estimate=NO_COST,
        name="place_rows",
    )(place, *received)


def masks(axis):
    mask = 1
    while mask < lax.axis_size(axis):
        yield mask
        mask *= 2


def row_exchange(ids, index_rows, place, rounds):
    width = index_rows.shape[1]

    def gathered(keep, send, place, gates=((), (), ())):
        keep = keep.reshape(1, -1, SLOTS, width)
        send = send.reshape(1, -1, SLOTS, width)
        held = None
        for mask in list(masks("req"))[:1:-1]:
            if held is not None:
                keep, send = held[:, :mask], held[:, mask:]
            other = swap(send, "req", mask)
            if mask == 4:
                other = after(other, *gates[0])
            held = jnp.concatenate([keep, other])
        others = [swap(held[:, mask], "req", mask) for mask in (1, 2, 3)]
        others = list(after(tuple(others), *gates[1]))
        held = [part.reshape(-1, width) for part in [held[:, 0]] + others]
        found = place_rows(place, held)
        found = after(found, *gates[2]).reshape(4, -1, width)
        parts = [swap(found[mask], "tp", mask) for mask in (1, 2, 3)]
        return found[0] + parts[0] + parts[1] + parts[2]

    def one_more(number, total):
        keep, send, place, _ = take_rows(number.reshape(1), ids, index_rows)
        return total + gathered(keep, send, place)

    def further(rows):
        return lax.fori_loop(1, rounds[0], one_more, rows)

    return lambda keep, send, *gates: gathered(keep, send, place, gates), further


def per_device(
    states,
    lengths,
    w_qkv,
    b_qkv,
    w_out,
    b_out,
    ln1_gain,
    ln1_shift,
    w_up,
    b_up,
    w_down,
    b_down,
    ln2_gain,
    ln2_shift,
    index_rows,
    cand_ids,
):
    from_chip = swap(states, "tp", 2)
    from_core = swap(states, "tp", 1)
    w_qkv_t = w_qkv.transpose(1, 0, 2)
    w_qkv_p = swap(w_qkv_t, "tp", 1)
    w_up_p = swap(w_up, "tp", 1)

    held = cand_ids.reshape(1, -1)
    for mask in masks("req"):
        other = swap(held, "req", mask)
        if mask * 2 == lax.axis_size("req"):
            w_half = half_of(after(w_out, held))
            other, w_half = lax.optimization_barrier((other, w_half))
        held = jnp.concatenate([held, other])
    from_chip, held, from_core, w_qkv_p = lax.optimization_barrier(
        (from_chip, held, from_core, w_qkv_p)
    )
    from_diag = swap(from_chip, "tp", 1)
    blocks = (states, from_core, from_chip, from_diag)
    ids = (held,) + tuple(swap(held, "tp", mask) for mask in (1, 2, 3))
    b_qkv_p = swap(b_qkv, "tp", 1)
    b_up_p = swap(b_up, "tp", 1)
    w_x0 = swap(w_half, "tp", 2)
    w_down_p = swap(after(w_down, from_diag, b_qkv_p, b_up_p), "tp", 1)
    w_out_p = swap(after(w_out, from_diag), "tp", 1)

    (context_0,) = attention(
        lengths, (after(states, w_up_p),) + blocks[1:], w_qkv_t, b_qkv, 2, "attention_own"
    )
    context_0x = swap(context_0, "tp", 2)
    w_x1 = swap(after(w_x0, context_0), "req", 1)
    context_1, numbers, place, rounds = attention(
        lengths, (after(states, context_0),) + blocks[1:], w_qkv_p, b_qkv_p, 6,
        "attention_partner", (ids, index_rows.shape[0]),
    )
    context_1x = swap(context_1, "tp", 2)
    w_d0 = swap(after(w_x0, context_0), "tp", 1)
    w_d1 = swap(after(w_x1, context_1), "tp", 1)

    base, keep, send = project_first(
        blocks, after(context_0, w_down_p), context_0x, w_out, (w_x0, w_x1), b_out[None], numbers,
        index_rows,
    )
    base = project_second(base, context_1, w_out_p)
    gathered, further = row_exchange(ids, index_rows, place, rounds)
    common = (
        context_1x, (w_d0, w_d1), ln1_gain[None], ln1_shift[None],
        (b_up[None], b_up_p[None]), b_down[None], (w_up, w_up_p),
        (w_down, w_down_p),
    )
    down_there = feed_forward(False, base, *common)
    down_x = swap(down_there, "tp", 2)
    down_here = feed_forward(True, after(base, down_there), *common)
    down_x = after(down_x, down_here)
    hidden, hidden_other, pool = finish(
        lengths, down_here, down_x, ln2_gain[None], ln2_shift[None]
    )

    rows = gathered(keep, send, (down_there,), (down_here,), (hidden,))
    pools = (pool,) + tuple(swap(pool, "tp", mask) for mask in (1, 2, 3))
    hidden_p = swap(hidden_other, "tp", 1)
    rows = further(after(rows, *pools))
    scores, hidden_out = score(lengths, pools, rows, hidden, hidden_p)
    return (hidden_out, scores)


def solution(mesh):
    placed = (
        P("req", "tp", None),
        P("req"),
        P(None, None, "tp"),
        P(None, "tp"),
        P("tp", None),
        P(),
        P(),
        P(),
        P(None, "tp"),
        P("tp"),
        P("tp", None),
        P(),
        P(),
        P(),
        P(("req", "tp"), None),
        P("req", "tp"),
    )
    return jax.shard_map(
        per_device,
        mesh=mesh,
        in_specs=placed,
        out_specs=(P("req", "tp", None), P("req", "tp")),
        check_vma=False,
    )
```

```python
import functools

import jax
import jax.numpy as jnp
from jax import lax
from jax.experimental import pallas as pl
from jax.experimental.pallas import tpu as pltpu
from jax.sharding import PartitionSpec as P

HEAD_DIM = 64
WINDOW = 512
SLOTS = 16
BF16 = jnp.bfloat16
F32 = jnp.float32
I32 = jnp.int32
MIB = 1024 * 1024
NO_COST = pl.CostEstimate(flops=1, bytes_accessed=1, transcendentals=0)


def cost(gflop):
    return pl.CostEstimate(flops=int(gflop * 10**9) + 1, bytes_accessed=MIB, transcendentals=0)


layer_eps = 1e-05
norm_eps = 1e-06

VMEM = pl.BlockSpec(memory_space=pltpu.VMEM)
SMEM = pl.BlockSpec(memory_space=pltpu.SMEM)
HBM = pl.BlockSpec(memory_space=pltpu.HBM)
ANY = pl.BlockSpec(memory_space=pl.ANY)


def layer_norm(values, gain, shift):
    centre = values - jnp.mean(values, axis=-1, keepdims=True)
    spread = jnp.mean(centre * centre, axis=-1, keepdims=True)
    return centre * lax.rsqrt(spread + layer_eps) * gain + shift


def in_hbm(array):
    return pltpu.with_memory_space_constraint(array, pltpu.HBM)


def swap(value, axis, mask):
    count = lax.axis_size(axis)
    return lax.ppermute(value, axis, [(i, i ^ mask) for i in range(count)])


def matmul(left, right):
    return jnp.dot(left, right, preferred_element_type=F32)


def params(mib):
    return pltpu.CompilerParams(vmem_limit_bytes=mib * MIB)


def after(value, *others):
    return lax.optimization_barrier((value,) + others)[0]


def half_kernel(w_out, half, sem):
    part = half.shape[0]
    first = pl.multiple_of((lax.axis_index("req") & 1) * part, part)
    copy = pltpu.make_async_copy(w_out.at[pl.ds(first, part)], half, sem)
    copy.start()
    copy.wait()


def half_of(w_out):
    return pl.pallas_call(
        half_kernel,
        out_shape=jax.ShapeDtypeStruct((w_out.shape[0] // 2, w_out.shape[1]), BF16),
        in_specs=[HBM],
        out_specs=VMEM,
        scratch_shapes=[pltpu.SemaphoreType.DMA],
        compiler_params=params(4),
        cost_estimate=NO_COST,
        name="half_of",
    )(in_hbm(w_out))


def first_attention_kernel(
    lengths, s0, s1, s2, s3, w, b, out, text, own, weights, parts, bias, sems
):
    core = lax.axis_index("tp") & 1
    copies = [pltpu.make_async_copy(s0.at[core], own, sems.at[3])]
    copies += [pltpu.make_async_copy(w.at[k], weights.at[k], sems.at[k]) for k in range(3)]
    for copy in copies:
        copy.start()
    copies[0].wait()
    text[...] = jnp.concatenate([own[...], s1[core], s2[core], s3[core]])
    for which in range(3):
        copies[1 + which].wait()
        project(which, text, weights, b, parts)
    attend(lengths, parts, bias, out)


def second_attention_kernel(
    rows_here, lengths, text, w, b, i0, i1, i2, i3, out, numbers, place, rounds, parts, bias
):
    plan_rows(0, rows_here, (i0, i1, i2, i3), numbers, place, rounds)
    for which in range(3):
        project(which, text, w, b, parts)
    attend(lengths, parts, bias, out)


def project(which, text, w, b, parts):
    parts[which] = (matmul(text[...], w[which]) + b[which : which + 1, :]).astype(BF16)


def attend(lengths, parts, bias, out):
    rank = lax.axis_index("tp")
    length = lengths[rank & 1]
    _, seq_len, wide = parts.shape
    share = seq_len // 4

    def position(index):
        return ((index // share) ^ rank) * share + index % share

    row_pos = position(lax.broadcasted_iota(I32, (seq_len, 1), 0))
    col_pos = position(lax.broadcasted_iota(I32, (1, seq_len), 1))
    keep = (jnp.abs(row_pos - col_pos) <= WINDOW // 2) & (col_pos < length)
    bias[...] = jnp.where(keep, F32(0.0), F32(-1e30))
    ones = jnp.ones((seq_len, 128), BF16)
    low = lax.broadcasted_iota(I32, (1, 128), 1) < HEAD_DIM
    scale = jnp.asarray(HEAD_DIM**-0.5, BF16)
    for pair in range(wide // 128):
        lanes = slice(pair * 128, (pair + 1) * 128)
        k_pair = parts[1, :, lanes]
        v_ones = jnp.concatenate([parts[2, :, lanes], ones], axis=1)
        for block in range(4):
            rows = slice(block * share, (block + 1) * share)
            q_pair = parts[0, rows, lanes] * scale
            found = []
            for head in range(2):
                chosen = low if head == 0 else jnp.logical_not(low)
                q_head = jnp.where(chosen, q_pair, jnp.zeros((), BF16))
                logits = lax.dot_general(
                    q_head, k_pair, (((1,), (1,)), ((), ())), preferred_element_type=F32
                )
                logits = logits + bias[rows, :]
                top = jnp.max(logits, axis=-1, keepdims=True)
                expo = jnp.exp(logits - top).astype(BF16)
                summed = matmul(expo, v_ones)
                found.append(summed[:, :128] / summed[:, 128:])
            context = jnp.where(low, found[0], found[1])
            context = jnp.where(row_pos[rows] < length, context, F32(0.0))
            out[rows, lanes] = context.astype(BF16)


def attention_scratch(seq_len, wide):
    return [pltpu.VMEM((3, seq_len, wide), BF16), pltpu.VMEM((seq_len, seq_len), F32)]


def first_attention(lengths, blocks, w, b):
    _, share, width = blocks[0].shape
    wide = w.shape[2]
    return pl.pallas_call(
        first_attention_kernel,
        out_shape=(
            jax.ShapeDtypeStruct((4 * share, wide), BF16),
            jax.ShapeDtypeStruct((4 * share, width), BF16),
        ),
        in_specs=[SMEM, HBM] + [VMEM] * 3 + [HBM, VMEM],
        out_specs=(VMEM, VMEM),
        scratch_shapes=[pltpu.VMEM((share, width), BF16), pltpu.VMEM(w.shape, BF16)]
        + attention_scratch(4 * share, wide)
        + [pltpu.SemaphoreType.DMA((4,))],
        compiler_params=params(14),
        cost_estimate=NO_COST,
        name="attention_own",
    )(in_hbm(lengths), in_hbm(blocks[0]), *blocks[1:], in_hbm(w), in_hbm(b))


def second_attention(lengths, text, w, b, ids, rows_here):
    seq_len = text.shape[0]
    wide = w.shape[2]
    groups, _, each = ids[0].shape
    return pl.pallas_call(
        functools.partial(second_attention_kernel, rows_here),
        out_shape=(
            jax.ShapeDtypeStruct((seq_len, wide), BF16),
            jax.ShapeDtypeStruct((2, groups * SLOTS), I32),
            jax.ShapeDtypeStruct((groups * SLOTS, 8 * each), BF16),
            jax.ShapeDtypeStruct((1,), I32),
        ),
        in_specs=[SMEM] + [VMEM] * 7,
        out_specs=(VMEM, VMEM, VMEM, SMEM),
        scratch_shapes=attention_scratch(seq_len, wide),
        compiler_params=params(12),
        cost_estimate=cost(6),
        name="attention_partner",
    )(in_hbm(lengths), text, w, b, *ids)


def joined(first, second):
    swapped = (lax.axis_index("req") & 1) != 0
    low = jnp.where(swapped, second[...], first[...])
    high = jnp.where(swapped, first[...], second[...])
    return jnp.concatenate([low, high])


def project_first_kernel(
    text, here, there, w, half_0, half_1, b, numbers, index, out, keep, send,
    chosen, tiles, rows, sems, sem,
):
    copy = pltpu.make_async_copy(numbers, chosen, sem)
    copy.start()
    half = text.shape[0] // 2
    w_there = joined(half_0, half_1)
    copy.wait()
    finish_rows = fetch_rows(chosen, index, tiles, rows, sems)
    for number in range(2):
        span = slice(number * half, (number + 1) * half)
        other = slice((1 - number) * half, (2 - number) * half)
        total = matmul(here[span, :], w[...]) + matmul(there[other, :], w_there)
        out[span, :] = total + (text[span, :].astype(F32) + b[...])
    finish_rows(keep, send)


def project_first(text, here, there, w, halves, b_out, numbers, index_rows):
    seq_len, width = text.shape
    slots = numbers.shape[1]
    half = jax.ShapeDtypeStruct((slots // 2, width), BF16)
    return pl.pallas_call(
        project_first_kernel,
        out_shape=(jax.ShapeDtypeStruct((seq_len, width), F32), half, half),
        in_specs=[VMEM] * 8 + [HBM],
        out_specs=(VMEM, VMEM, VMEM),
        scratch_shapes=fetch_scratch(slots, width),
        compiler_params=params(12 + slots // 16),
        cost_estimate=cost(1),
        name="project_first",
    )(text, here, there, w, *halves, b_out, numbers, in_hbm(index_rows))


def project_second_kernel(base, context, w, out):
    out[...] = base[...] + matmul(context[...], w[...])


def project_second(base, context, w):
    return pl.pallas_call(
        project_second_kernel,
        out_shape=jax.ShapeDtypeStruct(base.shape, F32),
        in_specs=[VMEM] * 3,
        out_specs=VMEM,
        input_output_aliases={0: 0},
        compiler_params=params(12),
        cost_estimate=cost(1),
        name="project_second",
    )(base, context, w)


def feed_kernel(
    keep_rest, base, c3, half_0, half_1, gain, shift, b0, b1, b_down,
    up_own, up_partner, down_own, down_partner, out, up_buf, down_buf, act, sems,
):
    hidden = up_own.shape[1]
    up_copy = pltpu.make_async_copy(up_own, up_buf, sems.at[0])
    down_copy = pltpu.make_async_copy(down_own, down_buf, sems.at[1])
    up_copy.start()
    down_copy.start()
    total = base[...] + matmul(c3[...], joined(half_0, half_1))
    normed = layer_norm(total, gain[...], shift[...]).astype(BF16)
    step = 512
    for part, (weight, bias) in enumerate(((up_partner, b1), (up_buf, b0))):
        if part == 1:
            up_copy.wait()
        for low in range(0, hidden, step):
            lanes = slice(low, low + step)
            up = matmul(normed, weight[:, lanes]) + bias[:, lanes]
            activated = 0.5 * up * (1.0 + lax.erf(up * F32(0.5**0.5)))
            act[:, part * hidden + low : part * hidden + low + step] = activated.astype(BF16)
    down = matmul(act[:, :hidden], down_partner[...])
    down_copy.wait()
    down = down + matmul(act[:, hidden:], down_buf[...])
    if keep_rest:
        down = down + (normed.astype(F32) + b_down[...])
    out[...] = down.astype(out.dtype)


def feed_forward(keep_rest, base, context, halves, gain, shift, biases, b_down, ups, downs):
    seq_len, width = base.shape
    half = seq_len // 2
    here = 0 if keep_rest else 1
    hidden = ups[0].shape[1]
    heads_wide = context.shape[1]
    base_spec = pl.BlockSpec((half, width), lambda i: (here, 0))
    context_spec = pl.BlockSpec((half, heads_wide), lambda i: (1 - here, 0))
    return pl.pallas_call(
        lambda *refs: feed_kernel(keep_rest, *refs),
        out_shape=jax.ShapeDtypeStruct((half, width), F32 if keep_rest else BF16),
        grid=(1,),
        in_specs=[base_spec, context_spec] + [VMEM] * 7
        + [HBM, VMEM, HBM, VMEM],
        out_specs=VMEM,
        scratch_shapes=[
            pltpu.VMEM((width, hidden), BF16),
            pltpu.VMEM((hidden, width), BF16),
            pltpu.VMEM((half, 2 * hidden), BF16),
            pltpu.SemaphoreType.DMA((2,)),
        ],
        compiler_params=params(20),
        cost_estimate=cost(8),
        name="feed_here" if keep_rest else "feed_there",
    )(base, context, *halves, gain, shift, *biases, b_down, in_hbm(ups[0]), ups[1],
      in_hbm(downs[0]), downs[1])


def finish_kernel(lengths, here, there, gain, shift, own, other, pool):
    rank = lax.axis_index("tp")
    length = lengths[rank & 1]
    share = own.shape[0]
    total = here[...] + there[...].astype(F32)
    hidden = layer_norm(total, gain[...], shift[...]).astype(BF16)
    own[...] = hidden[:share]
    other[...] = hidden[share:]
    index = lax.broadcasted_iota(I32, (2 * share, 1), 0)
    pos = ((index // share) ^ rank) * share + index % share
    valid = jnp.where(pos < length, hidden.astype(F32), F32(0.0))
    pool[...] = jnp.sum(valid, axis=0, keepdims=True)


def finish(lengths, here, there, gain, shift):
    half, width = here.shape
    block = jax.ShapeDtypeStruct((half // 2, width), BF16)
    return pl.pallas_call(
        finish_kernel,
        out_shape=(block, block, jax.ShapeDtypeStruct((1, width), F32)),
        in_specs=[SMEM] + [VMEM] * 4,
        out_specs=(VMEM, VMEM, VMEM),
        compiler_params=params(8),
        cost_estimate=cost(2),
        name="finish",
    )(lengths, here, there, gain, shift)


def score_kernel(
    lengths, pool, pool_core, pool_chip, pool_diag, rows, own, other, out, hidden_out
):
    core = lax.axis_index("tp") & 1
    width = pool.shape[1]
    mine = pool[...] + pool_chip[...]
    theirs = pool_core[...] + pool_diag[...]
    first = jnp.where(core == 0, mine, theirs) / lengths[0].astype(F32)
    second = jnp.where(core == 0, theirs, mine) / lengths[1].astype(F32)
    row = lax.broadcasted_iota(I32, (8, width), 0)
    pooled = jnp.where(row == 0, first, jnp.where(row == 1, second, F32(0.0)))
    scale = lax.rsqrt(jnp.mean(pooled * pooled, axis=-1, keepdims=True) + norm_eps)
    queries = (pooled * scale).astype(BF16)
    found = lax.dot_general(
        queries, rows[...], (((1,), (1,)), ((), ())), preferred_element_type=F32
    )
    each = rows.shape[0] // 2
    out[0:1, :] = found[0:1, :each]
    out[1:2, :] = found[1:2, each:]
    hidden_out[core] = own[...]
    hidden_out[1 - core] = other[...]


def score(lengths, pools, rows, own, other):
    return pl.pallas_call(
        score_kernel,
        out_shape=(
            jax.ShapeDtypeStruct((2, rows.shape[0] // 2), F32),
            jax.ShapeDtypeStruct((2,) + own.shape, BF16),
        ),
        in_specs=[SMEM] + [VMEM] * 7,
        out_specs=(VMEM, VMEM),
        compiler_params=params(8),
        cost_estimate=cost(1),
        name="score",
    )(lengths, *pools, rows, own, other)


def source_order(groups):
    order = [0]
    mask = groups // 2
    while mask >= 4:
        order = order + [entry + mask for entry in order]
        mask //= 2
    return [entry + last for last in range(4) for entry in order]


def as_ones(mask):
    return mask.astype(F32).astype(BF16)


def plan_rows(first_place, rows_here, parts, numbers, place, rounds):
    rank = lax.axis_index("tp")
    group = lax.axis_index("req")
    groups = parts[0].shape[0]
    slots = groups * SLOTS
    ids = jnp.concatenate([part[:, text, :] for part in parts for text in range(2)], axis=1)
    count = ids.shape[1]
    owner = lax.shift_right_logical(ids, I32(rows_here.bit_length() - 1))
    before = as_ones(
        lax.broadcasted_iota(I32, (count, count), 0)
        < lax.broadcasted_iota(I32, (count, count), 1)
    )
    ones = jnp.ones((count, 128), BF16)
    slot = lax.broadcasted_iota(I32, (SLOTS, 1), 0) + first_place

    mine = owner == group * 4 + rank
    asked = jnp.concatenate(
        [
            (owner[:1] == (group ^ source) * 4 + rank).astype(F32)
            for source in source_order(groups)
        ]
    )
    both = jnp.concatenate([mine.astype(F32), asked]).astype(BF16)
    ranks = matmul(both, before).astype(I32)
    send_rank = jnp.where(mine, ranks[:groups], -1)
    take_rank = jnp.where(asked > 0, ranks[groups:], -1)

    local = jnp.where(mine, ids - (group * 4 + rank) * rows_here, 0)
    high = (local >> 6).astype(F32).astype(BF16)
    low = (local & 63).astype(F32).astype(BF16)
    chosen = jnp.concatenate(
        [(send_rank[k : k + 1] == slot).astype(F32) for k in range(groups)]
    ).astype(BF16)
    spread = (((1,), (1,)), ((), ()))
    wanted = 64.0 * lax.dot_general(high, chosen, spread, preferred_element_type=F32)
    wanted = wanted + lax.dot_general(low, chosen, spread, preferred_element_type=F32)
    counts = matmul(as_ones(mine), jnp.ones((count, slots), BF16))
    own = lax.broadcasted_iota(I32, (groups, slots), 0) == lax.div(
        lax.broadcasted_iota(I32, (groups, slots), 1), I32(SLOTS)
    )
    numbers[0:1, :] = jnp.sum(jnp.where(own, wanted, 0.0), axis=0, keepdims=True).astype(I32)
    counts = jnp.sum(jnp.where(own, counts, 0.0), axis=0, keepdims=True).astype(I32)
    numbers[1:2, :] = counts - first_place

    for k in range(groups):
        place[k * SLOTS : (k + 1) * SLOTS, :] = as_ones(take_rank[k : k + 1] == slot)
    shard = lax.broadcasted_iota(I32, (4 * groups, 1), 0)
    load = jnp.concatenate(
        [(owner[k : k + 1] == shard).astype(F32) for k in range(groups)]
    ).astype(BF16)
    most = jnp.max(matmul(load, ones)).astype(I32)
    rounds[0] = (most + SLOTS - 1) // SLOTS


def fetch_rows(chosen, index, tiles, rows, sems):
    deep = tiles.shape[1]
    slots = tiles.shape[0]
    step = 4

    def tile_copy(slot):
        first = pl.multiple_of((chosen[0, slot] // deep) * deep, deep)
        return pltpu.make_async_copy(index.at[pl.ds(first, deep)], tiles.at[slot], sems.at[slot])

    def start(number, carry):
        for each in range(step):
            tile_copy(number * step + each).start()
        return carry

    def select(number, carry):
        for each in range(step):
            tile_copy(number * step + each).wait()
        for each in range(step):
            source = number * step + each
            line = lax.broadcasted_iota(I32, (deep, 1), 0) == chosen[0, source] % deep
            row = jnp.where(line, tiles[source].astype(F32), F32(0.0))
            rows[pl.ds(source, 1), :] = jnp.sum(row, axis=0, keepdims=True)
        return carry

    def each_group(action):
        def one(number, carry):
            first = number * (SLOTS // step)
            left = jnp.clip(chosen[1, number * SLOTS], 0, SLOTS)
            return lax.fori_loop(first, first + (left + step - 1) // step, action, carry)

        lax.fori_loop(0, slots // SLOTS, one, 0)

    rows[...] = jnp.zeros_like(rows)
    each_group(start)

    def finish_rows(keep, send):
        each_group(select)
        keep[...] = rows[: slots // 2, :].astype(BF16)
        send[...] = rows[slots // 2 :, :].astype(BF16)

    return finish_rows


def take_kernel(
    number, i0, i1, i2, i3, index, keep, send, place, rounds, numbers, chosen, tiles, rows,
    sems, sem,
):
    plan_rows(number[0] * SLOTS, index.shape[0], (i0, i1, i2, i3), numbers, place, rounds)
    copy = pltpu.make_async_copy(numbers, chosen, sem)
    copy.start()
    copy.wait()
    fetch_rows(chosen, index, tiles, rows, sems)(keep, send)


def fetch_scratch(slots, width):
    return [
        pltpu.SMEM((2, slots), I32),
        pltpu.VMEM((slots, 16, width), BF16),
        pltpu.VMEM((slots, width), F32),
        pltpu.SemaphoreType.DMA((slots,)),
        pltpu.SemaphoreType.DMA,
    ]


def take_rows(number, ids, index_rows):
    groups, _, each = ids[0].shape
    slots = groups * SLOTS
    width = index_rows.shape[1]
    half = jax.ShapeDtypeStruct((slots // 2, width), BF16)
    return pl.pallas_call(
        take_kernel,
        out_shape=(
            half,
            half,
            jax.ShapeDtypeStruct((slots, 8 * each), BF16),
            jax.ShapeDtypeStruct((1,), I32),
        ),
        in_specs=[SMEM] + [VMEM] * 4 + [HBM],
        out_specs=(VMEM, VMEM, VMEM, SMEM),
        scratch_shapes=[pltpu.VMEM((2, slots), I32)] + fetch_scratch(slots, width),
        compiler_params=params(8 + slots // 16),
        cost_estimate=NO_COST,
        name="take_rows",
    )(number, *ids, in_hbm(index_rows))


def place_kernel(place, h0, h1, h2, h3, out):
    received = jnp.concatenate([h0[...], h1[...], h2[...], h3[...]])
    chosen = lax.dot_general(
        place[...], received, (((0,), (0,)), ((), ())), preferred_element_type=F32
    )
    out[...] = chosen.astype(BF16)


def place_rows(place, received):
    return pl.pallas_call(
        place_kernel,
        out_shape=jax.ShapeDtypeStruct((place.shape[1], received[0].shape[1]), BF16),
        in_specs=[VMEM] * 5,
        out_specs=VMEM,
        compiler_params=params(8),
        cost_estimate=NO_COST,
        name="place_rows",
    )(place, *received)


def masks(axis):
    mask = 1
    while mask < lax.axis_size(axis):
        yield mask
        mask *= 2


def row_exchange(ids, index_rows, place, rounds):
    width = index_rows.shape[1]

    def gathered(keep, send, place, gates=((), (), ())):
        keep = keep.reshape(1, -1, SLOTS, width)
        send = send.reshape(1, -1, SLOTS, width)
        held = None
        for mask in list(masks("req"))[:1:-1]:
            if held is not None:
                keep, send = held[:, :mask], held[:, mask:]
            other = swap(send, "req", mask)
            if mask == 4:
                other = after(other, *gates[0])
            held = jnp.concatenate([keep, other])
        others = [swap(held[:, mask], "req", mask) for mask in (1, 2, 3)]
        others = list(after(tuple(others), *gates[1]))
        held = [part.reshape(-1, width) for part in [held[:, 0]] + others]
        found = place_rows(place, held)
        found = after(found, *gates[2]).reshape(4, -1, width)
        parts = [swap(found[mask], "tp", mask) for mask in (1, 2, 3)]
        return found[0] + parts[0] + parts[1] + parts[2]

    def one_more(number, total):
        keep, send, place, _ = take_rows(number.reshape(1), ids, index_rows)
        return total + gathered(keep, send, place)

    def further(rows):
        return lax.fori_loop(1, rounds[0], one_more, rows)

    return lambda keep, send, *gates: gathered(keep, send, place, gates), further


def per_device(
    states,
    lengths,
    w_qkv,
    b_qkv,
    w_out,
    b_out,
    ln1_gain,
    ln1_shift,
    w_up,
    b_up,
    w_down,
    b_down,
    ln2_gain,
    ln2_shift,
    index_rows,
    cand_ids,
):
    from_chip = swap(states, "tp", 2)
    from_core = swap(states, "tp", 1)
    w_qkv_t = w_qkv.transpose(1, 0, 2)
    w_qkv_p = swap(w_qkv_t, "tp", 1)
    b_qkv_p = swap(b_qkv, "tp", 1)
    b_up_p = swap(b_up, "tp", 1)

    held = cand_ids[None]
    for mask in masks("req"):
        other = swap(held, "req", mask)
        if mask * 2 == lax.axis_size("req"):
            w_half = half_of(after(w_out, held))
            other, w_half = lax.optimization_barrier((other, w_half))
        held = jnp.concatenate([held, other])
    w_out_p = swap(w_out, "tp", 1)
    from_chip, held, from_core, w_qkv_p, b_qkv_p, b_up_p, w_out_p = lax.optimization_barrier(
        (from_chip, held, from_core, w_qkv_p, b_qkv_p, b_up_p, w_out_p)
    )
    from_diag = swap(from_chip, "tp", 1)
    blocks = (states, from_core, from_chip, from_diag)
    ids = (held,) + tuple(swap(held, "tp", mask) for mask in (1, 2, 3))
    w_up_p = swap(after(w_up, from_diag, *ids), "tp", 1)
    w_down_p = swap(after(w_down, from_diag, *ids), "tp", 1)
    w_x0 = swap(after(w_half, ids[2]), "tp", 2)

    blocks, ids = lax.optimization_barrier((blocks, ids))
    context_0, text = first_attention(lengths, blocks, w_qkv_t, b_qkv)
    context_0x = swap(context_0, "tp", 2)
    w_x1 = swap(after(w_x0, context_0), "req", 1)
    context_1, numbers, place, rounds = second_attention(
        lengths, text, w_qkv_p, b_qkv_p, ids, index_rows.shape[0]
    )
    context_1x = swap(context_1, "tp", 2)
    w_d0 = swap(after(w_x0, context_0), "tp", 1)
    w_d1 = swap(after(w_x1, context_1), "tp", 1)

    base, keep, send = project_first(
        text, context_0, context_0x, w_out, (w_x0, w_x1), b_out[None], numbers,
        index_rows,
    )
    base = project_second(base, context_1, w_out_p)
    gathered, further = row_exchange(ids, index_rows, place, rounds)
    common = (
        context_1x, (w_d0, w_d1), ln1_gain[None], ln1_shift[None],
        (b_up[None], b_up_p[None]), b_down[None], (w_up, w_up_p),
        (w_down, w_down_p),
    )
    down_there = feed_forward(False, base, *common)
    down_x = swap(down_there, "tp", 2)
    down_here = feed_forward(True, after(base, down_there), *common)
    down_x = after(down_x, down_here)
    hidden, hidden_other, pool = finish(
        lengths, down_here, down_x, ln2_gain[None], ln2_shift[None]
    )

    rows = gathered(keep, after(send, down_there), (down_here,), (down_here,), (hidden,))
    pools = (pool,) + tuple(swap(pool, "tp", mask) for mask in (1, 2, 3))
    hidden_p = swap(hidden_other, "tp", 1)
    rows = further(after(rows, *pools))
    scores, hidden_out = score(lengths, pools, rows, hidden, hidden_p)
    return (hidden_out, scores)


def solution(mesh):
    placed = (
        P("req", "tp", None),
        P("req"),
        P(None, None, "tp"),
        P(None, "tp"),
        P("tp", None),
        P(),
        P(),
        P(),
        P(None, "tp"),
        P("tp"),
        P("tp", None),
        P(),
        P(),
        P(),
        P(("req", "tp"), None),
        P("req", "tp"),
    )
    return jax.shard_map(
        per_device,
        mesh=mesh,
        in_specs=placed,
        out_specs=(P("req", "tp", None), P("req", "tp")),
        check_vma=False,
    )
```

```python
import functools

import jax
import jax.numpy as jnp
from jax import lax
from jax.experimental import pallas as pl
from jax.experimental.pallas import tpu as pltpu
from jax.sharding import PartitionSpec as P

HEAD_DIM = 64
WINDOW = 512
SLOTS = 16
BF16 = jnp.bfloat16
F32 = jnp.float32
I32 = jnp.int32
MIB = 1024 * 1024
NO_COST = pl.CostEstimate(flops=1, bytes_accessed=1, transcendentals=0)


def cost(gflop):
    return pl.CostEstimate(flops=int(gflop * 10**9) + 1, bytes_accessed=MIB, transcendentals=0)


layer_eps = 1e-05
norm_eps = 1e-06

VMEM = pl.BlockSpec(memory_space=pltpu.VMEM)
SMEM = pl.BlockSpec(memory_space=pltpu.SMEM)
HBM = pl.BlockSpec(memory_space=pltpu.HBM)
ANY = pl.BlockSpec(memory_space=pl.ANY)


def layer_norm(values, gain, shift):
    centre = values - jnp.mean(values, axis=-1, keepdims=True)
    spread = jnp.mean(centre * centre, axis=-1, keepdims=True)
    return centre * lax.rsqrt(spread + layer_eps) * gain + shift


def in_hbm(array):
    return pltpu.with_memory_space_constraint(array, pltpu.HBM)


def swap(value, axis, mask):
    count = lax.axis_size(axis)
    return lax.ppermute(value, axis, [(i, i ^ mask) for i in range(count)])


def matmul(left, right):
    return jnp.dot(left, right, preferred_element_type=F32)


def params(mib):
    return pltpu.CompilerParams(vmem_limit_bytes=mib * MIB)


def after(value, *others):
    return lax.optimization_barrier((value,) + others)[0]


def load_kernel(states, w, w_out, mine, w_here, half, sems):
    part = half.shape[0]
    first = pl.multiple_of((lax.axis_index("req") & 1) * part, part)
    copies = [
        pltpu.make_async_copy(source, target, sems.at[number])
        for number, (source, target) in enumerate(
            (
                (w_out.at[pl.ds(first, part)], half),
                (states.at[lax.axis_index("tp") & 1], mine),
                (w, w_here),
            )
        )
    ]
    for copy in copies:
        copy.start()
    for copy in copies:
        copy.wait()


def load(states, w, w_out):
    return pl.pallas_call(
        load_kernel,
        out_shape=(
            jax.ShapeDtypeStruct(states.shape[1:], BF16),
            jax.ShapeDtypeStruct(w.shape, BF16),
            jax.ShapeDtypeStruct((w_out.shape[0] // 2, w_out.shape[1]), BF16),
        ),
        in_specs=[HBM] * 3,
        out_specs=(VMEM, VMEM, VMEM),
        scratch_shapes=[pltpu.SemaphoreType.DMA((3,))],
        compiler_params=params(6),
        cost_estimate=NO_COST,
        name="load",
    )(in_hbm(states), in_hbm(w), in_hbm(w_out))


def first_attention_kernel(lengths, mine, s1, s2, s3, w, b, out, text, parts, bias):
    core = lax.axis_index("tp") & 1
    text[...] = jnp.concatenate([mine[...], s1[core], s2[core], s3[core]])
    for which in range(3):
        project(which, text, w, b, parts)
    attend(lengths, parts, bias, out)


def second_attention_kernel(
    rows_here, lengths, text, w, b, i0, i1, i2, i3, out, numbers, place, rounds, parts, bias
):
    plan_rows(0, rows_here, (i0, i1, i2, i3), numbers, place, rounds)
    for which in range(3):
        project(which, text, w, b, parts)
    attend(lengths, parts, bias, out)


def project(which, text, w, b, parts):
    parts[which] = (matmul(text[...], w[which]) + b[which : which + 1, :]).astype(BF16)


def attend(lengths, parts, bias, out):
    rank = lax.axis_index("tp")
    length = lengths[rank & 1]
    _, seq_len, wide = parts.shape
    share = seq_len // 4

    def position(index):
        return ((index // share) ^ rank) * share + index % share

    row_pos = position(lax.broadcasted_iota(I32, (seq_len, 1), 0))
    col_pos = position(lax.broadcasted_iota(I32, (1, seq_len), 1))
    keep = (jnp.abs(row_pos - col_pos) <= WINDOW // 2) & (col_pos < length)
    bias[...] = jnp.where(keep, F32(0.0), F32(-1e30))
    ones = jnp.ones((seq_len, 128), BF16)
    low = lax.broadcasted_iota(I32, (1, 128), 1) < HEAD_DIM
    scale = jnp.asarray(HEAD_DIM**-0.5, BF16)
    for pair in range(wide // 128):
        lanes = slice(pair * 128, (pair + 1) * 128)
        k_pair = parts[1, :, lanes]
        v_ones = jnp.concatenate([parts[2, :, lanes], ones], axis=1)
        for block in range(4):
            rows = slice(block * share, (block + 1) * share)
            q_pair = parts[0, rows, lanes] * scale
            found = []
            for head in range(2):
                chosen = low if head == 0 else jnp.logical_not(low)
                q_head = jnp.where(chosen, q_pair, jnp.zeros((), BF16))
                logits = lax.dot_general(
                    q_head, k_pair, (((1,), (1,)), ((), ())), preferred_element_type=F32
                )
                logits = logits + bias[rows, :]
                top = jnp.max(logits, axis=-1, keepdims=True)
                expo = jnp.exp(logits - top).astype(BF16)
                summed = matmul(expo, v_ones)
                found.append(summed[:, :128] / summed[:, 128:])
            context = jnp.where(low, found[0], found[1])
            context = jnp.where(row_pos[rows] < length, context, F32(0.0))
            out[rows, lanes] = context.astype(BF16)


def attention_scratch(seq_len, wide):
    return [pltpu.VMEM((3, seq_len, wide), BF16), pltpu.VMEM((seq_len, seq_len), F32)]


def first_attention(lengths, blocks, w, b):
    share, width = blocks[0].shape
    wide = w.shape[2]
    return pl.pallas_call(
        first_attention_kernel,
        out_shape=(
            jax.ShapeDtypeStruct((4 * share, wide), BF16),
            jax.ShapeDtypeStruct((4 * share, width), BF16),
        ),
        in_specs=[SMEM] + [VMEM] * 6,
        out_specs=(VMEM, VMEM),
        scratch_shapes=attention_scratch(4 * share, wide),
        compiler_params=params(12),
        cost_estimate=NO_COST,
        name="attention_own",
    )(in_hbm(lengths), *blocks, w, in_hbm(b))


def second_attention(lengths, text, w, b, ids, rows_here):
    seq_len = text.shape[0]
    wide = w.shape[2]
    groups, each = ids[0].shape
    return pl.pallas_call(
        functools.partial(second_attention_kernel, rows_here),
        out_shape=(
            jax.ShapeDtypeStruct((seq_len, wide), BF16),
            jax.ShapeDtypeStruct((2, groups * SLOTS), I32),
            jax.ShapeDtypeStruct((groups * SLOTS, 4 * each), BF16),
            jax.ShapeDtypeStruct((1,), I32),
        ),
        in_specs=[SMEM] + [VMEM] * 7,
        out_specs=(VMEM, VMEM, VMEM, SMEM),
        scratch_shapes=attention_scratch(seq_len, wide),
        compiler_params=params(12),
        cost_estimate=cost(6),
        name="attention_partner",
    )(in_hbm(lengths), text, w, b, *ids)


def joined(first, second):
    swapped = (lax.axis_index("req") & 1) != 0
    low = jnp.where(swapped, second[...], first[...])
    high = jnp.where(swapped, first[...], second[...])
    return jnp.concatenate([low, high])


def project_first_kernel(
    text, here, there, w, half_0, half_1, b, numbers, index, out, keep, send,
    chosen, tiles, rows, sems, sem,
):
    copy = pltpu.make_async_copy(numbers, chosen, sem)
    copy.start()
    half = text.shape[0] // 2
    w_there = joined(half_0, half_1)
    copy.wait()
    finish_rows = fetch_rows(chosen, index, tiles, rows, sems)
    for number in range(2):
        span = slice(number * half, (number + 1) * half)
        other = slice((1 - number) * half, (2 - number) * half)
        total = matmul(here[span, :], w[...]) + matmul(there[other, :], w_there)
        out[span, :] = total + (text[span, :].astype(F32) + b[...])
    finish_rows(keep, send)


def project_first(text, here, there, w, halves, b_out, numbers, index_rows):
    seq_len, width = text.shape
    slots = numbers.shape[1]
    half = jax.ShapeDtypeStruct((slots // 2, width), BF16)
    return pl.pallas_call(
        project_first_kernel,
        out_shape=(jax.ShapeDtypeStruct((seq_len, width), F32), half, half),
        in_specs=[VMEM] * 8 + [HBM],
        out_specs=(VMEM, VMEM, VMEM),
        scratch_shapes=fetch_scratch(slots, width),
        compiler_params=params(12 + slots // 16),
        cost_estimate=cost(1),
        name="project_first",
    )(text, here, there, w, *halves, b_out, numbers, in_hbm(index_rows))


def project_second_kernel(base, context, w, out):
    out[...] = base[...] + matmul(context[...], w[...])


def project_second(base, context, w):
    return pl.pallas_call(
        project_second_kernel,
        out_shape=jax.ShapeDtypeStruct(base.shape, F32),
        in_specs=[VMEM] * 3,
        out_specs=VMEM,
        input_output_aliases={0: 0},
        compiler_params=params(12),
        cost_estimate=cost(1),
        name="project_second",
    )(base, context, w)


def feed_kernel(
    keep_rest, base, c3, half_0, half_1, gain, shift, b0, b1, b_down,
    up_own, up_partner, down_own, down_partner, out, up_buf, down_buf, act, sems,
):
    hidden = up_own.shape[1]
    up_copy = pltpu.make_async_copy(up_own, up_buf, sems.at[0])
    down_copy = pltpu.make_async_copy(down_own, down_buf, sems.at[1])
    up_copy.start()
    down_copy.start()
    total = base[...] + matmul(c3[...], joined(half_0, half_1))
    normed = layer_norm(total, gain[...], shift[...]).astype(BF16)
    step = 512
    for part, (weight, bias) in enumerate(((up_partner, b1), (up_buf, b0))):
        if part == 1:
            up_copy.wait()
        for low in range(0, hidden, step):
            lanes = slice(low, low + step)
            up = matmul(normed, weight[:, lanes]) + bias[:, lanes]
            activated = 0.5 * up * (1.0 + lax.erf(up * F32(0.5**0.5)))
            act[:, part * hidden + low : part * hidden + low + step] = activated.astype(BF16)
    down = matmul(act[:, :hidden], down_partner[...])
    down_copy.wait()
    down = down + matmul(act[:, hidden:], down_buf[...])
    if keep_rest:
        down = down + (normed.astype(F32) + b_down[...])
    out[...] = down.astype(out.dtype)


def feed_forward(keep_rest, base, context, halves, gain, shift, biases, b_down, ups, downs):
    seq_len, width = base.shape
    half = seq_len // 2
    here = 0 if keep_rest else 1
    hidden = ups[0].shape[1]
    heads_wide = context.shape[1]
    base_spec = pl.BlockSpec((half, width), lambda i: (here, 0))
    context_spec = pl.BlockSpec((half, heads_wide), lambda i: (1 - here, 0))
    return pl.pallas_call(
        lambda *refs: feed_kernel(keep_rest, *refs),
        out_shape=jax.ShapeDtypeStruct((half, width), F32 if keep_rest else BF16),
        grid=(1,),
        in_specs=[base_spec, context_spec] + [VMEM] * 7
        + [HBM, VMEM, HBM, VMEM],
        out_specs=VMEM,
        scratch_shapes=[
            pltpu.VMEM((width, hidden), BF16),
            pltpu.VMEM((hidden, width), BF16),
            pltpu.VMEM((half, 2 * hidden), BF16),
            pltpu.SemaphoreType.DMA((2,)),
        ],
        compiler_params=params(20),
        cost_estimate=cost(8),
        name="feed_here" if keep_rest else "feed_there",
    )(base, context, *halves, gain, shift, *biases, b_down, in_hbm(ups[0]), ups[1],
      in_hbm(downs[0]), downs[1])


def finish_kernel(lengths, here, there, gain, shift, own, other, pool):
    rank = lax.axis_index("tp")
    length = lengths[rank & 1]
    share = own.shape[0]
    total = here[...] + there[...].astype(F32)
    hidden = layer_norm(total, gain[...], shift[...]).astype(BF16)
    own[...] = hidden[:share]
    other[...] = hidden[share:]
    index = lax.broadcasted_iota(I32, (2 * share, 1), 0)
    pos = ((index // share) ^ rank) * share + index % share
    valid = jnp.where(pos < length, hidden.astype(F32), F32(0.0))
    pool[...] = jnp.sum(valid, axis=0, keepdims=True)


def finish(lengths, here, there, gain, shift):
    half, width = here.shape
    block = jax.ShapeDtypeStruct((half // 2, width), BF16)
    return pl.pallas_call(
        finish_kernel,
        out_shape=(block, block, jax.ShapeDtypeStruct((1, width), F32)),
        in_specs=[SMEM] + [VMEM] * 4,
        out_specs=(VMEM, VMEM, VMEM),
        compiler_params=params(8),
        cost_estimate=cost(2),
        name="finish",
    )(lengths, here, there, gain, shift)


def score_kernel(
    lengths, pool, pool_core, pool_chip, pool_diag, rows, own, other, out, hidden_out
):
    core = lax.axis_index("tp") & 1
    width = pool.shape[1]
    mine = pool[...] + pool_chip[...]
    theirs = pool_core[...] + pool_diag[...]
    first = jnp.where(core == 0, mine, theirs) / lengths[0].astype(F32)
    second = jnp.where(core == 0, theirs, mine) / lengths[1].astype(F32)
    row = lax.broadcasted_iota(I32, (8, width), 0)
    pooled = jnp.where(row == 0, first, jnp.where(row == 1, second, F32(0.0)))
    scale = lax.rsqrt(jnp.mean(pooled * pooled, axis=-1, keepdims=True) + norm_eps)
    queries = (pooled * scale).astype(BF16)
    found = lax.dot_general(
        queries, rows[...], (((1,), (1,)), ((), ())), preferred_element_type=F32
    )
    each = rows.shape[0] // 2
    out[0:1, :] = found[0:1, :each]
    out[1:2, :] = found[1:2, each:]
    hidden_out[core] = own[...]
    hidden_out[1 - core] = other[...]


def score(lengths, pools, rows, own, other):
    return pl.pallas_call(
        score_kernel,
        out_shape=(
            jax.ShapeDtypeStruct((2, rows.shape[0] // 2), F32),
            jax.ShapeDtypeStruct((2,) + own.shape, BF16),
        ),
        in_specs=[SMEM] + [VMEM] * 7,
        out_specs=(VMEM, VMEM),
        compiler_params=params(8),
        cost_estimate=cost(1),
        name="score",
    )(lengths, *pools, rows, own, other)


def source_order(groups):
    order = [0]
    mask = groups // 2
    while mask >= 4:
        order = order + [entry + mask for entry in order]
        mask //= 2
    return [entry + last for last in range(4) for entry in order]


def as_ones(mask):
    return mask.astype(F32).astype(BF16)


def plan_rows(first_place, rows_here, parts, numbers, place, rounds):
    rank = lax.axis_index("tp")
    group = lax.axis_index("req")
    groups = parts[0].shape[0]
    slots = groups * SLOTS
    ids = jnp.concatenate([part[...] for part in parts], axis=1)
    count = ids.shape[1]
    owner = lax.shift_right_logical(ids, I32(rows_here.bit_length() - 1))
    before = as_ones(
        lax.broadcasted_iota(I32, (count, count), 0)
        < lax.broadcasted_iota(I32, (count, count), 1)
    )
    ones = jnp.ones((count, 128), BF16)
    slot = lax.broadcasted_iota(I32, (SLOTS, 1), 0) + first_place

    mine = owner == group * 4 + rank
    asked = jnp.concatenate(
        [
            (owner[:1] == (group ^ source) * 4 + rank).astype(F32)
            for source in source_order(groups)
        ]
    )
    both = jnp.concatenate([mine.astype(F32), asked]).astype(BF16)
    ranks = matmul(both, before).astype(I32)
    send_rank = jnp.where(mine, ranks[:groups], -1)
    take_rank = jnp.where(asked > 0, ranks[groups:], -1)

    local = jnp.where(mine, ids - (group * 4 + rank) * rows_here, 0)
    high = (local >> 6).astype(F32).astype(BF16)
    low = (local & 63).astype(F32).astype(BF16)
    chosen = jnp.concatenate(
        [(send_rank[k : k + 1] == slot).astype(F32) for k in range(groups)]
    ).astype(BF16)
    spread = (((1,), (1,)), ((), ()))
    wanted = 64.0 * lax.dot_general(high, chosen, spread, preferred_element_type=F32)
    wanted = wanted + lax.dot_general(low, chosen, spread, preferred_element_type=F32)
    counts = matmul(as_ones(mine), jnp.ones((count, slots), BF16))
    own = lax.broadcasted_iota(I32, (groups, slots), 0) == lax.div(
        lax.broadcasted_iota(I32, (groups, slots), 1), I32(SLOTS)
    )
    numbers[0:1, :] = jnp.sum(jnp.where(own, wanted, 0.0), axis=0, keepdims=True).astype(I32)
    counts = jnp.sum(jnp.where(own, counts, 0.0), axis=0, keepdims=True).astype(I32)
    numbers[1:2, :] = counts - first_place

    for k in range(groups):
        place[k * SLOTS : (k + 1) * SLOTS, :] = as_ones(take_rank[k : k + 1] == slot)
    shard = lax.broadcasted_iota(I32, (4 * groups, 1), 0)
    load = jnp.concatenate(
        [(owner[k : k + 1] == shard).astype(F32) for k in range(groups)]
    ).astype(BF16)
    most = jnp.max(matmul(load, ones)).astype(I32)
    rounds[0] = (most + SLOTS - 1) // SLOTS


def fetch_rows(chosen, index, tiles, rows, sems):
    deep = tiles.shape[1]
    slots = tiles.shape[0]
    step = 4

    def tile_copy(slot):
        first = pl.multiple_of((chosen[0, slot] // deep) * deep, deep)
        return pltpu.make_async_copy(index.at[pl.ds(first, deep)], tiles.at[slot], sems.at[slot])

    def start(number, carry):
        for each in range(step):
            tile_copy(number * step + each).start()
        return carry

    def select(number, carry):
        for each in range(step):
            tile_copy(number * step + each).wait()
        for each in range(step):
            source = number * step + each
            line = lax.broadcasted_iota(I32, (deep, 1), 0) == chosen[0, source] % deep
            row = jnp.where(line, tiles[source].astype(F32), F32(0.0))
            rows[pl.ds(source, 1), :] = jnp.sum(row, axis=0, keepdims=True)
        return carry

    def each_group(action):
        def one(number, carry):
            first = number * (SLOTS // step)
            left = jnp.clip(chosen[1, number * SLOTS], 0, SLOTS)
            return lax.fori_loop(first, first + (left + step - 1) // step, action, carry)

        lax.fori_loop(0, slots // SLOTS, one, 0)

    rows[...] = jnp.zeros_like(rows)
    each_group(start)

    def finish_rows(keep, send):
        each_group(select)
        keep[...] = rows[: slots // 2, :].astype(BF16)
        send[...] = rows[slots // 2 :, :].astype(BF16)

    return finish_rows


def take_kernel(
    number, i0, i1, i2, i3, index, keep, send, place, rounds, numbers, chosen, tiles, rows,
    sems, sem,
):
    plan_rows(number[0] * SLOTS, index.shape[0], (i0, i1, i2, i3), numbers, place, rounds)
    copy = pltpu.make_async_copy(numbers, chosen, sem)
    copy.start()
    copy.wait()
    fetch_rows(chosen, index, tiles, rows, sems)(keep, send)


def fetch_scratch(slots, width):
    return [
        pltpu.SMEM((2, slots), I32),
        pltpu.VMEM((slots, 16, width), BF16),
        pltpu.VMEM((slots, width), F32),
        pltpu.SemaphoreType.DMA((slots,)),
        pltpu.SemaphoreType.DMA,
    ]


def take_rows(number, ids, index_rows):
    groups, each = ids[0].shape
    slots = groups * SLOTS
    width = index_rows.shape[1]
    half = jax.ShapeDtypeStruct((slots // 2, width), BF16)
    return pl.pallas_call(
        take_kernel,
        out_shape=(
            half,
            half,
            jax.ShapeDtypeStruct((slots, 4 * each), BF16),
            jax.ShapeDtypeStruct((1,), I32),
        ),
        in_specs=[SMEM] + [VMEM] * 4 + [HBM],
        out_specs=(VMEM, VMEM, VMEM, SMEM),
        scratch_shapes=[pltpu.VMEM((2, slots), I32)] + fetch_scratch(slots, width),
        compiler_params=params(8 + slots // 16),
        cost_estimate=NO_COST,
        name="take_rows",
    )(number, *ids, in_hbm(index_rows))


def place_kernel(place, h0, h1, h2, h3, out):
    received = jnp.concatenate([h0[...], h1[...], h2[...], h3[...]])
    chosen = lax.dot_general(
        place[...], received, (((0,), (0,)), ((), ())), preferred_element_type=F32
    )
    out[...] = chosen.astype(BF16)


def place_rows(place, received):
    return pl.pallas_call(
        place_kernel,
        out_shape=jax.ShapeDtypeStruct((place.shape[1], received[0].shape[1]), BF16),
        in_specs=[VMEM] * 5,
        out_specs=VMEM,
        compiler_params=params(8),
        cost_estimate=NO_COST,
        name="place_rows",
    )(place, *received)


def masks(axis):
    mask = 1
    while mask < lax.axis_size(axis):
        yield mask
        mask *= 2


def row_exchange(ids, index_rows, place, rounds):
    width = index_rows.shape[1]

    def gathered(keep, send, place, gates=((), (), ())):
        keep = keep.reshape(1, -1, SLOTS, width)
        send = send.reshape(1, -1, SLOTS, width)
        held = None
        for mask in list(masks("req"))[:1:-1]:
            if held is not None:
                keep, send = held[:, :mask], held[:, mask:]
            other = swap(send, "req", mask)
            if mask == 4:
                other = after(other, *gates[0])
            held = jnp.concatenate([keep, other])
        others = [swap(held[:, mask], "req", mask) for mask in (1, 2, 3)]
        others = list(after(tuple(others), *gates[1]))
        held = [part.reshape(-1, width) for part in [held[:, 0]] + others]
        found = place_rows(place, held)
        found = after(found, *gates[2]).reshape(4, -1, width)
        parts = [swap(found[mask], "tp", mask) for mask in (1, 2, 3)]
        return found[0] + parts[0] + parts[1] + parts[2]

    def one_more(number, total):
        keep, send, place, _ = take_rows(number.reshape(1), ids, index_rows)
        return total + gathered(keep, send, place)

    def further(rows):
        return lax.fori_loop(1, rounds[0], one_more, rows)

    return lambda keep, send, *gates: gathered(keep, send, place, gates), further


def per_device(
    states,
    lengths,
    w_qkv,
    b_qkv,
    w_out,
    b_out,
    ln1_gain,
    ln1_shift,
    w_up,
    b_up,
    w_down,
    b_down,
    ln2_gain,
    ln2_shift,
    index_rows,
    cand_ids,
):
    from_chip = swap(states, "tp", 2)
    from_core = swap(states, "tp", 1)
    w_qkv_t = w_qkv.transpose(1, 0, 2)
    w_qkv_p = swap(w_qkv_t, "tp", 1)
    b_qkv_p = swap(b_qkv, "tp", 1)
    b_up_p = swap(b_up, "tp", 1)

    held = cand_ids.reshape(1, -1)
    for mask in masks("req"):
        other = swap(held, "req", mask)
        if mask * 2 == lax.axis_size("req"):
            mine, w_here, w_half = load(states, w_qkv_t, after(w_out, held))
            other, mine = lax.optimization_barrier((other, mine))
        held = jnp.concatenate([held, other])
    from_chip, held, from_core, w_qkv_p, b_qkv_p, b_up_p = lax.optimization_barrier(
        (from_chip, held, from_core, w_qkv_p, b_qkv_p, b_up_p)
    )
    w_out_p = swap(after(w_out, from_chip), "tp", 1)
    from_diag = swap(from_chip, "tp", 1)
    blocks = (mine, from_core, from_chip, from_diag)
    ids = (held,) + tuple(swap(held, "tp", mask) for mask in (1, 2, 3))
    w_up_p = swap(after(w_up, from_diag, w_out_p, *ids), "tp", 1)
    w_down_p = swap(after(w_down, from_diag, w_out_p, *ids), "tp", 1)
    w_x0 = swap(after(w_half, ids[2]), "tp", 2)

    blocks, ids, w_out_p = lax.optimization_barrier((blocks, ids, w_out_p))
    context_0, text = first_attention(lengths, blocks, w_here, b_qkv)
    context_0x = swap(context_0, "tp", 2)
    w_x1 = swap(after(w_x0, context_0), "req", 1)
    context_1, numbers, place, rounds = second_attention(
        lengths, text, w_qkv_p, b_qkv_p, ids, index_rows.shape[0]
    )
    context_1x = swap(context_1, "tp", 2)
    w_d0 = swap(after(w_x0, context_0), "tp", 1)
    w_d1 = swap(after(w_x1, context_1), "tp", 1)

    base, keep, send = project_first(
        text, context_0, context_0x, w_out, (w_x0, w_x1), b_out[None], numbers,
        index_rows,
    )
    base = project_second(base, context_1, w_out_p)
    gathered, further = row_exchange(ids, index_rows, place, rounds)
    common = (
        context_1x, (w_d0, w_d1), ln1_gain[None], ln1_shift[None],
        (b_up[None], b_up_p[None]), b_down[None], (w_up, w_up_p),
        (w_down, w_down_p),
    )
    down_there = feed_forward(False, base, *common)
    down_x = swap(down_there, "tp", 2)
    down_here = feed_forward(True, after(base, down_there), *common)
    down_x = after(down_x, down_here)
    hidden, hidden_other, pool = finish(
        lengths, down_here, down_x, ln2_gain[None], ln2_shift[None]
    )

    rows = gathered(keep, send, (down_there,), (down_here,), ())
    pools = (pool,) + tuple(swap(pool, "tp", mask) for mask in (1, 2, 3))
    hidden_p = swap(hidden_other, "tp", 1)
    rows = further(after(rows, *pools))
    scores, hidden_out = score(lengths, pools, rows, hidden, hidden_p)
    return (hidden_out, scores)


def solution(mesh):
    placed = (
        P("req", "tp", None),
        P("req"),
        P(None, None, "tp"),
        P(None, "tp"),
        P("tp", None),
        P(),
        P(),
        P(),
        P(None, "tp"),
        P("tp"),
        P("tp", None),
        P(),
        P(),
        P(),
        P(("req", "tp"), None),
        P("req", "tp"),
    )
    return jax.shard_map(
        per_device,
        mesh=mesh,
        in_specs=placed,
        out_specs=(P("req", "tp", None), P("req", "tp")),
        check_vma=False,
    )
```

```python
import functools

import jax
import jax.numpy as jnp
from jax import lax
from jax.experimental import pallas as pl
from jax.experimental.pallas import tpu as pltpu
from jax.sharding import PartitionSpec as P

HEAD_DIM = 64
WINDOW = 512
SLOTS = 16
BF16 = jnp.bfloat16
F32 = jnp.float32
I32 = jnp.int32
MIB = 1024 * 1024
NO_COST = pl.CostEstimate(flops=1, bytes_accessed=1, transcendentals=0)


def cost(gflop):
    return pl.CostEstimate(flops=int(gflop * 10**9) + 1, bytes_accessed=MIB, transcendentals=0)


layer_eps = 1e-05
norm_eps = 1e-06

VMEM = pl.BlockSpec(memory_space=pltpu.VMEM)
SMEM = pl.BlockSpec(memory_space=pltpu.SMEM)
HBM = pl.BlockSpec(memory_space=pltpu.HBM)
ANY = pl.BlockSpec(memory_space=pl.ANY)


def layer_norm(values, gain, shift):
    centre = values - jnp.mean(values, axis=-1, keepdims=True)
    spread = jnp.mean(centre * centre, axis=-1, keepdims=True)
    return centre * lax.rsqrt(spread + layer_eps) * gain + shift


def in_hbm(array):
    return pltpu.with_memory_space_constraint(array, pltpu.HBM)


def swap(value, axis, mask):
    count = lax.axis_size(axis)
    return lax.ppermute(value, axis, [(i, i ^ mask) for i in range(count)])


def matmul(left, right):
    return jnp.dot(left, right, preferred_element_type=F32)


def params(mib):
    return pltpu.CompilerParams(vmem_limit_bytes=mib * MIB)


def after(value, *others):
    return lax.optimization_barrier((value,) + others)[0]


def load_kernel(states, w, w_out, mine, w_here, half, sems):
    part = half.shape[0]
    first = pl.multiple_of((lax.axis_index("req") & 1) * part, part)
    copies = [
        pltpu.make_async_copy(source, target, sems.at[number])
        for number, (source, target) in enumerate(
            (
                (w_out.at[pl.ds(first, part)], half),
                (states.at[lax.axis_index("tp") & 1], mine),
                (w, w_here),
            )
        )
    ]
    for copy in copies:
        copy.start()
    for copy in copies:
        copy.wait()


def load(states, w, w_out):
    return pl.pallas_call(
        load_kernel,
        out_shape=(
            jax.ShapeDtypeStruct(states.shape[1:], BF16),
            jax.ShapeDtypeStruct(w.shape, BF16),
            jax.ShapeDtypeStruct((w_out.shape[0] // 2, w_out.shape[1]), BF16),
        ),
        in_specs=[HBM] * 3,
        out_specs=(VMEM, VMEM, VMEM),
        scratch_shapes=[pltpu.SemaphoreType.DMA((3,))],
        compiler_params=params(6),
        cost_estimate=NO_COST,
        name="load",
    )(in_hbm(states), in_hbm(w), in_hbm(w_out))


def first_attention_kernel(lengths, mine, s1, s2, s3, w, b, out, text, parts, bias):
    core = lax.axis_index("tp") & 1
    text[...] = jnp.concatenate([mine[...], s1[core], s2[core], s3[core]])
    for which in range(3):
        project(which, text, w, b, parts)
    attend(lengths, parts, bias, out)


def second_attention_kernel(
    rows_here, lengths, text, w, b, i0, i1, out, numbers, place, rounds, parts, bias
):
    plan_rows(0, rows_here, (i0, i1), numbers, place, rounds)
    for which in range(3):
        project(which, text, w, b, parts)
    attend(lengths, parts, bias, out)


def project(which, text, w, b, parts):
    parts[which] = (matmul(text[...], w[which]) + b[which : which + 1, :]).astype(BF16)


def attend(lengths, parts, bias, out):
    rank = lax.axis_index("tp")
    length = lengths[rank & 1]
    _, seq_len, wide = parts.shape
    share = seq_len // 4

    def position(index):
        return ((index // share) ^ rank) * share + index % share

    row_pos = position(lax.broadcasted_iota(I32, (seq_len, 1), 0))
    col_pos = position(lax.broadcasted_iota(I32, (1, seq_len), 1))
    keep = (jnp.abs(row_pos - col_pos) <= WINDOW // 2) & (col_pos < length)
    bias[...] = jnp.where(keep, F32(0.0), F32(-1e30))
    ones = jnp.ones((seq_len, 128), BF16)
    low = lax.broadcasted_iota(I32, (1, 128), 1) < HEAD_DIM
    scale = jnp.asarray(HEAD_DIM**-0.5, BF16)
    for pair in range(wide // 128):
        lanes = slice(pair * 128, (pair + 1) * 128)
        k_pair = parts[1, :, lanes]
        v_ones = jnp.concatenate([parts[2, :, lanes], ones], axis=1)
        for block in range(4):
            rows = slice(block * share, (block + 1) * share)
            q_pair = parts[0, rows, lanes] * scale
            found = []
            for head in range(2):
                chosen = low if head == 0 else jnp.logical_not(low)
                q_head = jnp.where(chosen, q_pair, jnp.zeros((), BF16))
                logits = lax.dot_general(
                    q_head, k_pair, (((1,), (1,)), ((), ())), preferred_element_type=F32
                )
                logits = logits + bias[rows, :]
                top = jnp.max(logits, axis=-1, keepdims=True)
                expo = jnp.exp(logits - top).astype(BF16)
                summed = matmul(expo, v_ones)
                found.append(summed[:, :128] / summed[:, 128:])
            context = jnp.where(low, found[0], found[1])
            context = jnp.where(row_pos[rows] < length, context, F32(0.0))
            out[rows, lanes] = context.astype(BF16)


def attention_scratch(seq_len, wide):
    return [pltpu.VMEM((3, seq_len, wide), BF16), pltpu.VMEM((seq_len, seq_len), F32)]


def first_attention(lengths, blocks, w, b):
    share, width = blocks[0].shape
    wide = w.shape[2]
    return pl.pallas_call(
        first_attention_kernel,
        out_shape=(
            jax.ShapeDtypeStruct((4 * share, wide), BF16),
            jax.ShapeDtypeStruct((4 * share, width), BF16),
        ),
        in_specs=[SMEM] + [VMEM] * 6,
        out_specs=(VMEM, VMEM),
        scratch_shapes=attention_scratch(4 * share, wide),
        compiler_params=params(12),
        cost_estimate=NO_COST,
        name="attention_own",
    )(in_hbm(lengths), *blocks, w, in_hbm(b))


def second_attention(lengths, text, w, b, ids, rows_here):
    seq_len = text.shape[0]
    wide = w.shape[2]
    groups, each = ids[0].shape
    return pl.pallas_call(
        functools.partial(second_attention_kernel, rows_here),
        out_shape=(
            jax.ShapeDtypeStruct((seq_len, wide), BF16),
            jax.ShapeDtypeStruct((2, groups * SLOTS), I32),
            jax.ShapeDtypeStruct((groups * SLOTS, 2 * each), BF16),
            jax.ShapeDtypeStruct((1,), I32),
        ),
        in_specs=[SMEM] + [VMEM] * 5,
        out_specs=(VMEM, VMEM, VMEM, SMEM),
        scratch_shapes=attention_scratch(seq_len, wide),
        compiler_params=params(12),
        cost_estimate=cost(6),
        name="attention_partner",
    )(in_hbm(lengths), text, w, b, *ids)


def joined(first, second):
    swapped = (lax.axis_index("req") & 1) != 0
    low = jnp.where(swapped, second[...], first[...])
    high = jnp.where(swapped, first[...], second[...])
    return jnp.concatenate([low, high])


def project_first_kernel(
    text, here, there, w, half_0, half_1, b, numbers, index, out, keep, send,
    chosen, tiles, rows, sems, sem,
):
    copy = pltpu.make_async_copy(numbers, chosen, sem)
    copy.start()
    half = text.shape[0] // 2
    w_there = joined(half_0, half_1)
    copy.wait()
    finish_rows = fetch_rows(chosen, index, tiles, rows, sems)
    for number in range(2):
        span = slice(number * half, (number + 1) * half)
        other = slice((1 - number) * half, (2 - number) * half)
        total = matmul(here[span, :], w[...]) + matmul(there[other, :], w_there)
        out[span, :] = total + (text[span, :].astype(F32) + b[...])
    finish_rows(keep, send)


def project_first(text, here, there, w, halves, b_out, numbers, index_rows):
    seq_len, width = text.shape
    slots = numbers.shape[1]
    half = jax.ShapeDtypeStruct((slots // 2, width), BF16)
    return pl.pallas_call(
        project_first_kernel,
        out_shape=(jax.ShapeDtypeStruct((seq_len, width), F32), half, half),
        in_specs=[VMEM] * 8 + [HBM],
        out_specs=(VMEM, VMEM, VMEM),
        scratch_shapes=fetch_scratch(slots, width),
        compiler_params=params(12 + slots // 16),
        cost_estimate=cost(1),
        name="project_first",
    )(text, here, there, w, *halves, b_out, numbers, in_hbm(index_rows))


def project_second_kernel(base, context, w, out):
    out[...] = base[...] + matmul(context[...], w[...])


def project_second(base, context, w):
    return pl.pallas_call(
        project_second_kernel,
        out_shape=jax.ShapeDtypeStruct(base.shape, F32),
        in_specs=[VMEM] * 3,
        out_specs=VMEM,
        input_output_aliases={0: 0},
        compiler_params=params(12),
        cost_estimate=cost(1),
        name="project_second",
    )(base, context, w)


def feed_kernel(
    keep_rest, base, c3, half_0, half_1, gain, shift, b0, b1, b_down,
    up_own, up_partner, down_own, down_partner, out, up_buf, down_buf, act, sems,
):
    hidden = up_own.shape[1]
    up_copy = pltpu.make_async_copy(up_own, up_buf, sems.at[0])
    down_copy = pltpu.make_async_copy(down_own, down_buf, sems.at[1])
    up_copy.start()
    down_copy.start()
    total = base[...] + matmul(c3[...], joined(half_0, half_1))
    normed = layer_norm(total, gain[...], shift[...]).astype(BF16)
    step = 512
    for part, (weight, bias) in enumerate(((up_partner, b1), (up_buf, b0))):
        if part == 1:
            up_copy.wait()
        for low in range(0, hidden, step):
            lanes = slice(low, low + step)
            up = matmul(normed, weight[:, lanes]) + bias[:, lanes]
            activated = 0.5 * up * (1.0 + lax.erf(up * F32(0.5**0.5)))
            act[:, part * hidden + low : part * hidden + low + step] = activated.astype(BF16)
    down = matmul(act[:, :hidden], down_partner[...])
    down_copy.wait()
    down = down + matmul(act[:, hidden:], down_buf[...])
    if keep_rest:
        down = down + (normed.astype(F32) + b_down[...])
    out[...] = down.astype(out.dtype)


def feed_forward(keep_rest, base, context, halves, gain, shift, biases, b_down, ups, downs):
    seq_len, width = base.shape
    half = seq_len // 2
    here = 0 if keep_rest else 1
    hidden = ups[0].shape[1]
    heads_wide = context.shape[1]
    base_spec = pl.BlockSpec((half, width), lambda i: (here, 0))
    context_spec = pl.BlockSpec((half, heads_wide), lambda i: (1 - here, 0))
    return pl.pallas_call(
        lambda *refs: feed_kernel(keep_rest, *refs),
        out_shape=jax.ShapeDtypeStruct((half, width), F32 if keep_rest else BF16),
        grid=(1,),
        in_specs=[base_spec, context_spec] + [VMEM] * 7
        + [HBM, VMEM, HBM, VMEM],
        out_specs=VMEM,
        scratch_shapes=[
            pltpu.VMEM((width, hidden), BF16),
            pltpu.VMEM((hidden, width), BF16),
            pltpu.VMEM((half, 2 * hidden), BF16),
            pltpu.SemaphoreType.DMA((2,)),
        ],
        compiler_params=params(20),
        cost_estimate=cost(8),
        name="feed_here" if keep_rest else "feed_there",
    )(base, context, *halves, gain, shift, *biases, b_down, in_hbm(ups[0]), ups[1],
      in_hbm(downs[0]), downs[1])


def finish_kernel(lengths, here, there, gain, shift, own, other, pool):
    rank = lax.axis_index("tp")
    length = lengths[rank & 1]
    share = own.shape[0]
    total = here[...] + there[...].astype(F32)
    hidden = layer_norm(total, gain[...], shift[...]).astype(BF16)
    own[...] = hidden[:share]
    other[...] = hidden[share:]
    index = lax.broadcasted_iota(I32, (2 * share, 1), 0)
    pos = ((index // share) ^ rank) * share + index % share
    valid = jnp.where(pos < length, hidden.astype(F32), F32(0.0))
    pool[...] = jnp.sum(valid, axis=0, keepdims=True)


def finish(lengths, here, there, gain, shift):
    half, width = here.shape
    block = jax.ShapeDtypeStruct((half // 2, width), BF16)
    return pl.pallas_call(
        finish_kernel,
        out_shape=(block, block, jax.ShapeDtypeStruct((1, width), F32)),
        in_specs=[SMEM] + [VMEM] * 4,
        out_specs=(VMEM, VMEM, VMEM),
        compiler_params=params(8),
        cost_estimate=cost(2),
        name="finish",
    )(lengths, here, there, gain, shift)


def score_kernel(
    lengths, pool, pool_core, pool_chip, pool_diag, rows, own, other, out, hidden_out
):
    core = lax.axis_index("tp") & 1
    width = pool.shape[1]
    mine = pool[...] + pool_chip[...]
    theirs = pool_core[...] + pool_diag[...]
    first = jnp.where(core == 0, mine, theirs) / lengths[0].astype(F32)
    second = jnp.where(core == 0, theirs, mine) / lengths[1].astype(F32)
    row = lax.broadcasted_iota(I32, (8, width), 0)
    pooled = jnp.where(row == 0, first, jnp.where(row == 1, second, F32(0.0)))
    scale = lax.rsqrt(jnp.mean(pooled * pooled, axis=-1, keepdims=True) + norm_eps)
    queries = (pooled * scale).astype(BF16)
    found = lax.dot_general(
        queries, rows[...], (((1,), (1,)), ((), ())), preferred_element_type=F32
    )
    each = rows.shape[0] // 2
    out[0:1, :] = found[0:1, :each]
    out[1:2, :] = found[1:2, each:]
    hidden_out[core] = own[...]
    hidden_out[1 - core] = other[...]


def score(lengths, pools, rows, own, other):
    return pl.pallas_call(
        score_kernel,
        out_shape=(
            jax.ShapeDtypeStruct((2, rows.shape[0] // 2), F32),
            jax.ShapeDtypeStruct((2,) + own.shape, BF16),
        ),
        in_specs=[SMEM] + [VMEM] * 7,
        out_specs=(VMEM, VMEM),
        compiler_params=params(8),
        cost_estimate=cost(1),
        name="score",
    )(lengths, *pools, rows, own, other)


def source_order(groups):
    order = [0]
    mask = groups // 2
    while mask >= 4:
        order = order + [entry + mask for entry in order]
        mask //= 2
    return [entry + last for last in range(4) for entry in order]


def as_ones(mask):
    return mask.astype(F32).astype(BF16)


def plan_rows(first_place, rows_here, parts, numbers, place, rounds):
    rank = lax.axis_index("tp")
    group = lax.axis_index("req")
    groups = parts[0].shape[0]
    slots = groups * SLOTS
    ids = jnp.concatenate([part[...] for part in parts], axis=1)
    count = ids.shape[1]
    owner = lax.shift_right_logical(ids, I32(rows_here.bit_length() - 1))
    before = as_ones(
        lax.broadcasted_iota(I32, (count, count), 0)
        < lax.broadcasted_iota(I32, (count, count), 1)
    )
    ones = jnp.ones((count, 128), BF16)
    slot = lax.broadcasted_iota(I32, (SLOTS, 1), 0) + first_place

    mine = owner == group * 4 + rank
    asked = jnp.concatenate(
        [
            (owner[:1] == (group ^ source) * 4 + rank).astype(F32)
            for source in source_order(groups)
        ]
    )
    both = jnp.concatenate([mine.astype(F32), asked]).astype(BF16)
    ranks = matmul(both, before).astype(I32)
    send_rank = jnp.where(mine, ranks[:groups], -1)
    take_rank = jnp.where(asked > 0, ranks[groups:], -1)

    local = jnp.where(mine, ids - (group * 4 + rank) * rows_here, 0)
    high = (local >> 6).astype(F32).astype(BF16)
    low = (local & 63).astype(F32).astype(BF16)
    chosen = jnp.concatenate(
        [(send_rank[k : k + 1] == slot).astype(F32) for k in range(groups)]
    ).astype(BF16)
    spread = (((1,), (1,)), ((), ()))
    wanted = 64.0 * lax.dot_general(high, chosen, spread, preferred_element_type=F32)
    wanted = wanted + lax.dot_general(low, chosen, spread, preferred_element_type=F32)
    counts = matmul(as_ones(mine), jnp.ones((count, slots), BF16))
    own = lax.broadcasted_iota(I32, (groups, slots), 0) == lax.div(
        lax.broadcasted_iota(I32, (groups, slots), 1), I32(SLOTS)
    )
    numbers[0:1, :] = jnp.sum(jnp.where(own, wanted, 0.0), axis=0, keepdims=True).astype(I32)
    counts = jnp.sum(jnp.where(own, counts, 0.0), axis=0, keepdims=True).astype(I32)
    numbers[1:2, :] = counts - first_place

    for k in range(groups):
        place[k * SLOTS : (k + 1) * SLOTS, :] = as_ones(take_rank[k : k + 1] == slot)
    shard = lax.broadcasted_iota(I32, (4 * groups, 1), 0)
    load = jnp.concatenate(
        [(owner[k : k + 1] == shard).astype(F32) for k in range(groups)]
    ).astype(BF16)
    most = jnp.max(matmul(load, ones)).astype(I32)
    rounds[0] = (most + SLOTS - 1) // SLOTS - 1


def fetch_rows(chosen, index, tiles, rows, sems):
    deep = tiles.shape[1]
    slots = tiles.shape[0]
    step = 4

    def tile_copy(slot):
        first = pl.multiple_of((chosen[0, slot] // deep) * deep, deep)
        return pltpu.make_async_copy(index.at[pl.ds(first, deep)], tiles.at[slot], sems.at[slot])

    def start(number, carry):
        for each in range(step):
            tile_copy(number * step + each).start()
        return carry

    def select(number, carry):
        for each in range(step):
            tile_copy(number * step + each).wait()
        for each in range(step):
            source = number * step + each
            line = lax.broadcasted_iota(I32, (deep, 1), 0) == chosen[0, source] % deep
            row = jnp.where(line, tiles[source].astype(F32), F32(0.0))
            rows[pl.ds(source, 1), :] = jnp.sum(row, axis=0, keepdims=True)
        return carry

    def each_group(action):
        def one(number, carry):
            first = number * (SLOTS // step)
            left = jnp.clip(chosen[1, number * SLOTS], 0, SLOTS)
            return lax.fori_loop(first, first + (left + step - 1) // step, action, carry)

        lax.fori_loop(0, slots // SLOTS, one, 0)

    rows[...] = jnp.zeros_like(rows)
    each_group(start)

    def finish_rows(keep, send):
        each_group(select)
        keep[...] = rows[: slots // 2, :].astype(BF16)
        send[...] = rows[slots // 2 :, :].astype(BF16)

    return finish_rows


def take_kernel(
    number, i0, i1, index, keep, send, place, rounds, numbers, chosen, tiles, rows,
    sems, sem,
):
    plan_rows(number[0] * SLOTS, index.shape[0], (i0, i1), numbers, place, rounds)
    copy = pltpu.make_async_copy(numbers, chosen, sem)
    copy.start()
    copy.wait()
    fetch_rows(chosen, index, tiles, rows, sems)(keep, send)


def fetch_scratch(slots, width):
    return [
        pltpu.SMEM((2, slots), I32),
        pltpu.VMEM((slots, 16, width), BF16),
        pltpu.VMEM((slots, width), F32),
        pltpu.SemaphoreType.DMA((slots,)),
        pltpu.SemaphoreType.DMA,
    ]


def take_rows(number, ids, index_rows):
    groups, each = ids[0].shape
    slots = groups * SLOTS
    width = index_rows.shape[1]
    half = jax.ShapeDtypeStruct((slots // 2, width), BF16)
    return pl.pallas_call(
        take_kernel,
        out_shape=(
            half,
            half,
            jax.ShapeDtypeStruct((slots, 2 * each), BF16),
            jax.ShapeDtypeStruct((1,), I32),
        ),
        in_specs=[SMEM] + [VMEM] * 2 + [HBM],
        out_specs=(VMEM, VMEM, VMEM, SMEM),
        scratch_shapes=[pltpu.VMEM((2, slots), I32)] + fetch_scratch(slots, width),
        compiler_params=params(8 + slots // 16),
        cost_estimate=NO_COST,
        name="take_rows",
    )(number, *ids, in_hbm(index_rows))


def place_kernel(place, h0, h1, h2, h3, out):
    received = jnp.concatenate([h0[...], h1[...], h2[...], h3[...]])
    chosen = lax.dot_general(
        place[...], received, (((0,), (0,)), ((), ())), preferred_element_type=F32
    )
    out[...] = chosen.astype(BF16)


def place_rows(place, received):
    return pl.pallas_call(
        place_kernel,
        out_shape=jax.ShapeDtypeStruct((place.shape[1], received[0].shape[1]), BF16),
        in_specs=[VMEM] * 5,
        out_specs=VMEM,
        compiler_params=params(8),
        cost_estimate=NO_COST,
        name="place_rows",
    )(place, *received)


def masks(axis):
    mask = 1
    while mask < lax.axis_size(axis):
        yield mask
        mask *= 2


def row_exchange(ids, index_rows, place, rounds):
    width = index_rows.shape[1]

    def gathered(keep, send, place, gates=((), (), ())):
        keep = keep.reshape(1, -1, SLOTS, width)
        send = send.reshape(1, -1, SLOTS, width)
        held = None
        for mask in list(masks("req"))[:1:-1]:
            if held is not None:
                keep, send = held[:, :mask], held[:, mask:]
            other = swap(send, "req", mask)
            if mask == 4:
                other = after(other, *gates[0])
            held = jnp.concatenate([keep, other])
        others = [swap(held[:, mask], "req", mask) for mask in (1, 2, 3)]
        others = list(after(tuple(others), *gates[1]))
        held = [part.reshape(-1, width) for part in [held[:, 0]] + others]
        found = place_rows(place, held)
        found = after(found, *gates[2]).reshape(4, -1, width)
        parts = [swap(found[place], "tp", mask) for place, mask in ((1, 2), (2, 1), (3, 3))]
        return found[0] + parts[0] + parts[1] + parts[2]

    def one_more(state):
        number, total = state
        keep, send, place, _ = take_rows(number.reshape(1), ids, index_rows)
        return number - 1, total + gathered(keep, send, place)

    def further(rows, *gate):
        left = after(rounds, *gate)[0]
        return lax.while_loop(lambda state: state[0] > 0, one_more, (left, rows))[1]

    return lambda keep, send, *gates: gathered(keep, send, place, gates), further


def per_device(
    states,
    lengths,
    w_qkv,
    b_qkv,
    w_out,
    b_out,
    ln1_gain,
    ln1_shift,
    w_up,
    b_up,
    w_down,
    b_down,
    ln2_gain,
    ln2_shift,
    index_rows,
    cand_ids,
):
    from_core = swap(states, "tp", 1)
    w_qkv_t = w_qkv.transpose(1, 0, 2)
    w_qkv_p = swap(w_qkv_t, "tp", 1)
    b_qkv_p = swap(b_qkv, "tp", 1)
    b_up_p = swap(b_up, "tp", 1)

    held = cand_ids.reshape(1, -1)
    held = jnp.concatenate([held, swap(held, "tp", 2)], axis=1)
    from_chip = swap(after(states, held), "tp", 2)
    for mask in masks("req"):
        other = swap(held, "req", mask)
        if mask * 2 == lax.axis_size("req"):
            mine, w_here, w_half = load(states, w_qkv_t, after(w_out, held))
            other, mine = lax.optimization_barrier((other, mine))
        held = jnp.concatenate([held, other])
    from_chip, held, from_core, w_qkv_p, b_qkv_p, b_up_p = lax.optimization_barrier(
        (from_chip, held, from_core, w_qkv_p, b_qkv_p, b_up_p)
    )
    w_out_p = swap(after(w_out, from_chip), "tp", 1)
    from_diag = swap(from_chip, "tp", 1)
    blocks = (mine, from_core, from_chip, from_diag)
    ids = (held, swap(held, "tp", 1))
    w_up_p = swap(after(w_up, from_diag, w_out_p, *ids), "tp", 1)
    w_down_p = swap(after(w_down, from_diag, w_out_p, *ids), "tp", 1)
    w_x0 = swap(w_half, "tp", 2)

    blocks, ids, w_out_p = lax.optimization_barrier((blocks, ids, w_out_p))
    context_0, text = first_attention(lengths, blocks, w_here, b_qkv)
    context_0x = swap(context_0, "tp", 2)
    w_x1 = swap(after(w_x0, context_0), "req", 1)
    context_1, numbers, place, rounds = second_attention(
        lengths, after(text, w_up_p), w_qkv_p, b_qkv_p, ids, index_rows.shape[0]
    )
    context_1x = swap(context_1, "tp", 2)
    w_d0 = swap(after(w_x0, context_0), "tp", 1)

    base, keep, send = project_first(
        text, context_0, context_0x, w_out, (w_x0, w_x1), b_out[None], numbers,
        index_rows,
    )
    w_d1 = swap(after(w_x1, base), "tp", 1)
    base = project_second(base, context_1, w_out_p)
    gathered, further = row_exchange(ids, index_rows, place, rounds)
    common = (
        context_1x, (w_d0, w_d1), ln1_gain[None], ln1_shift[None],
        (b_up[None], b_up_p[None]), b_down[None], (w_up, w_up_p),
        (w_down, w_down_p),
    )
    down_there = feed_forward(False, base, *common)
    down_x = swap(down_there, "tp", 2)
    down_here = feed_forward(True, after(base, down_there), *common)
    down_x = after(down_x, down_here)
    hidden, hidden_other, pool = finish(
        lengths, down_here, down_x, ln2_gain[None], ln2_shift[None]
    )

    rows = gathered(keep, send, (down_there,), (down_here,), ())
    pools = (pool,) + tuple(swap(pool, "tp", mask) for mask in (1, 2, 3))
    hidden_p = swap(hidden_other, "tp", 1)
    rows = further(after(rows, *pools), *pools)
    scores, hidden_out = score(lengths, pools, rows, hidden, hidden_p)
    return (hidden_out, scores)


def solution(mesh):
    placed = (
        P("req", "tp", None),
        P("req"),
        P(None, None, "tp"),
        P(None, "tp"),
        P("tp", None),
        P(),
        P(),
        P(),
        P(None, "tp"),
        P("tp"),
        P("tp", None),
        P(),
        P(),
        P(),
        P(("req", "tp"), None),
        P("req", "tp"),
    )
    return jax.shard_map(
        per_device,
        mesh=mesh,
        in_specs=placed,
        out_specs=(P("req", "tp", None), P("req", "tp")),
        check_vma=False,
    )
```

```python
import functools

import jax
import jax.numpy as jnp
from jax import lax
from jax.experimental import pallas as pl
from jax.experimental.pallas import tpu as pltpu
from jax.sharding import PartitionSpec as P

HEAD_DIM = 64
WINDOW = 512
SLOTS = 16
BF16 = jnp.bfloat16
F32 = jnp.float32
I32 = jnp.int32
MIB = 1024 * 1024
NO_COST = pl.CostEstimate(flops=1, bytes_accessed=1, transcendentals=0)


def cost(gflop):
    return pl.CostEstimate(flops=int(gflop * 10**9) + 1, bytes_accessed=MIB, transcendentals=0)


layer_eps = 1e-05
norm_eps = 1e-06

VMEM = pl.BlockSpec(memory_space=pltpu.VMEM)
SMEM = pl.BlockSpec(memory_space=pltpu.SMEM)
HBM = pl.BlockSpec(memory_space=pltpu.HBM)
ANY = pl.BlockSpec(memory_space=pl.ANY)


def layer_norm(values, gain, shift):
    centre = values - jnp.mean(values, axis=-1, keepdims=True)
    spread = jnp.mean(centre * centre, axis=-1, keepdims=True)
    return centre * lax.rsqrt(spread + layer_eps) * gain + shift


def in_hbm(array):
    return pltpu.with_memory_space_constraint(array, pltpu.HBM)


def swap(value, axis, mask):
    count = lax.axis_size(axis)
    return lax.ppermute(value, axis, [(i, i ^ mask) for i in range(count)])


def matmul(left, right):
    return jnp.dot(left, right, preferred_element_type=F32)


def params(mib):
    return pltpu.CompilerParams(vmem_limit_bytes=mib * MIB)


def after(value, *others):
    return lax.optimization_barrier((value,) + others)[0]


def load_kernel(states, w, w_out, mine, w_here, half, sems):
    part = half.shape[0]
    first = pl.multiple_of((lax.axis_index("req") & 1) * part, part)
    copies = [
        pltpu.make_async_copy(source, target, sems.at[number])
        for number, (source, target) in enumerate(
            (
                (w_out.at[pl.ds(first, part)], half),
                (states.at[lax.axis_index("tp") & 1], mine),
                (w, w_here),
            )
        )
    ]
    for copy in copies:
        copy.start()
    for copy in copies:
        copy.wait()


def load(states, w, w_out):
    return pl.pallas_call(
        load_kernel,
        out_shape=(
            jax.ShapeDtypeStruct(states.shape[1:], BF16),
            jax.ShapeDtypeStruct(w.shape, BF16),
            jax.ShapeDtypeStruct((w_out.shape[0] // 2, w_out.shape[1]), BF16),
        ),
        in_specs=[HBM] * 3,
        out_specs=(VMEM, VMEM, VMEM),
        scratch_shapes=[pltpu.SemaphoreType.DMA((3,))],
        compiler_params=params(6),
        cost_estimate=NO_COST,
        name="load",
    )(in_hbm(states), in_hbm(w), in_hbm(w_out))


def first_attention_kernel(lengths, mine, s1, s2, s3, w, b, out, text, parts, bias):
    core = lax.axis_index("tp") & 1
    text[...] = jnp.concatenate([mine[...], s1[core], s2[core], s3[core]])
    for which in range(3):
        project(which, text, w, b, parts)
    attend(lengths, parts, bias, out)


def second_attention_kernel(
    rows_here, lengths, text, w, b, i0, i1, out, numbers, place, rounds, parts, bias
):
    plan_rows(0, rows_here, (i0, i1), numbers, place, rounds)
    for which in range(3):
        project(which, text, w, b, parts)
    attend(lengths, parts, bias, out)


def project(which, text, w, b, parts):
    parts[which] = (matmul(text[...], w[which]) + b[which : which + 1, :]).astype(BF16)


def attend(lengths, parts, bias, out):
    rank = lax.axis_index("tp")
    length = lengths[rank & 1]
    _, seq_len, wide = parts.shape
    share = seq_len // 4

    def position(index):
        return ((index // share) ^ rank) * share + index % share

    row_pos = position(lax.broadcasted_iota(I32, (seq_len, 1), 0))
    col_pos = position(lax.broadcasted_iota(I32, (1, seq_len), 1))
    keep = (jnp.abs(row_pos - col_pos) <= WINDOW // 2) & (col_pos < length)
    bias[...] = jnp.where(keep, F32(0.0), F32(-1e30))
    ones = jnp.ones((seq_len, 128), BF16)
    low = lax.broadcasted_iota(I32, (1, 128), 1) < HEAD_DIM
    scale = jnp.asarray(HEAD_DIM**-0.5, BF16)
    for pair in range(wide // 128):
        lanes = slice(pair * 128, (pair + 1) * 128)
        k_pair = parts[1, :, lanes]
        v_ones = jnp.concatenate([parts[2, :, lanes], ones], axis=1)
        for block in range(4):
            rows = slice(block * share, (block + 1) * share)
            q_pair = parts[0, rows, lanes] * scale
            found = []
            for head in range(2):
                chosen = low if head == 0 else jnp.logical_not(low)
                q_head = jnp.where(chosen, q_pair, jnp.zeros((), BF16))
                logits = lax.dot_general(
                    q_head, k_pair, (((1,), (1,)), ((), ())), preferred_element_type=F32
                )
                logits = logits + bias[rows, :]
                top = jnp.max(logits, axis=-1, keepdims=True)
                expo = jnp.exp(logits - top).astype(BF16)
                summed = matmul(expo, v_ones)
                found.append(summed[:, :128] / summed[:, 128:])
            context = jnp.where(low, found[0], found[1])
            context = jnp.where(row_pos[rows] < length, context, F32(0.0))
            out[rows, lanes] = context.astype(BF16)


def attention_scratch(seq_len, wide):
    return [pltpu.VMEM((3, seq_len, wide), BF16), pltpu.VMEM((seq_len, seq_len), F32)]


def first_attention(lengths, blocks, w, b):
    share, width = blocks[0].shape
    wide = w.shape[2]
    return pl.pallas_call(
        first_attention_kernel,
        out_shape=(
            jax.ShapeDtypeStruct((4 * share, wide), BF16),
            jax.ShapeDtypeStruct((4 * share, width), BF16),
        ),
        in_specs=[SMEM] + [VMEM] * 6,
        out_specs=(VMEM, VMEM),
        scratch_shapes=attention_scratch(4 * share, wide),
        compiler_params=params(12),
        cost_estimate=NO_COST,
        name="attention_own",
    )(in_hbm(lengths), *blocks, w, in_hbm(b))


def second_attention(lengths, text, w, b, ids, rows_here):
    seq_len = text.shape[0]
    wide = w.shape[2]
    groups, each = ids[0].shape
    return pl.pallas_call(
        functools.partial(second_attention_kernel, rows_here),
        out_shape=(
            jax.ShapeDtypeStruct((seq_len, wide), BF16),
            jax.ShapeDtypeStruct((2, groups * SLOTS), I32),
            jax.ShapeDtypeStruct((groups * SLOTS, 2 * each), BF16),
            jax.ShapeDtypeStruct((1,), I32),
        ),
        in_specs=[SMEM] + [VMEM] * 5,
        out_specs=(VMEM, VMEM, VMEM, SMEM),
        scratch_shapes=attention_scratch(seq_len, wide),
        compiler_params=params(12),
        cost_estimate=cost(6),
        name="attention_partner",
    )(in_hbm(lengths), text, w, b, *ids)


def joined(first, second):
    swapped = (lax.axis_index("req") & 1) != 0
    low = jnp.where(swapped, second[...], first[...])
    high = jnp.where(swapped, first[...], second[...])
    return jnp.concatenate([low, high])


def project_first_kernel(
    text, here, there, w, half_0, half_1, b, numbers, index, out, keep, send,
    chosen, tiles, rows, sems, sem,
):
    copy = pltpu.make_async_copy(numbers, chosen, sem)
    copy.start()
    half = text.shape[0] // 2
    w_there = joined(half_0, half_1)
    copy.wait()
    finish_rows = fetch_rows(chosen, index, tiles, rows, sems)
    for number in range(2):
        span = slice(number * half, (number + 1) * half)
        other = slice((1 - number) * half, (2 - number) * half)
        total = matmul(here[span, :], w[...]) + matmul(there[other, :], w_there)
        out[span, :] = total + (text[span, :].astype(F32) + b[...])
    finish_rows(keep, send)


def project_first(text, here, there, w, halves, b_out, numbers, index_rows):
    seq_len, width = text.shape
    slots = numbers.shape[1]
    half = jax.ShapeDtypeStruct((slots // 2, width), BF16)
    return pl.pallas_call(
        project_first_kernel,
        out_shape=(jax.ShapeDtypeStruct((seq_len, width), F32), half, half),
        in_specs=[VMEM] * 8 + [HBM],
        out_specs=(VMEM, VMEM, VMEM),
        scratch_shapes=fetch_scratch(slots, width),
        compiler_params=params(12 + slots // 16),
        cost_estimate=cost(1),
        name="project_first",
    )(text, here, there, w, *halves, b_out, numbers, in_hbm(index_rows))


def project_second_kernel(base, context, w, out):
    out[...] = base[...] + matmul(context[...], w[...])


def project_second(base, context, w):
    return pl.pallas_call(
        project_second_kernel,
        out_shape=jax.ShapeDtypeStruct(base.shape, F32),
        in_specs=[VMEM] * 3,
        out_specs=VMEM,
        input_output_aliases={0: 0},
        compiler_params=params(12),
        cost_estimate=cost(1),
        name="project_second",
    )(base, context, w)


def feed_kernel(
    keep_rest, base, c3, half_0, half_1, gain, shift, b0, b1, b_down,
    up_own, up_partner, down_own, down_partner, out, up_buf, down_buf, act, sems,
):
    hidden = up_own.shape[1]
    up_copy = pltpu.make_async_copy(up_own, up_buf, sems.at[0])
    down_copy = pltpu.make_async_copy(down_own, down_buf, sems.at[1])
    up_copy.start()
    down_copy.start()
    total = base[...] + matmul(c3[...], joined(half_0, half_1))
    normed = layer_norm(total, gain[...], shift[...]).astype(BF16)
    step = 512
    for part, (weight, bias) in enumerate(((up_partner, b1), (up_buf, b0))):
        if part == 1:
            up_copy.wait()
        for low in range(0, hidden, step):
            lanes = slice(low, low + step)
            up = matmul(normed, weight[:, lanes]) + bias[:, lanes]
            activated = 0.5 * up * (1.0 + lax.erf(up * F32(0.5**0.5)))
            act[:, part * hidden + low : part * hidden + low + step] = activated.astype(BF16)
    down = matmul(act[:, :hidden], down_partner[...])
    down_copy.wait()
    down = down + matmul(act[:, hidden:], down_buf[...])
    if keep_rest:
        down = down + (normed.astype(F32) + b_down[...])
    out[...] = down.astype(out.dtype)


def feed_forward(keep_rest, base, context, halves, gain, shift, biases, b_down, ups, downs):
    seq_len, width = base.shape
    half = seq_len // 2
    here = 0 if keep_rest else 1
    hidden = ups[0].shape[1]
    heads_wide = context.shape[1]
    base_spec = pl.BlockSpec((half, width), lambda i: (here, 0))
    context_spec = pl.BlockSpec((half, heads_wide), lambda i: (1 - here, 0))
    return pl.pallas_call(
        lambda *refs: feed_kernel(keep_rest, *refs),
        out_shape=jax.ShapeDtypeStruct((half, width), F32 if keep_rest else BF16),
        grid=(1,),
        in_specs=[base_spec, context_spec] + [VMEM] * 7
        + [HBM, VMEM, HBM, VMEM],
        out_specs=VMEM,
        scratch_shapes=[
            pltpu.VMEM((width, hidden), BF16),
            pltpu.VMEM((hidden, width), BF16),
            pltpu.VMEM((half, 2 * hidden), BF16),
            pltpu.SemaphoreType.DMA((2,)),
        ],
        compiler_params=params(20),
        cost_estimate=cost(8),
        name="feed_here" if keep_rest else "feed_there",
    )(base, context, *halves, gain, shift, *biases, b_down, in_hbm(ups[0]), ups[1],
      in_hbm(downs[0]), downs[1])


def finish_kernel(lengths, here, there, gain, shift, own, other, pool):
    rank = lax.axis_index("tp")
    length = lengths[rank & 1]
    share = own.shape[0]
    total = here[...] + there[...].astype(F32)
    hidden = layer_norm(total, gain[...], shift[...]).astype(BF16)
    own[...] = hidden[:share]
    other[...] = hidden[share:]
    index = lax.broadcasted_iota(I32, (2 * share, 1), 0)
    pos = ((index // share) ^ rank) * share + index % share
    valid = jnp.where(pos < length, hidden.astype(F32), F32(0.0))
    pool[...] = jnp.sum(valid, axis=0, keepdims=True)


def finish(lengths, here, there, gain, shift):
    half, width = here.shape
    block = jax.ShapeDtypeStruct((half // 2, width), BF16)
    return pl.pallas_call(
        finish_kernel,
        out_shape=(block, block, jax.ShapeDtypeStruct((1, width), F32)),
        in_specs=[SMEM] + [VMEM] * 4,
        out_specs=(VMEM, VMEM, VMEM),
        compiler_params=params(8),
        cost_estimate=cost(2),
        name="finish",
    )(lengths, here, there, gain, shift)


def score_kernel(
    lengths, pool, pool_core, pool_chip, pool_diag, rows, own, other, out, hidden_out
):
    core = lax.axis_index("tp") & 1
    width = pool.shape[1]
    mine = pool[...] + pool_chip[...]
    theirs = pool_core[...] + pool_diag[...]
    first = jnp.where(core == 0, mine, theirs) / lengths[0].astype(F32)
    second = jnp.where(core == 0, theirs, mine) / lengths[1].astype(F32)
    row = lax.broadcasted_iota(I32, (8, width), 0)
    pooled = jnp.where(row == 0, first, jnp.where(row == 1, second, F32(0.0)))
    scale = lax.rsqrt(jnp.mean(pooled * pooled, axis=-1, keepdims=True) + norm_eps)
    queries = (pooled * scale).astype(BF16)
    found = lax.dot_general(
        queries, rows[...], (((1,), (1,)), ((), ())), preferred_element_type=F32
    )
    each = rows.shape[0] // 2
    out[0:1, :] = found[0:1, :each]
    out[1:2, :] = found[1:2, each:]
    hidden_out[core] = own[...]
    hidden_out[1 - core] = other[...]


def score(lengths, pools, rows, own, other):
    return pl.pallas_call(
        score_kernel,
        out_shape=(
            jax.ShapeDtypeStruct((2, rows.shape[0] // 2), F32),
            jax.ShapeDtypeStruct((2,) + own.shape, BF16),
        ),
        in_specs=[SMEM] + [VMEM] * 7,
        out_specs=(VMEM, VMEM),
        compiler_params=params(8),
        cost_estimate=cost(1),
        name="score",
    )(lengths, *pools, rows, own, other)


def source_order(groups):
    order = [0]
    mask = groups // 2
    while mask >= 4:
        order = order + [entry + mask for entry in order]
        mask //= 2
    return [entry + last for last in range(4) for entry in order]


def as_ones(mask):
    return mask.astype(F32).astype(BF16)


def plan_rows(first_place, rows_here, parts, numbers, place, rounds):
    rank = lax.axis_index("tp")
    group = lax.axis_index("req")
    groups = parts[0].shape[0]
    slots = groups * SLOTS
    ids = jnp.concatenate([part[...] for part in parts], axis=1)
    count = ids.shape[1]
    owner = lax.shift_right_logical(ids, I32(rows_here.bit_length() - 1))
    before = as_ones(
        lax.broadcasted_iota(I32, (count, count), 0)
        < lax.broadcasted_iota(I32, (count, count), 1)
    )
    ones = jnp.ones((count, 128), BF16)
    slot = lax.broadcasted_iota(I32, (SLOTS, 1), 0) + first_place

    mine = owner == group * 4 + rank
    asked = jnp.concatenate(
        [
            (owner[:1] == (group ^ source) * 4 + rank).astype(F32)
            for source in source_order(groups)
        ]
    )
    both = jnp.concatenate([mine.astype(F32), asked]).astype(BF16)
    ranks = matmul(both, before).astype(I32)
    send_rank = jnp.where(mine, ranks[:groups], -1)
    take_rank = jnp.where(asked > 0, ranks[groups:], -1)

    local = jnp.where(mine, ids - (group * 4 + rank) * rows_here, 0)
    high = (local >> 6).astype(F32).astype(BF16)
    low = (local & 63).astype(F32).astype(BF16)
    chosen = jnp.concatenate(
        [(send_rank[k : k + 1] == slot).astype(F32) for k in range(groups)]
    ).astype(BF16)
    spread = (((1,), (1,)), ((), ()))
    wanted = 64.0 * lax.dot_general(high, chosen, spread, preferred_element_type=F32)
    wanted = wanted + lax.dot_general(low, chosen, spread, preferred_element_type=F32)
    counts = matmul(as_ones(mine), jnp.ones((count, slots), BF16))
    own = lax.broadcasted_iota(I32, (groups, slots), 0) == lax.div(
        lax.broadcasted_iota(I32, (groups, slots), 1), I32(SLOTS)
    )
    numbers[0:1, :] = jnp.sum(jnp.where(own, wanted, 0.0), axis=0, keepdims=True).astype(I32)
    counts = jnp.sum(jnp.where(own, counts, 0.0), axis=0, keepdims=True).astype(I32)
    numbers[1:2, :] = counts - first_place

    for k in range(groups):
        place[k * SLOTS : (k + 1) * SLOTS, :] = as_ones(take_rank[k : k + 1] == slot)
    shard = lax.broadcasted_iota(I32, (4 * groups, 1), 0)
    load = jnp.concatenate(
        [(owner[k : k + 1] == shard).astype(F32) for k in range(groups)]
    ).astype(BF16)
    most = jnp.max(matmul(load, ones)).astype(I32)
    rounds[0] = (most + SLOTS - 1) // SLOTS - 1


def fetch_rows(chosen, index, tiles, rows, sems):
    deep = tiles.shape[1]
    slots = tiles.shape[0]
    step = 4

    def tile_copy(slot):
        first = pl.multiple_of((chosen[0, slot] // deep) * deep, deep)
        return pltpu.make_async_copy(index.at[pl.ds(first, deep)], tiles.at[slot], sems.at[slot])

    def start(number, carry):
        for each in range(step):
            tile_copy(number * step + each).start()
        return carry

    def select(number, carry):
        for each in range(step):
            tile_copy(number * step + each).wait()
        for each in range(step):
            source = number * step + each
            line = lax.broadcasted_iota(I32, (deep, 1), 0) == chosen[0, source] % deep
            row = jnp.where(line, tiles[source].astype(F32), F32(0.0))
            rows[pl.ds(source, 1), :] = jnp.sum(row, axis=0, keepdims=True)
        return carry

    def each_group(action):
        def one(number, carry):
            first = number * (SLOTS // step)
            left = jnp.clip(chosen[1, number * SLOTS], 0, SLOTS)
            return lax.fori_loop(first, first + (left + step - 1) // step, action, carry)

        lax.fori_loop(0, slots // SLOTS, one, 0)

    rows[...] = jnp.zeros_like(rows)
    each_group(start)

    def finish_rows(keep, send):
        each_group(select)
        keep[...] = rows[: slots // 2, :].astype(BF16)
        send[...] = rows[slots // 2 :, :].astype(BF16)

    return finish_rows


def take_kernel(
    number, i0, i1, index, keep, send, place, rounds, numbers, chosen, tiles, rows,
    sems, sem,
):
    plan_rows(number[0] * SLOTS, index.shape[0], (i0, i1), numbers, place, rounds)
    copy = pltpu.make_async_copy(numbers, chosen, sem)
    copy.start()
    copy.wait()
    fetch_rows(chosen, index, tiles, rows, sems)(keep, send)


def fetch_scratch(slots, width):
    return [
        pltpu.SMEM((2, slots), I32),
        pltpu.VMEM((slots, 16, width), BF16),
        pltpu.VMEM((slots, width), F32),
        pltpu.SemaphoreType.DMA((slots,)),
        pltpu.SemaphoreType.DMA,
    ]


def take_rows(number, ids, index_rows):
    groups, each = ids[0].shape
    slots = groups * SLOTS
    width = index_rows.shape[1]
    half = jax.ShapeDtypeStruct((slots // 2, width), BF16)
    return pl.pallas_call(
        take_kernel,
        out_shape=(
            half,
            half,
            jax.ShapeDtypeStruct((slots, 2 * each), BF16),
            jax.ShapeDtypeStruct((1,), I32),
        ),
        in_specs=[SMEM] + [VMEM] * 2 + [HBM],
        out_specs=(VMEM, VMEM, VMEM, SMEM),
        scratch_shapes=[pltpu.VMEM((2, slots), I32)] + fetch_scratch(slots, width),
        compiler_params=params(8 + slots // 16),
        cost_estimate=NO_COST,
        name="take_rows",
    )(number, *ids, in_hbm(index_rows))


def place_kernel(place, h0, h1, h2, h3, out):
    received = jnp.concatenate([h0[...], h1[...], h2[...], h3[...]])
    chosen = lax.dot_general(
        place[...], received, (((0,), (0,)), ((), ())), preferred_element_type=F32
    )
    out[...] = chosen.astype(BF16)


def place_rows(place, received):
    return pl.pallas_call(
        place_kernel,
        out_shape=jax.ShapeDtypeStruct((place.shape[1], received[0].shape[1]), BF16),
        in_specs=[VMEM] * 5,
        out_specs=VMEM,
        compiler_params=params(8),
        cost_estimate=NO_COST,
        name="place_rows",
    )(place, *received)


def masks(axis):
    mask = 1
    while mask < lax.axis_size(axis):
        yield mask
        mask *= 2


def row_exchange(ids, index_rows, place, rounds):
    width = index_rows.shape[1]

    def gathered(keep, send, place, gates=((), (), ())):
        keep = keep.reshape(1, -1, SLOTS, width)
        send = send.reshape(1, -1, SLOTS, width)
        held = None
        for mask in list(masks("req"))[:1:-1]:
            if held is not None:
                keep, send = held[:, :mask], held[:, mask:]
            other = swap(send, "req", mask)
            if mask == 4:
                other = after(other, *gates[0])
            held = jnp.concatenate([keep, other])
        others = [swap(held[:, mask], "req", mask) for mask in (1, 2, 3)]
        others = list(after(tuple(others), *gates[1]))
        held = [part.reshape(-1, width) for part in [held[:, 0]] + others]
        found = place_rows(place, held)
        found = after(found, *gates[2]).reshape(4, -1, width)
        parts = [swap(found[place], "tp", mask) for place, mask in ((1, 2), (2, 1), (3, 3))]
        return found[0] + parts[0] + parts[1] + parts[2]

    def one_more(state):
        number, total = state
        keep, send, place, _ = take_rows(number.reshape(1), ids, index_rows)
        return number - 1, total + gathered(keep, send, place)

    def further(rows, *gate):
        left = after(rounds, *gate)[0]
        return lax.while_loop(lambda state: state[0] > 0, one_more, (left, rows))[1]

    return lambda keep, send, *gates: gathered(keep, send, place, gates), further


def per_device(
    states,
    lengths,
    w_qkv,
    b_qkv,
    w_out,
    b_out,
    ln1_gain,
    ln1_shift,
    w_up,
    b_up,
    w_down,
    b_down,
    ln2_gain,
    ln2_shift,
    index_rows,
    cand_ids,
):
    from_core = swap(states, "tp", 1)
    w_qkv_t = w_qkv.transpose(1, 0, 2)
    w_qkv_p = swap(w_qkv_t, "tp", 1)
    b_qkv_p = swap(b_qkv, "tp", 1)
    b_up_p = swap(b_up, "tp", 1)

    mine, w_here, w_half = load(states, w_qkv_t, w_out)
    held = cand_ids.reshape(1, -1)
    held = jnp.concatenate([held, swap(held, "tp", 2)], axis=1)
    w_x0 = swap(w_half, "tp", 2)
    from_chip = swap(after(states, held), "tp", 2)
    for mask in masks("req"):
        other = swap(held, "req", mask)
        if mask == 1:
            other, w_x0 = lax.optimization_barrier((other, w_x0))
        held = jnp.concatenate([held, other])
    from_chip, held, from_core, w_qkv_p, b_qkv_p, b_up_p = lax.optimization_barrier(
        (from_chip, held, from_core, w_qkv_p, b_qkv_p, b_up_p)
    )
    w_out_p = swap(after(w_out, from_chip), "tp", 1)
    from_diag = swap(from_chip, "tp", 1)
    blocks = (mine, from_core, from_chip, from_diag)
    ids = (held, swap(held, "tp", 1))
    w_up_p = swap(after(w_up, from_diag, w_out_p, *ids), "tp", 1)
    w_down_p = swap(after(w_down, from_diag, w_out_p, *ids), "tp", 1)
    w_x1 = swap(w_x0, "req", 1)

    blocks, ids, w_out_p = lax.optimization_barrier((blocks, ids, w_out_p))
    context_0, text = first_attention(lengths, blocks, w_here, b_qkv)
    context_0x = swap(context_0, "tp", 2)
    w_d0 = swap(after(w_x0, context_0), "tp", 1)
    context_1, numbers, place, rounds = second_attention(
        lengths, after(text, w_up_p), w_qkv_p, b_qkv_p, ids, index_rows.shape[0]
    )
    context_1x = swap(context_1, "tp", 2)

    base, keep, send = project_first(
        text, context_0, context_0x, w_out, (w_x0, w_x1), b_out[None], numbers,
        index_rows,
    )
    w_d1 = swap(after(w_x1, base), "tp", 1)
    base = project_second(base, context_1, w_out_p)
    gathered, further = row_exchange(ids, index_rows, place, rounds)
    common = (
        context_1x, (w_d0, w_d1), ln1_gain[None], ln1_shift[None],
        (b_up[None], b_up_p[None]), b_down[None], (w_up, w_up_p),
        (w_down, w_down_p),
    )
    down_there = feed_forward(False, base, *common)
    down_x = swap(down_there, "tp", 2)
    down_here = feed_forward(True, after(base, down_there), *common)
    down_x = after(down_x, down_here)
    hidden, hidden_other, pool = finish(
        lengths, down_here, down_x, ln2_gain[None], ln2_shift[None]
    )

    rows = gathered(keep, send, (down_there,), (down_here,), ())
    pools = (pool,) + tuple(swap(pool, "tp", mask) for mask in (1, 2, 3))
    hidden_p = swap(hidden_other, "tp", 1)
    rows = further(after(rows, *pools), *pools)
    scores, hidden_out = score(lengths, pools, rows, hidden, hidden_p)
    return (hidden_out, scores)


def solution(mesh):
    placed = (
        P("req", "tp", None),
        P("req"),
        P(None, None, "tp"),
        P(None, "tp"),
        P("tp", None),
        P(),
        P(),
        P(),
        P(None, "tp"),
        P("tp"),
        P("tp", None),
        P(),
        P(),
        P(),
        P(("req", "tp"), None),
        P("req", "tp"),
    )
    return jax.shard_map(
        per_device,
        mesh=mesh,
        in_specs=placed,
        out_specs=(P("req", "tp", None), P("req", "tp")),
        check_vma=False,
    )
```

```python
import functools

import jax
import jax.numpy as jnp
from jax import lax
from jax.experimental import pallas as pl
from jax.experimental.pallas import tpu as pltpu
from jax.sharding import PartitionSpec as P

HEAD_DIM = 64
WINDOW = 512
SLOTS = 16
BF16 = jnp.bfloat16
F32 = jnp.float32
I32 = jnp.int32
MIB = 1024 * 1024
NO_COST = pl.CostEstimate(flops=1, bytes_accessed=1, transcendentals=0)


def cost(gflop):
    return pl.CostEstimate(flops=int(gflop * 10**9) + 1, bytes_accessed=MIB, transcendentals=0)


layer_eps = 1e-05
norm_eps = 1e-06

VMEM = pl.BlockSpec(memory_space=pltpu.VMEM)
SMEM = pl.BlockSpec(memory_space=pltpu.SMEM)
HBM = pl.BlockSpec(memory_space=pltpu.HBM)
ANY = pl.BlockSpec(memory_space=pl.ANY)


def layer_norm(values, gain, shift):
    centre = values - jnp.mean(values, axis=-1, keepdims=True)
    spread = jnp.mean(centre * centre, axis=-1, keepdims=True)
    return centre * lax.rsqrt(spread + layer_eps) * gain + shift


def in_hbm(array):
    return pltpu.with_memory_space_constraint(array, pltpu.HBM)


def swap(value, axis, mask):
    count = lax.axis_size(axis)
    return lax.ppermute(value, axis, [(i, i ^ mask) for i in range(count)])


def matmul(left, right):
    return jnp.dot(left, right, preferred_element_type=F32)


def params(mib):
    return pltpu.CompilerParams(vmem_limit_bytes=mib * MIB)


def after(value, *others):
    return lax.optimization_barrier((value,) + others)[0]


def load_kernel(states, w, w_out, mine, w_here, half, sems):
    part = half.shape[0]
    first = pl.multiple_of((lax.axis_index("req") & 1) * part, part)
    copies = [
        pltpu.make_async_copy(source, target, sems.at[number])
        for number, (source, target) in enumerate(
            (
                (w_out.at[pl.ds(first, part)], half),
                (states.at[lax.axis_index("tp") & 1], mine),
                (w, w_here),
            )
        )
    ]
    for copy in copies:
        copy.start()
    for copy in copies:
        copy.wait()


def load(states, w, w_out):
    return pl.pallas_call(
        load_kernel,
        out_shape=(
            jax.ShapeDtypeStruct(states.shape[1:], BF16),
            jax.ShapeDtypeStruct(w.shape, BF16),
            jax.ShapeDtypeStruct((w_out.shape[0] // 2, w_out.shape[1]), BF16),
        ),
        in_specs=[HBM] * 3,
        out_specs=(VMEM, VMEM, VMEM),
        scratch_shapes=[pltpu.SemaphoreType.DMA((3,))],
        compiler_params=params(6),
        cost_estimate=NO_COST,
        name="load",
    )(in_hbm(states), in_hbm(w), in_hbm(w_out))


def first_attention_kernel(lengths, mine, s1, s2, s3, w, b, out, text, parts, bias):
    core = lax.axis_index("tp") & 1
    text[...] = jnp.concatenate([mine[...], s1[core], s2[core], s3[core]])
    for which in range(3):
        project(which, text, w, b, parts)
    attend(lengths, parts, bias, out)


def second_attention_kernel(
    rows_here, lengths, text, w, b, i0, i1, out, numbers, place, rounds, parts, bias
):
    plan_rows(0, rows_here, (i0, i1), numbers, place, rounds)
    for which in range(3):
        project(which, text, w, b, parts)
    attend(lengths, parts, bias, out)


def project(which, text, w, b, parts):
    parts[which] = (matmul(text[...], w[which]) + b[which : which + 1, :]).astype(BF16)


def attend(lengths, parts, bias, out):
    rank = lax.axis_index("tp")
    length = lengths[rank & 1]
    _, seq_len, wide = parts.shape
    share = seq_len // 4

    def position(index):
        return ((index // share) ^ rank) * share + index % share

    row_pos = position(lax.broadcasted_iota(I32, (seq_len, 1), 0))
    col_pos = position(lax.broadcasted_iota(I32, (1, seq_len), 1))
    keep = (jnp.abs(row_pos - col_pos) <= WINDOW // 2) & (col_pos < length)
    bias[...] = jnp.where(keep, F32(0.0), F32(-1e30))
    ones = jnp.ones((seq_len, 128), BF16)
    low = lax.broadcasted_iota(I32, (1, 128), 1) < HEAD_DIM
    scale = jnp.asarray(HEAD_DIM**-0.5, BF16)
    for pair in range(wide // 128):
        lanes = slice(pair * 128, (pair + 1) * 128)
        k_pair = parts[1, :, lanes]
        v_ones = jnp.concatenate([parts[2, :, lanes], ones], axis=1)
        for block in range(4):
            rows = slice(block * share, (block + 1) * share)
            q_pair = parts[0, rows, lanes] * scale
            found = []
            for head in range(2):
                chosen = low if head == 0 else jnp.logical_not(low)
                q_head = jnp.where(chosen, q_pair, jnp.zeros((), BF16))
                logits = lax.dot_general(
                    q_head, k_pair, (((1,), (1,)), ((), ())), preferred_element_type=F32
                )
                logits = logits + bias[rows, :]
                top = jnp.max(logits, axis=-1, keepdims=True)
                expo = jnp.exp(logits - top).astype(BF16)
                summed = matmul(expo, v_ones)
                found.append(summed[:, :128] / summed[:, 128:])
            context = jnp.where(low, found[0], found[1])
            context = jnp.where(row_pos[rows] < length, context, F32(0.0))
            out[rows, lanes] = context.astype(BF16)


def attention_scratch(seq_len, wide):
    return [pltpu.VMEM((3, seq_len, wide), BF16), pltpu.VMEM((seq_len, seq_len), F32)]


def first_attention(lengths, blocks, w, b):
    share, width = blocks[0].shape
    wide = w.shape[2]
    return pl.pallas_call(
        first_attention_kernel,
        out_shape=(
            jax.ShapeDtypeStruct((4 * share, wide), BF16),
            jax.ShapeDtypeStruct((4 * share, width), BF16),
        ),
        in_specs=[SMEM] + [VMEM] * 6,
        out_specs=(VMEM, VMEM),
        scratch_shapes=attention_scratch(4 * share, wide),
        compiler_params=params(12),
        cost_estimate=NO_COST,
        name="attention_own",
    )(in_hbm(lengths), *blocks, w, in_hbm(b))


def second_attention(lengths, text, w, b, ids, rows_here):
    seq_len = text.shape[0]
    wide = w.shape[2]
    groups, each = ids[0].shape
    return pl.pallas_call(
        functools.partial(second_attention_kernel, rows_here),
        out_shape=(
            jax.ShapeDtypeStruct((seq_len, wide), BF16),
            jax.ShapeDtypeStruct((2, groups * SLOTS), I32),
            jax.ShapeDtypeStruct((groups * SLOTS, 2 * each), BF16),
            jax.ShapeDtypeStruct((1,), I32),
        ),
        in_specs=[SMEM] + [VMEM] * 5,
        out_specs=(VMEM, VMEM, VMEM, SMEM),
        scratch_shapes=attention_scratch(seq_len, wide),
        compiler_params=params(12),
        cost_estimate=cost(6),
        name="attention_partner",
    )(in_hbm(lengths), text, w, b, *ids)


def joined(first, second):
    swapped = (lax.axis_index("req") & 1) != 0
    low = jnp.where(swapped, second[...], first[...])
    high = jnp.where(swapped, first[...], second[...])
    return jnp.concatenate([low, high])


def project_first_kernel(
    text, here, w, b, numbers, index, out, keep, send,
    chosen, tiles, rows, sems, sem,
):
    copy = pltpu.make_async_copy(numbers, chosen, sem)
    copy.start()
    copy.wait()
    finish_rows = fetch_rows(chosen, index, tiles, rows, sems)
    out[...] = matmul(here[...], w[...]) + (text[...].astype(F32) + b[...])
    finish_rows(keep, send)


def project_first(text, here, w, b_out, numbers, index_rows):
    seq_len, width = text.shape
    slots = numbers.shape[1]
    half = jax.ShapeDtypeStruct((slots // 2, width), BF16)
    return pl.pallas_call(
        project_first_kernel,
        out_shape=(jax.ShapeDtypeStruct((seq_len, width), F32), half, half),
        in_specs=[VMEM] * 5 + [HBM],
        out_specs=(VMEM, VMEM, VMEM),
        scratch_shapes=fetch_scratch(slots, width),
        compiler_params=params(12 + slots // 16),
        cost_estimate=cost(1),
        name="project_first",
    )(text, here, w, b_out, numbers, in_hbm(index_rows))


def project_second_kernel(base, context, w, there, half_0, half_1, out):
    half = base.shape[0] // 2
    w_there = joined(half_0, half_1)
    for number in range(2):
        span = slice(number * half, (number + 1) * half)
        other = slice((1 - number) * half, (2 - number) * half)
        total = matmul(context[span, :], w[...]) + matmul(there[other, :], w_there)
        out[span, :] = base[span, :] + total


def project_second(base, context, w, there, halves):
    return pl.pallas_call(
        project_second_kernel,
        out_shape=jax.ShapeDtypeStruct(base.shape, F32),
        in_specs=[VMEM] * 6,
        out_specs=VMEM,
        input_output_aliases={0: 0},
        compiler_params=params(12),
        cost_estimate=cost(1),
        name="project_second",
    )(base, context, w, there, *halves)


def feed_kernel(
    keep_rest, base, c3, half_0, half_1, gain, shift, b0, b1, b_down,
    up_own, up_partner, down_own, down_partner, out, up_buf, down_buf, act, sems,
):
    hidden = up_own.shape[1]
    up_copy = pltpu.make_async_copy(up_own, up_buf, sems.at[0])
    down_copy = pltpu.make_async_copy(down_own, down_buf, sems.at[1])
    up_copy.start()
    down_copy.start()
    total = base[...] + matmul(c3[...], joined(half_0, half_1))
    normed = layer_norm(total, gain[...], shift[...]).astype(BF16)
    step = 512
    for part, (weight, bias) in enumerate(((up_partner, b1), (up_buf, b0))):
        if part == 1:
            up_copy.wait()
        for low in range(0, hidden, step):
            lanes = slice(low, low + step)
            up = matmul(normed, weight[:, lanes]) + bias[:, lanes]
            activated = 0.5 * up * (1.0 + lax.erf(up * F32(0.5**0.5)))
            act[:, part * hidden + low : part * hidden + low + step] = activated.astype(BF16)
    down = matmul(act[:, :hidden], down_partner[...])
    down_copy.wait()
    down = down + matmul(act[:, hidden:], down_buf[...])
    if keep_rest:
        down = down + (normed.astype(F32) + b_down[...])
    out[...] = down.astype(out.dtype)


def feed_forward(keep_rest, base, context, halves, gain, shift, biases, b_down, ups, downs):
    seq_len, width = base.shape
    half = seq_len // 2
    here = 0 if keep_rest else 1
    hidden = ups[0].shape[1]
    heads_wide = context.shape[1]
    base_spec = pl.BlockSpec((half, width), lambda i: (here, 0))
    context_spec = pl.BlockSpec((half, heads_wide), lambda i: (1 - here, 0))
    return pl.pallas_call(
        lambda *refs: feed_kernel(keep_rest, *refs),
        out_shape=jax.ShapeDtypeStruct((half, width), F32 if keep_rest else BF16),
        grid=(1,),
        in_specs=[base_spec, context_spec] + [VMEM] * 7
        + [HBM, VMEM, HBM, VMEM],
        out_specs=VMEM,
        scratch_shapes=[
            pltpu.VMEM((width, hidden), BF16),
            pltpu.VMEM((hidden, width), BF16),
            pltpu.VMEM((half, 2 * hidden), BF16),
            pltpu.SemaphoreType.DMA((2,)),
        ],
        compiler_params=params(20),
        cost_estimate=cost(8),
        name="feed_here" if keep_rest else "feed_there",
    )(base, context, *halves, gain, shift, *biases, b_down, in_hbm(ups[0]), ups[1],
      in_hbm(downs[0]), downs[1])


def finish_kernel(lengths, here, there, gain, shift, own, other, pool):
    rank = lax.axis_index("tp")
    length = lengths[rank & 1]
    share = own.shape[0]
    total = here[...] + there[...].astype(F32)
    hidden = layer_norm(total, gain[...], shift[...]).astype(BF16)
    own[...] = hidden[:share]
    other[...] = hidden[share:]
    index = lax.broadcasted_iota(I32, (2 * share, 1), 0)
    pos = ((index // share) ^ rank) * share + index % share
    valid = jnp.where(pos < length, hidden.astype(F32), F32(0.0))
    pool[...] = jnp.sum(valid, axis=0, keepdims=True)


def finish(lengths, here, there, gain, shift):
    half, width = here.shape
    block = jax.ShapeDtypeStruct((half // 2, width), BF16)
    return pl.pallas_call(
        finish_kernel,
        out_shape=(block, block, jax.ShapeDtypeStruct((1, width), F32)),
        in_specs=[SMEM] + [VMEM] * 4,
        out_specs=(VMEM, VMEM, VMEM),
        compiler_params=params(8),
        cost_estimate=cost(2),
        name="finish",
    )(lengths, here, there, gain, shift)


def score_kernel(
    lengths, pool, pool_core, pool_chip, pool_diag, rows, own, other, out, hidden_out
):
    core = lax.axis_index("tp") & 1
    width = pool.shape[1]
    mine = pool[...] + pool_chip[...]
    theirs = pool_core[...] + pool_diag[...]
    first = jnp.where(core == 0, mine, theirs) / lengths[0].astype(F32)
    second = jnp.where(core == 0, theirs, mine) / lengths[1].astype(F32)
    row = lax.broadcasted_iota(I32, (8, width), 0)
    pooled = jnp.where(row == 0, first, jnp.where(row == 1, second, F32(0.0)))
    scale = lax.rsqrt(jnp.mean(pooled * pooled, axis=-1, keepdims=True) + norm_eps)
    queries = (pooled * scale).astype(BF16)
    found = lax.dot_general(
        queries, rows[...], (((1,), (1,)), ((), ())), preferred_element_type=F32
    )
    each = rows.shape[0] // 2
    out[0:1, :] = found[0:1, :each]
    out[1:2, :] = found[1:2, each:]
    hidden_out[core] = own[...]
    hidden_out[1 - core] = other[...]


def score(lengths, pools, rows, own, other):
    return pl.pallas_call(
        score_kernel,
        out_shape=(
            jax.ShapeDtypeStruct((2, rows.shape[0] // 2), F32),
            jax.ShapeDtypeStruct((2,) + own.shape, BF16),
        ),
        in_specs=[SMEM] + [VMEM] * 7,
        out_specs=(VMEM, VMEM),
        compiler_params=params(8),
        cost_estimate=cost(1),
        name="score",
    )(lengths, *pools, rows, own, other)


def source_order(groups):
    order = [0]
    mask = groups // 2
    while mask >= 4:
        order = order + [entry + mask for entry in order]
        mask //= 2
    return [entry + last for last in range(4) for entry in order]


def as_ones(mask):
    return mask.astype(F32).astype(BF16)


def plan_rows(first_place, rows_here, parts, numbers, place, rounds):
    rank = lax.axis_index("tp")
    group = lax.axis_index("req")
    groups = parts[0].shape[0]
    slots = groups * SLOTS
    ids = jnp.concatenate([part[...] for part in parts], axis=1)
    count = ids.shape[1]
    owner = lax.shift_right_logical(ids, I32(rows_here.bit_length() - 1))
    before = as_ones(
        lax.broadcasted_iota(I32, (count, count), 0)
        < lax.broadcasted_iota(I32, (count, count), 1)
    )
    ones = jnp.ones((count, 128), BF16)
    slot = lax.broadcasted_iota(I32, (SLOTS, 1), 0) + first_place

    mine = owner == group * 4 + rank
    asked = jnp.concatenate(
        [
            (owner[:1] == (group ^ source) * 4 + rank).astype(F32)
            for source in source_order(groups)
        ]
    )
    both = jnp.concatenate([mine.astype(F32), asked]).astype(BF16)
    ranks = matmul(both, before).astype(I32)
    send_rank = jnp.where(mine, ranks[:groups], -1)
    take_rank = jnp.where(asked > 0, ranks[groups:], -1)

    local = jnp.where(mine, ids - (group * 4 + rank) * rows_here, 0)
    high = (local >> 6).astype(F32).astype(BF16)
    low = (local & 63).astype(F32).astype(BF16)
    chosen = jnp.concatenate(
        [(send_rank[k : k + 1] == slot).astype(F32) for k in range(groups)]
    ).astype(BF16)
    spread = (((1,), (1,)), ((), ()))
    wanted = 64.0 * lax.dot_general(high, chosen, spread, preferred_element_type=F32)
    wanted = wanted + lax.dot_general(low, chosen, spread, preferred_element_type=F32)
    counts = matmul(as_ones(mine), jnp.ones((count, slots), BF16))
    own = lax.broadcasted_iota(I32, (groups, slots), 0) == lax.div(
        lax.broadcasted_iota(I32, (groups, slots), 1), I32(SLOTS)
    )
    numbers[0:1, :] = jnp.sum(jnp.where(own, wanted, 0.0), axis=0, keepdims=True).astype(I32)
    counts = jnp.sum(jnp.where(own, counts, 0.0), axis=0, keepdims=True).astype(I32)
    numbers[1:2, :] = counts - first_place

    for k in range(groups):
        place[k * SLOTS : (k + 1) * SLOTS, :] = as_ones(take_rank[k : k + 1] == slot)
    shard = lax.broadcasted_iota(I32, (4 * groups, 1), 0)
    load = jnp.concatenate(
        [(owner[k : k + 1] == shard).astype(F32) for k in range(groups)]
    ).astype(BF16)
    most = jnp.max(matmul(load, ones)).astype(I32)
    rounds[0] = (most + SLOTS - 1) // SLOTS - 1


def fetch_rows(chosen, index, tiles, rows, sems):
    deep = tiles.shape[1]
    slots = tiles.shape[0]
    step = 4

    def tile_copy(slot):
        first = pl.multiple_of((chosen[0, slot] // deep) * deep, deep)
        return pltpu.make_async_copy(index.at[pl.ds(first, deep)], tiles.at[slot], sems.at[slot])

    def start(number, carry):
        for each in range(step):
            tile_copy(number * step + each).start()
        return carry

    def select(number, carry):
        for each in range(step):
            tile_copy(number * step + each).wait()
        for each in range(step):
            source = number * step + each
            line = lax.broadcasted_iota(I32, (deep, 1), 0) == chosen[0, source] % deep
            row = jnp.where(line, tiles[source].astype(F32), F32(0.0))
            rows[pl.ds(source, 1), :] = jnp.sum(row, axis=0, keepdims=True)
        return carry

    def each_group(action):
        def one(number, carry):
            first = number * (SLOTS // step)
            left = jnp.clip(chosen[1, number * SLOTS], 0, SLOTS)
            return lax.fori_loop(first, first + (left + step - 1) // step, action, carry)

        lax.fori_loop(0, slots // SLOTS, one, 0)

    rows[...] = jnp.zeros_like(rows)
    each_group(start)

    def finish_rows(keep, send):
        each_group(select)
        keep[...] = rows[: slots // 2, :].astype(BF16)
        send[...] = rows[slots // 2 :, :].astype(BF16)

    return finish_rows


def take_kernel(
    number, i0, i1, index, keep, send, place, rounds, numbers, chosen, tiles, rows,
    sems, sem,
):
    plan_rows(number[0] * SLOTS, index.shape[0], (i0, i1), numbers, place, rounds)
    copy = pltpu.make_async_copy(numbers, chosen, sem)
    copy.start()
    copy.wait()
    fetch_rows(chosen, index, tiles, rows, sems)(keep, send)


def fetch_scratch(slots, width):
    return [
        pltpu.SMEM((2, slots), I32),
        pltpu.VMEM((slots, 16, width), BF16),
        pltpu.VMEM((slots, width), F32),
        pltpu.SemaphoreType.DMA((slots,)),
        pltpu.SemaphoreType.DMA,
    ]


def take_rows(number, ids, index_rows):
    groups, each = ids[0].shape
    slots = groups * SLOTS
    width = index_rows.shape[1]
    half = jax.ShapeDtypeStruct((slots // 2, width), BF16)
    return pl.pallas_call(
        take_kernel,
        out_shape=(
            half,
            half,
            jax.ShapeDtypeStruct((slots, 2 * each), BF16),
            jax.ShapeDtypeStruct((1,), I32),
        ),
        in_specs=[SMEM] + [VMEM] * 2 + [HBM],
        out_specs=(VMEM, VMEM, VMEM, SMEM),
        scratch_shapes=[pltpu.VMEM((2, slots), I32)] + fetch_scratch(slots, width),
        compiler_params=params(8 + slots // 16),
        cost_estimate=NO_COST,
        name="take_rows",
    )(number, *ids, in_hbm(index_rows))


def place_kernel(place, h0, h1, h2, h3, out):
    received = jnp.concatenate([h0[...], h1[...], h2[...], h3[...]])
    chosen = lax.dot_general(
        place[...], received, (((0,), (0,)), ((), ())), preferred_element_type=F32
    )
    out[...] = chosen.astype(BF16)


def place_rows(place, received):
    return pl.pallas_call(
        place_kernel,
        out_shape=jax.ShapeDtypeStruct((place.shape[1], received[0].shape[1]), BF16),
        in_specs=[VMEM] * 5,
        out_specs=VMEM,
        compiler_params=params(8),
        cost_estimate=NO_COST,
        name="place_rows",
    )(place, *received)


def masks(axis):
    mask = 1
    while mask < lax.axis_size(axis):
        yield mask
        mask *= 2


def row_exchange(ids, index_rows, place, rounds):
    width = index_rows.shape[1]

    def gathered(keep, send, place, gates=((), (), ())):
        keep = keep.reshape(1, -1, SLOTS, width)
        send = send.reshape(1, -1, SLOTS, width)
        held = None
        for mask in list(masks("req"))[:1:-1]:
            if held is not None:
                keep, send = held[:, :mask], held[:, mask:]
            other = swap(send, "req", mask)
            if mask == 4:
                other = after(other, *gates[0])
            held = jnp.concatenate([keep, other])
        others = [swap(held[:, mask], "req", mask) for mask in (1, 2, 3)]
        others = list(after(tuple(others), *gates[1]))
        held = [part.reshape(-1, width) for part in [held[:, 0]] + others]
        found = place_rows(place, held)
        found = after(found, *gates[2]).reshape(4, -1, width)
        parts = [swap(found[place], "tp", mask) for place, mask in ((1, 2), (2, 1), (3, 3))]
        return found[0] + parts[0] + parts[1] + parts[2]

    def one_more(state):
        number, total = state
        keep, send, place, _ = take_rows(number.reshape(1), ids, index_rows)
        return number - 1, total + gathered(keep, send, place)

    def further(rows, *gate):
        left = after(rounds, *gate)[0]
        return lax.while_loop(lambda state: state[0] > 0, one_more, (left, rows))[1]

    return lambda keep, send, *gates: gathered(keep, send, place, gates), further


def per_device(
    states,
    lengths,
    w_qkv,
    b_qkv,
    w_out,
    b_out,
    ln1_gain,
    ln1_shift,
    w_up,
    b_up,
    w_down,
    b_down,
    ln2_gain,
    ln2_shift,
    index_rows,
    cand_ids,
):
    from_core = swap(states, "tp", 1)
    w_qkv_t = w_qkv.transpose(1, 0, 2)
    w_qkv_p = swap(w_qkv_t, "tp", 1)
    b_qkv_p = swap(b_qkv, "tp", 1)
    b_up_p = swap(b_up, "tp", 1)

    held = cand_ids.reshape(1, -1)
    held = jnp.concatenate([held, swap(held, "tp", 2)], axis=1)
    from_chip = swap(after(states, held), "tp", 2)
    for mask in masks("req"):
        other = swap(held, "req", mask)
        if mask * 2 == lax.axis_size("req"):
            mine, w_here, w_half = load(states, w_qkv_t, after(w_out, held))
            other, mine = lax.optimization_barrier((other, mine))
        held = jnp.concatenate([held, other])
    from_chip, held, from_core, w_qkv_p, b_qkv_p, b_up_p = lax.optimization_barrier(
        (from_chip, held, from_core, w_qkv_p, b_qkv_p, b_up_p)
    )
    w_out_p = swap(after(w_out, from_chip), "tp", 1)
    from_diag = swap(from_chip, "tp", 1)
    blocks = (mine, from_core, from_chip, from_diag)
    ids = (held, swap(held, "tp", 1))
    w_up_p = swap(after(w_up, from_diag, w_out_p, *ids), "tp", 1)
    w_down_p = swap(after(w_down, from_diag, w_out_p, *ids), "tp", 1)
    w_x0 = swap(w_half, "tp", 2)

    blocks, ids, w_out_p = lax.optimization_barrier((blocks, ids, w_out_p))
    context_0, text = first_attention(lengths, blocks, w_here, b_qkv)
    context_0x = swap(context_0, "tp", 2)
    context_1, numbers, place, rounds = second_attention(
        lengths, after(text, w_up_p), w_qkv_p, b_qkv_p, ids, index_rows.shape[0]
    )
    context_1x = swap(context_1, "tp", 2)
    w_x1 = swap(after(w_x0, context_1), "req", 1)
    w_d0 = swap(after(w_x0, context_1), "tp", 1)

    base, keep, send = project_first(
        text, after(context_0, context_0x), w_out, b_out[None], numbers, index_rows
    )
    w_d1 = swap(after(w_x1, base), "tp", 1)
    base = project_second(base, context_1, w_out_p, context_0x, (w_x0, w_x1))
    gathered, further = row_exchange(ids, index_rows, place, rounds)
    common = (
        context_1x, (w_d0, w_d1), ln1_gain[None], ln1_shift[None],
        (b_up[None], b_up_p[None]), b_down[None], (w_up, w_up_p),
        (w_down, w_down_p),
    )
    down_there = feed_forward(False, base, *common)
    down_x = swap(down_there, "tp", 2)
    down_here = feed_forward(True, after(base, down_there), *common)
    down_x = after(down_x, down_here)
    hidden, hidden_other, pool = finish(
        lengths, down_here, down_x, ln2_gain[None], ln2_shift[None]
    )

    rows = gathered(keep, send, (down_there,), (down_here,), ())
    pools = (pool,) + tuple(swap(pool, "tp", mask) for mask in (1, 2, 3))
    hidden_p = swap(hidden_other, "tp", 1)
    rows = further(after(rows, *pools), *pools)
    scores, hidden_out = score(lengths, pools, rows, hidden, hidden_p)
    return (hidden_out, scores)


def solution(mesh):
    placed = (
        P("req", "tp", None),
        P("req"),
        P(None, None, "tp"),
        P(None, "tp"),
        P("tp", None),
        P(),
        P(),
        P(),
        P(None, "tp"),
        P("tp"),
        P("tp", None),
        P(),
        P(),
        P(),
        P(("req", "tp"), None),
        P("req", "tp"),
    )
    return jax.shard_map(
        per_device,
        mesh=mesh,
        in_specs=placed,
        out_specs=(P("req", "tp", None), P("req", "tp")),
        check_vma=False,
    )
```

```python
import functools

import jax
import jax.numpy as jnp
from jax import lax
from jax.experimental import pallas as pl
from jax.experimental.pallas import tpu as pltpu
from jax.sharding import PartitionSpec as P

HEAD_DIM = 64
WINDOW = 512
SLOTS = 16
BF16 = jnp.bfloat16
F32 = jnp.float32
I32 = jnp.int32
MIB = 1024 * 1024
NO_COST = pl.CostEstimate(flops=1, bytes_accessed=1, transcendentals=0)


def cost(gflop):
    return pl.CostEstimate(flops=int(gflop * 10**9) + 1, bytes_accessed=MIB, transcendentals=0)


layer_eps = 1e-05
norm_eps = 1e-06

VMEM = pl.BlockSpec(memory_space=pltpu.VMEM)
SMEM = pl.BlockSpec(memory_space=pltpu.SMEM)
HBM = pl.BlockSpec(memory_space=pltpu.HBM)
ANY = pl.BlockSpec(memory_space=pl.ANY)


def layer_norm(values, gain, shift):
    centre = values - jnp.mean(values, axis=-1, keepdims=True)
    spread = jnp.mean(centre * centre, axis=-1, keepdims=True)
    return centre * lax.rsqrt(spread + layer_eps) * gain + shift


def in_hbm(array):
    return pltpu.with_memory_space_constraint(array, pltpu.HBM)


def swap(value, axis, mask):
    count = lax.axis_size(axis)
    return lax.ppermute(value, axis, [(i, i ^ mask) for i in range(count)])


def matmul(left, right):
    return jnp.dot(left, right, preferred_element_type=F32)


def params(mib):
    return pltpu.CompilerParams(vmem_limit_bytes=mib * MIB)


def after(value, *others):
    return lax.optimization_barrier((value,) + others)[0]


def load_kernel(states, w, w_out, mine, w_here, half, sems):
    part = half.shape[0]
    first = pl.multiple_of((lax.axis_index("req") & 1) * part, part)
    copies = [
        pltpu.make_async_copy(source, target, sems.at[number])
        for number, (source, target) in enumerate(
            (
                (w_out.at[pl.ds(first, part)], half),
                (states.at[lax.axis_index("tp") & 1], mine),
                (w, w_here),
            )
        )
    ]
    for copy in copies:
        copy.start()
    for copy in copies:
        copy.wait()


def load(states, w, w_out):
    return pl.pallas_call(
        load_kernel,
        out_shape=(
            jax.ShapeDtypeStruct(states.shape[1:], BF16),
            jax.ShapeDtypeStruct(w.shape, BF16),
            jax.ShapeDtypeStruct((w_out.shape[0] // 2, w_out.shape[1]), BF16),
        ),
        in_specs=[HBM] * 3,
        out_specs=(VMEM, VMEM, VMEM),
        scratch_shapes=[pltpu.SemaphoreType.DMA((3,))],
        compiler_params=params(6),
        cost_estimate=NO_COST,
        name="load",
    )(in_hbm(states), in_hbm(w), in_hbm(w_out))


def first_attention_kernel(lengths, mine, s1, s2, s3, w, b, out, text, parts, bias):
    core = lax.axis_index("tp") & 1
    text[...] = jnp.concatenate([mine[...], s1[core], s2[core], s3[core]])
    for which in range(3):
        project(which, text, w, b, parts)
    attend(lengths, parts, bias, out)


def second_attention_kernel(
    rows_here, lengths, text, w, b, i0, i1, out, numbers, place, rounds, parts, bias
):
    plan_rows(0, rows_here, (i0, i1), numbers, place, rounds)
    for which in range(3):
        project(which, text, w, b, parts)
    attend(lengths, parts, bias, out)


def project(which, text, w, b, parts):
    parts[which] = (matmul(text[...], w[which]) + b[which : which + 1, :]).astype(BF16)


def attend(lengths, parts, bias, out):
    rank = lax.axis_index("tp")
    length = lengths[rank & 1]
    _, seq_len, wide = parts.shape
    share = seq_len // 4

    def position(index):
        return ((index // share) ^ rank) * share + index % share

    row_pos = position(lax.broadcasted_iota(I32, (seq_len, 1), 0))
    col_pos = position(lax.broadcasted_iota(I32, (1, seq_len), 1))
    keep = (jnp.abs(row_pos - col_pos) <= WINDOW // 2) & (col_pos < length)
    bias[...] = jnp.where(keep, F32(0.0), F32(-1e30))
    ones = jnp.ones((seq_len, 128), BF16)
    low = lax.broadcasted_iota(I32, (1, 128), 1) < HEAD_DIM
    scale = jnp.asarray(HEAD_DIM**-0.5, BF16)
    for pair in range(wide // 128):
        lanes = slice(pair * 128, (pair + 1) * 128)
        k_pair = parts[1, :, lanes]
        v_ones = jnp.concatenate([parts[2, :, lanes], ones], axis=1)
        for block in range(4):
            rows = slice(block * share, (block + 1) * share)
            q_pair = parts[0, rows, lanes] * scale
            zero = jnp.zeros((), BF16)
            q_heads = jnp.concatenate(
                [jnp.where(low, q_pair, zero), jnp.where(low, zero, q_pair)]
            )
            logits = lax.dot_general(
                q_heads, k_pair, (((1,), (1,)), ((), ())), preferred_element_type=F32
            )
            masked = bias[rows, :]
            logits = logits + jnp.concatenate([masked, masked])
            top = jnp.max(logits, axis=-1, keepdims=True)
            expo = jnp.exp(logits - top).astype(BF16)
            summed = matmul(expo, v_ones)
            found = summed[:, :128] / summed[:, 128:]
            context = jnp.where(low, found[:share], found[share:])
            context = jnp.where(row_pos[rows] < length, context, F32(0.0))
            out[rows, lanes] = context.astype(BF16)


def attention_scratch(seq_len, wide):
    return [pltpu.VMEM((3, seq_len, wide), BF16), pltpu.VMEM((seq_len, seq_len), F32)]


def first_attention(lengths, blocks, w, b):
    share, width = blocks[0].shape
    wide = w.shape[2]
    return pl.pallas_call(
        first_attention_kernel,
        out_shape=(
            jax.ShapeDtypeStruct((4 * share, wide), BF16),
            jax.ShapeDtypeStruct((4 * share, width), BF16),
        ),
        in_specs=[SMEM] + [VMEM] * 6,
        out_specs=(VMEM, VMEM),
        scratch_shapes=attention_scratch(4 * share, wide),
        compiler_params=params(12),
        cost_estimate=NO_COST,
        name="attention_own",
    )(in_hbm(lengths), *blocks, w, in_hbm(b))


def second_attention(lengths, text, w, b, ids, rows_here):
    seq_len = text.shape[0]
    wide = w.shape[2]
    groups, each = ids[0].shape
    return pl.pallas_call(
        functools.partial(second_attention_kernel, rows_here),
        out_shape=(
            jax.ShapeDtypeStruct((seq_len, wide), BF16),
            jax.ShapeDtypeStruct((2, groups * SLOTS), I32),
            jax.ShapeDtypeStruct((groups * SLOTS, 2 * each), BF16),
            jax.ShapeDtypeStruct((1,), I32),
        ),
        in_specs=[SMEM] + [VMEM] * 5,
        out_specs=(VMEM, VMEM, VMEM, SMEM),
        scratch_shapes=attention_scratch(seq_len, wide),
        compiler_params=params(12),
        cost_estimate=cost(6),
        name="attention_partner",
    )(in_hbm(lengths), text, w, b, *ids)


def joined(first, second):
    swapped = (lax.axis_index("req") & 1) != 0
    low = jnp.where(swapped, second[...], first[...])
    high = jnp.where(swapped, first[...], second[...])
    return jnp.concatenate([low, high])


def project_first_kernel(
    text, here, w, b, numbers, index, out, keep, send,
    chosen, tiles, rows, sems, sem,
):
    copy = pltpu.make_async_copy(numbers, chosen, sem)
    copy.start()
    copy.wait()
    finish_rows = fetch_rows(chosen, index, tiles, rows, sems)
    out[...] = matmul(here[...], w[...]) + (text[...].astype(F32) + b[...])
    finish_rows(keep, send)


def project_first(text, here, w, b_out, numbers, index_rows):
    seq_len, width = text.shape
    slots = numbers.shape[1]
    half = jax.ShapeDtypeStruct((slots // 2, width), BF16)
    return pl.pallas_call(
        project_first_kernel,
        out_shape=(jax.ShapeDtypeStruct((seq_len, width), F32), half, half),
        in_specs=[VMEM] * 5 + [HBM],
        out_specs=(VMEM, VMEM, VMEM),
        scratch_shapes=fetch_scratch(slots, width),
        compiler_params=params(12 + slots // 16),
        cost_estimate=cost(1),
        name="project_first",
    )(text, here, w, b_out, numbers, in_hbm(index_rows))


def project_second_kernel(base, context, w, there, half_0, half_1, out):
    half = base.shape[0] // 2
    w_there = joined(half_0, half_1)
    for number in range(2):
        span = slice(number * half, (number + 1) * half)
        other = slice((1 - number) * half, (2 - number) * half)
        total = matmul(context[span, :], w[...]) + matmul(there[other, :], w_there)
        out[span, :] = base[span, :] + total


def project_second(base, context, w, there, halves):
    return pl.pallas_call(
        project_second_kernel,
        out_shape=jax.ShapeDtypeStruct(base.shape, F32),
        in_specs=[VMEM] * 6,
        out_specs=VMEM,
        input_output_aliases={0: 0},
        compiler_params=params(12),
        cost_estimate=cost(1),
        name="project_second",
    )(base, context, w, there, *halves)


def feed_kernel(
    keep_rest, base, c3, half_0, half_1, gain, shift, b0, b1, b_down,
    up_own, up_partner, down_own, down_partner, out, up_buf, down_buf, act, sems,
):
    hidden = up_own.shape[1]
    up_copy = pltpu.make_async_copy(up_own, up_buf, sems.at[0])
    down_copy = pltpu.make_async_copy(down_own, down_buf, sems.at[1])
    up_copy.start()
    down_copy.start()
    total = base[...] + matmul(c3[...], joined(half_0, half_1))
    normed = layer_norm(total, gain[...], shift[...]).astype(BF16)
    step = 512
    for part, (weight, bias) in enumerate(((up_partner, b1), (up_buf, b0))):
        if part == 1:
            up_copy.wait()
        for low in range(0, hidden, step):
            lanes = slice(low, low + step)
            up = matmul(normed, weight[:, lanes]) + bias[:, lanes]
            activated = 0.5 * up * (1.0 + lax.erf(up * F32(0.5**0.5)))
            act[:, part * hidden + low : part * hidden + low + step] = activated.astype(BF16)
    down = matmul(act[:, :hidden], down_partner[...])
    down_copy.wait()
    down = down + matmul(act[:, hidden:], down_buf[...])
    if keep_rest:
        down = down + (normed.astype(F32) + b_down[...])
    out[...] = down.astype(out.dtype)


def feed_forward(keep_rest, base, context, halves, gain, shift, biases, b_down, ups, downs):
    seq_len, width = base.shape
    half = seq_len // 2
    here = 0 if keep_rest else 1
    hidden = ups[0].shape[1]
    heads_wide = context.shape[1]
    base_spec = pl.BlockSpec((half, width), lambda i: (here, 0))
    context_spec = pl.BlockSpec((half, heads_wide), lambda i: (1 - here, 0))
    return pl.pallas_call(
        lambda *refs: feed_kernel(keep_rest, *refs),
        out_shape=jax.ShapeDtypeStruct((half, width), F32 if keep_rest else BF16),
        grid=(1,),
        in_specs=[base_spec, context_spec] + [VMEM] * 7
        + [HBM, VMEM, HBM, VMEM],
        out_specs=VMEM,
        scratch_shapes=[
            pltpu.VMEM((width, hidden), BF16),
            pltpu.VMEM((hidden, width), BF16),
            pltpu.VMEM((half, 2 * hidden), BF16),
            pltpu.SemaphoreType.DMA((2,)),
        ],
        compiler_params=params(20),
        cost_estimate=cost(8),
        name="feed_here" if keep_rest else "feed_there",
    )(base, context, *halves, gain, shift, *biases, b_down, in_hbm(ups[0]), ups[1],
      in_hbm(downs[0]), downs[1])


def finish_kernel(lengths, here, there, gain, shift, own, other, pool):
    rank = lax.axis_index("tp")
    length = lengths[rank & 1]
    share = own.shape[0]
    total = here[...] + there[...].astype(F32)
    hidden = layer_norm(total, gain[...], shift[...]).astype(BF16)
    own[...] = hidden[:share]
    other[...] = hidden[share:]
    index = lax.broadcasted_iota(I32, (2 * share, 1), 0)
    pos = ((index // share) ^ rank) * share + index % share
    valid = jnp.where(pos < length, hidden.astype(F32), F32(0.0))
    pool[...] = jnp.sum(valid, axis=0, keepdims=True)


def finish(lengths, here, there, gain, shift):
    half, width = here.shape
    block = jax.ShapeDtypeStruct((half // 2, width), BF16)
    return pl.pallas_call(
        finish_kernel,
        out_shape=(block, block, jax.ShapeDtypeStruct((1, width), F32)),
        in_specs=[SMEM] + [VMEM] * 4,
        out_specs=(VMEM, VMEM, VMEM),
        compiler_params=params(8),
        cost_estimate=cost(2),
        name="finish",
    )(lengths, here, there, gain, shift)


def score_kernel(
    lengths, pool, pool_core, pool_chip, pool_diag, rows, own, other, out, hidden_out
):
    core = lax.axis_index("tp") & 1
    width = pool.shape[1]
    mine = pool[...] + pool_chip[...]
    theirs = pool_core[...] + pool_diag[...]
    first = jnp.where(core == 0, mine, theirs) / lengths[0].astype(F32)
    second = jnp.where(core == 0, theirs, mine) / lengths[1].astype(F32)
    row = lax.broadcasted_iota(I32, (8, width), 0)
    pooled = jnp.where(row == 0, first, jnp.where(row == 1, second, F32(0.0)))
    scale = lax.rsqrt(jnp.mean(pooled * pooled, axis=-1, keepdims=True) + norm_eps)
    queries = (pooled * scale).astype(BF16)
    found = lax.dot_general(
        queries, rows[...], (((1,), (1,)), ((), ())), preferred_element_type=F32
    )
    each = rows.shape[0] // 2
    out[0:1, :] = found[0:1, :each]
    out[1:2, :] = found[1:2, each:]
    hidden_out[core] = own[...]
    hidden_out[1 - core] = other[...]


def score(lengths, pools, rows, own, other):
    return pl.pallas_call(
        score_kernel,
        out_shape=(
            jax.ShapeDtypeStruct((2, rows.shape[0] // 2), F32),
            jax.ShapeDtypeStruct((2,) + own.shape, BF16),
        ),
        in_specs=[SMEM] + [VMEM] * 7,
        out_specs=(VMEM, VMEM),
        compiler_params=params(8),
        cost_estimate=cost(1),
        name="score",
    )(lengths, *pools, rows, own, other)


def source_order(groups):
    order = [0]
    mask = groups // 2
    while mask >= 4:
        order = order + [entry + mask for entry in order]
        mask //= 2
    return [entry + last for last in range(4) for entry in order]


def as_ones(mask):
    return mask.astype(F32).astype(BF16)


def plan_rows(first_place, rows_here, parts, numbers, place, rounds):
    rank = lax.axis_index("tp")
    group = lax.axis_index("req")
    groups = parts[0].shape[0]
    slots = groups * SLOTS
    ids = jnp.concatenate([part[...] for part in parts], axis=1)
    count = ids.shape[1]
    owner = lax.shift_right_logical(ids, I32(rows_here.bit_length() - 1))
    before = as_ones(
        lax.broadcasted_iota(I32, (count, count), 0)
        < lax.broadcasted_iota(I32, (count, count), 1)
    )
    ones = jnp.ones((count, 128), BF16)
    slot = lax.broadcasted_iota(I32, (SLOTS, 1), 0) + first_place

    mine = owner == group * 4 + rank
    asked = jnp.concatenate(
        [
            (owner[:1] == (group ^ source) * 4 + rank).astype(F32)
            for source in source_order(groups)
        ]
    )
    both = jnp.concatenate([mine.astype(F32), asked]).astype(BF16)
    ranks = matmul(both, before).astype(I32)
    send_rank = jnp.where(mine, ranks[:groups], -1)
    take_rank = jnp.where(asked > 0, ranks[groups:], -1)

    local = jnp.where(mine, ids - (group * 4 + rank) * rows_here, 0)
    high = (local >> 6).astype(F32).astype(BF16)
    low = (local & 63).astype(F32).astype(BF16)
    chosen = jnp.concatenate(
        [(send_rank[k : k + 1] == slot).astype(F32) for k in range(groups)]
    ).astype(BF16)
    spread = (((1,), (1,)), ((), ()))
    wanted = 64.0 * lax.dot_general(high, chosen, spread, preferred_element_type=F32)
    wanted = wanted + lax.dot_general(low, chosen, spread, preferred_element_type=F32)
    counts = matmul(as_ones(mine), jnp.ones((count, slots), BF16))
    own = lax.broadcasted_iota(I32, (groups, slots), 0) == lax.div(
        lax.broadcasted_iota(I32, (groups, slots), 1), I32(SLOTS)
    )
    numbers[0:1, :] = jnp.sum(jnp.where(own, wanted, 0.0), axis=0, keepdims=True).astype(I32)
    counts = jnp.sum(jnp.where(own, counts, 0.0), axis=0, keepdims=True).astype(I32)
    numbers[1:2, :] = counts - first_place

    for k in range(groups):
        place[k * SLOTS : (k + 1) * SLOTS, :] = as_ones(take_rank[k : k + 1] == slot)
    shard = lax.broadcasted_iota(I32, (4 * groups, 1), 0)
    load = jnp.concatenate(
        [(owner[k : k + 1] == shard).astype(F32) for k in range(groups)]
    ).astype(BF16)
    most = jnp.max(matmul(load, ones)).astype(I32)
    rounds[0] = (most + SLOTS - 1) // SLOTS - 1


def fetch_rows(chosen, index, tiles, rows, sems):
    deep = tiles.shape[1]
    slots = tiles.shape[0]
    step = 4

    def tile_copy(slot):
        first = pl.multiple_of((chosen[0, slot] // deep) * deep, deep)
        return pltpu.make_async_copy(index.at[pl.ds(first, deep)], tiles.at[slot], sems.at[slot])

    def start(number, carry):
        for each in range(step):
            tile_copy(number * step + each).start()
        return carry

    def select(number, carry):
        for each in range(step):
            tile_copy(number * step + each).wait()
        for each in range(step):
            source = number * step + each
            line = lax.broadcasted_iota(I32, (deep, 1), 0) == chosen[0, source] % deep
            row = jnp.where(line, tiles[source].astype(F32), F32(0.0))
            rows[pl.ds(source, 1), :] = jnp.sum(row, axis=0, keepdims=True)
        return carry

    def each_group(action):
        def one(number, carry):
            first = number * (SLOTS // step)
            left = jnp.clip(chosen[1, number * SLOTS], 0, SLOTS)
            return lax.fori_loop(first, first + (left + step - 1) // step, action, carry)

        lax.fori_loop(0, slots // SLOTS, one, 0)

    rows[...] = jnp.zeros_like(rows)
    each_group(start)

    def finish_rows(keep, send):
        each_group(select)
        keep[...] = rows[: slots // 2, :].astype(BF16)
        send[...] = rows[slots // 2 :, :].astype(BF16)

    return finish_rows


def take_kernel(
    number, i0, i1, index, keep, send, place, rounds, numbers, chosen, tiles, rows,
    sems, sem,
):
    plan_rows(number[0] * SLOTS, index.shape[0], (i0, i1), numbers, place, rounds)
    copy = pltpu.make_async_copy(numbers, chosen, sem)
    copy.start()
    copy.wait()
    fetch_rows(chosen, index, tiles, rows, sems)(keep, send)


def fetch_scratch(slots, width):
    return [
        pltpu.SMEM((2, slots), I32),
        pltpu.VMEM((slots, 16, width), BF16),
        pltpu.VMEM((slots, width), F32),
        pltpu.SemaphoreType.DMA((slots,)),
        pltpu.SemaphoreType.DMA,
    ]


def take_rows(number, ids, index_rows):
    groups, each = ids[0].shape
    slots = groups * SLOTS
    width = index_rows.shape[1]
    half = jax.ShapeDtypeStruct((slots // 2, width), BF16)
    return pl.pallas_call(
        take_kernel,
        out_shape=(
            half,
            half,
            jax.ShapeDtypeStruct((slots, 2 * each), BF16),
            jax.ShapeDtypeStruct((1,), I32),
        ),
        in_specs=[SMEM] + [VMEM] * 2 + [HBM],
        out_specs=(VMEM, VMEM, VMEM, SMEM),
        scratch_shapes=[pltpu.VMEM((2, slots), I32)] + fetch_scratch(slots, width),
        compiler_params=params(8 + slots // 16),
        cost_estimate=NO_COST,
        name="take_rows",
    )(number, *ids, in_hbm(index_rows))


def place_kernel(place, h0, h1, h2, h3, out):
    received = jnp.concatenate([h0[...], h1[...], h2[...], h3[...]])
    chosen = lax.dot_general(
        place[...], received, (((0,), (0,)), ((), ())), preferred_element_type=F32
    )
    out[...] = chosen.astype(BF16)


def place_rows(place, received):
    return pl.pallas_call(
        place_kernel,
        out_shape=jax.ShapeDtypeStruct((place.shape[1], received[0].shape[1]), BF16),
        in_specs=[VMEM] * 5,
        out_specs=VMEM,
        compiler_params=params(8),
        cost_estimate=NO_COST,
        name="place_rows",
    )(place, *received)


def masks(axis):
    mask = 1
    while mask < lax.axis_size(axis):
        yield mask
        mask *= 2


def row_exchange(ids, index_rows, place, rounds):
    width = index_rows.shape[1]

    def gathered(keep, send, place, gates=((), (), ())):
        keep = keep.reshape(1, -1, SLOTS, width)
        send = send.reshape(1, -1, SLOTS, width)
        held = None
        for mask in list(masks("req"))[:1:-1]:
            if held is not None:
                keep, send = held[:, :mask], held[:, mask:]
            other = swap(send, "req", mask)
            if mask == 4:
                other = after(other, *gates[0])
            held = jnp.concatenate([keep, other])
        others = [swap(held[:, mask], "req", mask) for mask in (1, 2, 3)]
        others = list(after(tuple(others), *gates[1]))
        held = [part.reshape(-1, width) for part in [held[:, 0]] + others]
        found = place_rows(place, held)
        found = after(found, *gates[2]).reshape(4, -1, width)
        parts = [swap(found[place], "tp", mask) for place, mask in ((1, 2), (2, 1), (3, 3))]
        return found[0] + parts[0] + parts[1] + parts[2]

    def one_more(state):
        number, total = state
        keep, send, place, _ = take_rows(number.reshape(1), ids, index_rows)
        return number - 1, total + gathered(keep, send, place)

    def further(rows, *gate):
        left = after(rounds, *gate)[0]
        return lax.while_loop(lambda state: state[0] > 0, one_more, (left, rows))[1]

    return lambda keep, send, *gates: gathered(keep, send, place, gates), further


def per_device(
    states,
    lengths,
    w_qkv,
    b_qkv,
    w_out,
    b_out,
    ln1_gain,
    ln1_shift,
    w_up,
    b_up,
    w_down,
    b_down,
    ln2_gain,
    ln2_shift,
    index_rows,
    cand_ids,
):
    from_core = swap(states, "tp", 1)
    w_qkv_t = w_qkv.transpose(1, 0, 2)
    w_qkv_p = swap(w_qkv_t, "tp", 1)
    b_qkv_p = swap(b_qkv, "tp", 1)
    b_up_p = swap(b_up, "tp", 1)

    held = cand_ids.reshape(1, -1)
    held = jnp.concatenate([held, swap(held, "tp", 2)], axis=1)
    from_chip = swap(after(states, held), "tp", 2)
    for mask in masks("req"):
        other = swap(held, "req", mask)
        if mask * 2 == lax.axis_size("req"):
            mine, w_here, w_half = load(states, w_qkv_t, after(w_out, held))
            other, mine = lax.optimization_barrier((other, mine))
        held = jnp.concatenate([held, other])
    from_chip, held, from_core, w_qkv_p, b_qkv_p, b_up_p = lax.optimization_barrier(
        (from_chip, held, from_core, w_qkv_p, b_qkv_p, b_up_p)
    )
    w_out_p = swap(after(w_out, from_chip), "tp", 1)
    from_diag = swap(from_chip, "tp", 1)
    blocks = (mine, from_core, from_chip, from_diag)
    ids = (held, swap(held, "tp", 1))
    w_up_p = swap(after(w_up, from_diag, w_out_p, *ids), "tp", 1)
    w_down_p = swap(after(w_down, from_diag, w_out_p, *ids), "tp", 1)
    w_x0 = swap(w_half, "tp", 2)

    blocks, ids, w_out_p = lax.optimization_barrier((blocks, ids, w_out_p))
    context_0, text = first_attention(lengths, blocks, w_here, b_qkv)
    context_0x = swap(context_0, "tp", 2)
    context_1, numbers, place, rounds = second_attention(
        lengths, after(text, w_up_p), w_qkv_p, b_qkv_p, ids, index_rows.shape[0]
    )
    context_1x = swap(context_1, "tp", 2)
    w_x1 = swap(after(w_x0, context_1), "req", 1)

    base, keep, send = project_first(
        text, after(context_0, context_0x), w_out, b_out[None], numbers, index_rows
    )
    w_d0 = swap(after(w_x0, base), "tp", 1)
    w_d1 = swap(after(w_x1, base), "tp", 1)
    base = project_second(base, context_1, w_out_p, context_0x, (w_x0, w_x1))
    gathered, further = row_exchange(ids, index_rows, place, rounds)
    common = (
        context_1x, (w_d0, w_d1), ln1_gain[None], ln1_shift[None],
        (b_up[None], b_up_p[None]), b_down[None], (w_up, w_up_p),
        (w_down, w_down_p),
    )
    down_there = feed_forward(False, base, *common)
    down_x = swap(down_there, "tp", 2)
    down_here = feed_forward(True, after(base, down_there), *common)
    down_x = after(down_x, down_here)
    hidden, hidden_other, pool = finish(
        lengths, down_here, down_x, ln2_gain[None], ln2_shift[None]
    )

    rows = gathered(keep, send, (down_there,), (down_here,), ())
    pools = (pool,) + tuple(swap(pool, "tp", mask) for mask in (1, 2, 3))
    hidden_p = swap(hidden_other, "tp", 1)
    rows = further(after(rows, *pools), *pools)
    scores, hidden_out = score(lengths, pools, rows, hidden, hidden_p)
    return (hidden_out, scores)


def solution(mesh):
    placed = (
        P("req", "tp", None),
        P("req"),
        P(None, None, "tp"),
        P(None, "tp"),
        P("tp", None),
        P(),
        P(),
        P(),
        P(None, "tp"),
        P("tp"),
        P("tp", None),
        P(),
        P(),
        P(),
        P(("req", "tp"), None),
        P("req", "tp"),
    )
    return jax.shard_map(
        per_device,
        mesh=mesh,
        in_specs=placed,
        out_specs=(P("req", "tp", None), P("req", "tp")),
        check_vma=False,
    )
```

```python
import functools

import jax
import jax.numpy as jnp
from jax import lax
from jax.experimental import pallas as pl
from jax.experimental.pallas import tpu as pltpu
from jax.sharding import PartitionSpec as P

HEAD_DIM = 64
WINDOW = 512
SLOTS = 16
BF16 = jnp.bfloat16
F32 = jnp.float32
I32 = jnp.int32
MIB = 1024 * 1024
NO_COST = pl.CostEstimate(flops=1, bytes_accessed=1, transcendentals=0)


def cost(gflop):
    return pl.CostEstimate(flops=int(gflop * 10**9) + 1, bytes_accessed=MIB, transcendentals=0)


layer_eps = 1e-05
norm_eps = 1e-06

VMEM = pl.BlockSpec(memory_space=pltpu.VMEM)
SMEM = pl.BlockSpec(memory_space=pltpu.SMEM)
HBM = pl.BlockSpec(memory_space=pltpu.HBM)
ANY = pl.BlockSpec(memory_space=pl.ANY)


def layer_norm(values, gain, shift):
    centre = values - jnp.mean(values, axis=-1, keepdims=True)
    spread = jnp.mean(centre * centre, axis=-1, keepdims=True)
    return centre * lax.rsqrt(spread + layer_eps) * gain + shift


def in_hbm(array):
    return pltpu.with_memory_space_constraint(array, pltpu.HBM)


def swap(value, axis, mask):
    count = lax.axis_size(axis)
    return lax.ppermute(value, axis, [(i, i ^ mask) for i in range(count)])


def matmul(left, right):
    return jnp.dot(left, right, preferred_element_type=F32)


def params(mib):
    return pltpu.CompilerParams(vmem_limit_bytes=mib * MIB)


def after(value, *others):
    return lax.optimization_barrier((value,) + others)[0]


def load_kernel(states, w, w_out, mine, w_here, half, sems):
    part = half.shape[0]
    first = pl.multiple_of((lax.axis_index("req") & 1) * part, part)
    copies = [
        pltpu.make_async_copy(source, target, sems.at[number])
        for number, (source, target) in enumerate(
            (
                (w_out.at[pl.ds(first, part)], half),
                (states.at[lax.axis_index("tp") & 1], mine),
                (w, w_here),
            )
        )
    ]
    for copy in copies:
        copy.start()
    for copy in copies:
        copy.wait()


def load(states, w, w_out):
    return pl.pallas_call(
        load_kernel,
        out_shape=(
            jax.ShapeDtypeStruct(states.shape[1:], BF16),
            jax.ShapeDtypeStruct(w.shape, BF16),
            jax.ShapeDtypeStruct((w_out.shape[0] // 2, w_out.shape[1]), BF16),
        ),
        in_specs=[HBM] * 3,
        out_specs=(VMEM, VMEM, VMEM),
        scratch_shapes=[pltpu.SemaphoreType.DMA((3,))],
        compiler_params=params(6),
        cost_estimate=NO_COST,
        name="load",
    )(in_hbm(states), in_hbm(w), in_hbm(w_out))


def first_attention_kernel(lengths, mine, s1, s2, s3, w, b, out, text, parts, bias):
    core = lax.axis_index("tp") & 1
    text[...] = jnp.concatenate([mine[...], s1[core], s2[core], s3[core]])
    for which in range(3):
        project(which, text, w, b, parts)
    attend(lengths, parts, bias, out)


def second_attention_kernel(
    rows_here, lengths, text, w, b, i0, i1, out, numbers, place, rounds, parts, bias
):
    plan_rows(0, rows_here, (i0, i1), numbers, place, rounds)
    for which in range(3):
        project(which, text, w, b, parts)
    attend(lengths, parts, bias, out)


def project(which, text, w, b, parts):
    parts[which] = (matmul(text[...], w[which]) + b[which : which + 1, :]).astype(BF16)


def attend(lengths, parts, bias, out):
    rank = lax.axis_index("tp")
    length = lengths[rank & 1]
    _, seq_len, wide = parts.shape
    share = seq_len // 4

    def position(index):
        return ((index // share) ^ rank) * share + index % share

    row_pos = position(lax.broadcasted_iota(I32, (seq_len, 1), 0))
    col_pos = position(lax.broadcasted_iota(I32, (1, seq_len), 1))
    keep = (jnp.abs(row_pos - col_pos) <= WINDOW // 2) & (col_pos < length)
    bias[...] = jnp.where(keep, F32(0.0), F32(-1e30))
    ones = jnp.ones((seq_len, 128), BF16)
    low = lax.broadcasted_iota(I32, (1, 128), 1) < HEAD_DIM
    scale = jnp.asarray(HEAD_DIM**-0.5, BF16)
    for pair in range(wide // 128):
        lanes = slice(pair * 128, (pair + 1) * 128)
        k_pair = parts[1, :, lanes]
        v_ones = jnp.concatenate([parts[2, :, lanes], ones], axis=1)
        for block in range(2):
            rows = slice(2 * block * share, 2 * (block + 1) * share)
            q_pair = parts[0, rows, lanes] * scale
            zero = jnp.zeros((), BF16)
            q_heads = jnp.concatenate(
                [jnp.where(low, q_pair, zero), jnp.where(low, zero, q_pair)]
            )
            logits = lax.dot_general(
                q_heads, k_pair, (((1,), (1,)), ((), ())), preferred_element_type=F32
            )
            masked = bias[rows, :]
            logits = logits + jnp.concatenate([masked, masked])
            top = jnp.max(logits, axis=-1, keepdims=True)
            expo = jnp.exp(logits - top).astype(BF16)
            summed = matmul(expo, v_ones)
            found = summed[:, :128] / summed[:, 128:]
            context = jnp.where(low, found[: 2 * share], found[2 * share :])
            context = jnp.where(row_pos[rows] < length, context, F32(0.0))
            out[rows, lanes] = context.astype(BF16)


def attention_scratch(seq_len, wide):
    return [pltpu.VMEM((3, seq_len, wide), BF16), pltpu.VMEM((seq_len, seq_len), F32)]


def first_attention(lengths, blocks, w, b):
    share, width = blocks[0].shape
    wide = w.shape[2]
    return pl.pallas_call(
        first_attention_kernel,
        out_shape=(
            jax.ShapeDtypeStruct((4 * share, wide), BF16),
            jax.ShapeDtypeStruct((4 * share, width), BF16),
        ),
        in_specs=[SMEM] + [VMEM] * 6,
        out_specs=(VMEM, VMEM),
        scratch_shapes=attention_scratch(4 * share, wide),
        compiler_params=params(12),
        cost_estimate=NO_COST,
        name="attention_own",
    )(in_hbm(lengths), *blocks, w, in_hbm(b))


def second_attention(lengths, text, w, b, ids, rows_here):
    seq_len = text.shape[0]
    wide = w.shape[2]
    groups, each = ids[0].shape
    return pl.pallas_call(
        functools.partial(second_attention_kernel, rows_here),
        out_shape=(
            jax.ShapeDtypeStruct((seq_len, wide), BF16),
            jax.ShapeDtypeStruct((2, groups * SLOTS), I32),
            jax.ShapeDtypeStruct((groups * SLOTS, 2 * each), BF16),
            jax.ShapeDtypeStruct((1,), I32),
        ),
        in_specs=[SMEM] + [VMEM] * 5,
        out_specs=(VMEM, VMEM, VMEM, SMEM),
        scratch_shapes=attention_scratch(seq_len, wide),
        compiler_params=params(12),
        cost_estimate=cost(6),
        name="attention_partner",
    )(in_hbm(lengths), text, w, b, *ids)


def joined(first, second):
    swapped = (lax.axis_index("req") & 1) != 0
    low = jnp.where(swapped, second[...], first[...])
    high = jnp.where(swapped, first[...], second[...])
    return jnp.concatenate([low, high])


def project_first_kernel(
    text, here, w, b, numbers, index, out, keep, send,
    chosen, tiles, rows, sems, sem,
):
    copy = pltpu.make_async_copy(numbers, chosen, sem)
    copy.start()
    copy.wait()
    finish_rows = fetch_rows(chosen, index, tiles, rows, sems)
    out[...] = matmul(here[...], w[...]) + (text[...].astype(F32) + b[...])
    finish_rows(keep, send)


def project_first(text, here, w, b_out, numbers, index_rows):
    seq_len, width = text.shape
    slots = numbers.shape[1]
    half = jax.ShapeDtypeStruct((slots // 2, width), BF16)
    return pl.pallas_call(
        project_first_kernel,
        out_shape=(jax.ShapeDtypeStruct((seq_len, width), F32), half, half),
        in_specs=[VMEM] * 5 + [HBM],
        out_specs=(VMEM, VMEM, VMEM),
        scratch_shapes=fetch_scratch(slots, width),
        compiler_params=params(12 + slots // 16),
        cost_estimate=cost(1),
        name="project_first",
    )(text, here, w, b_out, numbers, in_hbm(index_rows))


def project_second_kernel(base, context, w, there, half_0, half_1, out):
    half = base.shape[0] // 2
    w_there = joined(half_0, half_1)
    for number in range(2):
        span = slice(number * half, (number + 1) * half)
        other = slice((1 - number) * half, (2 - number) * half)
        total = matmul(context[span, :], w[...]) + matmul(there[other, :], w_there)
        out[span, :] = base[span, :] + total


def project_second(base, context, w, there, halves):
    return pl.pallas_call(
        project_second_kernel,
        out_shape=jax.ShapeDtypeStruct(base.shape, F32),
        in_specs=[VMEM] * 6,
        out_specs=VMEM,
        input_output_aliases={0: 0},
        compiler_params=params(12),
        cost_estimate=cost(1),
        name="project_second",
    )(base, context, w, there, *halves)


def feed_kernel(
    keep_rest, base, c3, half_0, half_1, gain, shift, b0, b1, b_down,
    up_own, up_partner, down_own, down_partner, out, up_buf, down_buf, act, sems,
):
    hidden = up_own.shape[1]
    up_copy = pltpu.make_async_copy(up_own, up_buf, sems.at[0])
    down_copy = pltpu.make_async_copy(down_own, down_buf, sems.at[1])
    up_copy.start()
    down_copy.start()
    total = base[...] + matmul(c3[...], joined(half_0, half_1))
    normed = layer_norm(total, gain[...], shift[...]).astype(BF16)
    step = 512
    for part, (weight, bias) in enumerate(((up_partner, b1), (up_buf, b0))):
        if part == 1:
            up_copy.wait()
        for low in range(0, hidden, step):
            lanes = slice(low, low + step)
            up = matmul(normed, weight[:, lanes]) + bias[:, lanes]
            activated = 0.5 * up * (1.0 + lax.erf(up * F32(0.5**0.5)))
            act[:, part * hidden + low : part * hidden + low + step] = activated.astype(BF16)
    down = matmul(act[:, :hidden], down_partner[...])
    down_copy.wait()
    down = down + matmul(act[:, hidden:], down_buf[...])
    if keep_rest:
        down = down + (normed.astype(F32) + b_down[...])
    out[...] = down.astype(out.dtype)


def feed_forward(keep_rest, base, context, halves, gain, shift, biases, b_down, ups, downs):
    seq_len, width = base.shape
    half = seq_len // 2
    here = 0 if keep_rest else 1
    hidden = ups[0].shape[1]
    heads_wide = context.shape[1]
    base_spec = pl.BlockSpec((half, width), lambda i: (here, 0))
    context_spec = pl.BlockSpec((half, heads_wide), lambda i: (1 - here, 0))
    return pl.pallas_call(
        lambda *refs: feed_kernel(keep_rest, *refs),
        out_shape=jax.ShapeDtypeStruct((half, width), F32 if keep_rest else BF16),
        grid=(1,),
        in_specs=[base_spec, context_spec] + [VMEM] * 7
        + [HBM, VMEM, HBM, VMEM],
        out_specs=VMEM,
        scratch_shapes=[
            pltpu.VMEM((width, hidden), BF16),
            pltpu.VMEM((hidden, width), BF16),
            pltpu.VMEM((half, 2 * hidden), BF16),
            pltpu.SemaphoreType.DMA((2,)),
        ],
        compiler_params=params(20),
        cost_estimate=cost(8),
        name="feed_here" if keep_rest else "feed_there",
    )(base, context, *halves, gain, shift, *biases, b_down, in_hbm(ups[0]), ups[1],
      in_hbm(downs[0]), downs[1])


def finish_kernel(lengths, here, there, gain, shift, own, other, pool):
    rank = lax.axis_index("tp")
    length = lengths[rank & 1]
    share = own.shape[0]
    total = here[...] + there[...].astype(F32)
    hidden = layer_norm(total, gain[...], shift[...]).astype(BF16)
    own[...] = hidden[:share]
    other[...] = hidden[share:]
    index = lax.broadcasted_iota(I32, (2 * share, 1), 0)
    pos = ((index // share) ^ rank) * share + index % share
    valid = jnp.where(pos < length, hidden.astype(F32), F32(0.0))
    pool[...] = jnp.sum(valid, axis=0, keepdims=True)


def finish(lengths, here, there, gain, shift):
    half, width = here.shape
    block = jax.ShapeDtypeStruct((half // 2, width), BF16)
    return pl.pallas_call(
        finish_kernel,
        out_shape=(block, block, jax.ShapeDtypeStruct((1, width), F32)),
        in_specs=[SMEM] + [VMEM] * 4,
        out_specs=(VMEM, VMEM, VMEM),
        compiler_params=params(8),
        cost_estimate=cost(2),
        name="finish",
    )(lengths, here, there, gain, shift)


def score_kernel(
    lengths, pool, pool_core, pool_chip, pool_diag, rows, own, other, out, hidden_out
):
    core = lax.axis_index("tp") & 1
    width = pool.shape[1]
    mine = pool[...] + pool_chip[...]
    theirs = pool_core[...] + pool_diag[...]
    first = jnp.where(core == 0, mine, theirs) / lengths[0].astype(F32)
    second = jnp.where(core == 0, theirs, mine) / lengths[1].astype(F32)
    row = lax.broadcasted_iota(I32, (8, width), 0)
    pooled = jnp.where(row == 0, first, jnp.where(row == 1, second, F32(0.0)))
    scale = lax.rsqrt(jnp.mean(pooled * pooled, axis=-1, keepdims=True) + norm_eps)
    queries = (pooled * scale).astype(BF16)
    found = lax.dot_general(
        queries, rows[...], (((1,), (1,)), ((), ())), preferred_element_type=F32
    )
    each = rows.shape[0] // 2
    out[0:1, :] = found[0:1, :each]
    out[1:2, :] = found[1:2, each:]
    hidden_out[core] = own[...]
    hidden_out[1 - core] = other[...]


def score(lengths, pools, rows, own, other):
    return pl.pallas_call(
        score_kernel,
        out_shape=(
            jax.ShapeDtypeStruct((2, rows.shape[0] // 2), F32),
            jax.ShapeDtypeStruct((2,) + own.shape, BF16),
        ),
        in_specs=[SMEM] + [VMEM] * 7,
        out_specs=(VMEM, VMEM),
        compiler_params=params(8),
        cost_estimate=cost(1),
        name="score",
    )(lengths, *pools, rows, own, other)


def source_order(groups):
    order = [0]
    mask = groups // 2
    while mask >= 4:
        order = order + [entry + mask for entry in order]
        mask //= 2
    return [entry + last for last in range(4) for entry in order]


def as_ones(mask):
    return mask.astype(F32).astype(BF16)


def plan_rows(first_place, rows_here, parts, numbers, place, rounds):
    rank = lax.axis_index("tp")
    group = lax.axis_index("req")
    groups = parts[0].shape[0]
    slots = groups * SLOTS
    ids = jnp.concatenate([part[...] for part in parts], axis=1)
    count = ids.shape[1]
    owner = lax.shift_right_logical(ids, I32(rows_here.bit_length() - 1))
    before = as_ones(
        lax.broadcasted_iota(I32, (count, count), 0)
        < lax.broadcasted_iota(I32, (count, count), 1)
    )
    ones = jnp.ones((count, 128), BF16)
    slot = lax.broadcasted_iota(I32, (SLOTS, 1), 0) + first_place

    mine = owner == group * 4 + rank
    asked = jnp.concatenate(
        [
            (owner[:1] == (group ^ source) * 4 + rank).astype(F32)
            for source in source_order(groups)
        ]
    )
    both = jnp.concatenate([mine.astype(F32), asked]).astype(BF16)
    ranks = matmul(both, before).astype(I32)
    send_rank = jnp.where(mine, ranks[:groups], -1)
    take_rank = jnp.where(asked > 0, ranks[groups:], -1)

    local = jnp.where(mine, ids - (group * 4 + rank) * rows_here, 0)
    high = (local >> 6).astype(F32).astype(BF16)
    low = (local & 63).astype(F32).astype(BF16)
    chosen = jnp.concatenate(
        [(send_rank[k : k + 1] == slot).astype(F32) for k in range(groups)]
    ).astype(BF16)
    spread = (((1,), (1,)), ((), ()))
    wanted = 64.0 * lax.dot_general(high, chosen, spread, preferred_element_type=F32)
    wanted = wanted + lax.dot_general(low, chosen, spread, preferred_element_type=F32)
    counts = matmul(as_ones(mine), jnp.ones((count, slots), BF16))
    own = lax.broadcasted_iota(I32, (groups, slots), 0) == lax.div(
        lax.broadcasted_iota(I32, (groups, slots), 1), I32(SLOTS)
    )
    numbers[0:1, :] = jnp.sum(jnp.where(own, wanted, 0.0), axis=0, keepdims=True).astype(I32)
    counts = jnp.sum(jnp.where(own, counts, 0.0), axis=0, keepdims=True).astype(I32)
    numbers[1:2, :] = counts - first_place

    for k in range(groups):
        place[k * SLOTS : (k + 1) * SLOTS, :] = as_ones(take_rank[k : k + 1] == slot)
    shard = lax.broadcasted_iota(I32, (4 * groups, 1), 0)
    load = jnp.concatenate(
        [(owner[k : k + 1] == shard).astype(F32) for k in range(groups)]
    ).astype(BF16)
    most = jnp.max(matmul(load, ones)).astype(I32)
    rounds[0] = (most + SLOTS - 1) // SLOTS - 1


def fetch_rows(chosen, index, tiles, rows, sems):
    deep = tiles.shape[1]
    slots = tiles.shape[0]
    step = 4

    def tile_copy(slot):
        first = pl.multiple_of((chosen[0, slot] // deep) * deep, deep)
        return pltpu.make_async_copy(index.at[pl.ds(first, deep)], tiles.at[slot], sems.at[slot])

    def start(number, carry):
        for each in range(step):
            tile_copy(number * step + each).start()
        return carry

    def select(number, carry):
        for each in range(step):
            tile_copy(number * step + each).wait()
        for each in range(step):
            source = number * step + each
            line = lax.broadcasted_iota(I32, (deep, 1), 0) == chosen[0, source] % deep
            row = jnp.where(line, tiles[source].astype(F32), F32(0.0))
            rows[pl.ds(source, 1), :] = jnp.sum(row, axis=0, keepdims=True)
        return carry

    def each_group(action):
        def one(number, carry):
            first = number * (SLOTS // step)
            left = jnp.clip(chosen[1, number * SLOTS], 0, SLOTS)
            return lax.fori_loop(first, first + (left + step - 1) // step, action, carry)

        lax.fori_loop(0, slots // SLOTS, one, 0)

    rows[...] = jnp.zeros_like(rows)
    each_group(start)

    def finish_rows(keep, send):
        each_group(select)
        keep[...] = rows[: slots // 2, :].astype(BF16)
        send[...] = rows[slots // 2 :, :].astype(BF16)

    return finish_rows


def take_kernel(
    number, i0, i1, index, keep, send, place, rounds, numbers, chosen, tiles, rows,
    sems, sem,
):
    plan_rows(number[0] * SLOTS, index.shape[0], (i0, i1), numbers, place, rounds)
    copy = pltpu.make_async_copy(numbers, chosen, sem)
    copy.start()
    copy.wait()
    fetch_rows(chosen, index, tiles, rows, sems)(keep, send)


def fetch_scratch(slots, width):
    return [
        pltpu.SMEM((2, slots), I32),
        pltpu.VMEM((slots, 16, width), BF16),
        pltpu.VMEM((slots, width), F32),
        pltpu.SemaphoreType.DMA((slots,)),
        pltpu.SemaphoreType.DMA,
    ]


def take_rows(number, ids, index_rows):
    groups, each = ids[0].shape
    slots = groups * SLOTS
    width = index_rows.shape[1]
    half = jax.ShapeDtypeStruct((slots // 2, width), BF16)
    return pl.pallas_call(
        take_kernel,
        out_shape=(
            half,
            half,
            jax.ShapeDtypeStruct((slots, 2 * each), BF16),
            jax.ShapeDtypeStruct((1,), I32),
        ),
        in_specs=[SMEM] + [VMEM] * 2 + [HBM],
        out_specs=(VMEM, VMEM, VMEM, SMEM),
        scratch_shapes=[pltpu.VMEM((2, slots), I32)] + fetch_scratch(slots, width),
        compiler_params=params(8 + slots // 16),
        cost_estimate=NO_COST,
        name="take_rows",
    )(number, *ids, in_hbm(index_rows))


def place_kernel(place, h0, h1, h2, h3, out):
    received = jnp.concatenate([h0[...], h1[...], h2[...], h3[...]])
    chosen = lax.dot_general(
        place[...], received, (((0,), (0,)), ((), ())), preferred_element_type=F32
    )
    out[...] = chosen.astype(BF16)


def place_rows(place, received):
    return pl.pallas_call(
        place_kernel,
        out_shape=jax.ShapeDtypeStruct((place.shape[1], received[0].shape[1]), BF16),
        in_specs=[VMEM] * 5,
        out_specs=VMEM,
        compiler_params=params(8),
        cost_estimate=NO_COST,
        name="place_rows",
    )(place, *received)


def masks(axis):
    mask = 1
    while mask < lax.axis_size(axis):
        yield mask
        mask *= 2


def row_exchange(ids, index_rows, place, rounds):
    width = index_rows.shape[1]

    def gathered(keep, send, place, gates=((), (), ())):
        keep = keep.reshape(1, -1, SLOTS, width)
        send = send.reshape(1, -1, SLOTS, width)
        held = None
        for mask in list(masks("req"))[:1:-1]:
            if held is not None:
                keep, send = held[:, :mask], held[:, mask:]
            other = swap(send, "req", mask)
            if mask == 4:
                other = after(other, *gates[0])
            held = jnp.concatenate([keep, other])
        others = [swap(held[:, mask], "req", mask) for mask in (1, 2, 3)]
        others = list(after(tuple(others), *gates[1]))
        held = [part.reshape(-1, width) for part in [held[:, 0]] + others]
        found = place_rows(place, held)
        found = after(found, *gates[2]).reshape(4, -1, width)
        parts = [swap(found[place], "tp", mask) for place, mask in ((1, 2), (2, 1), (3, 3))]
        return found[0] + parts[0] + parts[1] + parts[2]

    def one_more(state):
        number, total = state
        keep, send, place, _ = take_rows(number.reshape(1), ids, index_rows)
        return number - 1, total + gathered(keep, send, place)

    def further(rows, *gate):
        left = after(rounds, *gate)[0]
        return lax.while_loop(lambda state: state[0] > 0, one_more, (left, rows))[1]

    return lambda keep, send, *gates: gathered(keep, send, place, gates), further


def per_device(
    states,
    lengths,
    w_qkv,
    b_qkv,
    w_out,
    b_out,
    ln1_gain,
    ln1_shift,
    w_up,
    b_up,
    w_down,
    b_down,
    ln2_gain,
    ln2_shift,
    index_rows,
    cand_ids,
):
    from_core = swap(states, "tp", 1)
    w_qkv_t = w_qkv.transpose(1, 0, 2)
    w_qkv_p = swap(w_qkv_t, "tp", 1)
    b_qkv_p = swap(b_qkv, "tp", 1)
    b_up_p = swap(b_up, "tp", 1)

    held = jnp.concatenate(
        [cand_ids.reshape(1, -1), swap(cand_ids, "tp", 2).reshape(1, -1)], axis=1
    )
    from_chip = swap(after(states, held), "tp", 2)
    for mask in masks("req"):
        other = swap(held, "req", mask)
        if mask * 2 == lax.axis_size("req"):
            mine, w_here, w_half = load(states, w_qkv_t, after(w_out, held))
            other, mine = lax.optimization_barrier((other, mine))
        held = jnp.concatenate([held, other])
    from_chip, held, from_core, w_qkv_p, b_qkv_p, b_up_p = lax.optimization_barrier(
        (from_chip, held, from_core, w_qkv_p, b_qkv_p, b_up_p)
    )
    w_out_p = swap(after(w_out, from_chip), "tp", 1)
    from_diag = swap(from_chip, "tp", 1)
    blocks = (mine, from_core, from_chip, from_diag)
    ids = (held, swap(held, "tp", 1))
    w_up_p = swap(after(w_up, from_diag, w_out_p, *ids), "tp", 1)
    w_down_p = swap(after(w_down, from_diag, w_out_p, *ids), "tp", 1)
    w_x0 = swap(w_half, "tp", 2)

    blocks, ids, w_out_p = lax.optimization_barrier((blocks, ids, w_out_p))
    context_0, text = first_attention(lengths, blocks, w_here, b_qkv)
    context_0x = swap(context_0, "tp", 2)
    context_1, numbers, place, rounds = second_attention(
        lengths, after(text, w_up_p), w_qkv_p, b_qkv_p, ids, index_rows.shape[0]
    )
    context_1x = swap(context_1, "tp", 2)
    w_x1 = swap(after(w_x0, context_1), "req", 1)

    base, keep, send = project_first(
        text, after(context_0, context_0x), w_out, b_out[None], numbers, index_rows
    )
    w_d0 = swap(after(w_x0, base), "tp", 1)
    w_d1 = swap(after(w_x1, base), "tp", 1)
    base = project_second(base, context_1, w_out_p, context_0x, (w_x0, w_x1))
    gathered, further = row_exchange(ids, index_rows, place, rounds)
    common = (
        context_1x, (w_d0, w_d1), ln1_gain[None], ln1_shift[None],
        (b_up[None], b_up_p[None]), b_down[None], (w_up, w_up_p),
        (w_down, w_down_p),
    )
    down_there = feed_forward(False, base, *common)
    down_x = swap(down_there, "tp", 2)
    down_here = feed_forward(True, after(base, down_there), *common)
    down_x = after(down_x, down_here)
    hidden, hidden_other, pool = finish(
        lengths, down_here, down_x, ln2_gain[None], ln2_shift[None]
    )

    rows = gathered(keep, send, (down_there,), (down_here,), ())
    pools = (pool,) + tuple(swap(pool, "tp", mask) for mask in (1, 2, 3))
    hidden_p = swap(hidden_other, "tp", 1)
    rows = further(after(rows, *pools), *pools)
    scores, hidden_out = score(lengths, pools, rows, hidden, hidden_p)
    return (hidden_out, scores)


def solution(mesh):
    placed = (
        P("req", "tp", None),
        P("req"),
        P(None, None, "tp"),
        P(None, "tp"),
        P("tp", None),
        P(),
        P(),
        P(),
        P(None, "tp"),
        P("tp"),
        P("tp", None),
        P(),
        P(),
        P(),
        P(("req", "tp"), None),
        P("req", "tp"),
    )
    return jax.shard_map(
        per_device,
        mesh=mesh,
        in_specs=placed,
        out_specs=(P("req", "tp", None), P("req", "tp")),
        check_vma=False,
    )
```

```python
import functools

import jax
import jax.numpy as jnp
from jax import lax
from jax.experimental import pallas as pl
from jax.experimental.pallas import tpu as pltpu
from jax.sharding import PartitionSpec as P

HEAD_DIM = 64
WINDOW = 512
SLOTS = 16
BF16 = jnp.bfloat16
F32 = jnp.float32
I32 = jnp.int32
MIB = 1024 * 1024
NO_COST = pl.CostEstimate(flops=1, bytes_accessed=1, transcendentals=0)


def cost(gflop):
    return pl.CostEstimate(flops=int(gflop * 10**9) + 1, bytes_accessed=MIB, transcendentals=0)


layer_eps = 1e-05
norm_eps = 1e-06

VMEM = pl.BlockSpec(memory_space=pltpu.VMEM)
SMEM = pl.BlockSpec(memory_space=pltpu.SMEM)
HBM = pl.BlockSpec(memory_space=pltpu.HBM)
ANY = pl.BlockSpec(memory_space=pl.ANY)


def layer_norm(values, gain, shift):
    centre = values - jnp.mean(values, axis=-1, keepdims=True)
    spread = jnp.mean(centre * centre, axis=-1, keepdims=True)
    return centre * lax.rsqrt(spread + layer_eps) * gain + shift


def in_hbm(array):
    return pltpu.with_memory_space_constraint(array, pltpu.HBM)


def swap(value, axis, mask):
    count = lax.axis_size(axis)
    return lax.ppermute(value, axis, [(i, i ^ mask) for i in range(count)])


def matmul(left, right):
    return jnp.dot(left, right, preferred_element_type=F32)


def params(mib):
    return pltpu.CompilerParams(vmem_limit_bytes=mib * MIB)


def after(value, *others):
    return lax.optimization_barrier((value,) + others)[0]


def load_kernel(states, w, w_out, mine, w_here, half, sems):
    part = half.shape[0]
    first = pl.multiple_of((lax.axis_index("req") & 1) * part, part)
    copies = [
        pltpu.make_async_copy(source, target, sems.at[number])
        for number, (source, target) in enumerate(
            (
                (w_out.at[pl.ds(first, part)], half),
                (states.at[lax.axis_index("tp") & 1], mine),
                (w, w_here),
            )
        )
    ]
    for copy in copies:
        copy.start()
    for copy in copies:
        copy.wait()


def load(states, w, w_out):
    return pl.pallas_call(
        load_kernel,
        out_shape=(
            jax.ShapeDtypeStruct(states.shape[1:], BF16),
            jax.ShapeDtypeStruct(w.shape, BF16),
            jax.ShapeDtypeStruct((w_out.shape[0] // 2, w_out.shape[1]), BF16),
        ),
        in_specs=[HBM] * 3,
        out_specs=(VMEM, VMEM, VMEM),
        scratch_shapes=[pltpu.SemaphoreType.DMA((3,))],
        compiler_params=params(6),
        cost_estimate=NO_COST,
        name="load",
    )(in_hbm(states), in_hbm(w), in_hbm(w_out))


def first_attention_kernel(lengths, mine, s1, s2, s3, w, b, out, text, parts, bias):
    core = lax.axis_index("tp") & 1
    text[...] = jnp.concatenate([mine[...], s1[core], s2[core], s3[core]])
    for which in range(3):
        project(which, text, w, b, parts)
    attend(lengths, parts, bias, out)


def second_attention_kernel(
    rows_here, lengths, text, w, b, i0, i1, out, numbers, place, rounds, parts, bias
):
    plan_rows(0, rows_here, (i0, i1), numbers, place, rounds)
    for which in range(3):
        project(which, text, w, b, parts)
    attend(lengths, parts, bias, out)


def project(which, text, w, b, parts):
    parts[which] = (matmul(text[...], w[which]) + b[which : which + 1, :]).astype(BF16)


def attend(lengths, parts, bias, out):
    rank = lax.axis_index("tp")
    length = lengths[rank & 1]
    _, seq_len, wide = parts.shape
    share = seq_len // 4

    def position(index):
        return ((index // share) ^ rank) * share + index % share

    row_pos = position(lax.broadcasted_iota(I32, (seq_len, 1), 0))
    col_pos = position(lax.broadcasted_iota(I32, (1, seq_len), 1))
    keep = (jnp.abs(row_pos - col_pos) <= WINDOW // 2) & (col_pos < length)
    bias[...] = jnp.where(keep, F32(0.0), F32(-1e30))
    ones = jnp.ones((seq_len, 128), BF16)
    low = lax.broadcasted_iota(I32, (1, 128), 1) < HEAD_DIM
    scale = jnp.asarray(HEAD_DIM**-0.5, BF16)
    for pair in range(wide // 128):
        lanes = slice(pair * 128, (pair + 1) * 128)
        k_pair = parts[1, :, lanes]
        v_ones = jnp.concatenate([parts[2, :, lanes], ones], axis=1)
        for block in range(2):
            rows = slice(2 * block * share, 2 * (block + 1) * share)
            q_pair = parts[0, rows, lanes] * scale
            zero = jnp.zeros((), BF16)
            q_heads = jnp.concatenate(
                [jnp.where(low, q_pair, zero), jnp.where(low, zero, q_pair)]
            )
            logits = lax.dot_general(
                q_heads, k_pair, (((1,), (1,)), ((), ())), preferred_element_type=F32
            )
            masked = bias[rows, :]
            logits = logits + jnp.concatenate([masked, masked])
            top = jnp.max(logits, axis=-1, keepdims=True)
            expo = jnp.exp(logits - top).astype(BF16)
            summed = matmul(expo, v_ones)
            found = summed[:, :128] / summed[:, 128:]
            context = jnp.where(low, found[: 2 * share], found[2 * share :])
            context = jnp.where(row_pos[rows] < length, context, F32(0.0))
            out[rows, lanes] = context.astype(BF16)


def attention_scratch(seq_len, wide):
    return [pltpu.VMEM((3, seq_len, wide), BF16), pltpu.VMEM((seq_len, seq_len), F32)]


def first_attention(lengths, blocks, w, b):
    share, width = blocks[0].shape
    wide = w.shape[2]
    return pl.pallas_call(
        first_attention_kernel,
        out_shape=(
            jax.ShapeDtypeStruct((4 * share, wide), BF16),
            jax.ShapeDtypeStruct((4 * share, width), BF16),
        ),
        in_specs=[SMEM] + [VMEM] * 6,
        out_specs=(VMEM, VMEM),
        scratch_shapes=attention_scratch(4 * share, wide),
        compiler_params=params(12),
        cost_estimate=NO_COST,
        name="attention_own",
    )(in_hbm(lengths), *blocks, w, in_hbm(b))


def second_attention(lengths, text, w, b, ids, rows_here):
    seq_len = text.shape[0]
    wide = w.shape[2]
    groups, each = ids[0].shape
    return pl.pallas_call(
        functools.partial(second_attention_kernel, rows_here),
        out_shape=(
            jax.ShapeDtypeStruct((seq_len, wide), BF16),
            jax.ShapeDtypeStruct((2, groups * SLOTS), I32),
            jax.ShapeDtypeStruct((groups * SLOTS, 2 * each), BF16),
            jax.ShapeDtypeStruct((1,), I32),
        ),
        in_specs=[SMEM] + [VMEM] * 5,
        out_specs=(VMEM, VMEM, VMEM, SMEM),
        scratch_shapes=attention_scratch(seq_len, wide),
        compiler_params=params(12),
        cost_estimate=cost(6),
        name="attention_partner",
    )(in_hbm(lengths), text, w, b, *ids)


def joined(first, second):
    swapped = (lax.axis_index("req") & 1) != 0
    low = jnp.where(swapped, second[...], first[...])
    high = jnp.where(swapped, first[...], second[...])
    return jnp.concatenate([low, high])


def project_first_kernel(
    text, here, w, b, numbers, index, out, keep, send,
    chosen, tiles, rows, sems, sem,
):
    copy = pltpu.make_async_copy(numbers, chosen, sem)
    copy.start()
    copy.wait()
    finish_rows = fetch_rows(chosen, index, tiles, rows, sems)
    out[...] = matmul(here[...], w[...]) + (text[...].astype(F32) + b[...])
    finish_rows(keep, send)


def project_first(text, here, w, b_out, numbers, index_rows):
    seq_len, width = text.shape
    slots = numbers.shape[1]
    half = jax.ShapeDtypeStruct((slots // 2, width), BF16)
    return pl.pallas_call(
        project_first_kernel,
        out_shape=(jax.ShapeDtypeStruct((seq_len, width), F32), half, half),
        in_specs=[VMEM] * 5 + [HBM],
        out_specs=(VMEM, VMEM, VMEM),
        scratch_shapes=fetch_scratch(slots, width),
        compiler_params=params(12 + slots // 16),
        cost_estimate=cost(1),
        name="project_first",
    )(text, here, w, b_out, numbers, in_hbm(index_rows))


def project_second_kernel(base, context, w, there, half_0, half_1, out):
    half = base.shape[0] // 2
    w_there = joined(half_0, half_1)
    for number in range(2):
        span = slice(number * half, (number + 1) * half)
        other = slice((1 - number) * half, (2 - number) * half)
        total = matmul(context[span, :], w[...]) + matmul(there[other, :], w_there)
        out[span, :] = base[span, :] + total


def project_second(base, context, w, there, halves):
    return pl.pallas_call(
        project_second_kernel,
        out_shape=jax.ShapeDtypeStruct(base.shape, F32),
        in_specs=[VMEM] * 6,
        out_specs=VMEM,
        input_output_aliases={0: 0},
        compiler_params=params(12),
        cost_estimate=cost(1),
        name="project_second",
    )(base, context, w, there, *halves)


def feed_kernel(
    keep_rest, base, c3, half_0, half_1, gain, shift, b0, b1, b_down,
    up_own, up_partner, down_own, down_partner, out, up_buf, down_buf, act, sems,
):
    hidden = up_own.shape[1]
    up_copy = pltpu.make_async_copy(up_own, up_buf, sems.at[0])
    down_copy = pltpu.make_async_copy(down_own, down_buf, sems.at[1])
    up_copy.start()
    down_copy.start()
    total = base[...] + matmul(c3[...], joined(half_0, half_1))
    normed = layer_norm(total, gain[...], shift[...]).astype(BF16)
    step = 512
    for part, (weight, bias) in enumerate(((up_partner, b1), (up_buf, b0))):
        if part == 1:
            up_copy.wait()
        for low in range(0, hidden, step):
            lanes = slice(low, low + step)
            up = matmul(normed, weight[:, lanes]) + bias[:, lanes]
            activated = 0.5 * up * (1.0 + lax.erf(up * F32(0.5**0.5)))
            act[:, part * hidden + low : part * hidden + low + step] = activated.astype(BF16)
    down = matmul(act[:, :hidden], down_partner[...])
    down_copy.wait()
    down = down + matmul(act[:, hidden:], down_buf[...])
    if keep_rest:
        down = down + (normed.astype(F32) + b_down[...])
    out[...] = down.astype(out.dtype)


def feed_forward(keep_rest, base, context, halves, gain, shift, biases, b_down, ups, downs):
    seq_len, width = base.shape
    half = seq_len // 2
    here = 0 if keep_rest else 1
    hidden = ups[0].shape[1]
    heads_wide = context.shape[1]
    base_spec = pl.BlockSpec((half, width), lambda i: (here, 0))
    context_spec = pl.BlockSpec((half, heads_wide), lambda i: (1 - here, 0))
    return pl.pallas_call(
        lambda *refs: feed_kernel(keep_rest, *refs),
        out_shape=jax.ShapeDtypeStruct((half, width), F32 if keep_rest else BF16),
        grid=(1,),
        in_specs=[base_spec, context_spec] + [VMEM] * 7
        + [HBM, VMEM, HBM, VMEM],
        out_specs=VMEM,
        scratch_shapes=[
            pltpu.VMEM((width, hidden), BF16),
            pltpu.VMEM((hidden, width), BF16),
            pltpu.VMEM((half, 2 * hidden), BF16),
            pltpu.SemaphoreType.DMA((2,)),
        ],
        compiler_params=params(20),
        cost_estimate=cost(8),
        name="feed_here" if keep_rest else "feed_there",
    )(base, context, *halves, gain, shift, *biases, b_down, in_hbm(ups[0]), ups[1],
      in_hbm(downs[0]), downs[1])


def finish_kernel(lengths, here, there, gain, shift, own, other, pool):
    rank = lax.axis_index("tp")
    length = lengths[rank & 1]
    share = own.shape[0]
    total = here[...] + there[...].astype(F32)
    hidden = layer_norm(total, gain[...], shift[...]).astype(BF16)
    own[...] = hidden[:share]
    other[...] = hidden[share:]
    index = lax.broadcasted_iota(I32, (2 * share, 1), 0)
    pos = ((index // share) ^ rank) * share + index % share
    valid = jnp.where(pos < length, hidden.astype(F32), F32(0.0))
    pool[...] = jnp.sum(valid, axis=0, keepdims=True)


def finish(lengths, here, there, gain, shift):
    half, width = here.shape
    block = jax.ShapeDtypeStruct((half // 2, width), BF16)
    return pl.pallas_call(
        finish_kernel,
        out_shape=(block, block, jax.ShapeDtypeStruct((1, width), F32)),
        in_specs=[SMEM] + [VMEM] * 4,
        out_specs=(VMEM, VMEM, VMEM),
        compiler_params=params(8),
        cost_estimate=cost(2),
        name="finish",
    )(lengths, here, there, gain, shift)


def score_kernel(
    lengths, pool, pool_core, pool_chip, pool_diag, rows, own, other, out, hidden_out
):
    core = lax.axis_index("tp") & 1
    width = pool.shape[1]
    mine = pool[...] + pool_chip[...]
    theirs = pool_core[...] + pool_diag[...]
    first = jnp.where(core == 0, mine, theirs) / lengths[0].astype(F32)
    second = jnp.where(core == 0, theirs, mine) / lengths[1].astype(F32)
    row = lax.broadcasted_iota(I32, (8, width), 0)
    pooled = jnp.where(row == 0, first, jnp.where(row == 1, second, F32(0.0)))
    scale = lax.rsqrt(jnp.mean(pooled * pooled, axis=-1, keepdims=True) + norm_eps)
    queries = (pooled * scale).astype(BF16)
    found = lax.dot_general(
        queries, rows[...], (((1,), (1,)), ((), ())), preferred_element_type=F32
    )
    each = rows.shape[0] // 2
    out[0:1, :] = found[0:1, :each]
    out[1:2, :] = found[1:2, each:]
    hidden_out[core] = own[...]
    hidden_out[1 - core] = other[...]


def score(lengths, pools, rows, own, other):
    return pl.pallas_call(
        score_kernel,
        out_shape=(
            jax.ShapeDtypeStruct((2, rows.shape[0] // 2), F32),
            jax.ShapeDtypeStruct((2,) + own.shape, BF16),
        ),
        in_specs=[SMEM] + [VMEM] * 7,
        out_specs=(VMEM, VMEM),
        compiler_params=params(8),
        cost_estimate=cost(1),
        name="score",
    )(lengths, *pools, rows, own, other)


def source_order(groups):
    order = [0]
    mask = groups // 2
    while mask >= 4:
        order = order + [entry + mask for entry in order]
        mask //= 2
    return [entry + last for last in range(4) for entry in order]


def as_ones(mask):
    return mask.astype(F32).astype(BF16)


def plan_rows(first_place, rows_here, parts, numbers, place, rounds):
    rank = lax.axis_index("tp")
    group = lax.axis_index("req")
    groups = parts[0].shape[0]
    slots = groups * SLOTS
    ids = jnp.concatenate([part[...] for part in parts], axis=1)
    count = ids.shape[1]
    owner = lax.shift_right_logical(ids, I32(rows_here.bit_length() - 1))
    before = as_ones(
        lax.broadcasted_iota(I32, (count, count), 0)
        < lax.broadcasted_iota(I32, (count, count), 1)
    )
    ones = jnp.ones((count, 128), BF16)
    slot = lax.broadcasted_iota(I32, (SLOTS, 1), 0) + first_place

    mine = owner == group * 4 + rank
    asked = jnp.concatenate(
        [
            (owner[:1] == (group ^ source) * 4 + rank).astype(F32)
            for source in source_order(groups)
        ]
    )
    both = jnp.concatenate([mine.astype(F32), asked]).astype(BF16)
    ranks = matmul(both, before).astype(I32)
    send_rank = jnp.where(mine, ranks[:groups], -1)
    take_rank = jnp.where(asked > 0, ranks[groups:], -1)

    local = jnp.where(mine, ids - (group * 4 + rank) * rows_here, 0)
    high = (local >> 6).astype(F32).astype(BF16)
    low = (local & 63).astype(F32).astype(BF16)
    chosen = jnp.concatenate(
        [(send_rank[k : k + 1] == slot).astype(F32) for k in range(groups)]
    ).astype(BF16)
    spread = (((1,), (1,)), ((), ()))
    wanted = 64.0 * lax.dot_general(high, chosen, spread, preferred_element_type=F32)
    wanted = wanted + lax.dot_general(low, chosen, spread, preferred_element_type=F32)
    counts = matmul(as_ones(mine), jnp.ones((count, slots), BF16))
    own = lax.broadcasted_iota(I32, (groups, slots), 0) == lax.div(
        lax.broadcasted_iota(I32, (groups, slots), 1), I32(SLOTS)
    )
    numbers[0:1, :] = jnp.sum(jnp.where(own, wanted, 0.0), axis=0, keepdims=True).astype(I32)
    counts = jnp.sum(jnp.where(own, counts, 0.0), axis=0, keepdims=True).astype(I32)
    numbers[1:2, :] = counts - first_place

    for k in range(groups):
        place[k * SLOTS : (k + 1) * SLOTS, :] = as_ones(take_rank[k : k + 1] == slot)
    shard = lax.broadcasted_iota(I32, (4 * groups, 1), 0)
    load = jnp.concatenate(
        [(owner[k : k + 1] == shard).astype(F32) for k in range(groups)]
    ).astype(BF16)
    most = jnp.max(matmul(load, ones)).astype(I32)
    rounds[0] = (most + SLOTS - 1) // SLOTS - 1


def fetch_rows(chosen, index, tiles, rows, sems):
    deep = tiles.shape[1]
    slots = tiles.shape[0]
    step = 4

    def tile_copy(slot):
        first = pl.multiple_of((chosen[0, slot] // deep) * deep, deep)
        return pltpu.make_async_copy(index.at[pl.ds(first, deep)], tiles.at[slot], sems.at[slot])

    def start(number, carry):
        for each in range(step):
            tile_copy(number * step + each).start()
        return carry

    def select(number, carry):
        for each in range(step):
            tile_copy(number * step + each).wait()
        for each in range(step):
            source = number * step + each
            line = lax.broadcasted_iota(I32, (deep, 1), 0) == chosen[0, source] % deep
            row = jnp.where(line, tiles[source].astype(F32), F32(0.0))
            rows[pl.ds(source, 1), :] = jnp.sum(row, axis=0, keepdims=True)
        return carry

    def each_group(action):
        def one(number, carry):
            first = number * (SLOTS // step)
            left = jnp.clip(chosen[1, number * SLOTS], 0, SLOTS)
            return lax.fori_loop(first, first + (left + step - 1) // step, action, carry)

        lax.fori_loop(0, slots // SLOTS, one, 0)

    rows[...] = jnp.zeros_like(rows)
    each_group(start)

    def finish_rows(keep, send):
        each_group(select)
        keep[...] = rows[: slots // 2, :].astype(BF16)
        send[...] = rows[slots // 2 :, :].astype(BF16)

    return finish_rows


def take_kernel(
    number, i0, i1, index, keep, send, place, rounds, numbers, chosen, tiles, rows,
    sems, sem,
):
    plan_rows(number[0] * SLOTS, index.shape[0], (i0, i1), numbers, place, rounds)
    copy = pltpu.make_async_copy(numbers, chosen, sem)
    copy.start()
    copy.wait()
    fetch_rows(chosen, index, tiles, rows, sems)(keep, send)


def fetch_scratch(slots, width):
    return [
        pltpu.SMEM((2, slots), I32),
        pltpu.VMEM((slots, 16, width), BF16),
        pltpu.VMEM((slots, width), F32),
        pltpu.SemaphoreType.DMA((slots,)),
        pltpu.SemaphoreType.DMA,
    ]


def take_rows(number, ids, index_rows):
    groups, each = ids[0].shape
    slots = groups * SLOTS
    width = index_rows.shape[1]
    half = jax.ShapeDtypeStruct((slots // 2, width), BF16)
    return pl.pallas_call(
        take_kernel,
        out_shape=(
            half,
            half,
            jax.ShapeDtypeStruct((slots, 2 * each), BF16),
            jax.ShapeDtypeStruct((1,), I32),
        ),
        in_specs=[SMEM] + [VMEM] * 2 + [HBM],
        out_specs=(VMEM, VMEM, VMEM, SMEM),
        scratch_shapes=[pltpu.VMEM((2, slots), I32)] + fetch_scratch(slots, width),
        compiler_params=params(8 + slots // 16),
        cost_estimate=NO_COST,
        name="take_rows",
    )(number, *ids, in_hbm(index_rows))


def place_kernel(place, h0, h1, h2, h3, out):
    received = jnp.concatenate([h0[...], h1[...], h2[...], h3[...]])
    chosen = lax.dot_general(
        place[...], received, (((0,), (0,)), ((), ())), preferred_element_type=F32
    )
    out[...] = chosen.astype(BF16)


def place_rows(place, received):
    return pl.pallas_call(
        place_kernel,
        out_shape=jax.ShapeDtypeStruct((place.shape[1], received[0].shape[1]), BF16),
        in_specs=[VMEM] * 5,
        out_specs=VMEM,
        compiler_params=params(8),
        cost_estimate=NO_COST,
        name="place_rows",
    )(place, *received)


def masks(axis):
    mask = 1
    while mask < lax.axis_size(axis):
        yield mask
        mask *= 2


def row_exchange(ids, index_rows, place, rounds):
    width = index_rows.shape[1]

    def gathered(keep, send, place, gates=((), (), ())):
        keep = keep.reshape(1, -1, SLOTS, width)
        send = send.reshape(1, -1, SLOTS, width)
        held = None
        for mask in list(masks("req"))[:1:-1]:
            if held is not None:
                keep, send = held[:, :mask], held[:, mask:]
            other = swap(send, "req", mask)
            if mask == 4:
                other = after(other, *gates[0])
            held = jnp.concatenate([keep, other])
        others = [swap(held[:, mask], "req", mask) for mask in (1, 2, 3)]
        others = list(after(tuple(others), *gates[1]))
        held = [part.reshape(-1, width) for part in [held[:, 0]] + others]
        found = place_rows(place, held)
        found = after(found, *gates[2]).reshape(4, -1, width)
        parts = [swap(found[place], "tp", mask) for place, mask in ((1, 2), (2, 1), (3, 3))]
        return found[0] + parts[0] + parts[1] + parts[2]

    def one_more(state):
        number, total = state
        keep, send, place, _ = take_rows(number.reshape(1), ids, index_rows)
        return number - 1, total + gathered(keep, send, place)

    def further(rows, *gate):
        left = after(rounds, *gate)[0]
        return lax.while_loop(lambda state: state[0] > 0, one_more, (left, rows))[1]

    return lambda keep, send, *gates: gathered(keep, send, place, gates), further


def per_device(
    states,
    lengths,
    w_qkv,
    b_qkv,
    w_out,
    b_out,
    ln1_gain,
    ln1_shift,
    w_up,
    b_up,
    w_down,
    b_down,
    ln2_gain,
    ln2_shift,
    index_rows,
    cand_ids,
):
    from_core = swap(states, "tp", 1)
    w_qkv_t = w_qkv.transpose(1, 0, 2)
    w_qkv_p = swap(w_qkv_t, "tp", 1)
    b_qkv_p = swap(b_qkv, "tp", 1)
    b_up_p = swap(b_up, "tp", 1)

    held = jnp.concatenate(
        [cand_ids.reshape(1, -1), swap(cand_ids, "tp", 2).reshape(1, -1)], axis=1
    )
    from_chip = swap(after(states, held), "tp", 2)
    for mask in masks("req"):
        other = swap(held, "req", mask)
        if mask * 2 == lax.axis_size("req"):
            mine, w_here, w_half = load(states, w_qkv_t, after(w_out, held))
            other, mine = lax.optimization_barrier((other, mine))
        held = jnp.concatenate([held, other])
    from_chip, held, from_core, w_qkv_p, b_qkv_p, b_up_p = lax.optimization_barrier(
        (from_chip, held, from_core, w_qkv_p, b_qkv_p, b_up_p)
    )
    w_out_p = swap(after(w_out, from_chip), "tp", 1)
    from_diag = swap(from_chip, "tp", 1)
    blocks = (mine, from_core, from_chip, from_diag)
    ids = (held, swap(held, "tp", 1))
    w_up_p = swap(after(w_up, from_diag, w_out_p, *ids), "tp", 1)

    w_x0 = swap(w_half, "tp", 2)

    blocks, ids, w_out_p = lax.optimization_barrier((blocks, ids, w_out_p))
    context_0, text = first_attention(lengths, blocks, w_here, b_qkv)
    context_0x = swap(context_0, "tp", 2)
    context_1, numbers, place, rounds = second_attention(
        lengths, after(text, w_up_p), w_qkv_p, b_qkv_p, ids, index_rows.shape[0]
    )
    context_1x = swap(context_1, "tp", 2)
    w_down_p = swap(after(w_down, w_x0, context_0x, context_1), "tp", 1)
    w_x1 = swap(after(w_x0, context_1), "req", 1)

    base, keep, send = project_first(
        text, after(context_0, context_0x), w_out, b_out[None], numbers, index_rows
    )
    w_d0 = swap(after(w_x0, base), "tp", 1)
    w_d1 = swap(after(w_x1, base), "tp", 1)
    base = project_second(base, context_1, w_out_p, context_0x, (w_x0, w_x1))
    gathered, further = row_exchange(ids, index_rows, place, rounds)
    common = (
        context_1x, (w_d0, w_d1), ln1_gain[None], ln1_shift[None],
        (b_up[None], b_up_p[None]), b_down[None], (w_up, w_up_p),
        (w_down, w_down_p),
    )
    down_there = feed_forward(False, base, *common)
    down_x = swap(down_there, "tp", 2)
    down_here = feed_forward(True, after(base, down_there), *common)
    down_x = after(down_x, down_here)
    hidden, hidden_other, pool = finish(
        lengths, down_here, down_x, ln2_gain[None], ln2_shift[None]
    )

    rows = gathered(keep, send, (down_there,), (down_here,), ())
    pools = (pool,) + tuple(swap(pool, "tp", mask) for mask in (1, 2, 3))
    hidden_p = swap(hidden_other, "tp", 1)
    rows = further(after(rows, *pools), *pools)
    scores, hidden_out = score(lengths, pools, rows, hidden, hidden_p)
    return (hidden_out, scores)


def solution(mesh):
    placed = (
        P("req", "tp", None),
        P("req"),
        P(None, None, "tp"),
        P(None, "tp"),
        P("tp", None),
        P(),
        P(),
        P(),
        P(None, "tp"),
        P("tp"),
        P("tp", None),
        P(),
        P(),
        P(),
        P(("req", "tp"), None),
        P("req", "tp"),
    )
    return jax.shard_map(
        per_device,
        mesh=mesh,
        in_specs=placed,
        out_specs=(P("req", "tp", None), P("req", "tp")),
        check_vma=False,
    )
```
